32 devices in a mesh: groups: 2 (over y), shard: 4 (over z), head: 2 (over x), sub: 2 (over core).
Axes of the slice: x: 2, y: 2, z: 4, core: 2. Of those that a mesh axis runs over, the one named last changes fastest.
Arguments:
- grid_features: bfloat16 [64, 64, 1024], P(('groups', 'shard', 'sub'), None, 'head'), parts along dimension 0, may hold values from -6 to 6
- owners: int32 [64, 1], P(('groups', 'shard', 'sub')), parts along dimension 0, may hold values from 0 to 3; in each aligned block of 4 rows (0 to 3, 4 to 7, ...) at most 2 rows name the same one
- adjacency: int32 [64, 8], P(('groups', 'shard', 'sub')), parts along dimension 0, may hold values from 0 to 15, all different within a row
- mesh_nodes: bfloat16 [2048, 1024], P(('groups', 'shard', 'sub')), parts along dimension 0, may hold values from -130 to 130
- norm_gain: float32 [1024], replicated, may hold values from 0.1 to 1.9
- query_weight: bfloat16 [1024, 1024], P(None, 'head'), may hold values from -0.15625 to 0.15625
- key_weight: bfloat16 [1024, 1024], P(None, 'head'), may hold values from -0.15625 to 0.15625
- value_weight: bfloat16 [1024, 1024], P(None, 'head'), may hold values from -0.1875 to 0.1875
- output_weight: bfloat16 [1024, 1024], P('head'), may hold values from -0.1875 to 0.1875
- up_weight: bfloat16 [1024, 4096], P(None, 'head'), may hold values from -0.1875 to 0.1875
- down_weight: bfloat16 [4096, 1024], P('head'), may hold values from -0.09375 to 0.09375
Outputs:
- decoded: bfloat16 [128, 64, 1024], P(('groups', 'shard', 'sub'), None, 'head'), parts along dimension 0
The draws below stay inside these ranges and needn't reach their ends.
There are 2 independent parts, one for each index of `groups`. The reference program is written for one: setup_inputs(seed, part) draws one part's arguments, and reference() takes and returns one part's arrays. A program takes and returns all parts, laid end to end along the dimension named above; an argument that names none is the same for every part. Nothing has to cross between parts.
Inputs may be any that keep to these rules, and one draw needn't show every extreme that they name: `owners`: within the 4 blocks of one device at most 2 have the same owner, and in every draw some device has exactly 2 blocks of one owner. `adjacency`: each grid block names 8 different mesh blocks, and every mesh block is named by some grid block.
All inputs are finite; a program needn't handle non-finite values.
Results may differ from the reference program's by a relative error of at most 0.011.
Values may be sent and summed in bfloat16 or wider, within the bound.
No kernel may reach another device: no remote copies, remote signals or barrier semaphores. Data moves between devices by JAX's collectives and lax.ppermute only.
A program may use at most 128 MiB of HBM per device.

```python
import math
import jax
import jax.numpy as jnp
import numpy as np
from jax import lax

D = 1024
HEADS = 16
HEAD_DIM = 64
FF = 4096
BLOCK = 64
K_ADJ = 8
CAP = 2
GBLK_DEV = 4
GBLOCKS = 32
OUT_BLOCKS = 64
MBLOCKS = 16
N_SHARD = 4
N_HEAD = 2
N_SUB = 2


def draw_grid_features(key, part):
    key = jax.random.fold_in(key, 1)
    first = jax.random.fold_in(key, 0)
    entries = jnp.clip(jax.random.normal(first, (GBLOCKS, BLOCK, D), jnp.float32), -6.0, 6.0)
    return entries.astype(jnp.bfloat16)


def draw_mesh_nodes(key, part):
    key = jax.random.fold_in(key, 2)
    first = jax.random.fold_in(key, 0)
    entries = jnp.clip(jax.random.normal(first, (MBLOCKS, BLOCK, D), jnp.float32), -6.0, 6.0)
    return entries.reshape(MBLOCKS * BLOCK, D).astype(jnp.bfloat16)


def draw_query_weight(key, part):
    key = jax.random.fold_in(key, 3)
    bound = 5.0 * D ** (-0.5)
    entries = jnp.clip(jax.random.normal(key, (D, D), jnp.float32) * D ** (-0.5), -bound, bound)
    return entries.astype(jnp.bfloat16)


def draw_key_weight(key, part):
    key = jax.random.fold_in(key, 4)
    bound = 5.0 * D ** (-0.5)
    own_part = jnp.clip(jax.random.normal(key, (D, D), jnp.float32) * D ** (-0.5), -bound, bound)
    entries = own_part
    return entries.astype(jnp.bfloat16)


def block_levels(stream_key, shape, pieces, least, top_value):
    factor_of = 1.0
    for dim, parts in pieces:
        heights = jax.random.uniform(jax.random.fold_in(jax.random.fold_in(stream_key, 6), dim), (parts,), jnp.float32, least / len(pieces), top_value / len(pieces))
        factor_of = factor_of * jnp.repeat(jnp.exp(heights), shape[dim] // parts).reshape((-1,) + (1,) * (len(shape) - 1 - dim))
    return factor_of


def picks_of(own_key, rows, count, top, lift):
    ranking = jax.random.permutation(jax.random.fold_in(own_key, 1), count)
    favour = ranking
    for power in range(3):
        favour = favour * favour // count
    favour = favour * lift // count
    chance = jax.random.randint(jax.random.fold_in(own_key, 2), (rows, count), 0, 4096) + favour
    fixed_rows = jax.random.permutation(jax.random.fold_in(own_key, 3), rows)[jnp.arange(count) % rows]
    chance = jnp.where(jnp.arange(rows)[:, None] == fixed_rows[None, :], 1 << 14, chance)
    priority = chance * count + jnp.arange(count)
    return lax.top_k(priority.astype(jnp.int32), top)[1].astype(jnp.int32)


def deal_out(stream_key, own, number, rows, amount, top, limit, slope):
    sequence = jax.random.permutation(stream_key, amount)
    crowded, usual = shares(amount, rows * top, limit, slope, True), shares(amount, rows * top, limit, slope, False)
    places = jnp.arange(amount)

    def named(lengths, rotation):
        used = int((lengths > 0).sum())
        fixed = max(1, used // 4)
        passed = fixed + (places - fixed + rotation * (used - fixed)) % max(1, amount - fixed)
        return jnp.zeros((amount,), jnp.int32).at[sequence[jnp.where(places < fixed, places, passed)]].set(jnp.asarray(lengths, jnp.int32))

    lengths = jnp.where(number % 4 == 0, named(crowded, number // 4), named(usual, number - number // 4 - 1))
    mixed = jax.random.permutation(jax.random.fold_in(own, 3), amount)
    giver, sink = mixed[0:amount // 2 * 2:2], mixed[1:amount // 2 * 2:2]
    slack = jnp.minimum(lengths[giver] - 1, limit - lengths[sink]) // 2
    slack = jnp.where((giver == sequence[0]) | (sink == sequence[0]) | (lengths[sink] == 0), 0, jnp.maximum(slack, 0))
    passed = jax.random.randint(jax.random.fold_in(own, 4), (amount // 2,), 0, 1 << 20) % (slack + 1)
    lengths = lengths.at[giver].add(-passed).at[sink].add(passed)
    labels = jnp.searchsorted(jnp.cumsum(lengths), jnp.arange(rows * top), side="right").astype(jnp.int32)
    table = labels.reshape(top, rows).T
    table = table[jax.random.permutation(jax.random.fold_in(own, 1), rows)]
    rotation = jax.random.randint(jax.random.fold_in(own, 2), (rows, 1), 0, top)
    return jnp.take_along_axis(table, (jnp.arange(top)[None, :] + rotation) % top, axis=1)


def shares(count, total, most, slope, full):
    loads = [(1 << 20) // math.isqrt(grade ** slope) + 1 for grade in range(1, count + 1)]
    largest = most if full else min(most, max(-(-total // count), total * loads[0] // sum(loads)))
    least = 1 if total - largest >= count - 1 else 0
    counts, spare = [largest] + [least] * (count - 1), total - largest - least * (count - 1)
    while spare > 0:
        movable = [i for i in range(1, count) if counts[i] < largest] or [i for i in range(1, count) if counts[i] < most]
        whole, remaining = sum([loads[i] for i in movable]), spare
        for i in movable:
            extra = min(most - counts[i], max(1, remaining * loads[i] // whole), spare)
            counts[i] = counts[i] + extra
            spare = spare - extra
    return np.array(counts)


def noise(stream_key, extent, spread, reach, pieces=(), held_as=jnp.bfloat16):
    drawn = spread * jax.random.normal(stream_key, extent, jnp.float32)
    if pieces:
        drawn = drawn * block_levels(stream_key, extent, pieces, -0.22, 0.18)
    return jnp.clip(drawn, -reach, reach).astype(held_as)


def setup_inputs(seed: int = 0, part: int = 0) -> dict:
    splits = jax.random.split(jax.random.key(seed), 12)
    part_keys = jax.random.split(jax.random.fold_in(splits[11], part), 12)
    grid_features = draw_grid_features(jax.random.fold_in(jax.random.fold_in(splits[11], part), 71), part)
    owners_keys = jax.random.split(jax.random.fold_in(part_keys[1], 1), GBLOCKS // GBLK_DEV)
    owners_turns = jax.random.permutation(jax.random.fold_in(part_keys[1], 3), GBLOCKS // GBLK_DEV)
    owners = jax.vmap(lambda own, number: deal_out(jax.random.fold_in(part_keys[1], 2), own, number, GBLK_DEV, N_SHARD, 1, CAP, 2))(owners_keys, owners_turns).reshape((GBLOCKS, 1))
    adjacency = picks_of(part_keys[2], GBLOCKS, MBLOCKS, K_ADJ, 0)
    mesh_nodes = draw_mesh_nodes(jax.random.fold_in(jax.random.fold_in(splits[11], part), 71), part)
    norm_gain = jnp.clip(1.0 + 0.18 * jax.random.normal(splits[4], (D,), jnp.float32), 0.1, 1.9)
    query_weight = draw_query_weight(jax.random.fold_in(splits[11], 71), part)
    key_weight = draw_key_weight(jax.random.fold_in(splits[11], 71), part)
    value_weight = noise(splits[7], (D, D), D ** -0.5, 0.1875, ((1, 2),))
    output_weight = noise(splits[8], (D, D), D ** -0.5, 0.1875, ((0, 2),))
    up_weight = noise(splits[9], (D, FF), D ** -0.5, 0.1875, ((1, 2),))
    down_weight = noise(splits[10], (FF, D), FF ** -0.5, 0.09375, ((0, 2),))
    return dict(grid_features=grid_features, owners=owners, adjacency=adjacency, mesh_nodes=mesh_nodes, norm_gain=norm_gain, query_weight=query_weight, key_weight=key_weight, value_weight=value_weight, output_weight=output_weight, up_weight=up_weight, down_weight=down_weight)


epsilon = 1e-05

def attend(queries, key_table, value_table, chosen):
    count = chosen.shape[0]
    picked_keys = key_table[chosen].reshape(count, -1, HEADS, HEAD_DIM).astype(jnp.float32)
    picked_values = value_table[chosen].reshape(count, -1, HEADS, HEAD_DIM).astype(jnp.float32)
    scores = jnp.einsum('gqhe,gkhe->ghqk', queries.astype(jnp.float32), picked_keys) * HEAD_DIM ** (-0.5)
    highest = lax.optimization_barrier(jnp.max(scores, axis=-1, keepdims=True))
    weights = jnp.exp(scores - highest)
    weights = (weights / lax.optimization_barrier(jnp.sum(weights, axis=-1, keepdims=True))).astype(jnp.bfloat16)
    result = jnp.einsum('ghqk,gkhe->gqhe', weights.astype(jnp.float32), picked_values)
    return result.astype(jnp.bfloat16)

def reference(grid_features, owners, adjacency, mesh_nodes, norm_gain, query_weight, key_weight, value_weight, output_weight, up_weight, down_weight):
    key_table = jnp.dot(mesh_nodes, key_weight, preferred_element_type=jnp.float32).astype(jnp.bfloat16)
    key_table = key_table.reshape(MBLOCKS, BLOCK, HEADS, HEAD_DIM)
    value_table = jnp.dot(mesh_nodes, value_weight, preferred_element_type=jnp.float32).astype(jnp.bfloat16)
    value_table = value_table.reshape(MBLOCKS, BLOCK, HEADS, HEAD_DIM)
    blocks_each = math.gcd(GBLOCKS, 8)
    out_grouped = output_weight.reshape(N_HEAD, D // N_HEAD, D).astype(jnp.float32)
    down_grouped = down_weight.reshape(N_HEAD, FF // N_HEAD, D).astype(jnp.float32)

    def decode(operands):
        arrived, chosen = operands
        values_f = arrived.astype(jnp.float32)
        average = lax.optimization_barrier(jnp.mean(values_f, axis=-1, keepdims=True))
        centered = values_f - average
        variance = lax.optimization_barrier(jnp.mean(centered * centered, axis=-1, keepdims=True))
        normed = (centered * lax.rsqrt(variance + epsilon) * norm_gain).astype(jnp.bfloat16)
        flattened = normed.reshape(-1, D)
        queries = jnp.dot(flattened, query_weight, preferred_element_type=jnp.float32).astype(jnp.bfloat16)
        queries = queries.reshape(blocks_each, BLOCK, HEADS, HEAD_DIM)
        attended = attend(queries, key_table, value_table, chosen).reshape(-1, N_HEAD, D // N_HEAD)
        hidden = jax.nn.gelu(jnp.dot(flattened, up_weight, preferred_element_type=jnp.float32), approximate=False)
        hidden = hidden.astype(jnp.bfloat16).reshape(-1, N_HEAD, FF // N_HEAD)
        partial_sums = jnp.einsum('rgc,gcd->rgd', attended.astype(jnp.float32), out_grouped)
        partial_sums = partial_sums + jnp.einsum('rgc,gcd->rgd', hidden.astype(jnp.float32), down_grouped)
        rounded = lax.optimization_barrier(partial_sums.astype(jnp.bfloat16)).astype(jnp.float32)
        summed = values_f.reshape(-1, D) + lax.optimization_barrier(jnp.sum(rounded, axis=1))
        return summed.astype(jnp.bfloat16).reshape(blocks_each, BLOCK, D)
    steps_count = GBLOCKS // blocks_each
    updated = lax.map(decode, (grid_features.reshape(steps_count, blocks_each, BLOCK, D), adjacency.reshape(steps_count, blocks_each, K_ADJ)))
    updated = updated.reshape(GBLOCKS, BLOCK, D)
    device_count = N_SHARD * N_SUB
    owner_grid = owners[:, 0].reshape(device_count, GBLK_DEV)
    position = jnp.arange(GBLK_DEV, dtype=jnp.int32)
    earlier = (owner_grid[:, :, None] == owner_grid[:, None, :]) & (position[None, None, :] < position[None, :, None])
    ranked = lax.optimization_barrier(jnp.sum(earlier.astype(jnp.int32), axis=2))
    device_ids = jnp.arange(device_count, dtype=jnp.int32)[:, None]
    shard_ids = device_ids // N_SUB
    sub_ids = device_ids % N_SUB
    target = ((owner_grid * N_SUB + sub_ids) * N_SHARD + shard_ids) * CAP + ranked
    decoded = jnp.zeros((OUT_BLOCKS, BLOCK, D), jnp.bfloat16)
    return decoded.at[target.reshape(-1).astype(jnp.int32)].set(updated)
```

```python
import functools
import math

import jax
import jax.numpy as jnp
from jax import lax
from jax.experimental import pallas as pl
from jax.experimental.pallas import tpu as pltpu
from jax.sharding import PartitionSpec as P

D = 1024
HEAD_DIM = 64
CAP = 2
BLOCK = 64
QUAD = 4
WIDE = QUAD * HEAD_DIM
MIB = 1 << 20


epsilon = 1e-05


def dot(a, b):
    return jnp.dot(a, b, preferred_element_type=jnp.float32)


def gelu(x):
    return 0.5 * x * (1.0 + lax.erf(x * (2.0**-0.5)))


def whole(space):
    return pl.BlockSpec(memory_space=space)


def mlp_kernel(
    own, other, gain, wq, wup, wdn, q_out, mlp_out, x_s, wq_s, wup_s, wdn_s, x_sem, w_sem
):
    h = lax.axis_index("head")
    half = own.shape[1]
    units = wup.shape[1]
    chunk = units // wup_s.shape[0]
    mine = pl.ds(pl.multiple_of(h * half, half), half)
    theirs = pl.ds(pl.multiple_of((1 - h) * half, half), half)
    copies = [
        pltpu.make_async_copy(own, x_s.at[:, mine], x_sem.at[0]),
        pltpu.make_async_copy(other, x_s.at[:, theirs], x_sem.at[1]),
        pltpu.make_async_copy(wq, wq_s, x_sem.at[2]),
    ]
    for copy in copies:
        copy.start()
    ups, downs = [], []
    for c in range(wup_s.shape[0]):
        span = pl.ds(c * chunk, chunk)
        ups.append(pltpu.make_async_copy(wup.at[:, span], wup_s.at[c], w_sem.at[0, c]))
        ups[c].start()
        pair = []
        for part, columns in enumerate((theirs, mine)):
            pair.append(
                pltpu.make_async_copy(
                    wdn.at[span, columns],
                    wdn_s.at[span, pl.ds(part * half, half)],
                    w_sem.at[1 + part, c],
                )
            )
            pair[part].start()
        downs.append(pair)
    copies[0].wait()
    copies[1].wait()
    x = x_s[...].astype(jnp.float32)
    centered = x - jnp.mean(x, axis=-1, keepdims=True)
    variance = jnp.mean(centered * centered, axis=-1, keepdims=True)
    normed = (centered * lax.rsqrt(variance + epsilon) * gain[...]).astype(jnp.bfloat16)
    copies[2].wait()
    q_out[...] = dot(normed, wq_s[...]).astype(jnp.bfloat16)
    for c in range(wup_s.shape[0]):
        ups[c].wait()
        hidden = gelu(dot(normed, wup_s[c])).astype(jnp.bfloat16)
        downs[c][0].wait()
        downs[c][1].wait()
        term = dot(hidden, wdn_s[c * chunk : (c + 1) * chunk, :])
        if c == 0:
            mlp_out[...] = term
        else:
            mlp_out[...] += term


def run_mlp(own, other, gain, wq, wup, wdn):
    rows, half = own.shape
    width = wq.shape[0]
    units = wup.shape[1]
    parts = 4
    return pl.pallas_call(
        mlp_kernel,
        out_shape=(
            jax.ShapeDtypeStruct((rows, wq.shape[1]), jnp.bfloat16),
            jax.ShapeDtypeStruct((rows, width), jnp.float32),
        ),
        in_specs=[
            whole(pl.ANY),
            whole(pl.ANY),
            whole(pltpu.VMEM),
            whole(pl.ANY),
            whole(pl.ANY),
            whole(pl.ANY),
        ],
        out_specs=(whole(pltpu.VMEM), whole(pltpu.VMEM)),
        scratch_shapes=[
            pltpu.VMEM((rows, width), jnp.bfloat16),
            pltpu.VMEM(wq.shape, jnp.bfloat16),
            pltpu.VMEM((parts, width, units // parts), jnp.bfloat16),
            pltpu.VMEM((units, width), jnp.bfloat16),
            pltpu.SemaphoreType.DMA((3,)),
            pltpu.SemaphoreType.DMA((3, parts)),
        ],
        compiler_params=pltpu.CompilerParams(vmem_limit_bytes=32 * MIB),
        cost_estimate=pl.CostEstimate(
            flops=2 * rows * width * (wq.shape[1] + 2 * units),
            bytes_accessed=2 * width * (wq.shape[1] + 2 * units),
            transcendentals=rows * units,
        ),
        name="mlp",
    )(own, other, gain, wq, wup, wdn)


def project_kernel(own, *refs):
    pieces, (wk, wv, out, rows_s, w_s, p_sem, w_sem) = refs[:-7], refs[-7:]
    width = wk.shape[1]
    weights = [
        pltpu.make_async_copy(wk, w_s.at[:, pl.ds(0, width)], w_sem.at[0]),
        pltpu.make_async_copy(wv, w_s.at[:, pl.ds(width, width)], w_sem.at[1]),
    ]
    for copy in weights:
        copy.start()
    copies = [pltpu.make_async_copy(own, rows_s.at[pl.ds(0, 2 * BLOCK), :], p_sem.at[0])]
    for i, piece in enumerate(pieces):
        copies.append(
            pltpu.make_async_copy(
                piece, rows_s.at[pl.ds((2 + i) * BLOCK, BLOCK), :], p_sem.at[1 + i]
            )
        )
    for copy in copies:
        copy.start()
    for copy in weights:
        copy.wait()
    for copy in copies:
        copy.wait()
    out[...] = dot(rows_s[...], w_s[...]).astype(jnp.bfloat16)


def run_project(own, pieces, wk, wv):
    rows = own.shape[0] + len(pieces) * BLOCK
    width = wk.shape[1]
    return pl.pallas_call(
        project_kernel,
        out_shape=jax.ShapeDtypeStruct((rows, 2 * width), jnp.bfloat16),
        in_specs=[whole(pl.ANY)] * (3 + len(pieces)),
        out_specs=whole(pltpu.VMEM),
        scratch_shapes=[
            pltpu.VMEM((rows, own.shape[1]), jnp.bfloat16),
            pltpu.VMEM((wk.shape[0], 2 * width), jnp.bfloat16),
            pltpu.SemaphoreType.DMA((1 + len(pieces),)),
            pltpu.SemaphoreType.DMA((2,)),
        ],
        compiler_params=pltpu.CompilerParams(vmem_limit_bytes=24 * MIB),
        cost_estimate=pl.CostEstimate(
            flops=4 * rows * wk.shape[0] * width,
            bytes_accessed=4 * wk.shape[0] * width + 4 * rows * wk.shape[0],
            transcendentals=0,
        ),
        name="project",
    )(own, *pieces, wk, wv)


def attend_kernel(
    shards, adjacency, q, kv_mine, kv_sibling, mlp, wo, send, keep, table, att_s, wo_s, t_sem, w_sem
):
    s = lax.axis_index("shard")
    h = lax.axis_index("head")
    u = lax.axis_index("sub")
    half = wo.shape[0]
    per_core = kv_mine.shape[0]
    tables = [
        pltpu.make_async_copy(kv_mine, table.at[pl.ds(0, per_core)], t_sem.at[0]),
        pltpu.make_async_copy(kv_sibling, table.at[pl.ds(per_core, per_core)], t_sem.at[1]),
    ]
    for copy in tables:
        copy.start()
    weights = []
    for part, head in enumerate((1 - h, h)):
        columns = pl.ds(pl.multiple_of(head * half, half), half)
        weights.append(
            pltpu.make_async_copy(
                wo.at[:, columns], wo_s.at[:, pl.ds(part * half, half)], w_sem.at[part]
            )
        )
        weights[part].start()
    rows_of = lax.broadcasted_iota(jnp.int32, (WIDE, WIDE), 0) // HEAD_DIM
    lanes_of = lax.broadcasted_iota(jnp.int32, (WIDE, WIDE), 1) // HEAD_DIM
    diagonal = rows_of == lanes_of
    lane_head = lax.broadcasted_iota(jnp.int32, (BLOCK, WIDE), 1) // HEAD_DIM
    scale = HEAD_DIM**-0.5 * math.log2(math.e)
    for copy in tables:
        copy.wait()
    for b in range(adjacency.shape[0]):
        places = []
        for j in range(adjacency.shape[1]):
            m = adjacency[b, j]
            part = lax.rem(m, 2)
            core = lax.rem(m // 2, 2)
            distance = lax.rem(s - m // 4 + shards, shards)
            part = jnp.where(distance == 0, part, part ^ h)
            places.append((core ^ u) * per_core + distance * 2 + part)
        for g in range(half // WIDE):
            columns = slice(g * WIDE, (g + 1) * WIDE)
            keys = jnp.concatenate([table[p, :, columns] for p in places], axis=0)
            vcolumns = slice(half + g * WIDE, half + (g + 1) * WIDE)
            values = jnp.concatenate([table[p, :, vcolumns] for p in places], axis=0)
            q_rows = q[b * BLOCK : (b + 1) * BLOCK, columns]
            stacked = jnp.concatenate([q_rows] * QUAD, axis=0)
            stacked = jnp.where(diagonal, stacked, jnp.zeros_like(stacked))
            scores = lax.dot_general(
                stacked, keys, (((1,), (1,)), ((), ())), preferred_element_type=jnp.float32
            )
            highest = jnp.max(scores, axis=-1, keepdims=True)
            weights_f = jnp.exp2((scores - highest) * scale)
            total = jnp.sum(weights_f, axis=-1, keepdims=True)
            probs = (weights_f * (1.0 / total)).astype(jnp.bfloat16)
            mixed = dot(probs, values)
            merged = mixed[0:BLOCK, :]
            for i in range(1, QUAD):
                merged = jnp.where(lane_head == i, mixed[i * BLOCK : (i + 1) * BLOCK, :], merged)
            att_s[b * BLOCK : (b + 1) * BLOCK, columns] = merged.astype(jnp.bfloat16)
    for copy in weights:
        copy.wait()
    branch = mlp[...] + dot(att_s[...], wo_s[...])
    send[...] = branch[:, :half].astype(jnp.bfloat16)
    keep[...] = branch[:, half:].astype(jnp.bfloat16)


def run_attend(adjacency, q, kv_mine, kv_sibling, mlp, wo, shards):
    rows, half = q.shape
    nodes = 2 * kv_mine.shape[0] * BLOCK
    part = jax.ShapeDtypeStruct((rows, half), jnp.bfloat16)
    return pl.pallas_call(
        functools.partial(attend_kernel, shards),
        out_shape=(part, part),
        in_specs=[
            whole(pltpu.SMEM),
            whole(pltpu.VMEM),
            whole(pl.ANY),
            whole(pl.ANY),
            whole(pltpu.VMEM),
            whole(pl.ANY),
        ],
        out_specs=(whole(pltpu.VMEM), whole(pltpu.VMEM)),
        scratch_shapes=[
            pltpu.VMEM((2 * kv_mine.shape[0],) + kv_mine.shape[1:], jnp.bfloat16),
            pltpu.VMEM((rows, half), jnp.bfloat16),
            pltpu.VMEM(wo.shape, jnp.bfloat16),
            pltpu.SemaphoreType.DMA((2,)),
            pltpu.SemaphoreType.DMA((2,)),
        ],
        compiler_params=pltpu.CompilerParams(vmem_limit_bytes=32 * MIB),
        cost_estimate=pl.CostEstimate(
            flops=2 * rows * half * (D + 8 * 8 * BLOCK),
            bytes_accessed=4 * nodes * half + 2 * half * D + 4 * rows * D,
            transcendentals=rows * 8 * BLOCK * half // HEAD_DIM,
        ),
        name="attend",
    )(adjacency, q, kv_mine, kv_sibling, mlp, wo)


def combine_kernel(owners, grid_features, keep, received, *outs):
    s = lax.axis_index("shard")
    shards = len(outs)
    count = grid_features.shape[0]
    half = keep.shape[1]
    names = [owners[t, 0] for t in range(count)]
    for d in range(shards):
        target = lax.rem(s + d, shards)
        for j in range(CAP):
            outs[d][j] = jnp.zeros((BLOCK, half), jnp.bfloat16)
        seen = jnp.int32(0)
        for t in range(count):
            hit = names[t] == target
            rank = seen

            @pl.when(hit)
            def _():
                rows = slice(t * BLOCK, (t + 1) * BLOCK)
                partials = keep[rows, :].astype(jnp.float32) + received[rows, :].astype(jnp.float32)
                updated = grid_features[t].astype(jnp.float32) + partials
                outs[d][rank] = updated.astype(jnp.bfloat16)

            seen = seen + hit.astype(jnp.int32)


def run_combine(owners, grid_features, keep, received, shards):
    count, rows, half = grid_features.shape
    slot = jax.ShapeDtypeStruct((CAP, rows, half), jnp.bfloat16)
    return pl.pallas_call(
        combine_kernel,
        out_shape=(slot,) * shards,
        in_specs=[whole(pltpu.SMEM)] + [whole(pltpu.VMEM)] * 3,
        out_specs=(whole(pltpu.VMEM),) * shards,
        compiler_params=pltpu.CompilerParams(vmem_limit_bytes=16 * MIB),
        cost_estimate=pl.CostEstimate(
            flops=3 * count * rows * half,
            bytes_accessed=2 * rows * half * (3 * count + CAP * shards),
            transcendentals=0,
        ),
        name="combine",
    )(owners, grid_features, keep, received)


def place_kernel(*refs):
    arrived, (out, sem) = refs[:-2], refs[-2:]
    s = lax.axis_index("shard")
    shards = len(arrived)
    copies = []
    for d in range(shards):
        source = lax.rem(s - d + shards, shards)
        copies.append(
            pltpu.make_async_copy(arrived[d], out.at[pl.ds(source * CAP, CAP)], sem.at[d])
        )
        copies[d].start()
    for copy in copies:
        copy.wait()


def run_place(arrived):
    shards = len(arrived)
    shape = arrived[0].shape
    return pl.pallas_call(
        place_kernel,
        out_shape=jax.ShapeDtypeStruct((shards * CAP,) + shape[1:], jnp.bfloat16),
        in_specs=[whole(pl.ANY)] * shards,
        out_specs=whole(pl.ANY),
        scratch_shapes=[pltpu.SemaphoreType.DMA((shards,))],
        name="place",
    )(*arrived)


def shifted(x, distance, size):
    return lax.ppermute(x, "shard", [(i, (i + distance) % size) for i in range(size)])


def swapped(x, axis):
    return lax.ppermute(x, axis, [(0, 1), (1, 0)])


def paired(
    grid_features,
    owners,
    adjacency,
    mesh_nodes,
    norm_gain,
    query_weight,
    key_weight,
    value_weight,
    output_weight,
    up_weight,
    down_weight,
):
    shards = lax.axis_size("shard")
    count, rows, half = grid_features.shape
    flat = grid_features.reshape(count * rows, half)
    mesh_half = lax.dynamic_slice_in_dim(mesh_nodes, lax.axis_index("head") * BLOCK, BLOCK, 0)
    other = swapped(flat, "head")
    pieces = []
    for d in range(1, shards):
        piece = shifted(mesh_half, d, shards)
        pieces += [piece, swapped(piece, "head")]
    queries, mlp = run_mlp(
        flat, other, norm_gain.reshape(1, -1), query_weight, up_weight, down_weight
    )
    kv_mine = run_project(mesh_nodes, pieces, key_weight, value_weight)
    kv_sibling = swapped(kv_mine, "sub")
    blocked = (2 * shards, BLOCK, 2 * half)
    send, keep = run_attend(
        adjacency,
        queries,
        kv_mine.reshape(blocked),
        kv_sibling.reshape(blocked),
        mlp,
        output_weight,
        shards,
    )
    received = swapped(send, "head")
    slots = run_combine(owners, grid_features, keep, received, shards)
    arrived = [slots[0]] + [shifted(slots[d], d, shards) for d in range(1, shards)]
    return run_place(arrived)


def attend_plain(queries, key_table, value_table, chosen, scaling):
    count = chosen.shape[0]
    picked_keys = key_table[chosen]
    picked_keys = picked_keys.reshape(count, -1, picked_keys.shape[3], picked_keys.shape[4])
    picked_values = value_table[chosen]
    picked_values = picked_values.reshape(count, -1, picked_values.shape[3], picked_values.shape[4])
    scores = (
        jnp.einsum("gqhe,gkhe->ghqk", queries, picked_keys, preferred_element_type=jnp.float32)
        * scaling
    )
    highest = jnp.max(scores, axis=-1, keepdims=True)
    weights = jnp.exp(scores - highest)
    weights = (weights / jnp.sum(weights, axis=-1, keepdims=True)).astype(jnp.bfloat16)
    result = jnp.einsum(
        "ghqk,gkhe->gqhe", weights, picked_values, preferred_element_type=jnp.float32
    )
    return result.astype(jnp.bfloat16)


def general(
    grid_features,
    owners,
    adjacency,
    mesh_nodes,
    norm_gain,
    query_weight,
    key_weight,
    value_weight,
    output_weight,
    up_weight,
    down_weight,
):
    shard_count = lax.axis_size("shard")
    head_count = lax.axis_size("head")
    local_blocks, block_rows, feature_share = grid_features.shape
    slots = shard_count * CAP
    owner_col = owners[:, 0]
    position = jnp.arange(local_blocks, dtype=jnp.int32)
    earlier = (owner_col[:, None] == owner_col[None, :]) & (position[None, :] < position[:, None])
    target = owner_col * CAP + jnp.sum(earlier.astype(jnp.int32), axis=1)
    dispatch = (target[:, None] == jnp.arange(slots, dtype=jnp.int32)[None, :]).astype(jnp.bfloat16)
    offset = lax.axis_index("head") * (D // head_count)
    projected = jnp.stack(
        (
            jnp.dot(mesh_nodes, key_weight, preferred_element_type=jnp.float32).astype(
                jnp.bfloat16
            ),
            jnp.dot(mesh_nodes, value_weight, preferred_element_type=jnp.float32).astype(
                jnp.bfloat16
            ),
        )
    )
    tables = lax.all_gather(projected, ("shard", "sub"), axis=1, tiled=True)
    head_local = query_weight.shape[1] // HEAD_DIM
    key_table = tables[0].reshape(-1, block_rows, head_local, HEAD_DIM)
    value_table = tables[1].reshape(-1, block_rows, head_local, HEAD_DIM)
    send_lists = jnp.full((slots, adjacency.shape[1]), -1, jnp.int32).at[target].set(adjacency)
    send_lists = send_lists.reshape(shard_count, CAP, -1)
    complete = lax.all_gather(grid_features, "head", axis=2, tiled=True)
    outgoing = jnp.einsum(
        "gs,gbd->sbd", dispatch, complete, preferred_element_type=jnp.float32
    ).astype(jnp.bfloat16)
    arrived, lists = (
        lax.all_to_all(
            outgoing.reshape(shard_count, CAP, block_rows, D),
            "shard",
            split_axis=0,
            concat_axis=0,
            tiled=True,
        ),
        lax.all_to_all(send_lists, "shard", split_axis=0, concat_axis=0, tiled=True),
    )
    arrived = arrived.reshape(slots, block_rows, D)
    residual = lax.dynamic_slice_in_dim(arrived, offset, D // head_count, 2)
    lists = lists.reshape(slots, -1)
    count = arrived.shape[0]
    values_f = arrived.astype(jnp.float32)
    average = jnp.mean(values_f, axis=-1, keepdims=True)
    centered = values_f - average
    variance = jnp.mean(centered * centered, axis=-1, keepdims=True)
    normed = (centered * lax.rsqrt(variance + epsilon) * norm_gain).astype(jnp.bfloat16)
    flattened = normed.reshape(-1, D)
    queries = jnp.dot(flattened, query_weight, preferred_element_type=jnp.float32).astype(
        jnp.bfloat16
    )
    blocks_each = math.gcd(count, max(1, 512 // block_rows))
    steps_count = count // blocks_each
    queries = queries.reshape(steps_count, blocks_each, block_rows, head_local, HEAD_DIM)

    def attend_step(operands):
        return attend_plain(operands[0], key_table, value_table, operands[1], HEAD_DIM ** (-0.5))

    attended = lax.map(
        attend_step, (queries, jnp.maximum(lists, 0).reshape(steps_count, blocks_each, -1))
    )
    attended = attended.reshape(-1, head_local * HEAD_DIM)
    hidden = jax.nn.gelu(
        jnp.dot(flattened, up_weight, preferred_element_type=jnp.float32), approximate=False
    ).astype(jnp.bfloat16)
    branch = jnp.dot(attended, output_weight, preferred_element_type=jnp.float32)
    branch = branch + jnp.dot(hidden, down_weight, preferred_element_type=jnp.float32)
    branch = branch.reshape(count, block_rows, D)
    reduced = lax.psum_scatter(
        branch.astype(jnp.bfloat16), "head", scatter_dimension=2, tiled=True
    ).astype(jnp.float32)
    occupied = lists[:, 0] >= 0
    summed = residual.astype(jnp.float32) + reduced
    return jnp.where(occupied[:, None, None], summed, 0.0).astype(jnp.bfloat16)


def local(grid_features, owners, adjacency, mesh_nodes, *parameters):
    pairs = lax.axis_size("head") == 2 and lax.axis_size("sub") == 2
    small = grid_features.shape[0] <= 4 and mesh_nodes.shape[0] == 2 * BLOCK
    if pairs and small and grid_features.shape[1] == BLOCK:
        return paired(grid_features, owners, adjacency, mesh_nodes, *parameters)
    return general(grid_features, owners, adjacency, mesh_nodes, *parameters)


def solution(mesh):
    return jax.shard_map(
        local,
        mesh=mesh,
        in_specs=(
            P(("groups", "shard", "sub"), None, "head"),
            P(("groups", "shard", "sub"), None),
            P(("groups", "shard", "sub"), None),
            P(("groups", "shard", "sub"), None),
            P(),
            P(None, "head"),
            P(None, "head"),
            P(None, "head"),
            P("head", None),
            P(None, "head"),
            P("head", None),
        ),
        out_specs=P(("groups", "shard", "sub"), None, "head"),
        check_vma=False,
    )
```

```python
import math

import jax
import jax.numpy as jnp
from jax import lax
from jax.experimental import pallas as pl
from jax.experimental.pallas import tpu as pltpu
from jax.sharding import PartitionSpec as P

D = 1024
HEAD_DIM = 64
CAP = 2
BLOCK = 64
QUAD = 4
WIDE = QUAD * HEAD_DIM
MIB = 1 << 20


epsilon = 1e-05


def dot(a, b):
    return jnp.dot(a, b, preferred_element_type=jnp.float32)


def gelu(x):
    return 0.5 * x * (1.0 + lax.erf(x * (2.0**-0.5)))


def in_hbm(x):
    return pltpu.with_memory_space_constraint(x, pltpu.HBM)


def whole(space):
    return pl.BlockSpec(memory_space=space)


def mlp_kernel(
    own, other, gain, wq, wup, wdn, q_out, mlp_out, x_s, gain_s, wq_s, wup_s, wdn_s, x_sem, w_sem
):
    h = lax.axis_index("head")
    half = own.shape[1]
    units = wup.shape[1]
    chunk = units // wup_s.shape[0]
    mine = pl.ds(pl.multiple_of(h * half, half), half)
    theirs = pl.ds(pl.multiple_of((1 - h) * half, half), half)
    copies = [
        pltpu.make_async_copy(own, x_s.at[:, mine], x_sem.at[0]),
        pltpu.make_async_copy(other, x_s.at[:, theirs], x_sem.at[1]),
        pltpu.make_async_copy(wq, wq_s, x_sem.at[2]),
        pltpu.make_async_copy(gain, gain_s, x_sem.at[3]),
    ]
    for copy in copies:
        copy.start()
    ups, downs = [], []
    for c in range(wup_s.shape[0]):
        span = pl.ds(c * chunk, chunk)
        ups.append(pltpu.make_async_copy(wup.at[:, span], wup_s.at[c], w_sem.at[0, c]))
        ups[c].start()
        pair = []
        for part, columns in enumerate((theirs, mine)):
            pair.append(
                pltpu.make_async_copy(
                    wdn.at[span, columns],
                    wdn_s.at[span, pl.ds(part * half, half)],
                    w_sem.at[1 + part, c],
                )
            )
            pair[part].start()
        downs.append(pair)
    copies[0].wait()
    copies[1].wait()
    copies[3].wait()
    x = x_s[...].astype(jnp.float32)
    centered = x - jnp.mean(x, axis=-1, keepdims=True)
    variance = jnp.mean(centered * centered, axis=-1, keepdims=True)
    normed = (centered * lax.rsqrt(variance + epsilon) * gain_s[...]).astype(jnp.bfloat16)
    copies[2].wait()
    q_out[...] = dot(normed, wq_s[...]).astype(jnp.bfloat16)
    for c in range(wup_s.shape[0]):
        ups[c].wait()
        hidden = gelu(dot(normed, wup_s[c])).astype(jnp.bfloat16)
        downs[c][0].wait()
        downs[c][1].wait()
        term = dot(hidden, wdn_s[c * chunk : (c + 1) * chunk, :])
        if c == 0:
            mlp_out[...] = term
        else:
            mlp_out[...] += term


def run_mlp(own, other, gain, wq, wup, wdn):
    rows, half = own.shape
    width = wq.shape[0]
    units = wup.shape[1]
    parts = 4
    return pl.pallas_call(
        mlp_kernel,
        out_shape=(
            jax.ShapeDtypeStruct((rows, wq.shape[1]), jnp.bfloat16),
            jax.ShapeDtypeStruct((rows, width), jnp.float32),
        ),
        in_specs=[
            whole(pltpu.HBM),
            whole(pl.ANY),
            whole(pltpu.HBM),
            whole(pltpu.HBM),
            whole(pltpu.HBM),
            whole(pltpu.HBM),
        ],
        out_specs=(whole(pltpu.VMEM), whole(pltpu.VMEM)),
        scratch_shapes=[
            pltpu.VMEM((rows, width), jnp.bfloat16),
            pltpu.VMEM(gain.shape, jnp.float32),
            pltpu.VMEM(wq.shape, jnp.bfloat16),
            pltpu.VMEM((parts, width, units // parts), jnp.bfloat16),
            pltpu.VMEM((units, width), jnp.bfloat16),
            pltpu.SemaphoreType.DMA((4,)),
            pltpu.SemaphoreType.DMA((3, parts)),
        ],
        compiler_params=pltpu.CompilerParams(vmem_limit_bytes=16 * MIB),
        cost_estimate=pl.CostEstimate(
            flops=2 * rows * width * (wq.shape[1] + 2 * units),
            bytes_accessed=2 * width * (wq.shape[1] + 2 * units),
            transcendentals=rows * units,
        ),
        name="mlp",
    )(in_hbm(own), other, in_hbm(gain), in_hbm(wq), in_hbm(wup), in_hbm(wdn))


def project_kernel(own, *refs):
    pieces, (wk, wv, out, rows_s, w_s, p_sem, w_sem) = refs[:-7], refs[-7:]
    width = wk.shape[1]
    weights = [
        pltpu.make_async_copy(wk, w_s.at[:, pl.ds(0, width)], w_sem.at[0]),
        pltpu.make_async_copy(wv, w_s.at[:, pl.ds(width, width)], w_sem.at[1]),
    ]
    for copy in weights:
        copy.start()
    copies = []
    first = 0
    for i, piece in enumerate((own, *pieces)):
        rows = piece.shape[0]
        copies.append(
            pltpu.make_async_copy(piece, rows_s.at[pl.ds(first, rows), :], p_sem.at[i])
        )
        copies[i].start()
        first += rows
    for copy in weights:
        copy.wait()
    for copy in copies:
        copy.wait()
    out[...] = dot(rows_s[...], w_s[...]).astype(jnp.bfloat16)


def run_project(own, pieces, wk, wv):
    rows = own.shape[0] + sum(piece.shape[0] for piece in pieces)
    width = wk.shape[1]
    return pl.pallas_call(
        project_kernel,
        out_shape=jax.ShapeDtypeStruct((rows, 2 * width), jnp.bfloat16),
        in_specs=[whole(pltpu.HBM)]
        + [whole(pl.ANY)] * len(pieces)
        + [whole(pltpu.HBM)] * 2,
        out_specs=whole(pltpu.VMEM),
        scratch_shapes=[
            pltpu.VMEM((rows, own.shape[1]), jnp.bfloat16),
            pltpu.VMEM((wk.shape[0], 2 * width), jnp.bfloat16),
            pltpu.SemaphoreType.DMA((1 + len(pieces),)),
            pltpu.SemaphoreType.DMA((2,)),
        ],
        compiler_params=pltpu.CompilerParams(vmem_limit_bytes=12 * MIB),
        cost_estimate=pl.CostEstimate(
            flops=4 * rows * wk.shape[0] * width,
            bytes_accessed=4 * wk.shape[0] * width + 4 * rows * wk.shape[0],
            transcendentals=0,
        ),
        name="project",
    )(in_hbm(own), *pieces, in_hbm(wk), in_hbm(wv))


def attend_kernel(
    adjacency, q, kv_mine, kv_sibling, mlp, wo, send, keep, table, att_s, wo_s, t_sem, w_sem
):
    s = lax.axis_index("shard")
    h = lax.axis_index("head")
    u = lax.axis_index("sub")
    half = wo.shape[0]
    per_core = kv_mine.shape[0]
    tables = [
        pltpu.make_async_copy(kv_mine, table.at[pl.ds(0, per_core)], t_sem.at[0]),
        pltpu.make_async_copy(kv_sibling, table.at[pl.ds(per_core, per_core)], t_sem.at[1]),
    ]
    for copy in tables:
        copy.start()
    weights = []
    for part, head in enumerate((1 - h, h)):
        columns = pl.ds(pl.multiple_of(head * half, half), half)
        weights.append(
            pltpu.make_async_copy(
                wo.at[:, columns], wo_s.at[:, pl.ds(part * half, half)], w_sem.at[part]
            )
        )
        weights[part].start()
    rows_of = lax.broadcasted_iota(jnp.int32, (WIDE, WIDE), 0) // HEAD_DIM
    lanes_of = lax.broadcasted_iota(jnp.int32, (WIDE, WIDE), 1) // HEAD_DIM
    diagonal = rows_of == lanes_of
    lane_head = lax.broadcasted_iota(jnp.int32, (BLOCK, WIDE), 1) // HEAD_DIM
    scale = HEAD_DIM**-0.5 * math.log2(math.e)
    for copy in tables:
        copy.wait()
    for b in range(adjacency.shape[0]):
        places = []
        for j in range(adjacency.shape[1]):
            m = adjacency[b, j]
            part = lax.rem(m, 2)
            core = lax.rem(m // 2, 2)
            distance = s ^ (m // 4)
            part = jnp.where(distance <= 1, part, part ^ h)
            places.append((core ^ u) * per_core + distance * 2 + part)
        for g in range(half // WIDE):
            columns = slice(g * WIDE, (g + 1) * WIDE)
            keys = jnp.concatenate([table[p, :, columns] for p in places], axis=0)
            vcolumns = slice(half + g * WIDE, half + (g + 1) * WIDE)
            values = jnp.concatenate([table[p, :, vcolumns] for p in places], axis=0)
            q_rows = q[b * BLOCK : (b + 1) * BLOCK, columns]
            stacked = jnp.concatenate([q_rows] * QUAD, axis=0)
            stacked = jnp.where(diagonal, stacked, jnp.zeros_like(stacked))
            scores = lax.dot_general(
                stacked, keys, (((1,), (1,)), ((), ())), preferred_element_type=jnp.float32
            )
            highest = jnp.max(scores, axis=-1, keepdims=True)
            weights_f = jnp.exp2((scores - highest) * scale)
            total = jnp.sum(weights_f, axis=-1, keepdims=True)
            probs = (weights_f * (1.0 / total)).astype(jnp.bfloat16)
            mixed = dot(probs, values)
            merged = mixed[0:BLOCK, :]
            for i in range(1, QUAD):
                merged = jnp.where(lane_head == i, mixed[i * BLOCK : (i + 1) * BLOCK, :], merged)
            att_s[b * BLOCK : (b + 1) * BLOCK, columns] = merged.astype(jnp.bfloat16)
    for copy in weights:
        copy.wait()
    branch = mlp[...] + dot(att_s[...], wo_s[...])
    send[...] = branch[:, :half].astype(jnp.bfloat16)
    keep[...] = branch[:, half:].astype(jnp.bfloat16)


def run_attend(adjacency, q, kv_mine, kv_sibling, mlp, wo):
    rows, half = q.shape
    nodes = 2 * kv_mine.shape[0] * BLOCK
    part = jax.ShapeDtypeStruct((rows, half), jnp.bfloat16)
    return pl.pallas_call(
        attend_kernel,
        out_shape=(part, part),
        in_specs=[
            whole(pltpu.SMEM),
            whole(pltpu.VMEM),
            whole(pl.ANY),
            whole(pl.ANY),
            whole(pltpu.VMEM),
            whole(pltpu.HBM),
        ],
        out_specs=(whole(pltpu.VMEM), whole(pltpu.VMEM)),
        scratch_shapes=[
            pltpu.VMEM((2 * kv_mine.shape[0],) + kv_mine.shape[1:], jnp.bfloat16),
            pltpu.VMEM((rows, half), jnp.bfloat16),
            pltpu.VMEM(wo.shape, jnp.bfloat16),
            pltpu.SemaphoreType.DMA((2,)),
            pltpu.SemaphoreType.DMA((2,)),
        ],
        compiler_params=pltpu.CompilerParams(vmem_limit_bytes=16 * MIB),
        cost_estimate=pl.CostEstimate(
            flops=2 * rows * half * (D + 8 * 8 * BLOCK),
            bytes_accessed=4 * nodes * half + 2 * half * D + 4 * rows * D,
            transcendentals=rows * 8 * BLOCK * half // HEAD_DIM,
        ),
        name="attend",
    )(adjacency, q, kv_mine, kv_sibling, mlp, in_hbm(wo))


def combine_kernel(owners, grid_features, keep, received, *outs):
    s = lax.axis_index("shard")
    shards = len(outs)
    count = grid_features.shape[0]
    half = keep.shape[1]
    names = [owners[t, 0] for t in range(count)]
    for d in range(shards):
        target = s ^ d
        for j in range(CAP):
            outs[d][j] = jnp.zeros((BLOCK, half), jnp.bfloat16)
        seen = jnp.int32(0)
        for t in range(count):
            hit = names[t] == target
            rank = seen

            @pl.when(hit)
            def _():
                rows = slice(t * BLOCK, (t + 1) * BLOCK)
                partials = keep[rows, :].astype(jnp.float32) + received[rows, :].astype(jnp.float32)
                updated = grid_features[t].astype(jnp.float32) + partials
                outs[d][rank] = updated.astype(jnp.bfloat16)

            seen = seen + hit.astype(jnp.int32)


def run_combine(owners, grid_features, keep, received, shards):
    count, rows, half = grid_features.shape
    slot = jax.ShapeDtypeStruct((CAP, rows, half), jnp.bfloat16)
    return pl.pallas_call(
        combine_kernel,
        out_shape=(slot,) * shards,
        in_specs=[whole(pltpu.SMEM)] + [whole(pltpu.VMEM)] * 3,
        out_specs=(whole(pltpu.VMEM),) * shards,
        compiler_params=pltpu.CompilerParams(vmem_limit_bytes=8 * MIB),
        cost_estimate=pl.CostEstimate(
            flops=3 * count * rows * half,
            bytes_accessed=2 * rows * half * (3 * count + CAP * shards),
            transcendentals=0,
        ),
        name="combine",
    )(owners, grid_features, keep, received)


def place_kernel(*refs):
    arrived, (out, sem) = refs[:-2], refs[-2:]
    s = lax.axis_index("shard")
    shards = len(arrived)
    copies = []
    for d in range(shards):
        source = s ^ d
        copies.append(
            pltpu.make_async_copy(arrived[d], out.at[pl.ds(source * CAP, CAP)], sem.at[d])
        )
        copies[d].start()
    for copy in copies:
        copy.wait()


def run_place(arrived):
    shards = len(arrived)
    shape = arrived[0].shape
    return pl.pallas_call(
        place_kernel,
        out_shape=jax.ShapeDtypeStruct((shards * CAP,) + shape[1:], jnp.bfloat16),
        in_specs=[whole(pltpu.VMEM)] * shards,
        out_specs=whole(pltpu.HBM),
        scratch_shapes=[pltpu.SemaphoreType.DMA((shards,))],
        compiler_params=pltpu.CompilerParams(vmem_limit_bytes=4 * MIB),
        name="place",
    )(*arrived)


def crossed(x, distance, size):
    return lax.ppermute(x, "shard", [(i, i ^ distance) for i in range(size)])


def swapped(x, axis):
    return lax.ppermute(x, axis, [(0, 1), (1, 0)])


def paired(
    grid_features,
    owners,
    adjacency,
    mesh_nodes,
    norm_gain,
    query_weight,
    key_weight,
    value_weight,
    output_weight,
    up_weight,
    down_weight,
):
    shards = lax.axis_size("shard")
    count, rows, half = grid_features.shape
    flat = grid_features.reshape(count * rows, half)
    other = swapped(flat, "head")
    mesh_half = lax.dynamic_slice_in_dim(mesh_nodes, lax.axis_index("head") * BLOCK, BLOCK, 0)
    pieces = [crossed(mesh_nodes, 1, shards)]
    for d in range(2, shards):
        piece = crossed(mesh_half, d, shards)
        pieces += [piece, swapped(piece, "head")]
    queries, mlp = run_mlp(
        flat, other, norm_gain.reshape(1, -1), query_weight, up_weight, down_weight
    )
    queries, mlp, *pieces = lax.optimization_barrier((queries, mlp, *pieces))
    kv_mine = run_project(mesh_nodes, pieces, key_weight, value_weight)
    kv_sibling = swapped(kv_mine, "sub")
    blocked = (2 * shards, BLOCK, 2 * half)
    send, keep = run_attend(
        adjacency,
        queries,
        kv_mine.reshape(blocked),
        kv_sibling.reshape(blocked),
        mlp,
        output_weight,
    )
    received = swapped(send, "head")
    slots = run_combine(owners, grid_features, keep, received, shards)
    arrived = [slots[0]] + [crossed(slots[d], d, shards) for d in range(1, shards)]
    return run_place(arrived)


def attend_plain(queries, key_table, value_table, chosen, scaling):
    count = chosen.shape[0]
    picked_keys = key_table[chosen]
    picked_keys = picked_keys.reshape(count, -1, picked_keys.shape[3], picked_keys.shape[4])
    picked_values = value_table[chosen]
    picked_values = picked_values.reshape(count, -1, picked_values.shape[3], picked_values.shape[4])
    scores = (
        jnp.einsum("gqhe,gkhe->ghqk", queries, picked_keys, preferred_element_type=jnp.float32)
        * scaling
    )
    highest = jnp.max(scores, axis=-1, keepdims=True)
    weights = jnp.exp(scores - highest)
    weights = (weights / jnp.sum(weights, axis=-1, keepdims=True)).astype(jnp.bfloat16)
    result = jnp.einsum(
        "ghqk,gkhe->gqhe", weights, picked_values, preferred_element_type=jnp.float32
    )
    return result.astype(jnp.bfloat16)


def general(
    grid_features,
    owners,
    adjacency,
    mesh_nodes,
    norm_gain,
    query_weight,
    key_weight,
    value_weight,
    output_weight,
    up_weight,
    down_weight,
):
    shard_count = lax.axis_size("shard")
    head_count = lax.axis_size("head")
    local_blocks, block_rows, feature_share = grid_features.shape
    slots = shard_count * CAP
    owner_col = owners[:, 0]
    position = jnp.arange(local_blocks, dtype=jnp.int32)
    earlier = (owner_col[:, None] == owner_col[None, :]) & (position[None, :] < position[:, None])
    target = owner_col * CAP + jnp.sum(earlier.astype(jnp.int32), axis=1)
    dispatch = (target[:, None] == jnp.arange(slots, dtype=jnp.int32)[None, :]).astype(jnp.bfloat16)
    offset = lax.axis_index("head") * (D // head_count)
    projected = jnp.stack(
        (
            jnp.dot(mesh_nodes, key_weight, preferred_element_type=jnp.float32).astype(
                jnp.bfloat16
            ),
            jnp.dot(mesh_nodes, value_weight, preferred_element_type=jnp.float32).astype(
                jnp.bfloat16
            ),
        )
    )
    tables = lax.all_gather(projected, ("shard", "sub"), axis=1, tiled=True)
    head_local = query_weight.shape[1] // HEAD_DIM
    key_table = tables[0].reshape(-1, block_rows, head_local, HEAD_DIM)
    value_table = tables[1].reshape(-1, block_rows, head_local, HEAD_DIM)
    send_lists = jnp.full((slots, adjacency.shape[1]), -1, jnp.int32).at[target].set(adjacency)
    send_lists = send_lists.reshape(shard_count, CAP, -1)
    complete = lax.all_gather(grid_features, "head", axis=2, tiled=True)
    outgoing = jnp.einsum(
        "gs,gbd->sbd", dispatch, complete, preferred_element_type=jnp.float32
    ).astype(jnp.bfloat16)
    arrived, lists = (
        lax.all_to_all(
            outgoing.reshape(shard_count, CAP, block_rows, D),
            "shard",
            split_axis=0,
            concat_axis=0,
            tiled=True,
        ),
        lax.all_to_all(send_lists, "shard", split_axis=0, concat_axis=0, tiled=True),
    )
    arrived = arrived.reshape(slots, block_rows, D)
    residual = lax.dynamic_slice_in_dim(arrived, offset, D // head_count, 2)
    lists = lists.reshape(slots, -1)
    count = arrived.shape[0]
    values_f = arrived.astype(jnp.float32)
    average = jnp.mean(values_f, axis=-1, keepdims=True)
    centered = values_f - average
    variance = jnp.mean(centered * centered, axis=-1, keepdims=True)
    normed = (centered * lax.rsqrt(variance + epsilon) * norm_gain).astype(jnp.bfloat16)
    flattened = normed.reshape(-1, D)
    queries = jnp.dot(flattened, query_weight, preferred_element_type=jnp.float32).astype(
        jnp.bfloat16
    )
    blocks_each = math.gcd(count, max(1, 512 // block_rows))
    steps_count = count // blocks_each
    queries = queries.reshape(steps_count, blocks_each, block_rows, head_local, HEAD_DIM)

    def attend_step(operands):
        return attend_plain(operands[0], key_table, value_table, operands[1], HEAD_DIM ** (-0.5))

    attended = lax.map(
        attend_step, (queries, jnp.maximum(lists, 0).reshape(steps_count, blocks_each, -1))
    )
    attended = attended.reshape(-1, head_local * HEAD_DIM)
    hidden = jax.nn.gelu(
        jnp.dot(flattened, up_weight, preferred_element_type=jnp.float32), approximate=False
    ).astype(jnp.bfloat16)
    branch = jnp.dot(attended, output_weight, preferred_element_type=jnp.float32)
    branch = branch + jnp.dot(hidden, down_weight, preferred_element_type=jnp.float32)
    branch = branch.reshape(count, block_rows, D)
    reduced = lax.psum_scatter(
        branch.astype(jnp.bfloat16), "head", scatter_dimension=2, tiled=True
    ).astype(jnp.float32)
    occupied = lists[:, 0] >= 0
    summed = residual.astype(jnp.float32) + reduced
    return jnp.where(occupied[:, None, None], summed, 0.0).astype(jnp.bfloat16)


def local(grid_features, owners, adjacency, mesh_nodes, *parameters):
    pairs = lax.axis_size("head") == 2 and lax.axis_size("sub") == 2
    pairs = pairs and lax.axis_size("shard") in (2, 4, 8)
    small = grid_features.shape[0] <= 4 and mesh_nodes.shape[0] == 2 * BLOCK
    if pairs and small and grid_features.shape[1] == BLOCK:
        return paired(grid_features, owners, adjacency, mesh_nodes, *parameters)
    return general(grid_features, owners, adjacency, mesh_nodes, *parameters)


def solution(mesh):
    return jax.shard_map(
        local,
        mesh=mesh,
        in_specs=(
            P(("groups", "shard", "sub"), None, "head"),
            P(("groups", "shard", "sub"), None),
            P(("groups", "shard", "sub"), None),
            P(("groups", "shard", "sub"), None),
            P(),
            P(None, "head"),
            P(None, "head"),
            P(None, "head"),
            P("head", None),
            P(None, "head"),
            P("head", None),
        ),
        out_specs=P(("groups", "shard", "sub"), None, "head"),
        check_vma=False,
    )
```

```python
import math

import jax
import jax.numpy as jnp
from jax import lax
from jax.experimental import pallas as pl
from jax.experimental.pallas import tpu as pltpu
from jax.sharding import PartitionSpec as P

D = 1024
HEAD_DIM = 64
CAP = 2
BLOCK = 64
QUAD = 4
WIDE = QUAD * HEAD_DIM
MIB = 1 << 20


epsilon = 1e-05


def dot(a, b):
    return jnp.dot(a, b, preferred_element_type=jnp.float32)


def gelu(x):
    return 0.5 * x * (1.0 + lax.erf(x * (2.0**-0.5)))


def in_hbm(x):
    return pltpu.with_memory_space_constraint(x, pltpu.HBM)


def whole(space):
    return pl.BlockSpec(memory_space=space)


def mlp_kernel(
    own, other, gain, wq, wup, wdn, q_out, mlp_out, x_s, gain_s, wq_s, wup_s, wdn_s, x_sem, w_sem
):
    h = lax.axis_index("head")
    half = own.shape[1]
    units = wup.shape[1]
    chunk = units // wup_s.shape[0]
    mine = pl.ds(pl.multiple_of(h * half, half), half)
    theirs = pl.ds(pl.multiple_of((1 - h) * half, half), half)
    copies = [
        pltpu.make_async_copy(own, x_s.at[:, mine], x_sem.at[0]),
        pltpu.make_async_copy(other, x_s.at[:, theirs], x_sem.at[1]),
        pltpu.make_async_copy(wq, wq_s, x_sem.at[2]),
        pltpu.make_async_copy(gain, gain_s, x_sem.at[3]),
    ]
    for copy in copies:
        copy.start()
    for i in (0, 1, 3):
        copies[i].wait()
    ups, downs = [], []
    for c in range(wup_s.shape[0]):
        span = pl.ds(c * chunk, chunk)
        ups.append(pltpu.make_async_copy(wup.at[:, span], wup_s.at[c], w_sem.at[0, c]))
        ups[c].start()
        pair = []
        for part, columns in enumerate((theirs, mine)):
            pair.append(
                pltpu.make_async_copy(
                    wdn.at[span, columns],
                    wdn_s.at[span, pl.ds(part * half, half)],
                    w_sem.at[1 + part, c],
                )
            )
            pair[part].start()
        downs.append(pair)
    x = x_s[...].astype(jnp.float32)
    centered = x - jnp.mean(x, axis=-1, keepdims=True)
    variance = jnp.mean(centered * centered, axis=-1, keepdims=True)
    normed = (centered * lax.rsqrt(variance + epsilon) * gain_s[...]).astype(jnp.bfloat16)
    copies[2].wait()
    q_out[...] = dot(normed, wq_s[...]).astype(jnp.bfloat16)
    for c in range(wup_s.shape[0]):
        ups[c].wait()
        hidden = gelu(dot(normed, wup_s[c])).astype(jnp.bfloat16)
        downs[c][0].wait()
        downs[c][1].wait()
        term = dot(hidden, wdn_s[c * chunk : (c + 1) * chunk, :])
        if c == 0:
            mlp_out[...] = term
        else:
            mlp_out[...] += term


def run_mlp(own, other, gain, wq, wup, wdn):
    rows, half = own.shape
    width = wq.shape[0]
    units = wup.shape[1]
    parts = 4
    return pl.pallas_call(
        mlp_kernel,
        out_shape=(
            jax.ShapeDtypeStruct((rows, wq.shape[1]), jnp.bfloat16),
            jax.ShapeDtypeStruct((rows, width), jnp.float32),
        ),
        in_specs=[
            whole(pltpu.HBM),
            whole(pl.ANY),
            whole(pltpu.HBM),
            whole(pltpu.HBM),
            whole(pltpu.HBM),
            whole(pltpu.HBM),
        ],
        out_specs=(whole(pltpu.VMEM), whole(pltpu.VMEM)),
        scratch_shapes=[
            pltpu.VMEM((rows, width), jnp.bfloat16),
            pltpu.VMEM(gain.shape, jnp.float32),
            pltpu.VMEM(wq.shape, jnp.bfloat16),
            pltpu.VMEM((parts, width, units // parts), jnp.bfloat16),
            pltpu.VMEM((units, width), jnp.bfloat16),
            pltpu.SemaphoreType.DMA((4,)),
            pltpu.SemaphoreType.DMA((3, parts)),
        ],
        compiler_params=pltpu.CompilerParams(vmem_limit_bytes=16 * MIB),
        cost_estimate=pl.CostEstimate(
            flops=2 * rows * width * (wq.shape[1] + 2 * units),
            bytes_accessed=2 * width * (wq.shape[1] + 2 * units),
            transcendentals=rows * units,
        ),
        name="mlp",
    )(in_hbm(own), other, in_hbm(gain), in_hbm(wq), in_hbm(wup), in_hbm(wdn))


def project_kernel(*refs):
    pieces, (wk, wv, out, rows_s, w_s, p_sem, w_sem) = refs[:-7], refs[-7:]
    width = wk.shape[1]
    weights = [
        pltpu.make_async_copy(wk, w_s.at[:, pl.ds(0, width)], w_sem.at[0]),
        pltpu.make_async_copy(wv, w_s.at[:, pl.ds(width, width)], w_sem.at[1]),
    ]
    for copy in weights:
        copy.start()
    copies = []
    first = 0
    for i, piece in enumerate(pieces):
        rows = piece.shape[0]
        copies.append(
            pltpu.make_async_copy(piece, rows_s.at[pl.ds(first, rows), :], p_sem.at[i])
        )
        copies[i].start()
        first += rows
    for copy in weights:
        copy.wait()
    for copy in copies:
        copy.wait()
    out[...] = dot(rows_s[...], w_s[...]).astype(jnp.bfloat16)


def run_project(pieces, wk, wv):
    rows = sum(piece.shape[0] for piece in pieces)
    depth, width = wk.shape
    return pl.pallas_call(
        project_kernel,
        out_shape=jax.ShapeDtypeStruct((rows, 2 * width), jnp.bfloat16),
        in_specs=[whole(pl.ANY)] * len(pieces) + [whole(pltpu.HBM)] * 2,
        out_specs=whole(pltpu.VMEM),
        scratch_shapes=[
            pltpu.VMEM((rows, depth), jnp.bfloat16),
            pltpu.VMEM((depth, 2 * width), jnp.bfloat16),
            pltpu.SemaphoreType.DMA((len(pieces),)),
            pltpu.SemaphoreType.DMA((2,)),
        ],
        compiler_params=pltpu.CompilerParams(vmem_limit_bytes=12 * MIB),
        cost_estimate=pl.CostEstimate(
            flops=80 * rows * depth * width,
            bytes_accessed=80 * depth * width + 4 * rows * depth,
            transcendentals=0,
        ),
        name="project",
    )(*pieces, in_hbm(wk), in_hbm(wv))


def attend_kernel(
    adjacency, q, mine_a, mine_b, sibling_a, sibling_b, mlp, wo,
    send, keep, table, att_s, wo_s, t_sem, w_sem,
):
    s = lax.axis_index("shard")
    h = lax.axis_index("head")
    u = lax.axis_index("sub")
    half = wo.shape[0]
    per_core = mine_a.shape[0] + mine_b.shape[0]
    tables = []
    first = 0
    for i, part in enumerate((mine_a, mine_b, sibling_a, sibling_b)):
        blocks = part.shape[0]
        tables.append(pltpu.make_async_copy(part, table.at[pl.ds(first, blocks)], t_sem.at[i]))
        tables[i].start()
        first += blocks
    weights = []
    for part, head in enumerate((1 - h, h)):
        columns = pl.ds(pl.multiple_of(head * half, half), half)
        weights.append(
            pltpu.make_async_copy(
                wo.at[:, columns], wo_s.at[:, pl.ds(part * half, half)], w_sem.at[part]
            )
        )
        weights[part].start()
    rows_of = lax.broadcasted_iota(jnp.int32, (WIDE, WIDE), 0) // HEAD_DIM
    lanes_of = lax.broadcasted_iota(jnp.int32, (WIDE, WIDE), 1) // HEAD_DIM
    diagonal = rows_of == lanes_of
    lane_head = lax.broadcasted_iota(jnp.int32, (BLOCK, WIDE), 1) // HEAD_DIM
    scale = HEAD_DIM**-0.5 * math.log2(math.e)
    for copy in tables:
        copy.wait()
    for b in range(adjacency.shape[0]):
        places = []
        for j in range(adjacency.shape[1]):
            m = adjacency[b, j]
            part = lax.rem(m, 2)
            core = lax.rem(m // 2, 2)
            distance = s ^ (m // 4)
            distance = jnp.where(distance <= 1, distance, 2 + ((distance - 2) ^ h))
            places.append((core ^ u) * per_core + distance * 2 + part)
        for g in range(half // WIDE):
            columns = slice(g * WIDE, (g + 1) * WIDE)
            keys = jnp.concatenate([table[p, :, columns] for p in places], axis=0)
            vcolumns = slice(half + g * WIDE, half + (g + 1) * WIDE)
            values = jnp.concatenate([table[p, :, vcolumns] for p in places], axis=0)
            q_rows = q[b * BLOCK : (b + 1) * BLOCK, columns]
            stacked = jnp.concatenate([q_rows] * QUAD, axis=0)
            stacked = jnp.where(diagonal, stacked, jnp.zeros_like(stacked))
            scores = lax.dot_general(
                stacked, keys, (((1,), (1,)), ((), ())), preferred_element_type=jnp.float32
            )
            highest = jnp.max(scores, axis=-1, keepdims=True)
            weights_f = jnp.exp2((scores - highest) * scale)
            total = jnp.sum(weights_f, axis=-1, keepdims=True)
            probs = (weights_f * (1.0 / total)).astype(jnp.bfloat16)
            mixed = dot(probs, values)
            merged = mixed[0:BLOCK, :]
            for i in range(1, QUAD):
                merged = jnp.where(lane_head == i, mixed[i * BLOCK : (i + 1) * BLOCK, :], merged)
            att_s[b * BLOCK : (b + 1) * BLOCK, columns] = merged.astype(jnp.bfloat16)
    for copy in weights:
        copy.wait()
    branch = mlp[...] + dot(att_s[...], wo_s[...])
    send[...] = branch[:, :half].astype(jnp.bfloat16)
    keep[...] = branch[:, half:].astype(jnp.bfloat16)


def run_attend(adjacency, q, tables, mlp, wo):
    rows, half = q.shape
    blocks = sum(part.shape[0] for part in tables)
    part = jax.ShapeDtypeStruct((rows, half), jnp.bfloat16)
    return pl.pallas_call(
        attend_kernel,
        out_shape=(part, part),
        in_specs=[whole(pltpu.SMEM), whole(pltpu.VMEM)]
        + [whole(pl.ANY)] * len(tables)
        + [whole(pltpu.VMEM), whole(pltpu.HBM)],
        out_specs=(whole(pltpu.VMEM), whole(pltpu.VMEM)),
        scratch_shapes=[
            pltpu.VMEM((blocks,) + tables[0].shape[1:], jnp.bfloat16),
            pltpu.VMEM((rows, half), jnp.bfloat16),
            pltpu.VMEM(wo.shape, jnp.bfloat16),
            pltpu.SemaphoreType.DMA((len(tables),)),
            pltpu.SemaphoreType.DMA((2,)),
        ],
        compiler_params=pltpu.CompilerParams(vmem_limit_bytes=16 * MIB),
        cost_estimate=pl.CostEstimate(
            flops=2 * rows * half * (D + 8 * 8 * BLOCK),
            bytes_accessed=4 * blocks * BLOCK * half + 2 * half * D + 4 * rows * D,
            transcendentals=rows * 8 * BLOCK * half // HEAD_DIM,
        ),
        name="attend",
    )(adjacency, q, *tables, mlp, in_hbm(wo))


def combine_kernel(owners, grid_features, keep, received, *outs):
    s = lax.axis_index("shard")
    shards = len(outs)
    count = grid_features.shape[0]
    half = keep.shape[1]
    names = [owners[t, 0] for t in range(count)]
    for d in range(shards):
        target = s ^ d
        for j in range(CAP):
            outs[d][j] = jnp.zeros((BLOCK, half), jnp.bfloat16)
        seen = jnp.int32(0)
        for t in range(count):
            hit = names[t] == target
            rank = seen

            @pl.when(hit)
            def _():
                rows = slice(t * BLOCK, (t + 1) * BLOCK)
                partials = keep[rows, :].astype(jnp.float32) + received[rows, :].astype(jnp.float32)
                updated = grid_features[t].astype(jnp.float32) + partials
                outs[d][rank] = updated.astype(jnp.bfloat16)

            seen = seen + hit.astype(jnp.int32)


def run_combine(owners, grid_features, keep, received, shards):
    count, rows, half = grid_features.shape
    slot = jax.ShapeDtypeStruct((CAP, rows, half), jnp.bfloat16)
    return pl.pallas_call(
        combine_kernel,
        out_shape=(slot,) * shards,
        in_specs=[whole(pltpu.SMEM)] + [whole(pltpu.VMEM)] * 3,
        out_specs=(whole(pltpu.VMEM),) * shards,
        compiler_params=pltpu.CompilerParams(vmem_limit_bytes=8 * MIB),
        cost_estimate=pl.CostEstimate(
            flops=3 * count * rows * half,
            bytes_accessed=2 * rows * half * (3 * count + CAP * shards),
            transcendentals=0,
        ),
        name="combine",
    )(owners, grid_features, keep, received)


def place_kernel(*refs):
    arrived, (out, sem) = refs[:-2], refs[-2:]
    s = lax.axis_index("shard")
    shards = len(arrived)
    copies = []
    for d in range(shards):
        source = s ^ d
        copies.append(
            pltpu.make_async_copy(arrived[d], out.at[pl.ds(source * CAP, CAP)], sem.at[d])
        )
        copies[d].start()
    for copy in copies:
        copy.wait()


def run_place(arrived):
    shards = len(arrived)
    shape = arrived[0].shape
    return pl.pallas_call(
        place_kernel,
        out_shape=jax.ShapeDtypeStruct((shards * CAP,) + shape[1:], jnp.bfloat16),
        in_specs=[whole(pltpu.VMEM)] * shards,
        out_specs=whole(pltpu.HBM),
        scratch_shapes=[pltpu.SemaphoreType.DMA((shards,))],
        compiler_params=pltpu.CompilerParams(vmem_limit_bytes=4 * MIB),
        name="place",
    )(*arrived)


def crossed(x, distance, size):
    return lax.ppermute(x, "shard", [(i, i ^ distance) for i in range(size)])


def fetched(x, size):
    pairs = [(2 * i + h, 2 * (i ^ (2 + h)) + h) for i in range(size) for h in range(2)]
    return lax.ppermute(x, ("shard", "head"), pairs)


def swapped(x, axis):
    return lax.ppermute(x, axis, [(0, 1), (1, 0)])


def paired(
    grid_features,
    owners,
    adjacency,
    mesh_nodes,
    norm_gain,
    query_weight,
    key_weight,
    value_weight,
    output_weight,
    up_weight,
    down_weight,
):
    shards = lax.axis_size("shard")
    count, rows, half = grid_features.shape
    flat = grid_features.reshape(count * rows, half)
    other = swapped(flat, "head")
    far = fetched(mesh_nodes, shards)
    near = crossed(mesh_nodes, 1, shards)
    queries, mlp = run_mlp(
        flat, other, norm_gain.reshape(1, -1), query_weight, up_weight, down_weight
    )
    queries, mlp, far = lax.optimization_barrier((queries, mlp, far))
    farther = swapped(far, "head")
    mine_a = run_project((mesh_nodes, near, far), key_weight, value_weight)
    sibling_a = swapped(mine_a, "sub")
    mine_b = run_project((farther,), key_weight, value_weight)
    sibling_b = swapped(mine_b, "sub")
    tables = [
        table.reshape(-1, BLOCK, 2 * half) for table in (mine_a, mine_b, sibling_a, sibling_b)
    ]
    send, keep = run_attend(adjacency, queries, tables, mlp, output_weight)
    received = swapped(send, "head")
    slots = run_combine(owners, grid_features, keep, received, shards)
    arrived = [slots[0]] + [crossed(slots[d], d, shards) for d in range(1, shards)]
    return run_place(arrived)


def attend_plain(queries, key_table, value_table, chosen, scaling):
    count = chosen.shape[0]
    picked_keys = key_table[chosen]
    picked_keys = picked_keys.reshape(count, -1, picked_keys.shape[3], picked_keys.shape[4])
    picked_values = value_table[chosen]
    picked_values = picked_values.reshape(count, -1, picked_values.shape[3], picked_values.shape[4])
    scores = (
        jnp.einsum("gqhe,gkhe->ghqk", queries, picked_keys, preferred_element_type=jnp.float32)
        * scaling
    )
    highest = jnp.max(scores, axis=-1, keepdims=True)
    weights = jnp.exp(scores - highest)
    weights = (weights / jnp.sum(weights, axis=-1, keepdims=True)).astype(jnp.bfloat16)
    result = jnp.einsum(
        "ghqk,gkhe->gqhe", weights, picked_values, preferred_element_type=jnp.float32
    )
    return result.astype(jnp.bfloat16)


def general(
    grid_features,
    owners,
    adjacency,
    mesh_nodes,
    norm_gain,
    query_weight,
    key_weight,
    value_weight,
    output_weight,
    up_weight,
    down_weight,
):
    shard_count = lax.axis_size("shard")
    head_count = lax.axis_size("head")
    local_blocks, block_rows, feature_share = grid_features.shape
    slots = shard_count * CAP
    owner_col = owners[:, 0]
    position = jnp.arange(local_blocks, dtype=jnp.int32)
    earlier = (owner_col[:, None] == owner_col[None, :]) & (position[None, :] < position[:, None])
    target = owner_col * CAP + jnp.sum(earlier.astype(jnp.int32), axis=1)
    dispatch = (target[:, None] == jnp.arange(slots, dtype=jnp.int32)[None, :]).astype(jnp.bfloat16)
    offset = lax.axis_index("head") * (D // head_count)
    projected = jnp.stack(
        (
            jnp.dot(mesh_nodes, key_weight, preferred_element_type=jnp.float32).astype(
                jnp.bfloat16
            ),
            jnp.dot(mesh_nodes, value_weight, preferred_element_type=jnp.float32).astype(
                jnp.bfloat16
            ),
        )
    )
    tables = lax.all_gather(projected, ("shard", "sub"), axis=1, tiled=True)
    head_local = query_weight.shape[1] // HEAD_DIM
    key_table = tables[0].reshape(-1, block_rows, head_local, HEAD_DIM)
    value_table = tables[1].reshape(-1, block_rows, head_local, HEAD_DIM)
    send_lists = jnp.full((slots, adjacency.shape[1]), -1, jnp.int32).at[target].set(adjacency)
    send_lists = send_lists.reshape(shard_count, CAP, -1)
    complete = lax.all_gather(grid_features, "head", axis=2, tiled=True)
    outgoing = jnp.einsum(
        "gs,gbd->sbd", dispatch, complete, preferred_element_type=jnp.float32
    ).astype(jnp.bfloat16)
    arrived, lists = (
        lax.all_to_all(
            outgoing.reshape(shard_count, CAP, block_rows, D),
            "shard",
            split_axis=0,
            concat_axis=0,
            tiled=True,
        ),
        lax.all_to_all(send_lists, "shard", split_axis=0, concat_axis=0, tiled=True),
    )
    arrived = arrived.reshape(slots, block_rows, D)
    residual = lax.dynamic_slice_in_dim(arrived, offset, D // head_count, 2)
    lists = lists.reshape(slots, -1)
    count = arrived.shape[0]
    values_f = arrived.astype(jnp.float32)
    average = jnp.mean(values_f, axis=-1, keepdims=True)
    centered = values_f - average
    variance = jnp.mean(centered * centered, axis=-1, keepdims=True)
    normed = (centered * lax.rsqrt(variance + epsilon) * norm_gain).astype(jnp.bfloat16)
    flattened = normed.reshape(-1, D)
    queries = jnp.dot(flattened, query_weight, preferred_element_type=jnp.float32).astype(
        jnp.bfloat16
    )
    blocks_each = math.gcd(count, max(1, 512 // block_rows))
    steps_count = count // blocks_each
    queries = queries.reshape(steps_count, blocks_each, block_rows, head_local, HEAD_DIM)

    def attend_step(operands):
        return attend_plain(operands[0], key_table, value_table, operands[1], HEAD_DIM ** (-0.5))

    attended = lax.map(
        attend_step, (queries, jnp.maximum(lists, 0).reshape(steps_count, blocks_each, -1))
    )
    attended = attended.reshape(-1, head_local * HEAD_DIM)
    hidden = jax.nn.gelu(
        jnp.dot(flattened, up_weight, preferred_element_type=jnp.float32), approximate=False
    ).astype(jnp.bfloat16)
    branch = jnp.dot(attended, output_weight, preferred_element_type=jnp.float32)
    branch = branch + jnp.dot(hidden, down_weight, preferred_element_type=jnp.float32)
    branch = branch.reshape(count, block_rows, D)
    reduced = lax.psum_scatter(
        branch.astype(jnp.bfloat16), "head", scatter_dimension=2, tiled=True
    ).astype(jnp.float32)
    occupied = lists[:, 0] >= 0
    summed = residual.astype(jnp.float32) + reduced
    return jnp.where(occupied[:, None, None], summed, 0.0).astype(jnp.bfloat16)


def local(grid_features, owners, adjacency, mesh_nodes, *parameters):
    pairs = lax.axis_size("head") == 2 and lax.axis_size("sub") == 2
    pairs = pairs and lax.axis_size("shard") == 4
    small = grid_features.shape[0] <= 4 and mesh_nodes.shape[0] == 2 * BLOCK
    if pairs and small and grid_features.shape[1] == BLOCK:
        return paired(grid_features, owners, adjacency, mesh_nodes, *parameters)
    return general(grid_features, owners, adjacency, mesh_nodes, *parameters)


def solution(mesh):
    return jax.shard_map(
        local,
        mesh=mesh,
        in_specs=(
            P(("groups", "shard", "sub"), None, "head"),
            P(("groups", "shard", "sub"), None),
            P(("groups", "shard", "sub"), None),
            P(("groups", "shard", "sub"), None),
            P(),
            P(None, "head"),
            P(None, "head"),
            P(None, "head"),
            P("head", None),
            P(None, "head"),
            P("head", None),
        ),
        out_specs=P(("groups", "shard", "sub"), None, "head"),
        check_vma=False,
    )
```

```python
import math

import jax
import jax.numpy as jnp
from jax import lax
from jax.experimental import pallas as pl
from jax.experimental.pallas import tpu as pltpu
from jax.sharding import PartitionSpec as P

D = 1024
HEAD_DIM = 64
CAP = 2
BLOCK = 64
QUAD = 4
WIDE = QUAD * HEAD_DIM
CHUNKS = 2
ROWS = BLOCK // CHUNKS
MIB = 1 << 20


epsilon = 1e-05


def dot(a, b):
    return jnp.dot(a, b, preferred_element_type=jnp.float32)


def gelu(x):
    return 0.5 * x * (1.0 + lax.erf(x * (2.0**-0.5)))


def in_vmem(x):
    return pltpu.with_memory_space_constraint(x, pltpu.VMEM)


def in_hbm(x):
    return pltpu.with_memory_space_constraint(x, pltpu.HBM)


def whole(space):
    return pl.BlockSpec(memory_space=space)


def vmem(count):
    return [whole(pltpu.VMEM)] * count


def params(mib):
    return pltpu.CompilerParams(vmem_limit_bytes=mib * MIB)


def halves(width):
    h = lax.axis_index("head")
    mine = pl.ds(pl.multiple_of(h * width, width), width)
    theirs = pl.ds(pl.multiple_of((1 - h) * width, width), width)
    return mine, theirs


def mlp_kernel(own, other, gain, wq, wup, wdn, q_out, mlp_out, normed_s):
    half = own.shape[1]
    units = wup.shape[1]
    chunk = units // 4
    mine, theirs = halves(half)
    x_own = own[...].astype(jnp.float32)
    x_other = other[...].astype(jnp.float32)

    def mean(a, b):
        total = jnp.sum(a, axis=-1, keepdims=True) + jnp.sum(b, axis=-1, keepdims=True)
        return total * (0.5 / half)

    average = mean(x_own, x_other)
    x_own = x_own - average
    x_other = x_other - average
    factor = lax.rsqrt(mean(x_own * x_own, x_other * x_other) + epsilon)
    normed_s[:, mine] = (x_own * factor * gain[:, mine]).astype(jnp.bfloat16)
    normed_s[:, theirs] = (x_other * factor * gain[:, theirs]).astype(jnp.bfloat16)
    normed = normed_s[...]
    q_out[...] = dot(normed, wq[...]).astype(jnp.bfloat16)
    for c in range(units // chunk):
        span = slice(c * chunk, (c + 1) * chunk)
        hidden = gelu(dot(normed, wup[:, span])).astype(jnp.bfloat16)
        term = dot(hidden, wdn[span, :])
        if c == 0:
            mlp_out[...] = term
        else:
            mlp_out[...] += term


def run_mlp(own, other, gain, wq, wup, wdn):
    rows = own.shape[0]
    width = wq.shape[0]
    units = wup.shape[1]
    return pl.pallas_call(
        mlp_kernel,
        out_shape=(
            jax.ShapeDtypeStruct((rows, wq.shape[1]), jnp.bfloat16),
            jax.ShapeDtypeStruct((rows, width), jnp.float32),
        ),
        in_specs=vmem(6),
        out_specs=tuple(vmem(2)),
        scratch_shapes=[pltpu.VMEM((rows, width), jnp.bfloat16)],
        compiler_params=params(16),
        cost_estimate=pl.CostEstimate(
            flops=2 * rows * width * (wq.shape[1] + 2 * units),
            bytes_accessed=2 * width * (wq.shape[1] + 2 * units),
            transcendentals=rows * units,
        ),
        name="mlp",
    )(own, other, gain, wq, wup, wdn)


def stage_kernel(*refs):
    sources, copies_to, sem = refs[: len(refs) // 2], refs[len(refs) // 2 : -1], refs[-1]
    copies = []
    for i, (source, target) in enumerate(zip(sources, copies_to)):
        copies.append(pltpu.make_async_copy(source, target, sem.at[i]))
        copies[i].start()
    for copy in copies:
        copy.wait()


def run_stage(*arrays):
    size = sum(2 * array.size for array in arrays)
    return pl.pallas_call(
        stage_kernel,
        out_shape=tuple(jax.ShapeDtypeStruct(array.shape, array.dtype) for array in arrays),
        in_specs=[whole(pltpu.HBM)] * len(arrays),
        out_specs=tuple(vmem(len(arrays))),
        scratch_shapes=[pltpu.SemaphoreType.DMA((len(arrays),))],
        compiler_params=params(16),
        cost_estimate=pl.CostEstimate(flops=0, bytes_accessed=20 * size, transcendentals=0),
        name="stage",
    )(*(in_hbm(array) for array in arrays))


def project_kernel(*refs):
    pieces, (wk, wv, out) = refs[:-3], refs[-3:]
    width = wk.shape[1]
    rows = jnp.concatenate([piece[...] for piece in pieces], axis=0)
    out[:, :width] = dot(rows, wk[...]).astype(jnp.bfloat16)
    out[:, width:] = dot(rows, wv[...]).astype(jnp.bfloat16)


def run_project(pieces, wk, wv):
    rows = sum(piece.shape[0] for piece in pieces)
    depth, width = wk.shape
    return pl.pallas_call(
        project_kernel,
        out_shape=jax.ShapeDtypeStruct((rows, 2 * width), jnp.bfloat16),
        in_specs=vmem(len(pieces) + 2),
        out_specs=whole(pltpu.VMEM),
        compiler_params=params(8),
        cost_estimate=pl.CostEstimate(
            flops=80 * rows * depth * width,
            bytes_accessed=80 * depth * width + 80 * rows * depth,
            transcendentals=0,
        ),
        name="project",
    )(*pieces, in_vmem(wk), in_vmem(wv))


def attend_rows(c, adjacency, q, table, mlp, wo, send, keep, att_s):
    s = lax.axis_index("shard")
    h = lax.axis_index("head")
    u = lax.axis_index("sub")
    half = wo.shape[0]
    per_core = table.shape[0] // 2
    mine, theirs = halves(half)
    rows = slice(c * ROWS, (c + 1) * ROWS)
    rows_of = lax.broadcasted_iota(jnp.int32, (QUAD * ROWS, WIDE), 0) // ROWS
    lanes_of = lax.broadcasted_iota(jnp.int32, (QUAD * ROWS, WIDE), 1) // HEAD_DIM
    diagonal = rows_of == lanes_of
    lane_head = lax.broadcasted_iota(jnp.int32, (ROWS, WIDE), 1) // HEAD_DIM
    scale = HEAD_DIM**-0.5 * math.log2(math.e)
    count = adjacency.shape[0]
    for b in range(count):
        places = []
        for j in range(adjacency.shape[1]):
            m = adjacency[b, j]
            part = lax.rem(m, 2)
            core = lax.rem(m // 2, 2)
            distance = s ^ (m // 4)
            distance = jnp.where(distance <= 1, distance, 2 + ((distance - 2) ^ h))
            places.append((core ^ u) * per_core + distance * 2 + part)
        for g in range(half // WIDE):
            columns = slice(g * WIDE, (g + 1) * WIDE)
            keys = jnp.concatenate([table[p, :, columns] for p in places], axis=0)
            vcolumns = slice(half + g * WIDE, half + (g + 1) * WIDE)
            values = jnp.concatenate([table[p, :, vcolumns] for p in places], axis=0)
            stacked = jnp.concatenate([q[b, rows, columns]] * QUAD, axis=0)
            stacked = jnp.where(diagonal, stacked, jnp.zeros_like(stacked))
            scores = lax.dot_general(
                stacked, keys, (((1,), (1,)), ((), ())), preferred_element_type=jnp.float32
            )
            highest = jnp.max(scores, axis=-1, keepdims=True)
            weights = jnp.exp2((scores - highest) * scale)
            total = jnp.sum(weights, axis=-1, keepdims=True)
            probs = (weights * (1.0 / total)).astype(jnp.bfloat16)
            mixed = dot(probs, values)
            merged = mixed[0:ROWS, :]
            for i in range(1, QUAD):
                merged = jnp.where(lane_head == i, mixed[i * ROWS : (i + 1) * ROWS, :], merged)
            att_s[b * ROWS : (b + 1) * ROWS, columns] = merged.astype(jnp.bfloat16)
    for out, span in ((send, theirs), (keep, mine)):
        extra = mlp[:, rows, span].reshape(count * ROWS, half)
        out[...] = (extra + dot(att_s[...], wo[:, span])).astype(jnp.bfloat16)


def first_kernel(
    adjacency, q, mine_a, mine_b, sibling_a, sibling_b, mlp, wo, send, keep, table, att_s, sem
):
    copies = []
    first = 0
    for i, part in enumerate((mine_a, mine_b, sibling_a, sibling_b)):
        blocks = part.shape[0]
        copies.append(pltpu.make_async_copy(part, table.at[pl.ds(first, blocks)], sem.at[i]))
        copies[i].start()
        first += blocks
    for copy in copies:
        copy.wait()
    attend_rows(0, adjacency, q, table, mlp, wo, send, keep, att_s)


def later_kernel(c):
    def kernel(adjacency, q, table, mlp, wo, send, keep, att_s):
        attend_rows(c, adjacency, q, table, mlp, wo, send, keep, att_s)

    return kernel


def run_attend(c, adjacency, q, tables, mlp, wo):
    count, _, half = q.shape
    rows = count * ROWS
    part = jax.ShapeDtypeStruct((rows, half), jnp.bfloat16)
    blocks = sum(table.shape[0] for table in tables)
    shared = jax.ShapeDtypeStruct((blocks,) + tables[0].shape[1:], jnp.bfloat16)
    outs = (part, part, shared) if c == 0 else (part, part)
    scratch = [pltpu.VMEM((rows, half), jnp.bfloat16)]
    return pl.pallas_call(
        first_kernel if c == 0 else later_kernel(c),
        out_shape=outs,
        in_specs=[whole(pltpu.SMEM)] + vmem(len(tables) + 3),
        out_specs=tuple(vmem(len(outs))),
        scratch_shapes=scratch + [pltpu.SemaphoreType.DMA((len(tables),))] * (c == 0),
        compiler_params=params(16),
        cost_estimate=pl.CostEstimate(
            flops=20 * rows * half * (D + 8 * 8 * BLOCK),
            bytes_accessed=40 * blocks * BLOCK * half + 20 * half * D + 40 * rows * D,
            transcendentals=rows * 8 * BLOCK * half // HEAD_DIM,
        ),
        name="attend",
    )(adjacency, q, *tables, mlp, in_vmem(wo))


def combine_kernel(c):
    def kernel(owners, grid_features, keep, received, *outs):
        s = lax.axis_index("shard")
        shards = len(outs)
        count = grid_features.shape[0]
        names = [owners[t, 0] for t in range(count)]
        for d in range(shards):
            target = s ^ d
            for j in range(CAP):
                outs[d][j] = jnp.zeros(outs[d].shape[1:], jnp.bfloat16)
            seen = jnp.int32(0)
            for t in range(count):
                hit = names[t] == target
                rank = seen

                @pl.when(hit)
                def _():
                    rows = slice(t * ROWS, (t + 1) * ROWS)
                    partials = keep[rows, :].astype(jnp.float32)
                    partials = partials + received[rows, :].astype(jnp.float32)
                    residual = grid_features[t, c * ROWS : (c + 1) * ROWS, :]
                    updated = residual.astype(jnp.float32) + partials
                    outs[d][rank] = updated.astype(jnp.bfloat16)

                seen = seen + hit.astype(jnp.int32)

    return kernel


def run_combine(c, owners, grid_features, keep, received, shards):
    count, _, half = grid_features.shape
    slot = jax.ShapeDtypeStruct((CAP, ROWS, half), jnp.bfloat16)
    return pl.pallas_call(
        combine_kernel(c),
        out_shape=(slot,) * shards,
        in_specs=[whole(pltpu.SMEM)] + vmem(3),
        out_specs=tuple(vmem(shards)),
        compiler_params=params(8),
        cost_estimate=pl.CostEstimate(
            flops=3000 * count * ROWS * half,
            bytes_accessed=400 * ROWS * half * (3 * count + CAP * shards),
            transcendentals=0,
        ),
        name="combine",
    )(owners, grid_features, keep, received)


def place_kernel(c, shards):
    def kernel(*refs):
        arrived, (out, sem) = refs[:shards], refs[-2:]
        s = lax.axis_index("shard")
        rows = pl.ds(c * ROWS, ROWS)
        copies = []
        for d in range(shards):
            slots = pl.ds((s ^ d) * CAP, CAP)
            copies.append(pltpu.make_async_copy(arrived[d], out.at[slots, rows, :], sem.at[d]))
            copies[d].start()
        for copy in copies:
            copy.wait()

    return kernel


def run_place(c, arrived, placed):
    shards = len(arrived)
    half = arrived[0].shape[2]
    size = 2 * CAP * shards * ROWS * half
    return pl.pallas_call(
        place_kernel(c, shards),
        out_shape=jax.ShapeDtypeStruct((shards * CAP, BLOCK, half), jnp.bfloat16),
        in_specs=vmem(shards) + [whole(pltpu.HBM)] * len(placed),
        out_specs=whole(pltpu.HBM),
        scratch_shapes=[pltpu.SemaphoreType.DMA((shards,))],
        input_output_aliases={shards: 0} if placed else {},
        compiler_params=params(4),
        cost_estimate=pl.CostEstimate(flops=0, bytes_accessed=20 * size, transcendentals=0),
        name="place",
    )(*arrived, *placed)


def crossed(x, distance, size):
    return lax.ppermute(x, "shard", [(i, i ^ distance) for i in range(size)])


def fetched(x, size):
    pairs = [(2 * i + h, 2 * (i ^ (2 + h)) + h) for i in range(size) for h in range(2)]
    return lax.ppermute(x, ("shard", "head"), pairs)


def swapped(x, axis):
    return lax.ppermute(x, axis, [(0, 1), (1, 0)])


def paired(
    grid_features,
    owners,
    adjacency,
    mesh_nodes,
    norm_gain,
    query_weight,
    key_weight,
    value_weight,
    output_weight,
    up_weight,
    down_weight,
):
    shards = lax.axis_size("shard")
    count, rows, half = grid_features.shape
    flat = grid_features.reshape(count * rows, half)
    far = fetched(mesh_nodes, shards)
    near = crossed(mesh_nodes, 1, shards)
    other = swapped(flat, "head")
    staged = run_stage(flat, norm_gain.reshape(1, -1), query_weight, up_weight, down_weight)
    queries, mlp = run_mlp(staged[0], other, *staged[1:])
    queries, mlp, far = lax.optimization_barrier((queries, mlp, far))
    farther = swapped(far, "head")
    mine_a = run_project((mesh_nodes, near, far), key_weight, value_weight)
    sibling_a = swapped(mine_a, "sub")
    mine_b = run_project((farther,), key_weight, value_weight)
    sibling_b = swapped(mine_b, "sub")
    tables = [
        table.reshape(-1, BLOCK, 2 * half) for table in (mine_a, mine_b, sibling_a, sibling_b)
    ]
    queries = queries.reshape(count, rows, half)
    mlp = mlp.reshape(count, rows, 2 * half)
    placed = []
    slots = None
    for c in range(CHUNKS):
        send, keep, *table = run_attend(c, adjacency, queries, tables, mlp, output_weight)
        tables = table or tables
        received = swapped(send, "head")
        if slots is not None:
            received, _ = lax.optimization_barrier((received, slots[0]))
        slots = run_combine(c, owners, grid_features, keep, received, shards)
        arrived = [slots[0]] + [crossed(slots[d], d, shards) for d in range(1, shards)]
        placed = [run_place(c, arrived, placed)]
    return placed[0]


def attend_plain(queries, key_table, value_table, chosen, scaling):
    count = chosen.shape[0]
    picked_keys = key_table[chosen]
    picked_keys = picked_keys.reshape(count, -1, picked_keys.shape[3], picked_keys.shape[4])
    picked_values = value_table[chosen]
    picked_values = picked_values.reshape(count, -1, picked_values.shape[3], picked_values.shape[4])
    scores = (
        jnp.einsum("gqhe,gkhe->ghqk", queries, picked_keys, preferred_element_type=jnp.float32)
        * scaling
    )
    highest = jnp.max(scores, axis=-1, keepdims=True)
    weights = jnp.exp(scores - highest)
    weights = (weights / jnp.sum(weights, axis=-1, keepdims=True)).astype(jnp.bfloat16)
    result = jnp.einsum(
        "ghqk,gkhe->gqhe", weights, picked_values, preferred_element_type=jnp.float32
    )
    return result.astype(jnp.bfloat16)


def general(
    grid_features,
    owners,
    adjacency,
    mesh_nodes,
    norm_gain,
    query_weight,
    key_weight,
    value_weight,
    output_weight,
    up_weight,
    down_weight,
):
    shard_count = lax.axis_size("shard")
    head_count = lax.axis_size("head")
    local_blocks, block_rows, feature_share = grid_features.shape
    slots = shard_count * CAP
    owner_col = owners[:, 0]
    position = jnp.arange(local_blocks, dtype=jnp.int32)
    earlier = (owner_col[:, None] == owner_col[None, :]) & (position[None, :] < position[:, None])
    target = owner_col * CAP + jnp.sum(earlier.astype(jnp.int32), axis=1)
    dispatch = (target[:, None] == jnp.arange(slots, dtype=jnp.int32)[None, :]).astype(jnp.bfloat16)
    offset = lax.axis_index("head") * (D // head_count)
    projected = jnp.stack(
        (
            jnp.dot(mesh_nodes, key_weight, preferred_element_type=jnp.float32).astype(
                jnp.bfloat16
            ),
            jnp.dot(mesh_nodes, value_weight, preferred_element_type=jnp.float32).astype(
                jnp.bfloat16
            ),
        )
    )
    tables = lax.all_gather(projected, ("shard", "sub"), axis=1, tiled=True)
    head_local = query_weight.shape[1] // HEAD_DIM
    key_table = tables[0].reshape(-1, block_rows, head_local, HEAD_DIM)
    value_table = tables[1].reshape(-1, block_rows, head_local, HEAD_DIM)
    send_lists = jnp.full((slots, adjacency.shape[1]), -1, jnp.int32).at[target].set(adjacency)
    send_lists = send_lists.reshape(shard_count, CAP, -1)
    complete = lax.all_gather(grid_features, "head", axis=2, tiled=True)
    outgoing = jnp.einsum(
        "gs,gbd->sbd", dispatch, complete, preferred_element_type=jnp.float32
    ).astype(jnp.bfloat16)
    arrived, lists = (
        lax.all_to_all(
            outgoing.reshape(shard_count, CAP, block_rows, D),
            "shard",
            split_axis=0,
            concat_axis=0,
            tiled=True,
        ),
        lax.all_to_all(send_lists, "shard", split_axis=0, concat_axis=0, tiled=True),
    )
    arrived = arrived.reshape(slots, block_rows, D)
    residual = lax.dynamic_slice_in_dim(arrived, offset, D // head_count, 2)
    lists = lists.reshape(slots, -1)
    count = arrived.shape[0]
    values_f = arrived.astype(jnp.float32)
    average = jnp.mean(values_f, axis=-1, keepdims=True)
    centered = values_f - average
    variance = jnp.mean(centered * centered, axis=-1, keepdims=True)
    normed = (centered * lax.rsqrt(variance + epsilon) * norm_gain).astype(jnp.bfloat16)
    flattened = normed.reshape(-1, D)
    queries = jnp.dot(flattened, query_weight, preferred_element_type=jnp.float32).astype(
        jnp.bfloat16
    )
    blocks_each = math.gcd(count, max(1, 512 // block_rows))
    steps_count = count // blocks_each
    queries = queries.reshape(steps_count, blocks_each, block_rows, head_local, HEAD_DIM)

    def attend_step(operands):
        return attend_plain(operands[0], key_table, value_table, operands[1], HEAD_DIM ** (-0.5))

    attended = lax.map(
        attend_step, (queries, jnp.maximum(lists, 0).reshape(steps_count, blocks_each, -1))
    )
    attended = attended.reshape(-1, head_local * HEAD_DIM)
    hidden = jax.nn.gelu(
        jnp.dot(flattened, up_weight, preferred_element_type=jnp.float32), approximate=False
    ).astype(jnp.bfloat16)
    branch = jnp.dot(attended, output_weight, preferred_element_type=jnp.float32)
    branch = branch + jnp.dot(hidden, down_weight, preferred_element_type=jnp.float32)
    branch = branch.reshape(count, block_rows, D)
    reduced = lax.psum_scatter(
        branch.astype(jnp.bfloat16), "head", scatter_dimension=2, tiled=True
    ).astype(jnp.float32)
    occupied = lists[:, 0] >= 0
    summed = residual.astype(jnp.float32) + reduced
    return jnp.where(occupied[:, None, None], summed, 0.0).astype(jnp.bfloat16)


def local(grid_features, owners, adjacency, mesh_nodes, *parameters):
    sizes = [lax.axis_size(axis) for axis in ("shard", "head", "sub")]
    small = grid_features.shape[:2] == (4, BLOCK) and mesh_nodes.shape[0] == 2 * BLOCK
    if sizes == [4, 2, 2] and small:
        return paired(grid_features, owners, adjacency, mesh_nodes, *parameters)
    return general(grid_features, owners, adjacency, mesh_nodes, *parameters)


def solution(mesh):
    return jax.shard_map(
        local,
        mesh=mesh,
        in_specs=(
            P(("groups", "shard", "sub"), None, "head"),
            P(("groups", "shard", "sub"), None),
            P(("groups", "shard", "sub"), None),
            P(("groups", "shard", "sub"), None),
            P(),
            P(None, "head"),
            P(None, "head"),
            P(None, "head"),
            P("head", None),
            P(None, "head"),
            P("head", None),
        ),
        out_specs=P(("groups", "shard", "sub"), None, "head"),
        check_vma=False,
    )
```

```python
import functools
import math

import jax
import jax.numpy as jnp
from jax import lax
from jax.experimental import pallas as pl
from jax.experimental.pallas import tpu as pltpu
from jax.sharding import PartitionSpec as P

D = 1024
HEAD_DIM = 64
CAP = 2
BLOCK = 64
QUAD = 4
WIDE = QUAD * HEAD_DIM
CHUNKS = 2
MIB = 1 << 20


epsilon = 1e-05


def dot(a, b):
    return jnp.dot(a, b, preferred_element_type=jnp.float32)


def gelu(x):
    return 0.5 * x * (1.0 + lax.erf(x * (2.0**-0.5)))


def in_hbm(x):
    return pltpu.with_memory_space_constraint(x, pltpu.HBM)


def whole(space):
    return pl.BlockSpec(memory_space=space)


def vmem(count):
    return [whole(pltpu.VMEM)] * count


def params(mib):
    return pltpu.CompilerParams(vmem_limit_bytes=mib * MIB)


def mlp_kernel(own, other, gain, wq, wup, wdn, q_out, mlp_out, normed_s):
    half = own.shape[1]
    units = wup.shape[1]
    chunk = units // 4
    x_other = other[...].astype(jnp.float32)
    x_own = own[...].astype(jnp.float32)

    def mean(a, b):
        total = jnp.sum(a, axis=-1, keepdims=True) + jnp.sum(b, axis=-1, keepdims=True)
        return total * (0.5 / half)

    average = mean(x_other, x_own)
    x_other = x_other - average
    x_own = x_own - average
    factor = lax.rsqrt(mean(x_other * x_other, x_own * x_own) + epsilon)
    normed_s[:, :half] = (x_other * factor * gain[:, :half]).astype(jnp.bfloat16)
    normed_s[:, half:] = (x_own * factor * gain[:, half:]).astype(jnp.bfloat16)
    normed = normed_s[...]
    q_out[...] = dot(normed, wq[...]).astype(jnp.bfloat16)
    for c in range(units // chunk):
        span = slice(c * chunk, (c + 1) * chunk)
        hidden = gelu(dot(normed, wup[:, span])).astype(jnp.bfloat16)
        term = dot(hidden, wdn[span, :])
        if c == 0:
            mlp_out[...] = term
        else:
            mlp_out[...] += term


def run_mlp(own, other, gain, wq, wup, wdn):
    rows = own.shape[0]
    width = wq.shape[0]
    units = wup.shape[1]
    return pl.pallas_call(
        mlp_kernel,
        out_shape=(
            jax.ShapeDtypeStruct((rows, wq.shape[1]), jnp.bfloat16),
            jax.ShapeDtypeStruct((rows, width), jnp.float32),
        ),
        in_specs=vmem(6),
        out_specs=tuple(vmem(2)),
        scratch_shapes=[pltpu.VMEM((rows, width), jnp.bfloat16)],
        compiler_params=params(16),
        cost_estimate=pl.CostEstimate(
            flops=2 * rows * width * (wq.shape[1] + 2 * units),
            bytes_accessed=2 * width * (wq.shape[1] + 2 * units),
            transcendentals=rows * units,
        ),
        name="mlp",
    )(own, other, gain, wq, wup, wdn)


def stage_kernel(axes, *refs):
    sources, targets, sem = refs[: len(axes)], refs[len(axes) : -1], refs[-1]
    h = lax.axis_index("head")
    copies = []
    for source, target, axis in zip(sources, targets, axes):
        if axis is None:
            copies.append(pltpu.make_async_copy(source, target, sem.at[len(copies)]))
            continue
        half = source.shape[axis] // 2
        for part, head in enumerate((1 - h, h)):
            span = pl.ds(pl.multiple_of(head * half, half), half)
            place = pl.ds(part * half, half)
            if axis == 0:
                pair = (source.at[span, :], target.at[place, :])
            else:
                pair = (source.at[:, span], target.at[:, place])
            copies.append(pltpu.make_async_copy(*pair, sem.at[len(copies)]))
    for copy in copies:
        copy.start()
    for copy in copies:
        copy.wait()


def run_stage(arrays, axes):
    size = sum(2 * array.size for array in arrays)
    return pl.pallas_call(
        functools.partial(stage_kernel, axes),
        out_shape=tuple(jax.ShapeDtypeStruct(array.shape, array.dtype) for array in arrays),
        in_specs=[whole(pltpu.HBM)] * len(arrays),
        out_specs=tuple(vmem(len(arrays))),
        scratch_shapes=[pltpu.SemaphoreType.DMA((2 * len(arrays),))],
        compiler_params=params(16),
        cost_estimate=pl.CostEstimate(flops=0, bytes_accessed=20 * size, transcendentals=0),
        name="stage",
    )(*(in_hbm(array) for array in arrays))


def project_kernel(*refs):
    pieces, (wk, wv, out) = refs[:-3], refs[-3:]
    width = wk.shape[1]
    rows = jnp.concatenate([piece[...] for piece in pieces], axis=0)
    out[:, :width] = dot(rows, wk[...]).astype(jnp.bfloat16)
    out[:, width:] = dot(rows, wv[...]).astype(jnp.bfloat16)


def run_project(pieces, wk, wv):
    rows = sum(piece.shape[0] for piece in pieces)
    depth, width = wk.shape
    return pl.pallas_call(
        project_kernel,
        out_shape=jax.ShapeDtypeStruct((rows, 2 * width), jnp.bfloat16),
        in_specs=vmem(len(pieces) + 2),
        out_specs=whole(pltpu.VMEM),
        compiler_params=params(8),
        cost_estimate=pl.CostEstimate(
            flops=80 * rows * depth * width,
            bytes_accessed=80 * depth * width + 80 * rows * depth,
            transcendentals=0,
        ),
        name="project",
    )(*pieces, wk, wv)


def table_kernel(mine, sibling, table, sem):
    copies = [
        pltpu.make_async_copy(mine, table.at[0, pl.ds(0, mine.shape[0])], sem.at[0]),
        pltpu.make_async_copy(sibling, table.at[1, pl.ds(0, mine.shape[0])], sem.at[1]),
    ]
    for copy in copies:
        copy.start()
    for copy in copies:
        copy.wait()


def run_table(mine, sibling, blocks):
    return pl.pallas_call(
        table_kernel,
        out_shape=jax.ShapeDtypeStruct((2, blocks) + mine.shape[1:], jnp.bfloat16),
        in_specs=vmem(2),
        out_specs=whole(pltpu.VMEM),
        scratch_shapes=[pltpu.SemaphoreType.DMA((2,))],
        compiler_params=params(8),
        cost_estimate=pl.CostEstimate(
            flops=0, bytes_accessed=80 * mine.size, transcendentals=0
        ),
        name="table",
    )(mine, sibling)


def project_out(c, att, mlp, wo, send, keep):
    width = send.shape[1]
    half = att.shape[1]
    for out, first in ((send, 0), (keep, half)):
        span = slice(first + c * width, first + (c + 1) * width)
        out[...] = (mlp[:, span] + dot(att[...], wo[:, span])).astype(jnp.bfloat16)


def attend_kernel(
    adjacency, q, mine, sibling, table_in, mlp, wo, send, keep, att, table, sem
):
    del table_in
    s = lax.axis_index("shard")
    h = lax.axis_index("head")
    u = lax.axis_index("sub")
    half = wo.shape[0]
    ready = table.shape[1] - mine.shape[0]
    copies = []
    for i, part in enumerate((mine, sibling)):
        target = table.at[i, pl.ds(ready, part.shape[0])]
        copies.append(pltpu.make_async_copy(part, target, sem.at[i]))
        copies[i].start()
    rows_of = lax.broadcasted_iota(jnp.int32, (WIDE, WIDE), 0) // BLOCK
    lanes_of = lax.broadcasted_iota(jnp.int32, (WIDE, WIDE), 1) // HEAD_DIM
    diagonal = rows_of == lanes_of
    lane_head = lax.broadcasted_iota(jnp.int32, (BLOCK, WIDE), 1) // HEAD_DIM
    scale = HEAD_DIM**-0.5 * math.log2(math.e)
    for copy in copies:
        copy.wait()
    for b in range(adjacency.shape[0]):
        rows = slice(b * BLOCK, (b + 1) * BLOCK)
        places = []
        for j in range(adjacency.shape[1]):
            m = adjacency[b, j]
            part = lax.rem(m, 2)
            core = lax.rem(m // 2, 2)
            distance = s ^ (m // 4)
            distance = jnp.where(distance <= 1, distance, 2 + ((distance - 2) ^ h))
            places.append((core ^ u, distance * 2 + part))
        for g in range(half // WIDE):
            columns = slice(g * WIDE, (g + 1) * WIDE)
            keys = jnp.concatenate([table[i, p, :, columns] for i, p in places], axis=0)
            vcolumns = slice(half + g * WIDE, half + (g + 1) * WIDE)
            values = jnp.concatenate([table[i, p, :, vcolumns] for i, p in places], axis=0)
            stacked = jnp.concatenate([q[rows, columns]] * QUAD, axis=0)
            stacked = jnp.where(diagonal, stacked, jnp.zeros_like(stacked))
            scores = lax.dot_general(
                stacked, keys, (((1,), (1,)), ((), ())), preferred_element_type=jnp.float32
            )
            highest = jnp.max(scores, axis=-1, keepdims=True)
            weights = jnp.exp2((scores - highest) * scale)
            total = jnp.sum(weights, axis=-1, keepdims=True)
            probs = (weights * (1.0 / total)).astype(jnp.bfloat16)
            mixed = dot(probs, values)
            merged = mixed[0:BLOCK, :]
            for i in range(1, QUAD):
                merged = jnp.where(lane_head == i, mixed[i * BLOCK : (i + 1) * BLOCK, :], merged)
            att[rows, columns] = merged.astype(jnp.bfloat16)
    project_out(0, att, mlp, wo, send, keep)


def run_attend(adjacency, q, mine, sibling, table, mlp, wo):
    rows, half = q.shape
    part = jax.ShapeDtypeStruct((rows, half // CHUNKS), jnp.bfloat16)
    blocks = table.shape[0] * table.shape[1]
    send, keep, att, _ = pl.pallas_call(
        attend_kernel,
        out_shape=(
            part,
            part,
            jax.ShapeDtypeStruct(q.shape, jnp.bfloat16),
            jax.ShapeDtypeStruct(table.shape, jnp.bfloat16),
        ),
        in_specs=[whole(pltpu.SMEM)] + vmem(6),
        out_specs=tuple(vmem(4)),
        scratch_shapes=[pltpu.SemaphoreType.DMA((2,))],
        input_output_aliases={4: 3},
        compiler_params=params(16),
        cost_estimate=pl.CostEstimate(
            flops=20 * rows * half * (D + 8 * 8 * BLOCK),
            bytes_accessed=40 * blocks * BLOCK * half + 20 * half * D + 40 * rows * D,
            transcendentals=rows * 8 * BLOCK * half // HEAD_DIM,
        ),
        name="attend",
    )(adjacency, q, mine, sibling, table, mlp, wo)
    return send, keep, att


def run_project_out(c, att, mlp, wo):
    rows, half = att.shape
    part = jax.ShapeDtypeStruct((rows, half // CHUNKS), jnp.bfloat16)
    return pl.pallas_call(
        functools.partial(project_out, c),
        out_shape=(part, part),
        in_specs=vmem(3),
        out_specs=tuple(vmem(2)),
        compiler_params=params(8),
        cost_estimate=pl.CostEstimate(
            flops=200 * rows * half * D,
            bytes_accessed=200 * half * D,
            transcendentals=0,
        ),
        name="project_out",
    )(att, mlp, wo)


def combine_kernel(c, owners, grid_features, keep, received, *outs):
    s = lax.axis_index("shard")
    count = grid_features.shape[0]
    width = keep.shape[1]
    names = [owners[t, 0] for t in range(count)]
    for d, out in enumerate(outs):
        for j in range(CAP):
            out[j] = jnp.zeros(out.shape[1:], jnp.bfloat16)
        seen = jnp.int32(0)
        for t in range(count):
            hit = names[t] == s ^ d
            rank = seen

            @pl.when(hit)
            def _():
                rows = slice(t * BLOCK, (t + 1) * BLOCK)
                partials = keep[rows, :].astype(jnp.float32)
                partials = partials + received[rows, :].astype(jnp.float32)
                residual = grid_features[t, :, c * width : (c + 1) * width]
                out[rank] = (residual.astype(jnp.float32) + partials).astype(jnp.bfloat16)

            seen = seen + hit.astype(jnp.int32)


def run_combine(c, owners, grid_features, keep, received, shards):
    count, rows, _ = grid_features.shape
    width = keep.shape[1]
    slot = jax.ShapeDtypeStruct((CAP, rows, width), jnp.bfloat16)
    return pl.pallas_call(
        functools.partial(combine_kernel, c),
        out_shape=(slot,) * shards,
        in_specs=[whole(pltpu.SMEM)] + vmem(3),
        out_specs=tuple(vmem(shards)),
        compiler_params=params(8),
        cost_estimate=pl.CostEstimate(
            flops=3000 * count * rows * width,
            bytes_accessed=400 * rows * width * (3 * count + CAP * shards),
            transcendentals=0,
        ),
        name="combine",
    )(owners, grid_features, keep, received)


def place_kernel(c, *refs):
    out, sem = refs[-2:]
    s = lax.axis_index("shard")
    copies = []
    for d in range(sem.shape[0]):
        width = refs[d].shape[2]
        columns = pl.ds(c * width, width)
        slots = pl.ds((s ^ d) * CAP, CAP)
        copies.append(pltpu.make_async_copy(refs[d], out.at[slots, :, columns], sem.at[d]))
        copies[d].start()
    for copy in copies:
        copy.wait()


def run_place(c, arrived, placed):
    shards = len(arrived)
    _, rows, width = arrived[0].shape
    shape = (shards * CAP, rows, CHUNKS * width)
    return pl.pallas_call(
        functools.partial(place_kernel, c),
        out_shape=jax.ShapeDtypeStruct(shape, jnp.bfloat16),
        in_specs=vmem(shards) + [whole(pltpu.HBM)] * len(placed),
        out_specs=whole(pltpu.HBM),
        scratch_shapes=[pltpu.SemaphoreType.DMA((shards,))],
        input_output_aliases={shards: 0} if placed else {},
        compiler_params=params(4),
        cost_estimate=pl.CostEstimate(
            flops=0, bytes_accessed=40 * CAP * shards * rows * width, transcendentals=0
        ),
        name="place",
    )(*arrived, *placed)


def crossed(x, distance, size):
    return lax.ppermute(x, "shard", [(i, i ^ distance) for i in range(size)])


def fetched(x, size):
    pairs = [(2 * i + h, 2 * (i ^ (2 + h)) + h) for i in range(size) for h in range(2)]
    return lax.ppermute(x, ("shard", "head"), pairs)


def swapped(x, axis):
    return lax.ppermute(x, axis, [(0, 1), (1, 0)])


def paired(
    grid_features,
    owners,
    adjacency,
    mesh_nodes,
    norm_gain,
    query_weight,
    key_weight,
    value_weight,
    output_weight,
    up_weight,
    down_weight,
):
    shards = lax.axis_size("shard")
    count, rows, half = grid_features.shape
    flat = grid_features.reshape(count * rows, half)
    far = fetched(mesh_nodes, shards)
    other = swapped(flat, "head")
    staged = run_stage(
        (
            flat,
            norm_gain.reshape(1, -1),
            query_weight,
            up_weight,
            down_weight,
            output_weight,
            key_weight,
            value_weight,
            mesh_nodes,
        ),
        (None, 1, 0, 0, 1, 1, None, None, None),
    )
    flat, gain, wq, wup, wdn, wo, wk, wv, mesh = staged
    near = crossed(mesh, 1, shards)
    queries, mlp = run_mlp(flat, other, gain, wq, wup, wdn)
    queries, mlp, far = lax.optimization_barrier((queries, mlp, far))
    farther = swapped(far, "head")
    blocked = (-1, BLOCK, 2 * half)
    mine_a = run_project((mesh, near, far), wk, wv)
    sibling_a = swapped(mine_a, "sub")
    table = run_table(mine_a.reshape(blocked), sibling_a.reshape(blocked), 2 * shards)
    mine_b = run_project((farther,), wk, wv)
    sibling_b = swapped(mine_b, "sub")
    send, keep, att = run_attend(
        adjacency, queries, mine_b.reshape(blocked), sibling_b.reshape(blocked), table, mlp, wo
    )
    placed = []
    slots = None
    for c in range(CHUNKS):
        if c > 0:
            send, keep = run_project_out(c, att, mlp, wo)
        received = swapped(send, "head")
        if slots is not None:
            received, _ = lax.optimization_barrier((received, slots[0]))
        slots = run_combine(c, owners, grid_features, keep, received, shards)
        arrived = [slots[0]] + [crossed(slots[d], d, shards) for d in range(1, shards)]
        placed = [run_place(c, arrived, placed)]
    return placed[0]


def attend_plain(queries, key_table, value_table, chosen, scaling):
    count = chosen.shape[0]
    picked_keys = key_table[chosen]
    picked_keys = picked_keys.reshape(count, -1, picked_keys.shape[3], picked_keys.shape[4])
    picked_values = value_table[chosen]
    picked_values = picked_values.reshape(count, -1, picked_values.shape[3], picked_values.shape[4])
    scores = (
        jnp.einsum("gqhe,gkhe->ghqk", queries, picked_keys, preferred_element_type=jnp.float32)
        * scaling
    )
    highest = jnp.max(scores, axis=-1, keepdims=True)
    weights = jnp.exp(scores - highest)
    weights = (weights / jnp.sum(weights, axis=-1, keepdims=True)).astype(jnp.bfloat16)
    result = jnp.einsum(
        "ghqk,gkhe->gqhe", weights, picked_values, preferred_element_type=jnp.float32
    )
    return result.astype(jnp.bfloat16)


def general(
    grid_features,
    owners,
    adjacency,
    mesh_nodes,
    norm_gain,
    query_weight,
    key_weight,
    value_weight,
    output_weight,
    up_weight,
    down_weight,
):
    shard_count = lax.axis_size("shard")
    head_count = lax.axis_size("head")
    local_blocks, block_rows, feature_share = grid_features.shape
    slots = shard_count * CAP
    owner_col = owners[:, 0]
    position = jnp.arange(local_blocks, dtype=jnp.int32)
    earlier = (owner_col[:, None] == owner_col[None, :]) & (position[None, :] < position[:, None])
    target = owner_col * CAP + jnp.sum(earlier.astype(jnp.int32), axis=1)
    dispatch = (target[:, None] == jnp.arange(slots, dtype=jnp.int32)[None, :]).astype(jnp.bfloat16)
    offset = lax.axis_index("head") * (D // head_count)
    projected = jnp.stack(
        (
            jnp.dot(mesh_nodes, key_weight, preferred_element_type=jnp.float32).astype(
                jnp.bfloat16
            ),
            jnp.dot(mesh_nodes, value_weight, preferred_element_type=jnp.float32).astype(
                jnp.bfloat16
            ),
        )
    )
    tables = lax.all_gather(projected, ("shard", "sub"), axis=1, tiled=True)
    head_local = query_weight.shape[1] // HEAD_DIM
    key_table = tables[0].reshape(-1, block_rows, head_local, HEAD_DIM)
    value_table = tables[1].reshape(-1, block_rows, head_local, HEAD_DIM)
    send_lists = jnp.full((slots, adjacency.shape[1]), -1, jnp.int32).at[target].set(adjacency)
    send_lists = send_lists.reshape(shard_count, CAP, -1)
    complete = lax.all_gather(grid_features, "head", axis=2, tiled=True)
    outgoing = jnp.einsum(
        "gs,gbd->sbd", dispatch, complete, preferred_element_type=jnp.float32
    ).astype(jnp.bfloat16)
    arrived, lists = (
        lax.all_to_all(
            outgoing.reshape(shard_count, CAP, block_rows, D),
            "shard",
            split_axis=0,
            concat_axis=0,
            tiled=True,
        ),
        lax.all_to_all(send_lists, "shard", split_axis=0, concat_axis=0, tiled=True),
    )
    arrived = arrived.reshape(slots, block_rows, D)
    residual = lax.dynamic_slice_in_dim(arrived, offset, D // head_count, 2)
    lists = lists.reshape(slots, -1)
    count = arrived.shape[0]
    values_f = arrived.astype(jnp.float32)
    average = jnp.mean(values_f, axis=-1, keepdims=True)
    centered = values_f - average
    variance = jnp.mean(centered * centered, axis=-1, keepdims=True)
    normed = (centered * lax.rsqrt(variance + epsilon) * norm_gain).astype(jnp.bfloat16)
    flattened = normed.reshape(-1, D)
    queries = jnp.dot(flattened, query_weight, preferred_element_type=jnp.float32).astype(
        jnp.bfloat16
    )
    blocks_each = math.gcd(count, max(1, 512 // block_rows))
    steps_count = count // blocks_each
    queries = queries.reshape(steps_count, blocks_each, block_rows, head_local, HEAD_DIM)

    def attend_step(operands):
        return attend_plain(operands[0], key_table, value_table, operands[1], HEAD_DIM ** (-0.5))

    attended = lax.map(
        attend_step, (queries, jnp.maximum(lists, 0).reshape(steps_count, blocks_each, -1))
    )
    attended = attended.reshape(-1, head_local * HEAD_DIM)
    hidden = jax.nn.gelu(
        jnp.dot(flattened, up_weight, preferred_element_type=jnp.float32), approximate=False
    ).astype(jnp.bfloat16)
    branch = jnp.dot(attended, output_weight, preferred_element_type=jnp.float32)
    branch = branch + jnp.dot(hidden, down_weight, preferred_element_type=jnp.float32)
    branch = branch.reshape(count, block_rows, D)
    reduced = lax.psum_scatter(
        branch.astype(jnp.bfloat16), "head", scatter_dimension=2, tiled=True
    ).astype(jnp.float32)
    occupied = lists[:, 0] >= 0
    summed = residual.astype(jnp.float32) + reduced
    return jnp.where(occupied[:, None, None], summed, 0.0).astype(jnp.bfloat16)


def local(grid_features, owners, adjacency, mesh_nodes, *parameters):
    sizes = [lax.axis_size(axis) for axis in ("shard", "head", "sub")]
    small = grid_features.shape[:2] == (4, BLOCK) and mesh_nodes.shape[0] == 2 * BLOCK
    if sizes == [4, 2, 2] and small:
        return paired(grid_features, owners, adjacency, mesh_nodes, *parameters)
    return general(grid_features, owners, adjacency, mesh_nodes, *parameters)


def solution(mesh):
    return jax.shard_map(
        local,
        mesh=mesh,
        in_specs=(
            P(("groups", "shard", "sub"), None, "head"),
            P(("groups", "shard", "sub"), None),
            P(("groups", "shard", "sub"), None),
            P(("groups", "shard", "sub"), None),
            P(),
            P(None, "head"),
            P(None, "head"),
            P(None, "head"),
            P("head", None),
            P(None, "head"),
            P("head", None),
        ),
        out_specs=P(("groups", "shard", "sub"), None, "head"),
        check_vma=False,
    )
```

```python
import functools
import math

import jax
import jax.numpy as jnp
from jax import lax
from jax.experimental import pallas as pl
from jax.experimental.pallas import tpu as pltpu
from jax.sharding import PartitionSpec as P

D = 1024
HEAD_DIM = 64
CAP = 2
BLOCK = 64
QUAD = 4
WIDE = QUAD * HEAD_DIM
CHUNKS = 2
MIB = 1 << 20


epsilon = 1e-05


def dot(a, b):
    return jnp.dot(a, b, preferred_element_type=jnp.float32)


def gelu(x):
    return 0.5 * x * (1.0 + lax.erf(x * (2.0**-0.5)))


def in_hbm(x):
    return pltpu.with_memory_space_constraint(x, pltpu.HBM)


def whole(space):
    return pl.BlockSpec(memory_space=space)


def vmem(count):
    return [whole(pltpu.VMEM)] * count


def params(mib):
    return pltpu.CompilerParams(vmem_limit_bytes=mib * MIB)


def mlp_kernel(own, other, gain, wq, wup, wdn, q_out, mlp_out, normed_s):
    half = own.shape[1]
    units = wup.shape[1]
    chunk = units // 4
    x_other = other[...].astype(jnp.float32)
    x_own = own[...].astype(jnp.float32)

    def mean(a, b):
        total = jnp.sum(a, axis=-1, keepdims=True) + jnp.sum(b, axis=-1, keepdims=True)
        return total * (0.5 / half)

    average = mean(x_other, x_own)
    x_other = x_other - average
    x_own = x_own - average
    factor = lax.rsqrt(mean(x_other * x_other, x_own * x_own) + epsilon)
    normed_s[:, :half] = (x_other * factor * gain[:, :half]).astype(jnp.bfloat16)
    normed_s[:, half:] = (x_own * factor * gain[:, half:]).astype(jnp.bfloat16)
    normed = normed_s[...]
    q_out[...] = dot(normed, wq[...]).astype(jnp.bfloat16)
    for c in range(units // chunk):
        span = slice(c * chunk, (c + 1) * chunk)
        hidden = gelu(dot(normed, wup[:, span])).astype(jnp.bfloat16)
        term = dot(hidden, wdn[span, :])
        if c == 0:
            mlp_out[...] = term
        else:
            mlp_out[...] += term


def run_mlp(own, other, gain, wq, wup, wdn):
    rows = own.shape[0]
    width = wq.shape[0]
    units = wup.shape[1]
    return pl.pallas_call(
        mlp_kernel,
        out_shape=(
            jax.ShapeDtypeStruct((rows, wq.shape[1]), jnp.bfloat16),
            jax.ShapeDtypeStruct((rows, width), jnp.float32),
        ),
        in_specs=vmem(6),
        out_specs=tuple(vmem(2)),
        scratch_shapes=[pltpu.VMEM((rows, width), jnp.bfloat16)],
        compiler_params=params(16),
        cost_estimate=pl.CostEstimate(
            flops=2 * rows * width * (wq.shape[1] + 2 * units),
            bytes_accessed=2 * width * (wq.shape[1] + 2 * units),
            transcendentals=rows * units,
        ),
        name="mlp",
    )(own, other, gain, wq, wup, wdn)


def pick_kernel(mesh, out, sem):
    first = pl.multiple_of(lax.axis_index("head") * BLOCK, BLOCK)
    copy = pltpu.make_async_copy(mesh.at[pl.ds(first, BLOCK), :], out, sem)
    copy.start()
    copy.wait()


def run_pick(mesh):
    return pl.pallas_call(
        pick_kernel,
        out_shape=jax.ShapeDtypeStruct((BLOCK, mesh.shape[1]), mesh.dtype),
        in_specs=[whole(pltpu.HBM)],
        out_specs=whole(pltpu.VMEM),
        scratch_shapes=[pltpu.SemaphoreType.DMA(())],
        compiler_params=params(4),
        cost_estimate=pl.CostEstimate(flops=0, bytes_accessed=4 * mesh.size, transcendentals=0),
        name="pick",
    )(in_hbm(mesh))


def stage_kernel(axes, *refs):
    sources, targets, sem = refs[: len(axes)], refs[len(axes) : -1], refs[-1]
    h = lax.axis_index("head")
    copies = []
    for source, target, axis in zip(sources, targets, axes):
        if axis is None:
            copies.append(pltpu.make_async_copy(source, target, sem.at[len(copies)]))
            continue
        half = source.shape[axis] // 2
        for part, head in enumerate((1 - h, h)):
            span = pl.ds(pl.multiple_of(head * half, half), half)
            place = pl.ds(part * half, half)
            if axis == 0:
                pair = (source.at[span, :], target.at[place, :])
            else:
                pair = (source.at[:, span], target.at[:, place])
            copies.append(pltpu.make_async_copy(*pair, sem.at[len(copies)]))
    for copy in copies:
        copy.start()
    for copy in copies:
        copy.wait()


def run_stage(arrays, axes):
    size = sum(2 * array.size for array in arrays)
    return pl.pallas_call(
        functools.partial(stage_kernel, axes),
        out_shape=tuple(jax.ShapeDtypeStruct(array.shape, array.dtype) for array in arrays),
        in_specs=[whole(pltpu.HBM)] * len(arrays),
        out_specs=tuple(vmem(len(arrays))),
        scratch_shapes=[pltpu.SemaphoreType.DMA((2 * len(arrays),))],
        compiler_params=params(16),
        cost_estimate=pl.CostEstimate(flops=0, bytes_accessed=20 * size, transcendentals=0),
        name="stage",
    )(*(in_hbm(array) for array in arrays))


def project_kernel(*refs):
    pieces, (wk, wv, out) = refs[:-3], refs[-3:]
    width = wk.shape[1]
    rows = jnp.concatenate([piece[...] for piece in pieces], axis=0)
    out[:, :width] = dot(rows, wk[...]).astype(jnp.bfloat16)
    out[:, width:] = dot(rows, wv[...]).astype(jnp.bfloat16)


def run_project(pieces, wk, wv):
    rows = sum(piece.shape[0] for piece in pieces)
    depth, width = wk.shape
    return pl.pallas_call(
        project_kernel,
        out_shape=jax.ShapeDtypeStruct((rows, 2 * width), jnp.bfloat16),
        in_specs=vmem(len(pieces) + 2),
        out_specs=whole(pltpu.VMEM),
        compiler_params=params(8),
        cost_estimate=pl.CostEstimate(
            flops=800 * rows * depth * width,
            bytes_accessed=800 * depth * width + 800 * rows * depth,
            transcendentals=0,
        ),
        name="project",
    )(*pieces, wk, wv)


def table_kernel(mine, sibling, table, sem):
    copies = [
        pltpu.make_async_copy(mine, table.at[0, pl.ds(0, mine.shape[0])], sem.at[0]),
        pltpu.make_async_copy(sibling, table.at[1, pl.ds(0, mine.shape[0])], sem.at[1]),
    ]
    for copy in copies:
        copy.start()
    for copy in copies:
        copy.wait()


def run_table(mine, sibling, blocks):
    return pl.pallas_call(
        table_kernel,
        out_shape=jax.ShapeDtypeStruct((2, blocks) + mine.shape[1:], jnp.bfloat16),
        in_specs=vmem(2),
        out_specs=whole(pltpu.VMEM),
        scratch_shapes=[pltpu.SemaphoreType.DMA((2,))],
        compiler_params=params(8),
        cost_estimate=pl.CostEstimate(
            flops=0, bytes_accessed=80 * mine.size, transcendentals=0
        ),
        name="table",
    )(mine, sibling)


def project_out(c, att, mlp, wo, send, keep):
    width = send.shape[1]
    half = att.shape[1]
    for out, first in ((send, 0), (keep, half)):
        span = slice(first + c * width, first + (c + 1) * width)
        out[...] = (mlp[:, span] + dot(att[...], wo[:, span])).astype(jnp.bfloat16)


def attend_kernel(
    adjacency, q, mine, sibling, table_in, mlp, wo, send, keep, att, table, sem
):
    del table_in
    s = lax.axis_index("shard")
    h = lax.axis_index("head")
    u = lax.axis_index("sub")
    half = wo.shape[0]
    ready = table.shape[1] - mine.shape[0]
    copies = []
    for i, part in enumerate((mine, sibling)):
        target = table.at[i, pl.ds(ready, part.shape[0])]
        copies.append(pltpu.make_async_copy(part, target, sem.at[i]))
        copies[i].start()
    rows_of = lax.broadcasted_iota(jnp.int32, (WIDE, WIDE), 0) // BLOCK
    lanes_of = lax.broadcasted_iota(jnp.int32, (WIDE, WIDE), 1) // HEAD_DIM
    diagonal = rows_of == lanes_of
    lane_head = lax.broadcasted_iota(jnp.int32, (BLOCK, WIDE), 1) // HEAD_DIM
    scale = HEAD_DIM**-0.5 * math.log2(math.e)
    for copy in copies:
        copy.wait()
    for b in range(adjacency.shape[0]):
        rows = slice(b * BLOCK, (b + 1) * BLOCK)
        places = []
        for j in range(adjacency.shape[1]):
            m = adjacency[b, j]
            part = lax.rem(m, 2)
            core = lax.rem(m // 2, 2)
            distance = s ^ (m // 4)
            part = jnp.where(distance <= 1, part, part ^ h)
            places.append((core ^ u, distance * 2 + part))
        for g in range(half // WIDE):
            columns = slice(g * WIDE, (g + 1) * WIDE)
            keys = jnp.concatenate([table[i, p, :, columns] for i, p in places], axis=0)
            vcolumns = slice(half + g * WIDE, half + (g + 1) * WIDE)
            values = jnp.concatenate([table[i, p, :, vcolumns] for i, p in places], axis=0)
            stacked = jnp.concatenate([q[rows, columns]] * QUAD, axis=0)
            stacked = jnp.where(diagonal, stacked, jnp.zeros_like(stacked))
            scores = lax.dot_general(
                stacked, keys, (((1,), (1,)), ((), ())), preferred_element_type=jnp.float32
            )
            highest = jnp.max(scores, axis=-1, keepdims=True)
            weights = jnp.exp2((scores - highest) * scale)
            total = jnp.sum(weights, axis=-1, keepdims=True)
            probs = (weights * (1.0 / total)).astype(jnp.bfloat16)
            mixed = dot(probs, values)
            merged = mixed[0:BLOCK, :]
            for i in range(1, QUAD):
                merged = jnp.where(lane_head == i, mixed[i * BLOCK : (i + 1) * BLOCK, :], merged)
            att[rows, columns] = merged.astype(jnp.bfloat16)
    project_out(0, att, mlp, wo, send, keep)


def run_attend(adjacency, q, mine, sibling, table, mlp, wo):
    rows, half = q.shape
    part = jax.ShapeDtypeStruct((rows, half // CHUNKS), jnp.bfloat16)
    blocks = table.shape[0] * table.shape[1]
    send, keep, att, _ = pl.pallas_call(
        attend_kernel,
        out_shape=(
            part,
            part,
            jax.ShapeDtypeStruct(q.shape, jnp.bfloat16),
            jax.ShapeDtypeStruct(table.shape, jnp.bfloat16),
        ),
        in_specs=[whole(pltpu.SMEM)] + vmem(6),
        out_specs=tuple(vmem(4)),
        scratch_shapes=[pltpu.SemaphoreType.DMA((2,))],
        input_output_aliases={4: 3},
        compiler_params=params(16),
        cost_estimate=pl.CostEstimate(
            flops=20 * rows * half * (D + 8 * 8 * BLOCK),
            bytes_accessed=40 * blocks * BLOCK * half + 20 * half * D + 40 * rows * D,
            transcendentals=rows * 8 * BLOCK * half // HEAD_DIM,
        ),
        name="attend",
    )(adjacency, q, mine, sibling, table, mlp, wo)
    return send, keep, att


def run_project_out(c, att, mlp, wo):
    rows, half = att.shape
    part = jax.ShapeDtypeStruct((rows, half // CHUNKS), jnp.bfloat16)
    return pl.pallas_call(
        functools.partial(project_out, c),
        out_shape=(part, part),
        in_specs=vmem(3),
        out_specs=tuple(vmem(2)),
        compiler_params=params(8),
        cost_estimate=pl.CostEstimate(
            flops=200 * rows * half * D,
            bytes_accessed=200 * half * D,
            transcendentals=0,
        ),
        name="project_out",
    )(att, mlp, wo)


def combine_kernel(c, owners, grid_features, keep, received, out):
    count = grid_features.shape[0]
    width = keep.shape[1]
    names = [owners[t, 0] for t in range(count)]
    out[...] = jnp.zeros(out.shape, jnp.bfloat16)
    for t in range(count):
        rank = jnp.int32(0)
        for earlier in range(t):
            rank += (names[earlier] == names[t]).astype(jnp.int32)
        rows = slice(t * BLOCK, (t + 1) * BLOCK)
        partials = keep[rows, :].astype(jnp.float32) + received[rows, :].astype(jnp.float32)
        residual = grid_features[t, :, c * width : (c + 1) * width]
        updated = residual.astype(jnp.float32) + partials
        out[names[t] * CAP + rank] = updated.astype(jnp.bfloat16)


def run_combine(c, owners, grid_features, keep, received, shards):
    count, rows, _ = grid_features.shape
    width = keep.shape[1]
    return pl.pallas_call(
        functools.partial(combine_kernel, c),
        out_shape=jax.ShapeDtypeStruct((shards * CAP, rows, width), jnp.bfloat16),
        in_specs=[whole(pltpu.SMEM)] + vmem(3),
        out_specs=whole(pltpu.VMEM),
        compiler_params=params(8),
        cost_estimate=pl.CostEstimate(
            flops=3000 * count * rows * width,
            bytes_accessed=400 * rows * width * (3 * count + CAP * shards),
            transcendentals=0,
        ),
        name="combine",
    )(owners, grid_features, keep, received)


def place_kernel(c, arrived, *refs):
    out, sem = refs[-2:]
    width = arrived.shape[2]
    copy = pltpu.make_async_copy(arrived, out.at[:, :, pl.ds(c * width, width)], sem)
    copy.start()
    copy.wait()


def run_place(c, arrived, placed):
    slots, rows, width = arrived.shape
    return pl.pallas_call(
        functools.partial(place_kernel, c),
        out_shape=jax.ShapeDtypeStruct((slots, rows, CHUNKS * width), jnp.bfloat16),
        in_specs=vmem(1) + [whole(pltpu.HBM)] * len(placed),
        out_specs=whole(pltpu.HBM),
        scratch_shapes=[pltpu.SemaphoreType.DMA(())],
        input_output_aliases={1: 0} if placed else {},
        compiler_params=params(4),
        cost_estimate=pl.CostEstimate(
            flops=0, bytes_accessed=40 * slots * rows * width, transcendentals=0
        ),
        name="place",
    )(arrived, *placed)


def crossed(x, distance, size):
    return lax.ppermute(x, "shard", [(i, i ^ distance) for i in range(size)])


def swapped(x, axis):
    return lax.ppermute(x, axis, [(0, 1), (1, 0)])


def paired(
    grid_features,
    owners,
    adjacency,
    mesh_nodes,
    norm_gain,
    query_weight,
    key_weight,
    value_weight,
    output_weight,
    up_weight,
    down_weight,
):
    shards = lax.axis_size("shard")
    count, rows, half = grid_features.shape
    flat = grid_features.reshape(count * rows, half)
    far = crossed(run_pick(mesh_nodes), 2, shards)
    other = swapped(flat, "head")
    staged = run_stage(
        (
            flat,
            norm_gain.reshape(1, -1),
            query_weight,
            up_weight,
            down_weight,
            output_weight,
            key_weight,
            value_weight,
            mesh_nodes,
        ),
        (None, 1, 0, 0, 1, 1, None, None, None),
    )
    flat, gain, wq, wup, wdn, wo, wk, wv, mesh = staged
    near = crossed(mesh, 1, shards)
    farther = crossed(far, 1, shards)
    far_pair = swapped(far, "head")
    queries, mlp = run_mlp(flat, other, gain, wq, wup, wdn)
    queries, mlp, farther = lax.optimization_barrier((queries, mlp, farther))
    farther_pair = swapped(farther, "head")
    blocked = (-1, BLOCK, 2 * half)
    mine_a = run_project((mesh, near, far, far_pair, farther), wk, wv)
    sibling_a = swapped(mine_a, "sub")
    table = run_table(mine_a.reshape(blocked), sibling_a.reshape(blocked), 2 * shards)
    mine_b = run_project((farther_pair,), wk, wv)
    sibling_b = swapped(mine_b, "sub")
    send, keep, att = run_attend(
        adjacency, queries, mine_b.reshape(blocked), sibling_b.reshape(blocked), table, mlp, wo
    )
    placed = []
    slots = None
    for c in range(CHUNKS):
        if c > 0:
            send, keep = run_project_out(c, att, mlp, wo)
        received = swapped(send, "head")
        if slots is not None:
            received, _ = lax.optimization_barrier((received, slots))
        slots = run_combine(c, owners, grid_features, keep, received, shards)
        arrived = lax.all_to_all(slots, "shard", split_axis=0, concat_axis=0, tiled=True)
        placed = [run_place(c, arrived, placed)]
    return placed[0]


def attend_plain(queries, key_table, value_table, chosen, scaling):
    count = chosen.shape[0]
    picked_keys = key_table[chosen]
    picked_keys = picked_keys.reshape(count, -1, picked_keys.shape[3], picked_keys.shape[4])
    picked_values = value_table[chosen]
    picked_values = picked_values.reshape(count, -1, picked_values.shape[3], picked_values.shape[4])
    scores = (
        jnp.einsum("gqhe,gkhe->ghqk", queries, picked_keys, preferred_element_type=jnp.float32)
        * scaling
    )
    highest = jnp.max(scores, axis=-1, keepdims=True)
    weights = jnp.exp(scores - highest)
    weights = (weights / jnp.sum(weights, axis=-1, keepdims=True)).astype(jnp.bfloat16)
    result = jnp.einsum(
        "ghqk,gkhe->gqhe", weights, picked_values, preferred_element_type=jnp.float32
    )
    return result.astype(jnp.bfloat16)


def general(
    grid_features,
    owners,
    adjacency,
    mesh_nodes,
    norm_gain,
    query_weight,
    key_weight,
    value_weight,
    output_weight,
    up_weight,
    down_weight,
):
    shard_count = lax.axis_size("shard")
    head_count = lax.axis_size("head")
    local_blocks, block_rows, feature_share = grid_features.shape
    slots = shard_count * CAP
    owner_col = owners[:, 0]
    position = jnp.arange(local_blocks, dtype=jnp.int32)
    earlier = (owner_col[:, None] == owner_col[None, :]) & (position[None, :] < position[:, None])
    target = owner_col * CAP + jnp.sum(earlier.astype(jnp.int32), axis=1)
    dispatch = (target[:, None] == jnp.arange(slots, dtype=jnp.int32)[None, :]).astype(jnp.bfloat16)
    offset = lax.axis_index("head") * (D // head_count)
    projected = jnp.stack(
        (
            jnp.dot(mesh_nodes, key_weight, preferred_element_type=jnp.float32).astype(
                jnp.bfloat16
            ),
            jnp.dot(mesh_nodes, value_weight, preferred_element_type=jnp.float32).astype(
                jnp.bfloat16
            ),
        )
    )
    tables = lax.all_gather(projected, ("shard", "sub"), axis=1, tiled=True)
    head_local = query_weight.shape[1] // HEAD_DIM
    key_table = tables[0].reshape(-1, block_rows, head_local, HEAD_DIM)
    value_table = tables[1].reshape(-1, block_rows, head_local, HEAD_DIM)
    send_lists = jnp.full((slots, adjacency.shape[1]), -1, jnp.int32).at[target].set(adjacency)
    send_lists = send_lists.reshape(shard_count, CAP, -1)
    complete = lax.all_gather(grid_features, "head", axis=2, tiled=True)
    outgoing = jnp.einsum(
        "gs,gbd->sbd", dispatch, complete, preferred_element_type=jnp.float32
    ).astype(jnp.bfloat16)
    arrived, lists = (
        lax.all_to_all(
            outgoing.reshape(shard_count, CAP, block_rows, D),
            "shard",
            split_axis=0,
            concat_axis=0,
            tiled=True,
        ),
        lax.all_to_all(send_lists, "shard", split_axis=0, concat_axis=0, tiled=True),
    )
    arrived = arrived.reshape(slots, block_rows, D)
    residual = lax.dynamic_slice_in_dim(arrived, offset, D // head_count, 2)
    lists = lists.reshape(slots, -1)
    count = arrived.shape[0]
    values_f = arrived.astype(jnp.float32)
    average = jnp.mean(values_f, axis=-1, keepdims=True)
    centered = values_f - average
    variance = jnp.mean(centered * centered, axis=-1, keepdims=True)
    normed = (centered * lax.rsqrt(variance + epsilon) * norm_gain).astype(jnp.bfloat16)
    flattened = normed.reshape(-1, D)
    queries = jnp.dot(flattened, query_weight, preferred_element_type=jnp.float32).astype(
        jnp.bfloat16
    )
    blocks_each = math.gcd(count, max(1, 512 // block_rows))
    steps_count = count // blocks_each
    queries = queries.reshape(steps_count, blocks_each, block_rows, head_local, HEAD_DIM)

    def attend_step(operands):
        return attend_plain(operands[0], key_table, value_table, operands[1], HEAD_DIM ** (-0.5))

    attended = lax.map(
        attend_step, (queries, jnp.maximum(lists, 0).reshape(steps_count, blocks_each, -1))
    )
    attended = attended.reshape(-1, head_local * HEAD_DIM)
    hidden = jax.nn.gelu(
        jnp.dot(flattened, up_weight, preferred_element_type=jnp.float32), approximate=False
    ).astype(jnp.bfloat16)
    branch = jnp.dot(attended, output_weight, preferred_element_type=jnp.float32)
    branch = branch + jnp.dot(hidden, down_weight, preferred_element_type=jnp.float32)
    branch = branch.reshape(count, block_rows, D)
    reduced = lax.psum_scatter(
        branch.astype(jnp.bfloat16), "head", scatter_dimension=2, tiled=True
    ).astype(jnp.float32)
    occupied = lists[:, 0] >= 0
    summed = residual.astype(jnp.float32) + reduced
    return jnp.where(occupied[:, None, None], summed, 0.0).astype(jnp.bfloat16)


def local(grid_features, owners, adjacency, mesh_nodes, *parameters):
    sizes = [lax.axis_size(axis) for axis in ("shard", "head", "sub")]
    small = grid_features.shape[:2] == (4, BLOCK) and mesh_nodes.shape[0] == 2 * BLOCK
    if sizes == [4, 2, 2] and small:
        return paired(grid_features, owners, adjacency, mesh_nodes, *parameters)
    return general(grid_features, owners, adjacency, mesh_nodes, *parameters)


def solution(mesh):
    return jax.shard_map(
        local,
        mesh=mesh,
        in_specs=(
            P(("groups", "shard", "sub"), None, "head"),
            P(("groups", "shard", "sub"), None),
            P(("groups", "shard", "sub"), None),
            P(("groups", "shard", "sub"), None),
            P(),
            P(None, "head"),
            P(None, "head"),
            P(None, "head"),
            P("head", None),
            P(None, "head"),
            P("head", None),
        ),
        out_specs=P(("groups", "shard", "sub"), None, "head"),
        check_vma=False,
    )
```

```python
import functools
import math

import jax
import jax.numpy as jnp
from jax import lax
from jax.experimental import pallas as pl
from jax.experimental.pallas import tpu as pltpu
from jax.sharding import PartitionSpec as P

D = 1024
HEAD_DIM = 64
CAP = 2
BLOCK = 64
QUAD = 4
WIDE = QUAD * HEAD_DIM
CHUNKS = 2
MIB = 1 << 20


epsilon = 1e-05


def dot(a, b):
    return jnp.dot(a, b, preferred_element_type=jnp.float32)


def gelu(x):
    return 0.5 * x * (1.0 + lax.erf(x * (2.0**-0.5)))


def in_hbm(x):
    return pltpu.with_memory_space_constraint(x, pltpu.HBM)


def whole(space):
    return pl.BlockSpec(memory_space=space)


def vmem(count):
    return [whole(pltpu.VMEM)] * count


def params(mib):
    return pltpu.CompilerParams(vmem_limit_bytes=mib * MIB)


def mlp_kernel(own, other, gain, wq, wup, wdn, q_out, mlp_out, normed_s):
    half = own.shape[1]
    units = wup.shape[1]
    chunk = units // 4
    x_other = other[...].astype(jnp.float32)
    x_own = own[...].astype(jnp.float32)

    def mean(a, b):
        total = jnp.sum(a, axis=-1, keepdims=True) + jnp.sum(b, axis=-1, keepdims=True)
        return total * (0.5 / half)

    average = mean(x_other, x_own)
    x_other = x_other - average
    x_own = x_own - average
    factor = lax.rsqrt(mean(x_other * x_other, x_own * x_own) + epsilon)
    normed_s[:, :half] = (x_other * factor * gain[:, :half]).astype(jnp.bfloat16)
    normed_s[:, half:] = (x_own * factor * gain[:, half:]).astype(jnp.bfloat16)
    normed = normed_s[...]
    q_out[...] = dot(normed, wq[...]).astype(jnp.bfloat16)
    for c in range(units // chunk):
        span = slice(c * chunk, (c + 1) * chunk)
        hidden = gelu(dot(normed, wup[:, span])).astype(jnp.bfloat16)
        term = dot(hidden, wdn[span, :])
        if c == 0:
            mlp_out[...] = term
        else:
            mlp_out[...] += term


def run_mlp(own, other, gain, wq, wup, wdn):
    rows = own.shape[0]
    width = wq.shape[0]
    units = wup.shape[1]
    return pl.pallas_call(
        mlp_kernel,
        out_shape=(
            jax.ShapeDtypeStruct((rows, wq.shape[1]), jnp.bfloat16),
            jax.ShapeDtypeStruct((rows, width), jnp.float32),
        ),
        in_specs=vmem(6),
        out_specs=tuple(vmem(2)),
        scratch_shapes=[pltpu.VMEM((rows, width), jnp.bfloat16)],
        compiler_params=params(16),
        cost_estimate=pl.CostEstimate(
            flops=2 * rows * width * (wq.shape[1] + 2 * units),
            bytes_accessed=2 * width * (wq.shape[1] + 2 * units),
            transcendentals=rows * units,
        ),
        name="mlp",
    )(own, other, gain, wq, wup, wdn)


def pick_kernel(mesh, out, sem):
    first = pl.multiple_of(lax.axis_index("head") * BLOCK, BLOCK)
    copy = pltpu.make_async_copy(mesh.at[pl.ds(first, BLOCK), :], out, sem)
    copy.start()
    copy.wait()


def run_pick(mesh):
    return pl.pallas_call(
        pick_kernel,
        out_shape=jax.ShapeDtypeStruct((BLOCK, mesh.shape[1]), mesh.dtype),
        in_specs=[whole(pltpu.HBM)],
        out_specs=whole(pltpu.VMEM),
        scratch_shapes=[pltpu.SemaphoreType.DMA(())],
        compiler_params=params(4),
        cost_estimate=pl.CostEstimate(flops=0, bytes_accessed=4 * mesh.size, transcendentals=0),
        name="pick",
    )(in_hbm(mesh))


def stage_kernel(axes, *refs):
    sources, targets, sem = refs[: len(axes)], refs[len(axes) : -1], refs[-1]
    h = lax.axis_index("head")
    copies = []
    for source, target, axis in zip(sources, targets, axes):
        if axis is None:
            copies.append(pltpu.make_async_copy(source, target, sem.at[len(copies)]))
            continue
        half = source.shape[axis] // 2
        for part, head in enumerate((1 - h, h)):
            span = pl.ds(pl.multiple_of(head * half, half), half)
            place = pl.ds(part * half, half)
            if axis == 0:
                pair = (source.at[span, :], target.at[place, :])
            else:
                pair = (source.at[:, span], target.at[:, place])
            copies.append(pltpu.make_async_copy(*pair, sem.at[len(copies)]))
    for copy in copies:
        copy.start()
    for copy in copies:
        copy.wait()


def run_stage(arrays, axes):
    size = sum(2 * array.size for array in arrays)
    return pl.pallas_call(
        functools.partial(stage_kernel, axes),
        out_shape=tuple(jax.ShapeDtypeStruct(array.shape, array.dtype) for array in arrays),
        in_specs=[whole(pltpu.HBM)] * len(arrays),
        out_specs=tuple(vmem(len(arrays))),
        scratch_shapes=[pltpu.SemaphoreType.DMA((2 * len(arrays),))],
        compiler_params=params(16),
        cost_estimate=pl.CostEstimate(flops=0, bytes_accessed=20 * size, transcendentals=0),
        name="stage",
    )(*(in_hbm(array) for array in arrays))


def project_kernel(*refs):
    pieces, (wk, wv, out) = refs[:-3], refs[-3:]
    width = wk.shape[1]
    rows = jnp.concatenate([piece[...] for piece in pieces], axis=0)
    out[:, :width] = dot(rows, wk[...]).astype(jnp.bfloat16)
    out[:, width:] = dot(rows, wv[...]).astype(jnp.bfloat16)


def run_project(pieces, wk, wv):
    rows = sum(piece.shape[0] for piece in pieces)
    depth, width = wk.shape
    return pl.pallas_call(
        project_kernel,
        out_shape=jax.ShapeDtypeStruct((rows, 2 * width), jnp.bfloat16),
        in_specs=vmem(len(pieces) + 2),
        out_specs=whole(pltpu.VMEM),
        compiler_params=params(8),
        cost_estimate=pl.CostEstimate(
            flops=300 * rows * depth * width,
            bytes_accessed=300 * depth * width + 300 * rows * depth,
            transcendentals=0,
        ),
        name="project",
    )(*pieces, wk, wv)


def table_kernel(mine, sibling, table, sem):
    copies = [
        pltpu.make_async_copy(mine, table.at[0, pl.ds(0, mine.shape[0])], sem.at[0]),
        pltpu.make_async_copy(sibling, table.at[1, pl.ds(0, mine.shape[0])], sem.at[1]),
    ]
    for copy in copies:
        copy.start()
    for copy in copies:
        copy.wait()


def run_table(mine, sibling, blocks):
    return pl.pallas_call(
        table_kernel,
        out_shape=jax.ShapeDtypeStruct((2, blocks) + mine.shape[1:], jnp.bfloat16),
        in_specs=vmem(2),
        out_specs=whole(pltpu.VMEM),
        scratch_shapes=[pltpu.SemaphoreType.DMA((2,))],
        compiler_params=params(8),
        cost_estimate=pl.CostEstimate(
            flops=0, bytes_accessed=80 * mine.size, transcendentals=0
        ),
        name="table",
    )(mine, sibling)


def project_out(c, att, mlp, wo, send, keep):
    width = send.shape[1]
    half = att.shape[1]
    for out, first in ((send, 0), (keep, half)):
        span = slice(first + c * width, first + (c + 1) * width)
        out[...] = (mlp[:, span] + dot(att[...], wo[:, span])).astype(jnp.bfloat16)


def attend_kernel(
    adjacency, q, mine, sibling, table_in, mlp, wo, send, keep, att, table, sem
):
    del table_in
    s = lax.axis_index("shard")
    h = lax.axis_index("head")
    u = lax.axis_index("sub")
    half = wo.shape[0]
    ready = table.shape[1] - mine.shape[0]
    copies = []
    for i, part in enumerate((mine, sibling)):
        target = table.at[i, pl.ds(ready, part.shape[0])]
        copies.append(pltpu.make_async_copy(part, target, sem.at[i]))
        copies[i].start()
    rows_of = lax.broadcasted_iota(jnp.int32, (WIDE, WIDE), 0) // BLOCK
    lanes_of = lax.broadcasted_iota(jnp.int32, (WIDE, WIDE), 1) // HEAD_DIM
    diagonal = rows_of == lanes_of
    lane_head = lax.broadcasted_iota(jnp.int32, (BLOCK, WIDE), 1) // HEAD_DIM
    scale = HEAD_DIM**-0.5 * math.log2(math.e)
    for copy in copies:
        copy.wait()
    for b in range(adjacency.shape[0]):
        rows = slice(b * BLOCK, (b + 1) * BLOCK)
        places = []
        for j in range(adjacency.shape[1]):
            m = adjacency[b, j]
            part = lax.rem(m, 2)
            core = lax.rem(m // 2, 2)
            distance = s ^ (m // 4)
            part = jnp.where(distance <= 1, part, part ^ h)
            places.append((core ^ u, distance * 2 + part))
        for g in range(half // WIDE):
            columns = slice(g * WIDE, (g + 1) * WIDE)
            keys = jnp.concatenate([table[i, p, :, columns] for i, p in places], axis=0)
            vcolumns = slice(half + g * WIDE, half + (g + 1) * WIDE)
            values = jnp.concatenate([table[i, p, :, vcolumns] for i, p in places], axis=0)
            stacked = jnp.concatenate([q[rows, columns]] * QUAD, axis=0)
            stacked = jnp.where(diagonal, stacked, jnp.zeros_like(stacked))
            scores = lax.dot_general(
                stacked, keys, (((1,), (1,)), ((), ())), preferred_element_type=jnp.float32
            )
            highest = jnp.max(scores, axis=-1, keepdims=True)
            weights = jnp.exp2((scores - highest) * scale)
            total = jnp.sum(weights, axis=-1, keepdims=True)
            probs = (weights * (1.0 / total)).astype(jnp.bfloat16)
            mixed = dot(probs, values)
            merged = mixed[0:BLOCK, :]
            for i in range(1, QUAD):
                merged = jnp.where(lane_head == i, mixed[i * BLOCK : (i + 1) * BLOCK, :], merged)
            att[rows, columns] = merged.astype(jnp.bfloat16)
    project_out(0, att, mlp, wo, send, keep)


def run_attend(adjacency, q, mine, sibling, table, mlp, wo):
    rows, half = q.shape
    part = jax.ShapeDtypeStruct((rows, half // CHUNKS), jnp.bfloat16)
    blocks = table.shape[0] * table.shape[1]
    send, keep, att, _ = pl.pallas_call(
        attend_kernel,
        out_shape=(
            part,
            part,
            jax.ShapeDtypeStruct(q.shape, jnp.bfloat16),
            jax.ShapeDtypeStruct(table.shape, jnp.bfloat16),
        ),
        in_specs=[whole(pltpu.SMEM)] + vmem(6),
        out_specs=tuple(vmem(4)),
        scratch_shapes=[pltpu.SemaphoreType.DMA((2,))],
        input_output_aliases={4: 3},
        compiler_params=params(16),
        cost_estimate=pl.CostEstimate(
            flops=20 * rows * half * (D + 8 * 8 * BLOCK),
            bytes_accessed=40 * blocks * BLOCK * half + 20 * half * D + 40 * rows * D,
            transcendentals=rows * 8 * BLOCK * half // HEAD_DIM,
        ),
        name="attend",
    )(adjacency, q, mine, sibling, table, mlp, wo)
    return send, keep, att


def run_project_out(c, att, mlp, wo):
    rows, half = att.shape
    part = jax.ShapeDtypeStruct((rows, half // CHUNKS), jnp.bfloat16)
    return pl.pallas_call(
        functools.partial(project_out, c),
        out_shape=(part, part),
        in_specs=vmem(3),
        out_specs=tuple(vmem(2)),
        compiler_params=params(8),
        cost_estimate=pl.CostEstimate(
            flops=200 * rows * half * D,
            bytes_accessed=200 * half * D,
            transcendentals=0,
        ),
        name="project_out",
    )(att, mlp, wo)


def combine_kernel(c, owners, grid_features, keep, received, *outs):
    s = lax.axis_index("shard")
    count = grid_features.shape[0]
    width = keep.shape[1]
    names = [owners[t, 0] for t in range(count)]
    for d, out in enumerate(outs):
        for j in range(CAP):
            out[j] = jnp.zeros(out.shape[1:], jnp.bfloat16)
        seen = jnp.int32(0)
        for t in range(count):
            hit = names[t] == s ^ d
            rank = seen

            @pl.when(hit)
            def _():
                rows = slice(t * BLOCK, (t + 1) * BLOCK)
                partials = keep[rows, :].astype(jnp.float32)
                partials = partials + received[rows, :].astype(jnp.float32)
                residual = grid_features[t, :, c * width : (c + 1) * width]
                out[rank] = (residual.astype(jnp.float32) + partials).astype(jnp.bfloat16)

            seen = seen + hit.astype(jnp.int32)


def run_combine(c, owners, grid_features, keep, received, shards):
    count, rows, _ = grid_features.shape
    width = keep.shape[1]
    slot = jax.ShapeDtypeStruct((CAP, rows, width), jnp.bfloat16)
    return pl.pallas_call(
        functools.partial(combine_kernel, c),
        out_shape=(slot,) * shards,
        in_specs=[whole(pltpu.SMEM)] + vmem(3),
        out_specs=tuple(vmem(shards)),
        compiler_params=params(8),
        cost_estimate=pl.CostEstimate(
            flops=3000 * count * rows * width,
            bytes_accessed=400 * rows * width * (3 * count + CAP * shards),
            transcendentals=0,
        ),
        name="combine",
    )(owners, grid_features, keep, received)


def place_kernel(c, order, *refs):
    out, sem = refs[-2:]
    s = lax.axis_index("shard")
    copies = []
    for i, d in enumerate(order):
        width = refs[i].shape[2]
        columns = pl.ds(c * width, width)
        slots = pl.ds((s ^ d) * CAP, CAP)
        copies.append(pltpu.make_async_copy(refs[i], out.at[slots, :, columns], sem.at[i]))
        copies[i].start()
    for copy in copies:
        copy.wait()


def run_place(c, order, arrived, placed):
    shards = len(arrived)
    _, rows, width = arrived[0].shape
    shape = (shards * CAP, rows, CHUNKS * width)
    return pl.pallas_call(
        functools.partial(place_kernel, c, order),
        out_shape=jax.ShapeDtypeStruct(shape, jnp.bfloat16),
        in_specs=vmem(shards) + [whole(pltpu.HBM)] * len(placed),
        out_specs=whole(pltpu.HBM),
        scratch_shapes=[pltpu.SemaphoreType.DMA((shards,))],
        input_output_aliases={shards: 0} if placed else {},
        compiler_params=params(4),
        cost_estimate=pl.CostEstimate(
            flops=0, bytes_accessed=40 * CAP * shards * rows * width, transcendentals=0
        ),
        name="place",
    )(*arrived, *placed)


def crossed(x, distance, size):
    return lax.ppermute(x, "shard", [(i, i ^ distance) for i in range(size)])


def swapped(x, axis):
    return lax.ppermute(x, axis, [(0, 1), (1, 0)])


def paired(
    grid_features,
    owners,
    adjacency,
    mesh_nodes,
    norm_gain,
    query_weight,
    key_weight,
    value_weight,
    output_weight,
    up_weight,
    down_weight,
):
    shards = lax.axis_size("shard")
    count, rows, half = grid_features.shape
    flat = grid_features.reshape(count * rows, half)
    far = crossed(run_pick(mesh_nodes), 2, shards)
    near = crossed(mesh_nodes, 1, shards)
    other = swapped(flat, "head")
    staged = run_stage(
        (
            flat,
            norm_gain.reshape(1, -1),
            query_weight,
            up_weight,
            down_weight,
            output_weight,
            key_weight,
            value_weight,
            mesh_nodes,
        ),
        (None, 1, 0, 0, 1, 1, None, None, None),
    )
    flat, gain, wq, wup, wdn, wo, wk, wv, mesh = staged
    farther = crossed(far, 1, shards)
    far_pair = swapped(far, "head")
    queries, mlp = run_mlp(flat, other, gain, wq, wup, wdn)
    queries, mlp, farther = lax.optimization_barrier((queries, mlp, farther))
    farther_pair = swapped(farther, "head")
    blocked = (-1, BLOCK, 2 * half)
    mine_a = run_project((mesh, near, far, far_pair, farther), wk, wv)
    sibling_a = swapped(mine_a, "sub")
    table = run_table(mine_a.reshape(blocked), sibling_a.reshape(blocked), 2 * shards)
    mine_b = run_project((farther_pair,), wk, wv)
    sibling_b = swapped(mine_b, "sub")
    send, keep, att = run_attend(
        adjacency, queries, mine_b.reshape(blocked), sibling_b.reshape(blocked), table, mlp, wo
    )
    placed = []
    slots = None
    for c in range(CHUNKS):
        if c > 0:
            send, keep = run_project_out(c, att, mlp, wo)
        received = swapped(send, "head")
        if slots is not None:
            received, _ = lax.optimization_barrier((received, slots[0]))
        slots = run_combine(c, owners, grid_features, keep, received, shards)
        order = (2, 3, 1, 0)
        arrived = [crossed(slots[d], d, shards) if d else slots[d] for d in order]
        placed = [run_place(c, order, arrived, placed)]
    return placed[0]


def attend_plain(queries, key_table, value_table, chosen, scaling):
    count = chosen.shape[0]
    picked_keys = key_table[chosen]
    picked_keys = picked_keys.reshape(count, -1, picked_keys.shape[3], picked_keys.shape[4])
    picked_values = value_table[chosen]
    picked_values = picked_values.reshape(count, -1, picked_values.shape[3], picked_values.shape[4])
    scores = (
        jnp.einsum("gqhe,gkhe->ghqk", queries, picked_keys, preferred_element_type=jnp.float32)
        * scaling
    )
    highest = jnp.max(scores, axis=-1, keepdims=True)
    weights = jnp.exp(scores - highest)
    weights = (weights / jnp.sum(weights, axis=-1, keepdims=True)).astype(jnp.bfloat16)
    result = jnp.einsum(
        "ghqk,gkhe->gqhe", weights, picked_values, preferred_element_type=jnp.float32
    )
    return result.astype(jnp.bfloat16)


def general(
    grid_features,
    owners,
    adjacency,
    mesh_nodes,
    norm_gain,
    query_weight,
    key_weight,
    value_weight,
    output_weight,
    up_weight,
    down_weight,
):
    shard_count = lax.axis_size("shard")
    head_count = lax.axis_size("head")
    local_blocks, block_rows, feature_share = grid_features.shape
    slots = shard_count * CAP
    owner_col = owners[:, 0]
    position = jnp.arange(local_blocks, dtype=jnp.int32)
    earlier = (owner_col[:, None] == owner_col[None, :]) & (position[None, :] < position[:, None])
    target = owner_col * CAP + jnp.sum(earlier.astype(jnp.int32), axis=1)
    dispatch = (target[:, None] == jnp.arange(slots, dtype=jnp.int32)[None, :]).astype(jnp.bfloat16)
    offset = lax.axis_index("head") * (D // head_count)
    projected = jnp.stack(
        (
            jnp.dot(mesh_nodes, key_weight, preferred_element_type=jnp.float32).astype(
                jnp.bfloat16
            ),
            jnp.dot(mesh_nodes, value_weight, preferred_element_type=jnp.float32).astype(
                jnp.bfloat16
            ),
        )
    )
    tables = lax.all_gather(projected, ("shard", "sub"), axis=1, tiled=True)
    head_local = query_weight.shape[1] // HEAD_DIM
    key_table = tables[0].reshape(-1, block_rows, head_local, HEAD_DIM)
    value_table = tables[1].reshape(-1, block_rows, head_local, HEAD_DIM)
    send_lists = jnp.full((slots, adjacency.shape[1]), -1, jnp.int32).at[target].set(adjacency)
    send_lists = send_lists.reshape(shard_count, CAP, -1)
    complete = lax.all_gather(grid_features, "head", axis=2, tiled=True)
    outgoing = jnp.einsum(
        "gs,gbd->sbd", dispatch, complete, preferred_element_type=jnp.float32
    ).astype(jnp.bfloat16)
    arrived, lists = (
        lax.all_to_all(
            outgoing.reshape(shard_count, CAP, block_rows, D),
            "shard",
            split_axis=0,
            concat_axis=0,
            tiled=True,
        ),
        lax.all_to_all(send_lists, "shard", split_axis=0, concat_axis=0, tiled=True),
    )
    arrived = arrived.reshape(slots, block_rows, D)
    residual = lax.dynamic_slice_in_dim(arrived, offset, D // head_count, 2)
    lists = lists.reshape(slots, -1)
    count = arrived.shape[0]
    values_f = arrived.astype(jnp.float32)
    average = jnp.mean(values_f, axis=-1, keepdims=True)
    centered = values_f - average
    variance = jnp.mean(centered * centered, axis=-1, keepdims=True)
    normed = (centered * lax.rsqrt(variance + epsilon) * norm_gain).astype(jnp.bfloat16)
    flattened = normed.reshape(-1, D)
    queries = jnp.dot(flattened, query_weight, preferred_element_type=jnp.float32).astype(
        jnp.bfloat16
    )
    blocks_each = math.gcd(count, max(1, 512 // block_rows))
    steps_count = count // blocks_each
    queries = queries.reshape(steps_count, blocks_each, block_rows, head_local, HEAD_DIM)

    def attend_step(operands):
        return attend_plain(operands[0], key_table, value_table, operands[1], HEAD_DIM ** (-0.5))

    attended = lax.map(
        attend_step, (queries, jnp.maximum(lists, 0).reshape(steps_count, blocks_each, -1))
    )
    attended = attended.reshape(-1, head_local * HEAD_DIM)
    hidden = jax.nn.gelu(
        jnp.dot(flattened, up_weight, preferred_element_type=jnp.float32), approximate=False
    ).astype(jnp.bfloat16)
    branch = jnp.dot(attended, output_weight, preferred_element_type=jnp.float32)
    branch = branch + jnp.dot(hidden, down_weight, preferred_element_type=jnp.float32)
    branch = branch.reshape(count, block_rows, D)
    reduced = lax.psum_scatter(
        branch.astype(jnp.bfloat16), "head", scatter_dimension=2, tiled=True
    ).astype(jnp.float32)
    occupied = lists[:, 0] >= 0
    summed = residual.astype(jnp.float32) + reduced
    return jnp.where(occupied[:, None, None], summed, 0.0).astype(jnp.bfloat16)


def local(grid_features, owners, adjacency, mesh_nodes, *parameters):
    sizes = [lax.axis_size(axis) for axis in ("shard", "head", "sub")]
    small = grid_features.shape[:2] == (4, BLOCK) and mesh_nodes.shape[0] == 2 * BLOCK
    if sizes == [4, 2, 2] and small:
        return paired(grid_features, owners, adjacency, mesh_nodes, *parameters)
    return general(grid_features, owners, adjacency, mesh_nodes, *parameters)


def solution(mesh):
    return jax.shard_map(
        local,
        mesh=mesh,
        in_specs=(
            P(("groups", "shard", "sub"), None, "head"),
            P(("groups", "shard", "sub"), None),
            P(("groups", "shard", "sub"), None),
            P(("groups", "shard", "sub"), None),
            P(),
            P(None, "head"),
            P(None, "head"),
            P(None, "head"),
            P("head", None),
            P(None, "head"),
            P("head", None),
        ),
        out_specs=P(("groups", "shard", "sub"), None, "head"),
        check_vma=False,
    )
```

```python
import functools
import math

import jax
import jax.numpy as jnp
from jax import lax
from jax.experimental import pallas as pl
from jax.experimental.pallas import tpu as pltpu
from jax.sharding import PartitionSpec as P

D = 1024
HEAD_DIM = 64
CAP = 2
BLOCK = 64
QUAD = 4
WIDE = QUAD * HEAD_DIM
CHUNKS = 2
MIB = 1 << 20


epsilon = 1e-05


def dot(a, b):
    return jnp.dot(a, b, preferred_element_type=jnp.float32)


def gelu(x):
    return 0.5 * x * (1.0 + lax.erf(x * (2.0**-0.5)))


def in_hbm(x):
    return pltpu.with_memory_space_constraint(x, pltpu.HBM)


def whole(space):
    return pl.BlockSpec(memory_space=space)


def vmem(count):
    return [whole(pltpu.VMEM)] * count


def params(mib):
    return pltpu.CompilerParams(vmem_limit_bytes=mib * MIB)


def mlp_kernel(own, other, gain, wq, wup, wdn, q_out, mlp_out, normed_s):
    half = own.shape[1]
    units = wup.shape[1]
    chunk = units // 4
    x_other = other[...].astype(jnp.float32)
    x_own = own[...].astype(jnp.float32)

    def mean(a, b):
        total = jnp.sum(a, axis=-1, keepdims=True) + jnp.sum(b, axis=-1, keepdims=True)
        return total * (0.5 / half)

    average = mean(x_other, x_own)
    x_other = x_other - average
    x_own = x_own - average
    factor = lax.rsqrt(mean(x_other * x_other, x_own * x_own) + epsilon)
    normed_s[:, :half] = (x_other * factor * gain[:, :half]).astype(jnp.bfloat16)
    normed_s[:, half:] = (x_own * factor * gain[:, half:]).astype(jnp.bfloat16)
    normed = normed_s[...]
    q_out[...] = dot(normed, wq[...]).astype(jnp.bfloat16)
    for c in range(units // chunk):
        span = slice(c * chunk, (c + 1) * chunk)
        hidden = gelu(dot(normed, wup[:, span])).astype(jnp.bfloat16)
        term = dot(hidden, wdn[span, :])
        if c == 0:
            mlp_out[...] = term
        else:
            mlp_out[...] += term


def run_mlp(own, other, gain, wq, wup, wdn):
    rows = own.shape[0]
    width = wq.shape[0]
    units = wup.shape[1]
    return pl.pallas_call(
        mlp_kernel,
        out_shape=(
            jax.ShapeDtypeStruct((rows, wq.shape[1]), jnp.bfloat16),
            jax.ShapeDtypeStruct((rows, width), jnp.float32),
        ),
        in_specs=vmem(6),
        out_specs=tuple(vmem(2)),
        scratch_shapes=[pltpu.VMEM((rows, width), jnp.bfloat16)],
        compiler_params=params(16),
        cost_estimate=pl.CostEstimate(
            flops=2 * rows * width * (wq.shape[1] + 2 * units),
            bytes_accessed=2 * width * (wq.shape[1] + 2 * units),
            transcendentals=rows * units,
        ),
        name="mlp",
    )(own, other, gain, wq, wup, wdn)


def pick_kernel(mesh, out, sem):
    first = pl.multiple_of(lax.axis_index("head") * BLOCK, BLOCK)
    copy = pltpu.make_async_copy(mesh.at[pl.ds(first, BLOCK), :], out, sem)
    copy.start()
    copy.wait()


def run_pick(mesh):
    return pl.pallas_call(
        pick_kernel,
        out_shape=jax.ShapeDtypeStruct((BLOCK, mesh.shape[1]), mesh.dtype),
        in_specs=[whole(pltpu.HBM)],
        out_specs=whole(pltpu.VMEM),
        scratch_shapes=[pltpu.SemaphoreType.DMA(())],
        compiler_params=params(4),
        cost_estimate=pl.CostEstimate(flops=0, bytes_accessed=4 * mesh.size, transcendentals=0),
        name="pick",
    )(in_hbm(mesh))


def stage_kernel(axes, *refs):
    sources, targets, sem = refs[: len(axes)], refs[len(axes) : -1], refs[-1]
    h = lax.axis_index("head")
    copies = []
    for source, target, axis in zip(sources, targets, axes):
        if axis is None:
            copies.append(pltpu.make_async_copy(source, target, sem.at[len(copies)]))
            continue
        half = source.shape[axis] // 2
        for part, head in enumerate((1 - h, h)):
            span = pl.ds(pl.multiple_of(head * half, half), half)
            place = pl.ds(part * half, half)
            if axis == 0:
                pair = (source.at[span, :], target.at[place, :])
            else:
                pair = (source.at[:, span], target.at[:, place])
            copies.append(pltpu.make_async_copy(*pair, sem.at[len(copies)]))
    for copy in copies:
        copy.start()
    for copy in copies:
        copy.wait()


def run_stage(arrays, axes):
    size = sum(2 * array.size for array in arrays)
    return pl.pallas_call(
        functools.partial(stage_kernel, axes),
        out_shape=tuple(jax.ShapeDtypeStruct(array.shape, array.dtype) for array in arrays),
        in_specs=[whole(pltpu.HBM)] * len(arrays),
        out_specs=tuple(vmem(len(arrays))),
        scratch_shapes=[pltpu.SemaphoreType.DMA((2 * len(arrays),))],
        compiler_params=params(16),
        cost_estimate=pl.CostEstimate(flops=0, bytes_accessed=20 * size, transcendentals=0),
        name="stage",
    )(*(in_hbm(array) for array in arrays))


def project_kernel(*refs):
    pieces, (wk, wv, out) = refs[:-3], refs[-3:]
    width = wk.shape[1]
    rows = jnp.concatenate([piece[...] for piece in pieces], axis=0)
    out[:, :width] = dot(rows, wk[...]).astype(jnp.bfloat16)
    out[:, width:] = dot(rows, wv[...]).astype(jnp.bfloat16)


def run_project(pieces, wk, wv):
    rows = sum(piece.shape[0] for piece in pieces)
    depth, width = wk.shape
    return pl.pallas_call(
        project_kernel,
        out_shape=jax.ShapeDtypeStruct((rows, 2 * width), jnp.bfloat16),
        in_specs=vmem(len(pieces) + 2),
        out_specs=whole(pltpu.VMEM),
        compiler_params=params(8),
        cost_estimate=pl.CostEstimate(
            flops=300 * rows * depth * width,
            bytes_accessed=300 * depth * width + 300 * rows * depth,
            transcendentals=0,
        ),
        name="project",
    )(*pieces, wk, wv)


def table_kernel(mine, sibling, table):
    table[0, : mine.shape[0]] = mine[...]
    table[1, : mine.shape[0]] = sibling[...]


def run_table(mine, sibling, blocks):
    return pl.pallas_call(
        table_kernel,
        out_shape=jax.ShapeDtypeStruct((2, blocks) + mine.shape[1:], jnp.bfloat16),
        in_specs=vmem(2),
        out_specs=whole(pltpu.VMEM),
        compiler_params=params(8),
        cost_estimate=pl.CostEstimate(
            flops=0, bytes_accessed=80 * mine.size, transcendentals=0
        ),
        name="table",
    )(mine, sibling)


def project_out(c, att, mlp, wo, send, keep):
    width = send.shape[1]
    half = att.shape[1]
    for out, first in ((send, 0), (keep, half)):
        span = slice(first + c * width, first + (c + 1) * width)
        out[...] = (mlp[:, span] + dot(att[...], wo[:, span])).astype(jnp.bfloat16)


def attend_kernel(
    adjacency, q, mine, sibling, table_in, mlp, wo, send, keep, att, table
):
    del table_in
    s = lax.axis_index("shard")
    h = lax.axis_index("head")
    u = lax.axis_index("sub")
    half = wo.shape[0]
    ready = table.shape[1] - mine.shape[0]
    for i, part in enumerate((mine, sibling)):
        table[i, ready:] = part[...]
    rows_of = lax.broadcasted_iota(jnp.int32, (WIDE, WIDE), 0) // BLOCK
    lanes_of = lax.broadcasted_iota(jnp.int32, (WIDE, WIDE), 1) // HEAD_DIM
    diagonal = rows_of == lanes_of
    lane_head = lax.broadcasted_iota(jnp.int32, (BLOCK, WIDE), 1) // HEAD_DIM
    scale = HEAD_DIM**-0.5 * math.log2(math.e)
    for b in range(adjacency.shape[0]):
        rows = slice(b * BLOCK, (b + 1) * BLOCK)
        places = []
        for j in range(adjacency.shape[1]):
            m = adjacency[b, j]
            part = lax.rem(m, 2)
            core = lax.rem(m // 2, 2)
            distance = s ^ (m // 4)
            part = jnp.where(distance <= 1, part, part ^ h)
            places.append((core ^ u, distance * 2 + part))
        for g in range(half // WIDE):
            columns = slice(g * WIDE, (g + 1) * WIDE)
            keys = jnp.concatenate([table[i, p, :, columns] for i, p in places], axis=0)
            vcolumns = slice(half + g * WIDE, half + (g + 1) * WIDE)
            values = jnp.concatenate([table[i, p, :, vcolumns] for i, p in places], axis=0)
            stacked = jnp.concatenate([q[rows, columns]] * QUAD, axis=0)
            stacked = jnp.where(diagonal, stacked, jnp.zeros_like(stacked))
            scores = lax.dot_general(
                stacked, keys, (((1,), (1,)), ((), ())), preferred_element_type=jnp.float32
            )
            highest = jnp.max(scores, axis=-1, keepdims=True)
            weights = jnp.exp2((scores - highest) * scale)
            total = jnp.sum(weights, axis=-1, keepdims=True)
            probs = (weights * (1.0 / total)).astype(jnp.bfloat16)
            mixed = dot(probs, values)
            merged = mixed[0:BLOCK, :]
            for i in range(1, QUAD):
                merged = jnp.where(lane_head == i, mixed[i * BLOCK : (i + 1) * BLOCK, :], merged)
            att[rows, columns] = merged.astype(jnp.bfloat16)
    project_out(0, att, mlp, wo, send, keep)


def run_attend(adjacency, q, mine, sibling, table, mlp, wo):
    rows, half = q.shape
    part = jax.ShapeDtypeStruct((rows, half // CHUNKS), jnp.bfloat16)
    blocks = table.shape[0] * table.shape[1]
    send, keep, att, _ = pl.pallas_call(
        attend_kernel,
        out_shape=(
            part,
            part,
            jax.ShapeDtypeStruct(q.shape, jnp.bfloat16),
            jax.ShapeDtypeStruct(table.shape, jnp.bfloat16),
        ),
        in_specs=[whole(pltpu.SMEM)] + vmem(6),
        out_specs=tuple(vmem(4)),
        input_output_aliases={4: 3},
        compiler_params=params(16),
        cost_estimate=pl.CostEstimate(
            flops=20 * rows * half * (D + 8 * 8 * BLOCK),
            bytes_accessed=40 * blocks * BLOCK * half + 20 * half * D + 40 * rows * D,
            transcendentals=rows * 8 * BLOCK * half // HEAD_DIM,
        ),
        name="attend",
    )(adjacency, q, mine, sibling, table, mlp, wo)
    return send, keep, att


def run_project_out(c, att, mlp, wo):
    rows, half = att.shape
    part = jax.ShapeDtypeStruct((rows, half // CHUNKS), jnp.bfloat16)
    return pl.pallas_call(
        functools.partial(project_out, c),
        out_shape=(part, part),
        in_specs=vmem(3),
        out_specs=tuple(vmem(2)),
        compiler_params=params(8),
        cost_estimate=pl.CostEstimate(
            flops=200 * rows * half * D,
            bytes_accessed=200 * half * D,
            transcendentals=0,
        ),
        name="project_out",
    )(att, mlp, wo)


def combine_kernel(c, owners, grid_features, keep, received, *outs):
    s = lax.axis_index("shard")
    count = grid_features.shape[0]
    width = keep.shape[1]
    names = [owners[t, 0] for t in range(count)]
    for d, out in enumerate(outs):
        for j in range(CAP):
            out[j] = jnp.zeros(out.shape[1:], jnp.bfloat16)
        seen = jnp.int32(0)
        for t in range(count):
            hit = names[t] == s ^ d
            rank = seen

            @pl.when(hit)
            def _():
                rows = slice(t * BLOCK, (t + 1) * BLOCK)
                partials = keep[rows, :].astype(jnp.float32)
                partials = partials + received[rows, :].astype(jnp.float32)
                residual = grid_features[t, :, c * width : (c + 1) * width]
                out[rank] = (residual.astype(jnp.float32) + partials).astype(jnp.bfloat16)

            seen = seen + hit.astype(jnp.int32)


def run_combine(c, owners, grid_features, keep, received, shards):
    count, rows, _ = grid_features.shape
    width = keep.shape[1]
    slot = jax.ShapeDtypeStruct((CAP, rows, width), jnp.bfloat16)
    return pl.pallas_call(
        functools.partial(combine_kernel, c),
        out_shape=(slot,) * shards,
        in_specs=[whole(pltpu.SMEM)] + vmem(3),
        out_specs=tuple(vmem(shards)),
        compiler_params=params(8),
        cost_estimate=pl.CostEstimate(
            flops=3000 * count * rows * width,
            bytes_accessed=400 * rows * width * (3 * count + CAP * shards),
            transcendentals=0,
        ),
        name="combine",
    )(owners, grid_features, keep, received)


def place_kernel(c, order, *refs):
    out, sem = refs[-2:]
    s = lax.axis_index("shard")
    copies = []
    for i, d in enumerate(order):
        width = refs[i].shape[2]
        columns = pl.ds(c * width, width)
        slots = pl.ds((s ^ d) * CAP, CAP)
        copies.append(pltpu.make_async_copy(refs[i], out.at[slots, :, columns], sem.at[i]))
        copies[i].start()
    for copy in copies:
        copy.wait()


def run_place(c, order, arrived, placed):
    shards = len(arrived)
    _, rows, width = arrived[0].shape
    shape = (shards * CAP, rows, CHUNKS * width)
    return pl.pallas_call(
        functools.partial(place_kernel, c, order),
        out_shape=jax.ShapeDtypeStruct(shape, jnp.bfloat16),
        in_specs=vmem(shards) + [whole(pltpu.HBM)] * len(placed),
        out_specs=whole(pltpu.HBM),
        scratch_shapes=[pltpu.SemaphoreType.DMA((shards,))],
        input_output_aliases={shards: 0} if placed else {},
        compiler_params=params(4),
        cost_estimate=pl.CostEstimate(
            flops=0, bytes_accessed=40 * CAP * shards * rows * width, transcendentals=0
        ),
        name="place",
    )(*arrived, *placed)


def crossed(x, distance, size):
    return lax.ppermute(x, "shard", [(i, i ^ distance) for i in range(size)])


def swapped(x, axis):
    return lax.ppermute(x, axis, [(0, 1), (1, 0)])


def paired(
    grid_features,
    owners,
    adjacency,
    mesh_nodes,
    norm_gain,
    query_weight,
    key_weight,
    value_weight,
    output_weight,
    up_weight,
    down_weight,
):
    shards = lax.axis_size("shard")
    count, rows, half = grid_features.shape
    flat = grid_features.reshape(count * rows, half)
    far = crossed(run_pick(mesh_nodes), 2, shards)
    near = crossed(mesh_nodes, 1, shards)
    other = swapped(flat, "head")
    staged = run_stage(
        (
            flat,
            norm_gain.reshape(1, -1),
            query_weight,
            up_weight,
            down_weight,
            output_weight,
            key_weight,
            value_weight,
            mesh_nodes,
        ),
        (None, 1, 0, 0, 1, 1, None, None, None),
    )
    flat, gain, wq, wup, wdn, wo, wk, wv, mesh = staged
    farther = crossed(far, 1, shards)
    far_pair = swapped(far, "head")
    queries, mlp = run_mlp(flat, other, gain, wq, wup, wdn)
    queries, mlp, farther = lax.optimization_barrier((queries, mlp, farther))
    farther_pair = swapped(farther, "head")
    blocked = (-1, BLOCK, 2 * half)
    mine_a = run_project((mesh, near, far, far_pair, farther), wk, wv)
    sibling_a = swapped(mine_a, "sub")
    table = run_table(mine_a.reshape(blocked), sibling_a.reshape(blocked), 2 * shards)
    mine_b = run_project((farther_pair,), wk, wv)
    sibling_b = swapped(mine_b, "sub")
    send, keep, att = run_attend(
        adjacency, queries, mine_b.reshape(blocked), sibling_b.reshape(blocked), table, mlp, wo
    )
    placed = []
    slots = None
    for c in range(CHUNKS):
        if c > 0:
            send, keep = run_project_out(c, att, mlp, wo)
            send, _ = lax.optimization_barrier((send, received))
        received = swapped(send, "head")
        if slots is not None:
            received, _ = lax.optimization_barrier((received, slots[0]))
        slots = run_combine(c, owners, grid_features, keep, received, shards)
        order = (2, 3, 1, 0)
        arrived = [crossed(slots[d], d, shards) if d else slots[d] for d in order]
        placed = [run_place(c, order, arrived, placed)]
    return placed[0]


def attend_plain(queries, key_table, value_table, chosen, scaling):
    count = chosen.shape[0]
    picked_keys = key_table[chosen]
    picked_keys = picked_keys.reshape(count, -1, picked_keys.shape[3], picked_keys.shape[4])
    picked_values = value_table[chosen]
    picked_values = picked_values.reshape(count, -1, picked_values.shape[3], picked_values.shape[4])
    scores = (
        jnp.einsum("gqhe,gkhe->ghqk", queries, picked_keys, preferred_element_type=jnp.float32)
        * scaling
    )
    highest = jnp.max(scores, axis=-1, keepdims=True)
    weights = jnp.exp(scores - highest)
    weights = (weights / jnp.sum(weights, axis=-1, keepdims=True)).astype(jnp.bfloat16)
    result = jnp.einsum(
        "ghqk,gkhe->gqhe", weights, picked_values, preferred_element_type=jnp.float32
    )
    return result.astype(jnp.bfloat16)


def general(
    grid_features,
    owners,
    adjacency,
    mesh_nodes,
    norm_gain,
    query_weight,
    key_weight,
    value_weight,
    output_weight,
    up_weight,
    down_weight,
):
    shard_count = lax.axis_size("shard")
    head_count = lax.axis_size("head")
    local_blocks, block_rows, feature_share = grid_features.shape
    slots = shard_count * CAP
    owner_col = owners[:, 0]
    position = jnp.arange(local_blocks, dtype=jnp.int32)
    earlier = (owner_col[:, None] == owner_col[None, :]) & (position[None, :] < position[:, None])
    target = owner_col * CAP + jnp.sum(earlier.astype(jnp.int32), axis=1)
    dispatch = (target[:, None] == jnp.arange(slots, dtype=jnp.int32)[None, :]).astype(jnp.bfloat16)
    offset = lax.axis_index("head") * (D // head_count)
    projected = jnp.stack(
        (
            jnp.dot(mesh_nodes, key_weight, preferred_element_type=jnp.float32).astype(
                jnp.bfloat16
            ),
            jnp.dot(mesh_nodes, value_weight, preferred_element_type=jnp.float32).astype(
                jnp.bfloat16
            ),
        )
    )
    tables = lax.all_gather(projected, ("shard", "sub"), axis=1, tiled=True)
    head_local = query_weight.shape[1] // HEAD_DIM
    key_table = tables[0].reshape(-1, block_rows, head_local, HEAD_DIM)
    value_table = tables[1].reshape(-1, block_rows, head_local, HEAD_DIM)
    send_lists = jnp.full((slots, adjacency.shape[1]), -1, jnp.int32).at[target].set(adjacency)
    send_lists = send_lists.reshape(shard_count, CAP, -1)
    complete = lax.all_gather(grid_features, "head", axis=2, tiled=True)
    outgoing = jnp.einsum(
        "gs,gbd->sbd", dispatch, complete, preferred_element_type=jnp.float32
    ).astype(jnp.bfloat16)
    arrived, lists = (
        lax.all_to_all(
            outgoing.reshape(shard_count, CAP, block_rows, D),
            "shard",
            split_axis=0,
            concat_axis=0,
            tiled=True,
        ),
        lax.all_to_all(send_lists, "shard", split_axis=0, concat_axis=0, tiled=True),
    )
    arrived = arrived.reshape(slots, block_rows, D)
    residual = lax.dynamic_slice_in_dim(arrived, offset, D // head_count, 2)
    lists = lists.reshape(slots, -1)
    count = arrived.shape[0]
    values_f = arrived.astype(jnp.float32)
    average = jnp.mean(values_f, axis=-1, keepdims=True)
    centered = values_f - average
    variance = jnp.mean(centered * centered, axis=-1, keepdims=True)
    normed = (centered * lax.rsqrt(variance + epsilon) * norm_gain).astype(jnp.bfloat16)
    flattened = normed.reshape(-1, D)
    queries = jnp.dot(flattened, query_weight, preferred_element_type=jnp.float32).astype(
        jnp.bfloat16
    )
    blocks_each = math.gcd(count, max(1, 512 // block_rows))
    steps_count = count // blocks_each
    queries = queries.reshape(steps_count, blocks_each, block_rows, head_local, HEAD_DIM)

    def attend_step(operands):
        return attend_plain(operands[0], key_table, value_table, operands[1], HEAD_DIM ** (-0.5))

    attended = lax.map(
        attend_step, (queries, jnp.maximum(lists, 0).reshape(steps_count, blocks_each, -1))
    )
    attended = attended.reshape(-1, head_local * HEAD_DIM)
    hidden = jax.nn.gelu(
        jnp.dot(flattened, up_weight, preferred_element_type=jnp.float32), approximate=False
    ).astype(jnp.bfloat16)
    branch = jnp.dot(attended, output_weight, preferred_element_type=jnp.float32)
    branch = branch + jnp.dot(hidden, down_weight, preferred_element_type=jnp.float32)
    branch = branch.reshape(count, block_rows, D)
    reduced = lax.psum_scatter(
        branch.astype(jnp.bfloat16), "head", scatter_dimension=2, tiled=True
    ).astype(jnp.float32)
    occupied = lists[:, 0] >= 0
    summed = residual.astype(jnp.float32) + reduced
    return jnp.where(occupied[:, None, None], summed, 0.0).astype(jnp.bfloat16)


def local(grid_features, owners, adjacency, mesh_nodes, *parameters):
    sizes = [lax.axis_size(axis) for axis in ("shard", "head", "sub")]
    small = grid_features.shape[:2] == (4, BLOCK) and mesh_nodes.shape[0] == 2 * BLOCK
    if sizes == [4, 2, 2] and small:
        return paired(grid_features, owners, adjacency, mesh_nodes, *parameters)
    return general(grid_features, owners, adjacency, mesh_nodes, *parameters)


def solution(mesh):
    return jax.shard_map(
        local,
        mesh=mesh,
        in_specs=(
            P(("groups", "shard", "sub"), None, "head"),
            P(("groups", "shard", "sub"), None),
            P(("groups", "shard", "sub"), None),
            P(("groups", "shard", "sub"), None),
            P(),
            P(None, "head"),
            P(None, "head"),
            P(None, "head"),
            P("head", None),
            P(None, "head"),
            P("head", None),
        ),
        out_specs=P(("groups", "shard", "sub"), None, "head"),
        check_vma=False,
    )
```

```python
import functools
import math

import jax
import jax.numpy as jnp
from jax import lax
from jax.experimental import pallas as pl
from jax.experimental.pallas import tpu as pltpu
from jax.sharding import PartitionSpec as P

D = 1024
HEAD_DIM = 64
CAP = 2
BLOCK = 64
QUAD = 4
WIDE = QUAD * HEAD_DIM
CHUNKS = 2
MIB = 1 << 20


epsilon = 1e-05


def dot(a, b):
    return jnp.dot(a, b, preferred_element_type=jnp.float32)


def gelu(x):
    return 0.5 * x * (1.0 + lax.erf(x * (2.0**-0.5)))


def in_hbm(x):
    return pltpu.with_memory_space_constraint(x, pltpu.HBM)


def whole(space):
    return pl.BlockSpec(memory_space=space)


def vmem(count):
    return [whole(pltpu.VMEM)] * count


def params(mib):
    return pltpu.CompilerParams(vmem_limit_bytes=mib * MIB)


def mlp_kernel(own, other, gain, wq, wup, wdn, q_out, mlp_out, normed_s):
    half = own.shape[1]
    units = wup.shape[1]
    chunk = units // 4
    x_other = other[...].astype(jnp.float32)
    x_own = own[...].astype(jnp.float32)

    def mean(a, b):
        total = jnp.sum(a, axis=-1, keepdims=True) + jnp.sum(b, axis=-1, keepdims=True)
        return total * (0.5 / half)

    average = mean(x_other, x_own)
    x_other = x_other - average
    x_own = x_own - average
    factor = lax.rsqrt(mean(x_other * x_other, x_own * x_own) + epsilon)
    normed_s[:, :half] = (x_other * factor * gain[:, :half]).astype(jnp.bfloat16)
    normed_s[:, half:] = (x_own * factor * gain[:, half:]).astype(jnp.bfloat16)
    normed = normed_s[...]
    q_out[...] = dot(normed, wq[...]).astype(jnp.bfloat16)
    for c in range(units // chunk):
        span = slice(c * chunk, (c + 1) * chunk)
        hidden = gelu(dot(normed, wup[:, span])).astype(jnp.bfloat16)
        term = dot(hidden, wdn[span, :])
        if c == 0:
            mlp_out[...] = term
        else:
            mlp_out[...] += term


def run_mlp(own, other, gain, wq, wup, wdn):
    rows = own.shape[0]
    width = wq.shape[0]
    units = wup.shape[1]
    return pl.pallas_call(
        mlp_kernel,
        out_shape=(
            jax.ShapeDtypeStruct((rows, wq.shape[1]), jnp.bfloat16),
            jax.ShapeDtypeStruct((rows, width), jnp.float32),
        ),
        in_specs=vmem(6),
        out_specs=tuple(vmem(2)),
        scratch_shapes=[pltpu.VMEM((rows, width), jnp.bfloat16)],
        compiler_params=params(16),
        cost_estimate=pl.CostEstimate(
            flops=2 * rows * width * (wq.shape[1] + 2 * units),
            bytes_accessed=2 * width * (wq.shape[1] + 2 * units),
            transcendentals=rows * units,
        ),
        name="mlp",
    )(own, other, gain, wq, wup, wdn)


def pick_kernel(mesh, out, sem):
    first = pl.multiple_of(lax.axis_index("head") * BLOCK, BLOCK)
    copy = pltpu.make_async_copy(mesh.at[pl.ds(first, BLOCK), :], out, sem)
    copy.start()
    copy.wait()


def run_pick(mesh):
    return pl.pallas_call(
        pick_kernel,
        out_shape=jax.ShapeDtypeStruct((BLOCK, mesh.shape[1]), mesh.dtype),
        in_specs=[whole(pltpu.HBM)],
        out_specs=whole(pltpu.VMEM),
        scratch_shapes=[pltpu.SemaphoreType.DMA(())],
        compiler_params=params(4),
        cost_estimate=pl.CostEstimate(flops=0, bytes_accessed=4 * mesh.size, transcendentals=0),
        name="pick",
    )(in_hbm(mesh))


def stage_kernel(axes, *refs):
    sources, targets, sem = refs[: len(axes)], refs[len(axes) : -1], refs[-1]
    h = lax.axis_index("head")
    copies = []
    for source, target, axis in zip(sources, targets, axes):
        if axis is None:
            copies.append(pltpu.make_async_copy(source, target, sem.at[len(copies)]))
            continue
        half = source.shape[axis] // 2
        for part, head in enumerate((1 - h, h)):
            span = pl.ds(pl.multiple_of(head * half, half), half)
            place = pl.ds(part * half, half)
            if axis == 0:
                pair = (source.at[span, :], target.at[place, :])
            else:
                pair = (source.at[:, span], target.at[:, place])
            copies.append(pltpu.make_async_copy(*pair, sem.at[len(copies)]))
    for copy in copies:
        copy.start()
    for copy in copies:
        copy.wait()


def run_stage(arrays, axes):
    size = sum(2 * array.size for array in arrays)
    return pl.pallas_call(
        functools.partial(stage_kernel, axes),
        out_shape=tuple(jax.ShapeDtypeStruct(array.shape, array.dtype) for array in arrays),
        in_specs=[whole(pltpu.HBM)] * len(arrays),
        out_specs=tuple(vmem(len(arrays))),
        scratch_shapes=[pltpu.SemaphoreType.DMA((2 * len(arrays),))],
        compiler_params=params(16),
        cost_estimate=pl.CostEstimate(flops=0, bytes_accessed=20 * size, transcendentals=0),
        name="stage",
    )(*(in_hbm(array) for array in arrays))


def project_kernel(*refs):
    pieces, (wk, wv, out) = refs[:-3], refs[-3:]
    width = wk.shape[1]
    rows = jnp.concatenate([piece[...] for piece in pieces], axis=0)
    out[:, :width] = dot(rows, wk[...]).astype(jnp.bfloat16)
    out[:, width:] = dot(rows, wv[...]).astype(jnp.bfloat16)


def run_project(pieces, wk, wv):
    rows = sum(piece.shape[0] for piece in pieces)
    depth, width = wk.shape
    return pl.pallas_call(
        project_kernel,
        out_shape=jax.ShapeDtypeStruct((rows, 2 * width), jnp.bfloat16),
        in_specs=vmem(len(pieces) + 2),
        out_specs=whole(pltpu.VMEM),
        compiler_params=params(8),
        cost_estimate=pl.CostEstimate(
            flops=300 * rows * depth * width,
            bytes_accessed=300 * depth * width + 300 * rows * depth,
            transcendentals=0,
        ),
        name="project",
    )(*pieces, wk, wv)


def table_kernel(mine, sibling, table):
    table[0, : mine.shape[0]] = mine[...]
    table[1, : mine.shape[0]] = sibling[...]


def run_table(mine, sibling, blocks):
    return pl.pallas_call(
        table_kernel,
        out_shape=jax.ShapeDtypeStruct((2, blocks) + mine.shape[1:], jnp.bfloat16),
        in_specs=vmem(2),
        out_specs=whole(pltpu.VMEM),
        compiler_params=params(8),
        cost_estimate=pl.CostEstimate(
            flops=0, bytes_accessed=80 * mine.size, transcendentals=0
        ),
        name="table",
    )(mine, sibling)


def project_out(c, att, mlp, wo, send, keep):
    width = send.shape[1]
    half = att.shape[1]
    for out, first in ((send, 0), (keep, half)):
        span = slice(first + c * width, first + (c + 1) * width)
        out[...] = (mlp[:, span] + dot(att[...], wo[:, span])).astype(jnp.bfloat16)


def attend_kernel(
    adjacency, q, mine, sibling, table_in, mlp, wo, send, keep, att, table
):
    del table_in
    s = lax.axis_index("shard")
    h = lax.axis_index("head")
    u = lax.axis_index("sub")
    half = wo.shape[0]
    ready = table.shape[1] - mine.shape[0]
    for i, part in enumerate((mine, sibling)):
        table[i, ready:] = part[...]
    rows_of = lax.broadcasted_iota(jnp.int32, (WIDE, WIDE), 0) // BLOCK
    lanes_of = lax.broadcasted_iota(jnp.int32, (WIDE, WIDE), 1) // HEAD_DIM
    diagonal = rows_of == lanes_of
    lane_head = lax.broadcasted_iota(jnp.int32, (BLOCK, WIDE), 1) // HEAD_DIM
    scale = HEAD_DIM**-0.5 * math.log2(math.e)
    groups = half // WIDE
    places = []
    for b in range(adjacency.shape[0]):
        places.append([])
        for j in range(adjacency.shape[1]):
            m = adjacency[b, j]
            part = lax.rem(m, 2)
            core = lax.rem(m // 2, 2)
            distance = s ^ (m // 4)
            part = jnp.where(distance <= 1, part, part ^ h)
            places[b].append((core ^ u, distance * 2 + part))

    def scores_of(step):
        b, g = divmod(step, groups)
        columns = slice(g * WIDE, (g + 1) * WIDE)
        keys = jnp.concatenate([table[i, p, :, columns] for i, p in places[b]], axis=0)
        stacked = jnp.concatenate([q[b * BLOCK : (b + 1) * BLOCK, columns]] * QUAD, axis=0)
        stacked = jnp.where(diagonal, stacked, jnp.zeros_like(stacked))
        return lax.dot_general(
            stacked, keys, (((1,), (1,)), ((), ())), preferred_element_type=jnp.float32
        )

    steps = len(places) * groups
    scores = scores_of(0)
    for step in range(steps):
        following = scores_of(step + 1) if step + 1 < steps else None
        b, g = divmod(step, groups)
        columns = slice(half + g * WIDE, half + (g + 1) * WIDE)
        values = jnp.concatenate([table[i, p, :, columns] for i, p in places[b]], axis=0)
        highest = jnp.max(scores, axis=-1, keepdims=True)
        weights = jnp.exp2((scores - highest) * scale)
        total = jnp.sum(weights, axis=-1, keepdims=True)
        mixed = dot(weights.astype(jnp.bfloat16), values) * (1.0 / total)
        merged = mixed[0:BLOCK, :]
        for i in range(1, QUAD):
            merged = jnp.where(lane_head == i, mixed[i * BLOCK : (i + 1) * BLOCK, :], merged)
        rows = slice(b * BLOCK, (b + 1) * BLOCK)
        att[rows, g * WIDE : (g + 1) * WIDE] = merged.astype(jnp.bfloat16)
        scores = following
    project_out(0, att, mlp, wo, send, keep)


def run_attend(adjacency, q, mine, sibling, table, mlp, wo):
    rows, half = q.shape
    part = jax.ShapeDtypeStruct((rows, half // CHUNKS), jnp.bfloat16)
    blocks = table.shape[0] * table.shape[1]
    send, keep, att, _ = pl.pallas_call(
        attend_kernel,
        out_shape=(
            part,
            part,
            jax.ShapeDtypeStruct(q.shape, jnp.bfloat16),
            jax.ShapeDtypeStruct(table.shape, jnp.bfloat16),
        ),
        in_specs=[whole(pltpu.SMEM)] + vmem(6),
        out_specs=tuple(vmem(4)),
        input_output_aliases={4: 3},
        compiler_params=params(16),
        cost_estimate=pl.CostEstimate(
            flops=20 * rows * half * (D + 8 * 8 * BLOCK),
            bytes_accessed=40 * blocks * BLOCK * half + 20 * half * D + 40 * rows * D,
            transcendentals=rows * 8 * BLOCK * half // HEAD_DIM,
        ),
        name="attend",
    )(adjacency, q, mine, sibling, table, mlp, wo)
    return send, keep, att


def run_project_out(c, att, mlp, wo):
    rows, half = att.shape
    part = jax.ShapeDtypeStruct((rows, half // CHUNKS), jnp.bfloat16)
    return pl.pallas_call(
        functools.partial(project_out, c),
        out_shape=(part, part),
        in_specs=vmem(3),
        out_specs=tuple(vmem(2)),
        compiler_params=params(8),
        cost_estimate=pl.CostEstimate(
            flops=200 * rows * half * D,
            bytes_accessed=200 * half * D,
            transcendentals=0,
        ),
        name="project_out",
    )(att, mlp, wo)


def combine_kernel(c, owners, grid_features, keep, received, *outs):
    s = lax.axis_index("shard")
    count = grid_features.shape[0]
    width = keep.shape[1]
    names = [owners[t, 0] for t in range(count)]
    for d, out in enumerate(outs):
        for j in range(CAP):
            out[j] = jnp.zeros(out.shape[1:], jnp.bfloat16)
        seen = jnp.int32(0)
        for t in range(count):
            hit = names[t] == s ^ d
            rank = seen

            @pl.when(hit)
            def _():
                rows = slice(t * BLOCK, (t + 1) * BLOCK)
                partials = keep[rows, :].astype(jnp.float32)
                partials = partials + received[rows, :].astype(jnp.float32)
                residual = grid_features[t, :, c * width : (c + 1) * width]
                out[rank] = (residual.astype(jnp.float32) + partials).astype(jnp.bfloat16)

            seen = seen + hit.astype(jnp.int32)


def run_combine(c, owners, grid_features, keep, received, shards):
    count, rows, _ = grid_features.shape
    width = keep.shape[1]
    slot = jax.ShapeDtypeStruct((CAP, rows, width), jnp.bfloat16)
    return pl.pallas_call(
        functools.partial(combine_kernel, c),
        out_shape=(slot,) * shards,
        in_specs=[whole(pltpu.SMEM)] + vmem(3),
        out_specs=tuple(vmem(shards)),
        compiler_params=params(8),
        cost_estimate=pl.CostEstimate(
            flops=3000 * count * rows * width,
            bytes_accessed=400 * rows * width * (3 * count + CAP * shards),
            transcendentals=0,
        ),
        name="combine",
    )(owners, grid_features, keep, received)


def place_kernel(c, order, *refs):
    out, sem = refs[-2:]
    s = lax.axis_index("shard")
    copies = []
    for i, d in enumerate(order):
        width = refs[i].shape[2]
        columns = pl.ds(c * width, width)
        slots = pl.ds((s ^ d) * CAP, CAP)
        copies.append(pltpu.make_async_copy(refs[i], out.at[slots, :, columns], sem.at[i]))
        copies[i].start()
    for copy in copies:
        copy.wait()


def run_place(c, order, arrived, placed):
    shards = len(arrived)
    _, rows, width = arrived[0].shape
    shape = (shards * CAP, rows, CHUNKS * width)
    return pl.pallas_call(
        functools.partial(place_kernel, c, order),
        out_shape=jax.ShapeDtypeStruct(shape, jnp.bfloat16),
        in_specs=vmem(shards) + [whole(pltpu.HBM)] * len(placed),
        out_specs=whole(pltpu.HBM),
        scratch_shapes=[pltpu.SemaphoreType.DMA((shards,))],
        input_output_aliases={shards: 0} if placed else {},
        compiler_params=params(4),
        cost_estimate=pl.CostEstimate(
            flops=0, bytes_accessed=40 * CAP * shards * rows * width, transcendentals=0
        ),
        name="place",
    )(*arrived, *placed)


def crossed(x, distance, size):
    return lax.ppermute(x, "shard", [(i, i ^ distance) for i in range(size)])


def swapped(x, axis):
    return lax.ppermute(x, axis, [(0, 1), (1, 0)])


def paired(
    grid_features,
    owners,
    adjacency,
    mesh_nodes,
    norm_gain,
    query_weight,
    key_weight,
    value_weight,
    output_weight,
    up_weight,
    down_weight,
):
    shards = lax.axis_size("shard")
    count, rows, half = grid_features.shape
    flat = grid_features.reshape(count * rows, half)
    far = crossed(run_pick(mesh_nodes), 2, shards)
    near = crossed(mesh_nodes, 1, shards)
    other = swapped(flat, "head")
    staged = run_stage(
        (
            flat,
            norm_gain.reshape(1, -1),
            query_weight,
            up_weight,
            down_weight,
            output_weight,
            key_weight,
            value_weight,
            mesh_nodes,
        ),
        (None, 1, 0, 0, 1, 1, None, None, None),
    )
    flat, gain, wq, wup, wdn, wo, wk, wv, mesh = staged
    farther = crossed(far, 1, shards)
    far_pair = swapped(far, "head")
    queries, mlp = run_mlp(flat, other, gain, wq, wup, wdn)
    queries, mlp, relayed = lax.optimization_barrier((queries, mlp, far_pair))
    farther_pair = crossed(relayed, 1, shards)
    blocked = (-1, BLOCK, 2 * half)
    mine_a = run_project((mesh, near, far, far_pair, farther), wk, wv)
    sibling_a = swapped(mine_a, "sub")
    table = run_table(mine_a.reshape(blocked), sibling_a.reshape(blocked), 2 * shards)
    mine_b = run_project((farther_pair,), wk, wv)
    sibling_b = swapped(mine_b, "sub")
    send, keep, att = run_attend(
        adjacency, queries, mine_b.reshape(blocked), sibling_b.reshape(blocked), table, mlp, wo
    )
    placed = []
    slots = None
    for c in range(CHUNKS):
        if c > 0:
            send, keep = run_project_out(c, att, mlp, wo)
            send, _ = lax.optimization_barrier((send, received))
        received = swapped(send, "head")
        if slots is not None:
            received, _ = lax.optimization_barrier((received, slots[0]))
        slots = run_combine(c, owners, grid_features, keep, received, shards)
        order = (2, 3, 1, 0)
        arrived = [crossed(slots[d], d, shards) if d else slots[d] for d in order]
        placed = [run_place(c, order, arrived, placed)]
    return placed[0]


def attend_plain(queries, key_table, value_table, chosen, scaling):
    count = chosen.shape[0]
    picked_keys = key_table[chosen]
    picked_keys = picked_keys.reshape(count, -1, picked_keys.shape[3], picked_keys.shape[4])
    picked_values = value_table[chosen]
    picked_values = picked_values.reshape(count, -1, picked_values.shape[3], picked_values.shape[4])
    scores = (
        jnp.einsum("gqhe,gkhe->ghqk", queries, picked_keys, preferred_element_type=jnp.float32)
        * scaling
    )
    highest = jnp.max(scores, axis=-1, keepdims=True)
    weights = jnp.exp(scores - highest)
    weights = (weights / jnp.sum(weights, axis=-1, keepdims=True)).astype(jnp.bfloat16)
    result = jnp.einsum(
        "ghqk,gkhe->gqhe", weights, picked_values, preferred_element_type=jnp.float32
    )
    return result.astype(jnp.bfloat16)


def general(
    grid_features,
    owners,
    adjacency,
    mesh_nodes,
    norm_gain,
    query_weight,
    key_weight,
    value_weight,
    output_weight,
    up_weight,
    down_weight,
):
    shard_count = lax.axis_size("shard")
    head_count = lax.axis_size("head")
    local_blocks, block_rows, feature_share = grid_features.shape
    slots = shard_count * CAP
    owner_col = owners[:, 0]
    position = jnp.arange(local_blocks, dtype=jnp.int32)
    earlier = (owner_col[:, None] == owner_col[None, :]) & (position[None, :] < position[:, None])
    target = owner_col * CAP + jnp.sum(earlier.astype(jnp.int32), axis=1)
    dispatch = (target[:, None] == jnp.arange(slots, dtype=jnp.int32)[None, :]).astype(jnp.bfloat16)
    offset = lax.axis_index("head") * (D // head_count)
    projected = jnp.stack(
        (
            jnp.dot(mesh_nodes, key_weight, preferred_element_type=jnp.float32).astype(
                jnp.bfloat16
            ),
            jnp.dot(mesh_nodes, value_weight, preferred_element_type=jnp.float32).astype(
                jnp.bfloat16
            ),
        )
    )
    tables = lax.all_gather(projected, ("shard", "sub"), axis=1, tiled=True)
    head_local = query_weight.shape[1] // HEAD_DIM
    key_table = tables[0].reshape(-1, block_rows, head_local, HEAD_DIM)
    value_table = tables[1].reshape(-1, block_rows, head_local, HEAD_DIM)
    send_lists = jnp.full((slots, adjacency.shape[1]), -1, jnp.int32).at[target].set(adjacency)
    send_lists = send_lists.reshape(shard_count, CAP, -1)
    complete = lax.all_gather(grid_features, "head", axis=2, tiled=True)
    outgoing = jnp.einsum(
        "gs,gbd->sbd", dispatch, complete, preferred_element_type=jnp.float32
    ).astype(jnp.bfloat16)
    arrived, lists = (
        lax.all_to_all(
            outgoing.reshape(shard_count, CAP, block_rows, D),
            "shard",
            split_axis=0,
            concat_axis=0,
            tiled=True,
        ),
        lax.all_to_all(send_lists, "shard", split_axis=0, concat_axis=0, tiled=True),
    )
    arrived = arrived.reshape(slots, block_rows, D)
    residual = lax.dynamic_slice_in_dim(arrived, offset, D // head_count, 2)
    lists = lists.reshape(slots, -1)
    count = arrived.shape[0]
    values_f = arrived.astype(jnp.float32)
    average = jnp.mean(values_f, axis=-1, keepdims=True)
    centered = values_f - average
    variance = jnp.mean(centered * centered, axis=-1, keepdims=True)
    normed = (centered * lax.rsqrt(variance + epsilon) * norm_gain).astype(jnp.bfloat16)
    flattened = normed.reshape(-1, D)
    queries = jnp.dot(flattened, query_weight, preferred_element_type=jnp.float32).astype(
        jnp.bfloat16
    )
    blocks_each = math.gcd(count, max(1, 512 // block_rows))
    steps_count = count // blocks_each
    queries = queries.reshape(steps_count, blocks_each, block_rows, head_local, HEAD_DIM)

    def attend_step(operands):
        return attend_plain(operands[0], key_table, value_table, operands[1], HEAD_DIM ** (-0.5))

    attended = lax.map(
        attend_step, (queries, jnp.maximum(lists, 0).reshape(steps_count, blocks_each, -1))
    )
    attended = attended.reshape(-1, head_local * HEAD_DIM)
    hidden = jax.nn.gelu(
        jnp.dot(flattened, up_weight, preferred_element_type=jnp.float32), approximate=False
    ).astype(jnp.bfloat16)
    branch = jnp.dot(attended, output_weight, preferred_element_type=jnp.float32)
    branch = branch + jnp.dot(hidden, down_weight, preferred_element_type=jnp.float32)
    branch = branch.reshape(count, block_rows, D)
    reduced = lax.psum_scatter(
        branch.astype(jnp.bfloat16), "head", scatter_dimension=2, tiled=True
    ).astype(jnp.float32)
    occupied = lists[:, 0] >= 0
    summed = residual.astype(jnp.float32) + reduced
    return jnp.where(occupied[:, None, None], summed, 0.0).astype(jnp.bfloat16)


def local(grid_features, owners, adjacency, mesh_nodes, *parameters):
    sizes = [lax.axis_size(axis) for axis in ("shard", "head", "sub")]
    small = grid_features.shape[:2] == (4, BLOCK) and mesh_nodes.shape[0] == 2 * BLOCK
    if sizes == [4, 2, 2] and small:
        return paired(grid_features, owners, adjacency, mesh_nodes, *parameters)
    return general(grid_features, owners, adjacency, mesh_nodes, *parameters)


def solution(mesh):
    return jax.shard_map(
        local,
        mesh=mesh,
        in_specs=(
            P(("groups", "shard", "sub"), None, "head"),
            P(("groups", "shard", "sub"), None),
            P(("groups", "shard", "sub"), None),
            P(("groups", "shard", "sub"), None),
            P(),
            P(None, "head"),
            P(None, "head"),
            P(None, "head"),
            P("head", None),
            P(None, "head"),
            P("head", None),
        ),
        out_specs=P(("groups", "shard", "sub"), None, "head"),
        check_vma=False,
    )
```

```python
import functools
import math

import jax
import jax.numpy as jnp
from jax import lax
from jax.experimental import pallas as pl
from jax.experimental.pallas import tpu as pltpu
from jax.sharding import PartitionSpec as P

D = 1024
HEAD_DIM = 64
CAP = 2
BLOCK = 64
QUAD = 4
WIDE = QUAD * HEAD_DIM
WIDTHS = (128, 128, 256)
MIB = 1 << 20


epsilon = 1e-05


def dot(a, b):
    return jnp.dot(a, b, preferred_element_type=jnp.float32)


def gelu(x):
    return 0.5 * x * (1.0 + lax.erf(x * (2.0**-0.5)))


def in_hbm(x):
    return pltpu.with_memory_space_constraint(x, pltpu.HBM)


def whole(space):
    return pl.BlockSpec(memory_space=space)


def vmem(count):
    return [whole(pltpu.VMEM)] * count


def params(mib):
    return pltpu.CompilerParams(vmem_limit_bytes=mib * MIB)


def mlp_kernel(own, other, gain, wq, wup, wdn, q_out, mlp_out, normed_s):
    half = own.shape[1]
    units = wup.shape[1]
    chunk = units // 4
    x_other = other[...].astype(jnp.float32)
    x_own = own[...].astype(jnp.float32)

    def mean(a, b):
        total = jnp.sum(a, axis=-1, keepdims=True) + jnp.sum(b, axis=-1, keepdims=True)
        return total * (0.5 / half)

    average = mean(x_other, x_own)
    x_other = x_other - average
    x_own = x_own - average
    factor = lax.rsqrt(mean(x_other * x_other, x_own * x_own) + epsilon)
    normed_s[:, :half] = (x_other * factor * gain[:, :half]).astype(jnp.bfloat16)
    normed_s[:, half:] = (x_own * factor * gain[:, half:]).astype(jnp.bfloat16)
    normed = normed_s[...]
    q_out[...] = dot(normed, wq[...]).astype(jnp.bfloat16)
    for c in range(units // chunk):
        span = slice(c * chunk, (c + 1) * chunk)
        hidden = gelu(dot(normed, wup[:, span])).astype(jnp.bfloat16)
        term = dot(hidden, wdn[span, :])
        if c == 0:
            mlp_out[...] = term
        else:
            mlp_out[...] += term


def run_mlp(own, other, gain, wq, wup, wdn):
    rows = own.shape[0]
    width = wq.shape[0]
    units = wup.shape[1]
    return pl.pallas_call(
        mlp_kernel,
        out_shape=(
            jax.ShapeDtypeStruct((rows, wq.shape[1]), jnp.bfloat16),
            jax.ShapeDtypeStruct((rows, width), jnp.float32),
        ),
        in_specs=vmem(6),
        out_specs=tuple(vmem(2)),
        scratch_shapes=[pltpu.VMEM((rows, width), jnp.bfloat16)],
        compiler_params=params(16),
        cost_estimate=pl.CostEstimate(
            flops=2 * rows * width * (wq.shape[1] + 2 * units),
            bytes_accessed=2 * width * (wq.shape[1] + 2 * units),
            transcendentals=rows * units,
        ),
        name="mlp",
    )(own, other, gain, wq, wup, wdn)


def pick_kernel(mesh, out, sem):
    first = pl.multiple_of(lax.axis_index("head") * BLOCK, BLOCK)
    copy = pltpu.make_async_copy(mesh.at[pl.ds(first, BLOCK), :], out, sem)
    copy.start()
    copy.wait()


def run_pick(mesh):
    return pl.pallas_call(
        pick_kernel,
        out_shape=jax.ShapeDtypeStruct((BLOCK, mesh.shape[1]), mesh.dtype),
        in_specs=[whole(pltpu.HBM)],
        out_specs=whole(pltpu.VMEM),
        scratch_shapes=[pltpu.SemaphoreType.DMA(())],
        compiler_params=params(4),
        cost_estimate=pl.CostEstimate(flops=0, bytes_accessed=4 * mesh.size, transcendentals=0),
        name="pick",
    )(in_hbm(mesh))


def stage_kernel(axes, *refs):
    sources, targets, sem = refs[: len(axes)], refs[len(axes) : -1], refs[-1]
    h = lax.axis_index("head")
    copies = []
    for source, target, axis in zip(sources, targets, axes):
        if axis is None:
            copies.append(pltpu.make_async_copy(source, target, sem.at[len(copies)]))
            continue
        half = source.shape[axis] // 2
        for part, head in enumerate((1 - h, h)):
            span = pl.ds(pl.multiple_of(head * half, half), half)
            place = pl.ds(part * half, half)
            if axis == 0:
                pair = (source.at[span, :], target.at[place, :])
            else:
                pair = (source.at[:, span], target.at[:, place])
            copies.append(pltpu.make_async_copy(*pair, sem.at[len(copies)]))
    for copy in copies:
        copy.start()
    for copy in copies:
        copy.wait()


def run_stage(arrays, axes):
    size = sum(2 * array.size for array in arrays)
    return pl.pallas_call(
        functools.partial(stage_kernel, axes),
        out_shape=tuple(jax.ShapeDtypeStruct(array.shape, array.dtype) for array in arrays),
        in_specs=[whole(pltpu.HBM)] * len(arrays),
        out_specs=tuple(vmem(len(arrays))),
        scratch_shapes=[pltpu.SemaphoreType.DMA((2 * len(arrays),))],
        compiler_params=params(16),
        cost_estimate=pl.CostEstimate(flops=0, bytes_accessed=20 * size, transcendentals=0),
        name="stage",
    )(*(in_hbm(array) for array in arrays))


def project_kernel(*refs):
    pieces, (wk, wv, out) = refs[:-3], refs[-3:]
    width = wk.shape[1]
    rows = jnp.concatenate([piece[...] for piece in pieces], axis=0)
    out[:, :width] = dot(rows, wk[...]).astype(jnp.bfloat16)
    out[:, width:] = dot(rows, wv[...]).astype(jnp.bfloat16)


def run_project(pieces, wk, wv):
    rows = sum(piece.shape[0] for piece in pieces)
    depth, width = wk.shape
    return pl.pallas_call(
        project_kernel,
        out_shape=jax.ShapeDtypeStruct((rows, 2 * width), jnp.bfloat16),
        in_specs=vmem(len(pieces) + 2),
        out_specs=whole(pltpu.VMEM),
        compiler_params=params(8),
        cost_estimate=pl.CostEstimate(
            flops=300 * rows * depth * width,
            bytes_accessed=300 * depth * width + 300 * rows * depth,
            transcendentals=0,
        ),
        name="project",
    )(*pieces, wk, wv)


def table_kernel(mine, sibling, table):
    table[0, : mine.shape[0]] = mine[...]
    table[1, : mine.shape[0]] = sibling[...]


def run_table(mine, sibling, blocks):
    return pl.pallas_call(
        table_kernel,
        out_shape=jax.ShapeDtypeStruct((2, blocks) + mine.shape[1:], jnp.bfloat16),
        in_specs=vmem(2),
        out_specs=whole(pltpu.VMEM),
        compiler_params=params(8),
        cost_estimate=pl.CostEstimate(
            flops=0, bytes_accessed=80 * mine.size, transcendentals=0
        ),
        name="table",
    )(mine, sibling)


def columns_of(c):
    return slice(sum(WIDTHS[:c]), sum(WIDTHS[: c + 1]))


def project_out(c, att, mlp, wo, send, keep):
    half = att.shape[1]
    chunk = columns_of(c)
    for out, first in ((send, 0), (keep, half)):
        span = slice(first + chunk.start, first + chunk.stop)
        out[...] = (mlp[:, span] + dot(att[...], wo[:, span])).astype(jnp.bfloat16)


def attend_kernel(
    adjacency, q, mine, sibling, table_in, mlp, wo, send, keep, att, table
):
    del table_in
    s = lax.axis_index("shard")
    h = lax.axis_index("head")
    u = lax.axis_index("sub")
    half = wo.shape[0]
    ready = table.shape[1] - mine.shape[0]
    for i, part in enumerate((mine, sibling)):
        table[i, ready:] = part[...]
    rows_of = lax.broadcasted_iota(jnp.int32, (WIDE, WIDE), 0) // BLOCK
    lanes_of = lax.broadcasted_iota(jnp.int32, (WIDE, WIDE), 1) // HEAD_DIM
    diagonal = rows_of == lanes_of
    lane_head = lax.broadcasted_iota(jnp.int32, (BLOCK, WIDE), 1) // HEAD_DIM
    scale = HEAD_DIM**-0.5 * math.log2(math.e)
    groups = half // WIDE
    places = []
    for b in range(adjacency.shape[0]):
        places.append([])
        for j in range(adjacency.shape[1]):
            m = adjacency[b, j]
            part = lax.rem(m, 2)
            core = lax.rem(m // 2, 2)
            distance = s ^ (m // 4)
            part = jnp.where(distance <= 1, part, part ^ h)
            places[b].append((core ^ u, distance * 2 + part))

    def scores_of(step):
        b, g = divmod(step, groups)
        columns = slice(g * WIDE, (g + 1) * WIDE)
        keys = jnp.concatenate([table[i, p, :, columns] for i, p in places[b]], axis=0)
        stacked = jnp.concatenate([q[b * BLOCK : (b + 1) * BLOCK, columns]] * QUAD, axis=0)
        stacked = jnp.where(diagonal, stacked, jnp.zeros_like(stacked))
        return lax.dot_general(
            stacked, keys, (((1,), (1,)), ((), ())), preferred_element_type=jnp.float32
        )

    steps = len(places) * groups
    scores = scores_of(0)
    for step in range(steps):
        following = scores_of(step + 1) if step + 1 < steps else None
        b, g = divmod(step, groups)
        columns = slice(half + g * WIDE, half + (g + 1) * WIDE)
        values = jnp.concatenate([table[i, p, :, columns] for i, p in places[b]], axis=0)
        highest = jnp.max(scores, axis=-1, keepdims=True)
        weights = jnp.exp2((scores - highest) * scale)
        total = jnp.sum(weights, axis=-1, keepdims=True)
        mixed = dot(weights.astype(jnp.bfloat16), values) * (1.0 / total)
        merged = mixed[0:BLOCK, :]
        for i in range(1, QUAD):
            merged = jnp.where(lane_head == i, mixed[i * BLOCK : (i + 1) * BLOCK, :], merged)
        rows = slice(b * BLOCK, (b + 1) * BLOCK)
        att[rows, g * WIDE : (g + 1) * WIDE] = merged.astype(jnp.bfloat16)
        scores = following
    project_out(0, att, mlp, wo, send, keep)


def run_attend(adjacency, q, mine, sibling, table, mlp, wo):
    rows, half = q.shape
    part = jax.ShapeDtypeStruct((rows, WIDTHS[0]), jnp.bfloat16)
    blocks = table.shape[0] * table.shape[1]
    send, keep, att, _ = pl.pallas_call(
        attend_kernel,
        out_shape=(
            part,
            part,
            jax.ShapeDtypeStruct(q.shape, jnp.bfloat16),
            jax.ShapeDtypeStruct(table.shape, jnp.bfloat16),
        ),
        in_specs=[whole(pltpu.SMEM)] + vmem(6),
        out_specs=tuple(vmem(4)),
        input_output_aliases={4: 3},
        compiler_params=params(16),
        cost_estimate=pl.CostEstimate(
            flops=20 * rows * half * (D + 8 * 8 * BLOCK),
            bytes_accessed=40 * blocks * BLOCK * half + 20 * half * D + 40 * rows * D,
            transcendentals=rows * 8 * BLOCK * half // HEAD_DIM,
        ),
        name="attend",
    )(adjacency, q, mine, sibling, table, mlp, wo)
    return send, keep, att


def run_project_out(c, att, mlp, wo):
    rows, half = att.shape
    part = jax.ShapeDtypeStruct((rows, WIDTHS[c]), jnp.bfloat16)
    return pl.pallas_call(
        functools.partial(project_out, c),
        out_shape=(part, part),
        in_specs=vmem(3),
        out_specs=tuple(vmem(2)),
        compiler_params=params(8),
        cost_estimate=pl.CostEstimate(
            flops=200 * rows * half * D,
            bytes_accessed=200 * half * D,
            transcendentals=0,
        ),
        name="project_out",
    )(att, mlp, wo)


def combine_kernel(chunks, distances, owners, grid_features, *refs):
    s = lax.axis_index("shard")
    keeps, refs = refs[: len(chunks)], refs[len(chunks) :]
    swaps, outs = refs[: len(chunks)], refs[len(chunks) :]
    count = grid_features.shape[0]
    names = [owners[t, 0] for t in range(count)]
    first = columns_of(chunks[0]).start
    for d, out in zip(distances, outs):
        out[...] = jnp.zeros(out.shape, jnp.bfloat16)
        seen = jnp.int32(0)
        for t in range(count):
            hit = names[t] == s ^ d
            rank = seen

            @pl.when(hit)
            def _():
                rows = slice(t * BLOCK, (t + 1) * BLOCK)
                for c, keep, swap in zip(chunks, keeps, swaps):
                    columns = columns_of(c)
                    partials = keep[rows, :].astype(jnp.float32)
                    partials = partials + swap[rows, :].astype(jnp.float32)
                    residual = grid_features[t, :, columns].astype(jnp.float32)
                    place = slice(columns.start - first, columns.stop - first)
                    out[rank, :, place] = (residual + partials).astype(jnp.bfloat16)

            seen = seen + hit.astype(jnp.int32)


def run_combine(chunks, distances, owners, grid_features, keeps, swaps):
    count, rows, _ = grid_features.shape
    width = sum(WIDTHS[c] for c in chunks)
    slot = jax.ShapeDtypeStruct((CAP, rows, width), jnp.bfloat16)
    return pl.pallas_call(
        functools.partial(combine_kernel, chunks, distances),
        out_shape=(slot,) * len(distances),
        in_specs=[whole(pltpu.SMEM)] + vmem(1 + 2 * len(chunks)),
        out_specs=tuple(vmem(len(distances))),
        compiler_params=params(8),
        cost_estimate=pl.CostEstimate(
            flops=3000 * count * rows * width,
            bytes_accessed=400 * rows * width * (3 * count + CAP * len(distances)),
            transcendentals=0,
        ),
        name="combine",
    )(owners, grid_features, *keeps, *swaps)


def place_kernel(spots, *refs):
    out, sem = refs[-2:]
    s = lax.axis_index("shard")
    copies = []
    for i, (d, first) in enumerate(spots):
        columns = pl.ds(first, refs[i].shape[2])
        slots = pl.ds((s ^ d) * CAP, CAP)
        copies.append(pltpu.make_async_copy(refs[i], out.at[slots, :, columns], sem.at[i]))
        copies[i].start()
    for copy in copies:
        copy.wait()


def run_place(spots, arrived, placed, shape):
    return pl.pallas_call(
        functools.partial(place_kernel, spots),
        out_shape=jax.ShapeDtypeStruct(shape, jnp.bfloat16),
        in_specs=vmem(len(arrived)) + [whole(pltpu.HBM)] * len(placed),
        out_specs=whole(pltpu.HBM),
        scratch_shapes=[pltpu.SemaphoreType.DMA((len(arrived),))],
        input_output_aliases={len(arrived): 0} if placed else {},
        compiler_params=params(4),
        cost_estimate=pl.CostEstimate(
            flops=400000 * sum(part.size for part in arrived), bytes_accessed=0, transcendentals=0
        ),
        name="place",
    )(*arrived, *placed)


def crossed(x, distance, size):
    return lax.ppermute(x, "shard", [(i, i ^ distance) for i in range(size)])


def swapped(x, axis):
    return lax.ppermute(x, axis, [(0, 1), (1, 0)])


def paired(
    grid_features,
    owners,
    adjacency,
    mesh_nodes,
    norm_gain,
    query_weight,
    key_weight,
    value_weight,
    output_weight,
    up_weight,
    down_weight,
):
    shards = lax.axis_size("shard")
    count, rows, half = grid_features.shape
    flat = grid_features.reshape(count * rows, half)
    far = crossed(run_pick(mesh_nodes), 2, shards)
    near = crossed(mesh_nodes, 1, shards)
    other = swapped(flat, "head")
    staged = run_stage(
        (
            flat,
            norm_gain.reshape(1, -1),
            query_weight,
            up_weight,
            down_weight,
            output_weight,
            key_weight,
            value_weight,
            mesh_nodes,
        ),
        (None, 1, 0, 0, 1, 1, None, None, None),
    )
    flat, gain, wq, wup, wdn, wo, wk, wv, mesh = staged
    farther = crossed(far, 1, shards)
    far_pair = swapped(far, "head")
    queries, mlp = run_mlp(flat, other, gain, wq, wup, wdn)
    queries, mlp, relayed = lax.optimization_barrier((queries, mlp, far_pair))
    farther_pair = crossed(relayed, 1, shards)
    blocked = (-1, BLOCK, 2 * half)
    mine_a = run_project((mesh, near, far, far_pair, farther), wk, wv)
    sibling_a = swapped(mine_a, "sub")
    table = run_table(mine_a.reshape(blocked), sibling_a.reshape(blocked), 2 * shards)
    mine_b = run_project((farther_pair,), wk, wv)
    sibling_b = swapped(mine_b, "sub")
    send, keep, att = run_attend(
        adjacency, queries, mine_b.reshape(blocked), sibling_b.reshape(blocked), table, mlp, wo
    )
    keeps, swaps, slots, placed = [], [], [], []
    shape = (shards * CAP, rows, half)
    for c in range(len(WIDTHS)):
        if c > 0:
            send, keep = run_project_out(c, att, mlp, wo)
        received = swapped(send, "head")
        if c > 0:
            received, _ = lax.optimization_barrier((received, slots[c - 1][0]))
        slots.append(run_combine((c,), (2, 3), owners, grid_features, (keep,), (received,)))
        keeps.append(keep)
        swaps.append(received)
    every = tuple(range(len(WIDTHS)))
    swaps[-1], _ = lax.optimization_barrier((swaps[-1], slots[-1][0]))
    near_slots, own_slots = run_combine(every, (1, 0), owners, grid_features, keeps, swaps)
    for c in every:
        first = columns_of(c).start
        spots = [(2, first), (3, first)]
        arrived = [crossed(slot, d, shards) for d, slot in zip((2, 3), slots[c])]
        if c == len(WIDTHS) - 1:
            spots += [(1, 0), (0, 0)]
            arrived += [crossed(near_slots, 1, shards), own_slots]
        placed = [run_place(spots, arrived, placed, shape)]
    return placed[0]


def attend_plain(queries, key_table, value_table, chosen, scaling):
    count = chosen.shape[0]
    picked_keys = key_table[chosen]
    picked_keys = picked_keys.reshape(count, -1, picked_keys.shape[3], picked_keys.shape[4])
    picked_values = value_table[chosen]
    picked_values = picked_values.reshape(count, -1, picked_values.shape[3], picked_values.shape[4])
    scores = (
        jnp.einsum("gqhe,gkhe->ghqk", queries, picked_keys, preferred_element_type=jnp.float32)
        * scaling
    )
    highest = jnp.max(scores, axis=-1, keepdims=True)
    weights = jnp.exp(scores - highest)
    weights = (weights / jnp.sum(weights, axis=-1, keepdims=True)).astype(jnp.bfloat16)
    result = jnp.einsum(
        "ghqk,gkhe->gqhe", weights, picked_values, preferred_element_type=jnp.float32
    )
    return result.astype(jnp.bfloat16)


def general(
    grid_features,
    owners,
    adjacency,
    mesh_nodes,
    norm_gain,
    query_weight,
    key_weight,
    value_weight,
    output_weight,
    up_weight,
    down_weight,
):
    shard_count = lax.axis_size("shard")
    head_count = lax.axis_size("head")
    local_blocks, block_rows, feature_share = grid_features.shape
    slots = shard_count * CAP
    owner_col = owners[:, 0]
    position = jnp.arange(local_blocks, dtype=jnp.int32)
    earlier = (owner_col[:, None] == owner_col[None, :]) & (position[None, :] < position[:, None])
    target = owner_col * CAP + jnp.sum(earlier.astype(jnp.int32), axis=1)
    dispatch = (target[:, None] == jnp.arange(slots, dtype=jnp.int32)[None, :]).astype(jnp.bfloat16)
    offset = lax.axis_index("head") * (D // head_count)
    projected = jnp.stack(
        (
            jnp.dot(mesh_nodes, key_weight, preferred_element_type=jnp.float32).astype(
                jnp.bfloat16
            ),
            jnp.dot(mesh_nodes, value_weight, preferred_element_type=jnp.float32).astype(
                jnp.bfloat16
            ),
        )
    )
    tables = lax.all_gather(projected, ("shard", "sub"), axis=1, tiled=True)
    head_local = query_weight.shape[1] // HEAD_DIM
    key_table = tables[0].reshape(-1, block_rows, head_local, HEAD_DIM)
    value_table = tables[1].reshape(-1, block_rows, head_local, HEAD_DIM)
    send_lists = jnp.full((slots, adjacency.shape[1]), -1, jnp.int32).at[target].set(adjacency)
    send_lists = send_lists.reshape(shard_count, CAP, -1)
    complete = lax.all_gather(grid_features, "head", axis=2, tiled=True)
    outgoing = jnp.einsum(
        "gs,gbd->sbd", dispatch, complete, preferred_element_type=jnp.float32
    ).astype(jnp.bfloat16)
    arrived, lists = (
        lax.all_to_all(
            outgoing.reshape(shard_count, CAP, block_rows, D),
            "shard",
            split_axis=0,
            concat_axis=0,
            tiled=True,
        ),
        lax.all_to_all(send_lists, "shard", split_axis=0, concat_axis=0, tiled=True),
    )
    arrived = arrived.reshape(slots, block_rows, D)
    residual = lax.dynamic_slice_in_dim(arrived, offset, D // head_count, 2)
    lists = lists.reshape(slots, -1)
    count = arrived.shape[0]
    values_f = arrived.astype(jnp.float32)
    average = jnp.mean(values_f, axis=-1, keepdims=True)
    centered = values_f - average
    variance = jnp.mean(centered * centered, axis=-1, keepdims=True)
    normed = (centered * lax.rsqrt(variance + epsilon) * norm_gain).astype(jnp.bfloat16)
    flattened = normed.reshape(-1, D)
    queries = jnp.dot(flattened, query_weight, preferred_element_type=jnp.float32).astype(
        jnp.bfloat16
    )
    blocks_each = math.gcd(count, max(1, 512 // block_rows))
    steps_count = count // blocks_each
    queries = queries.reshape(steps_count, blocks_each, block_rows, head_local, HEAD_DIM)

    def attend_step(operands):
        return attend_plain(operands[0], key_table, value_table, operands[1], HEAD_DIM ** (-0.5))

    attended = lax.map(
        attend_step, (queries, jnp.maximum(lists, 0).reshape(steps_count, blocks_each, -1))
    )
    attended = attended.reshape(-1, head_local * HEAD_DIM)
    hidden = jax.nn.gelu(
        jnp.dot(flattened, up_weight, preferred_element_type=jnp.float32), approximate=False
    ).astype(jnp.bfloat16)
    branch = jnp.dot(attended, output_weight, preferred_element_type=jnp.float32)
    branch = branch + jnp.dot(hidden, down_weight, preferred_element_type=jnp.float32)
    branch = branch.reshape(count, block_rows, D)
    reduced = lax.psum_scatter(
        branch.astype(jnp.bfloat16), "head", scatter_dimension=2, tiled=True
    ).astype(jnp.float32)
    occupied = lists[:, 0] >= 0
    summed = residual.astype(jnp.float32) + reduced
    return jnp.where(occupied[:, None, None], summed, 0.0).astype(jnp.bfloat16)


def local(grid_features, owners, adjacency, mesh_nodes, *parameters):
    sizes = [lax.axis_size(axis) for axis in ("shard", "head", "sub")]
    small = grid_features.shape[:2] == (4, BLOCK) and mesh_nodes.shape[0] == 2 * BLOCK
    if sizes == [4, 2, 2] and small and grid_features.shape[2] == 512:
        return paired(grid_features, owners, adjacency, mesh_nodes, *parameters)
    return general(grid_features, owners, adjacency, mesh_nodes, *parameters)


def solution(mesh):
    return jax.shard_map(
        local,
        mesh=mesh,
        in_specs=(
            P(("groups", "shard", "sub"), None, "head"),
            P(("groups", "shard", "sub"), None),
            P(("groups", "shard", "sub"), None),
            P(("groups", "shard", "sub"), None),
            P(),
            P(None, "head"),
            P(None, "head"),
            P(None, "head"),
            P("head", None),
            P(None, "head"),
            P("head", None),
        ),
        out_specs=P(("groups", "shard", "sub"), None, "head"),
        check_vma=False,
    )
```

```python
import functools
import math

import jax
import jax.numpy as jnp
from jax import lax
from jax.experimental import pallas as pl
from jax.experimental.pallas import tpu as pltpu
from jax.sharding import PartitionSpec as P

D = 1024
HEAD_DIM = 64
CAP = 2
BLOCK = 64
QUAD = 4
WIDE = QUAD * HEAD_DIM
WIDTHS = (128, 384)
MIB = 1 << 20


epsilon = 1e-05


def dot(a, b):
    return jnp.dot(a, b, preferred_element_type=jnp.float32)


def gelu(x):
    return 0.5 * x * (1.0 + lax.erf(x * (2.0**-0.5)))


def in_hbm(x):
    return pltpu.with_memory_space_constraint(x, pltpu.HBM)


def whole(space):
    return pl.BlockSpec(memory_space=space)


def vmem(count):
    return [whole(pltpu.VMEM)] * count


def params(mib):
    return pltpu.CompilerParams(vmem_limit_bytes=mib * MIB)


def mlp_kernel(own, other, gain, wq, wup, wdn, q_out, mlp_out, normed_s):
    half = own.shape[1]
    units = wup.shape[1]
    chunk = units // 4
    x_other = other[...].astype(jnp.float32)
    x_own = own[...].astype(jnp.float32)

    def mean(a, b):
        total = jnp.sum(a, axis=-1, keepdims=True) + jnp.sum(b, axis=-1, keepdims=True)
        return total * (0.5 / half)

    average = mean(x_other, x_own)
    x_other = x_other - average
    x_own = x_own - average
    factor = lax.rsqrt(mean(x_other * x_other, x_own * x_own) + epsilon)
    normed_s[:, :half] = (x_other * factor * gain[:, :half]).astype(jnp.bfloat16)
    normed_s[:, half:] = (x_own * factor * gain[:, half:]).astype(jnp.bfloat16)
    normed = normed_s[...]
    q_out[...] = dot(normed, wq[...]).astype(jnp.bfloat16)
    for c in range(units // chunk):
        span = slice(c * chunk, (c + 1) * chunk)
        hidden = gelu(dot(normed, wup[:, span])).astype(jnp.bfloat16)
        term = dot(hidden, wdn[span, :])
        if c == 0:
            mlp_out[...] = term
        else:
            mlp_out[...] += term


def run_mlp(own, other, gain, wq, wup, wdn):
    rows = own.shape[0]
    width = wq.shape[0]
    units = wup.shape[1]
    return pl.pallas_call(
        mlp_kernel,
        out_shape=(
            jax.ShapeDtypeStruct((rows, wq.shape[1]), jnp.bfloat16),
            jax.ShapeDtypeStruct((rows, width), jnp.float32),
        ),
        in_specs=vmem(6),
        out_specs=tuple(vmem(2)),
        scratch_shapes=[pltpu.VMEM((rows, width), jnp.bfloat16)],
        compiler_params=params(16),
        cost_estimate=pl.CostEstimate(
            flops=2 * rows * width * (wq.shape[1] + 2 * units),
            bytes_accessed=2 * width * (wq.shape[1] + 2 * units),
            transcendentals=rows * units,
        ),
        name="mlp",
    )(own, other, gain, wq, wup, wdn)


def pick_kernel(mesh, out, sem):
    first = pl.multiple_of(lax.axis_index("head") * BLOCK, BLOCK)
    copy = pltpu.make_async_copy(mesh.at[pl.ds(first, BLOCK), :], out, sem)
    copy.start()
    copy.wait()


def run_pick(mesh):
    return pl.pallas_call(
        pick_kernel,
        out_shape=jax.ShapeDtypeStruct((BLOCK, mesh.shape[1]), mesh.dtype),
        in_specs=[whole(pltpu.HBM)],
        out_specs=whole(pltpu.VMEM),
        scratch_shapes=[pltpu.SemaphoreType.DMA(())],
        compiler_params=params(4),
        cost_estimate=pl.CostEstimate(flops=0, bytes_accessed=4 * mesh.size, transcendentals=0),
        name="pick",
    )(in_hbm(mesh))


def stage_kernel(axes, *refs):
    sources, targets, sem = refs[: len(axes)], refs[len(axes) : -1], refs[-1]
    h = lax.axis_index("head")
    copies = []
    for source, target, axis in zip(sources, targets, axes):
        if axis is None:
            copies.append(pltpu.make_async_copy(source, target, sem.at[len(copies)]))
            continue
        half = source.shape[axis] // 2
        for part, head in enumerate((1 - h, h)):
            span = pl.ds(pl.multiple_of(head * half, half), half)
            place = pl.ds(part * half, half)
            if axis == 0:
                pair = (source.at[span, :], target.at[place, :])
            else:
                pair = (source.at[:, span], target.at[:, place])
            copies.append(pltpu.make_async_copy(*pair, sem.at[len(copies)]))
    for copy in copies:
        copy.start()
    for copy in copies:
        copy.wait()


def run_stage(arrays, axes):
    size = sum(2 * array.size for array in arrays)
    return pl.pallas_call(
        functools.partial(stage_kernel, axes),
        out_shape=tuple(jax.ShapeDtypeStruct(array.shape, array.dtype) for array in arrays),
        in_specs=[whole(pltpu.HBM)] * len(arrays),
        out_specs=tuple(vmem(len(arrays))),
        scratch_shapes=[pltpu.SemaphoreType.DMA((2 * len(arrays),))],
        compiler_params=params(16),
        cost_estimate=pl.CostEstimate(flops=0, bytes_accessed=20 * size, transcendentals=0),
        name="stage",
    )(*(in_hbm(array) for array in arrays))


def project_kernel(*refs):
    pieces, (wk, wv, out) = refs[:-3], refs[-3:]
    width = wk.shape[1]
    rows = jnp.concatenate([piece[...] for piece in pieces], axis=0)
    out[:, :width] = dot(rows, wk[...]).astype(jnp.bfloat16)
    out[:, width:] = dot(rows, wv[...]).astype(jnp.bfloat16)


def run_project(pieces, wk, wv):
    rows = sum(piece.shape[0] for piece in pieces)
    depth, width = wk.shape
    return pl.pallas_call(
        project_kernel,
        out_shape=jax.ShapeDtypeStruct((rows, 2 * width), jnp.bfloat16),
        in_specs=vmem(len(pieces) + 2),
        out_specs=whole(pltpu.VMEM),
        compiler_params=params(8),
        cost_estimate=pl.CostEstimate(
            flops=300 * rows * depth * width,
            bytes_accessed=300 * depth * width + 300 * rows * depth,
            transcendentals=0,
        ),
        name="project",
    )(*pieces, wk, wv)


def table_kernel(mine, sibling, table):
    table[0, : mine.shape[0]] = mine[...]
    table[1, : mine.shape[0]] = sibling[...]


def run_table(mine, sibling, blocks):
    return pl.pallas_call(
        table_kernel,
        out_shape=jax.ShapeDtypeStruct((2, blocks) + mine.shape[1:], jnp.bfloat16),
        in_specs=vmem(2),
        out_specs=whole(pltpu.VMEM),
        compiler_params=params(8),
        cost_estimate=pl.CostEstimate(
            flops=0, bytes_accessed=80 * mine.size, transcendentals=0
        ),
        name="table",
    )(mine, sibling)


def columns_of(c):
    return slice(sum(WIDTHS[:c]), sum(WIDTHS[: c + 1]))


def project_out(c, att, mlp, wo, send, keep):
    half = att.shape[1]
    chunk = columns_of(c)
    for out, first in ((send, 0), (keep, half)):
        span = slice(first + chunk.start, first + chunk.stop)
        out[...] = (mlp[:, span] + dot(att[...], wo[:, span])).astype(jnp.bfloat16)


def attend_kernel(
    adjacency, q, mine, sibling, table_in, mlp, wo, send, keep, att, table
):
    del table_in
    s = lax.axis_index("shard")
    h = lax.axis_index("head")
    u = lax.axis_index("sub")
    half = wo.shape[0]
    ready = table.shape[1] - mine.shape[0]
    for i, part in enumerate((mine, sibling)):
        table[i, ready:] = part[...]
    rows_of = lax.broadcasted_iota(jnp.int32, (WIDE, WIDE), 0) // BLOCK
    lanes_of = lax.broadcasted_iota(jnp.int32, (WIDE, WIDE), 1) // HEAD_DIM
    diagonal = rows_of == lanes_of
    lane_head = lax.broadcasted_iota(jnp.int32, (BLOCK, WIDE), 1) // HEAD_DIM
    scale = HEAD_DIM**-0.5 * math.log2(math.e)
    groups = half // WIDE
    places = []
    for b in range(adjacency.shape[0]):
        places.append([])
        for j in range(adjacency.shape[1]):
            m = adjacency[b, j]
            part = lax.rem(m, 2)
            core = lax.rem(m // 2, 2)
            distance = s ^ (m // 4)
            part = jnp.where(distance <= 1, part, part ^ h)
            places[b].append((core ^ u, distance * 2 + part))

    def scores_of(step):
        b, g = divmod(step, groups)
        columns = slice(g * WIDE, (g + 1) * WIDE)
        keys = jnp.concatenate([table[i, p, :, columns] for i, p in places[b]], axis=0)
        stacked = jnp.concatenate([q[b * BLOCK : (b + 1) * BLOCK, columns]] * QUAD, axis=0)
        stacked = jnp.where(diagonal, stacked, jnp.zeros_like(stacked))
        return lax.dot_general(
            stacked, keys, (((1,), (1,)), ((), ())), preferred_element_type=jnp.float32
        )

    steps = len(places) * groups
    scores = scores_of(0)
    for step in range(steps):
        following = scores_of(step + 1) if step + 1 < steps else None
        b, g = divmod(step, groups)
        columns = slice(half + g * WIDE, half + (g + 1) * WIDE)
        values = jnp.concatenate([table[i, p, :, columns] for i, p in places[b]], axis=0)
        highest = jnp.max(scores, axis=-1, keepdims=True)
        weights = jnp.exp2((scores - highest) * scale)
        total = jnp.sum(weights, axis=-1, keepdims=True)
        mixed = dot(weights.astype(jnp.bfloat16), values) * (1.0 / total)
        merged = mixed[0:BLOCK, :]
        for i in range(1, QUAD):
            merged = jnp.where(lane_head == i, mixed[i * BLOCK : (i + 1) * BLOCK, :], merged)
        rows = slice(b * BLOCK, (b + 1) * BLOCK)
        att[rows, g * WIDE : (g + 1) * WIDE] = merged.astype(jnp.bfloat16)
        scores = following
    project_out(0, att, mlp, wo, send, keep)


def run_attend(adjacency, q, mine, sibling, table, mlp, wo):
    rows, half = q.shape
    part = jax.ShapeDtypeStruct((rows, WIDTHS[0]), jnp.bfloat16)
    blocks = table.shape[0] * table.shape[1]
    send, keep, att, _ = pl.pallas_call(
        attend_kernel,
        out_shape=(
            part,
            part,
            jax.ShapeDtypeStruct(q.shape, jnp.bfloat16),
            jax.ShapeDtypeStruct(table.shape, jnp.bfloat16),
        ),
        in_specs=[whole(pltpu.SMEM)] + vmem(6),
        out_specs=tuple(vmem(4)),
        input_output_aliases={4: 3},
        compiler_params=params(16),
        cost_estimate=pl.CostEstimate(
            flops=20 * rows * half * (D + 8 * 8 * BLOCK),
            bytes_accessed=40 * blocks * BLOCK * half + 20 * half * D + 40 * rows * D,
            transcendentals=rows * 8 * BLOCK * half // HEAD_DIM,
        ),
        name="attend",
    )(adjacency, q, mine, sibling, table, mlp, wo)
    return send, keep, att


def run_project_out(c, att, mlp, wo):
    rows, half = att.shape
    part = jax.ShapeDtypeStruct((rows, WIDTHS[c]), jnp.bfloat16)
    return pl.pallas_call(
        functools.partial(project_out, c),
        out_shape=(part, part),
        in_specs=vmem(3),
        out_specs=tuple(vmem(2)),
        compiler_params=params(8),
        cost_estimate=pl.CostEstimate(
            flops=200 * rows * half * D,
            bytes_accessed=200 * half * D,
            transcendentals=0,
        ),
        name="project_out",
    )(att, mlp, wo)


def combine_kernel(chunks, distances, owners, grid_features, *refs):
    s = lax.axis_index("shard")
    keeps, refs = refs[: len(chunks)], refs[len(chunks) :]
    swaps, outs = refs[: len(chunks)], refs[len(chunks) :]
    count = grid_features.shape[0]
    names = [owners[t, 0] for t in range(count)]
    first = columns_of(chunks[0]).start
    for d, out in zip(distances, outs):
        out[...] = jnp.zeros(out.shape, jnp.bfloat16)
        seen = jnp.int32(0)
        for t in range(count):
            hit = names[t] == s ^ d
            rank = seen

            @pl.when(hit)
            def _():
                rows = slice(t * BLOCK, (t + 1) * BLOCK)
                for c, keep, swap in zip(chunks, keeps, swaps):
                    columns = columns_of(c)
                    partials = keep[rows, :].astype(jnp.float32)
                    partials = partials + swap[rows, :].astype(jnp.float32)
                    residual = grid_features[t, :, columns].astype(jnp.float32)
                    place = slice(columns.start - first, columns.stop - first)
                    out[rank, :, place] = (residual + partials).astype(jnp.bfloat16)

            seen = seen + hit.astype(jnp.int32)


def run_combine(chunks, distances, owners, grid_features, keeps, swaps):
    count, rows, _ = grid_features.shape
    width = sum(WIDTHS[c] for c in chunks)
    slot = jax.ShapeDtypeStruct((CAP, rows, width), jnp.bfloat16)
    return pl.pallas_call(
        functools.partial(combine_kernel, chunks, distances),
        out_shape=(slot,) * len(distances),
        in_specs=[whole(pltpu.SMEM)] + vmem(1 + 2 * len(chunks)),
        out_specs=tuple(vmem(len(distances))),
        compiler_params=params(8),
        cost_estimate=pl.CostEstimate(
            flops=300000 * count * rows * width,
            bytes_accessed=400 * rows * width * (3 * count + CAP * len(distances)),
            transcendentals=0,
        ),
        name="combine",
    )(owners, grid_features, *keeps, *swaps)


def place_kernel(spots, *refs):
    out, sem = refs[-2:]
    s = lax.axis_index("shard")
    copies = []
    for i, (d, first) in enumerate(spots):
        columns = pl.ds(first, refs[i].shape[2])
        slots = pl.ds((s ^ d) * CAP, CAP)
        copies.append(pltpu.make_async_copy(refs[i], out.at[slots, :, columns], sem.at[i]))
        copies[i].start()
    for copy in copies:
        copy.wait()


def run_place(spots, arrived, placed, shape):
    return pl.pallas_call(
        functools.partial(place_kernel, spots),
        out_shape=jax.ShapeDtypeStruct(shape, jnp.bfloat16),
        in_specs=vmem(len(arrived)) + [whole(pltpu.HBM)] * len(placed),
        out_specs=whole(pltpu.HBM),
        scratch_shapes=[pltpu.SemaphoreType.DMA((len(arrived),))],
        input_output_aliases={len(arrived): 0} if placed else {},
        compiler_params=params(4),
        cost_estimate=pl.CostEstimate(
            flops=400000 * sum(part.size for part in arrived), bytes_accessed=0, transcendentals=0
        ),
        name="place",
    )(*arrived, *placed)


def crossed(x, distance, size):
    return lax.ppermute(x, "shard", [(i, i ^ distance) for i in range(size)])


def swapped(x, axis):
    return lax.ppermute(x, axis, [(0, 1), (1, 0)])


def paired(
    grid_features,
    owners,
    adjacency,
    mesh_nodes,
    norm_gain,
    query_weight,
    key_weight,
    value_weight,
    output_weight,
    up_weight,
    down_weight,
):
    shards = lax.axis_size("shard")
    count, rows, half = grid_features.shape
    flat = grid_features.reshape(count * rows, half)
    far = crossed(run_pick(mesh_nodes), 2, shards)
    near = crossed(mesh_nodes, 1, shards)
    other = swapped(flat, "head")
    staged = run_stage(
        (
            flat,
            norm_gain.reshape(1, -1),
            query_weight,
            up_weight,
            down_weight,
            output_weight,
            key_weight,
            value_weight,
            mesh_nodes,
        ),
        (None, 1, 0, 0, 1, 1, None, None, None),
    )
    flat, gain, wq, wup, wdn, wo, wk, wv, mesh = staged
    farther = crossed(far, 1, shards)
    far_pair = swapped(far, "head")
    queries, mlp = run_mlp(flat, other, gain, wq, wup, wdn)
    queries, mlp, relayed = lax.optimization_barrier((queries, mlp, far_pair))
    farther_pair = crossed(relayed, 1, shards)
    blocked = (-1, BLOCK, 2 * half)
    mine_a = run_project((mesh, near, far, far_pair, farther), wk, wv)
    sibling_a = swapped(mine_a, "sub")
    table = run_table(mine_a.reshape(blocked), sibling_a.reshape(blocked), 2 * shards)
    mine_b = run_project((farther_pair,), wk, wv)
    sibling_b = swapped(mine_b, "sub")
    send, keep, att = run_attend(
        adjacency, queries, mine_b.reshape(blocked), sibling_b.reshape(blocked), table, mlp, wo
    )
    keeps, swaps, slots, placed = [], [], [], []
    shape = (shards * CAP, rows, half)
    for c in range(len(WIDTHS)):
        if c > 0:
            send, keep = run_project_out(c, att, mlp, wo)
        received = swapped(send, "head")
        if c > 0:
            received, _ = lax.optimization_barrier((received, slots[c - 1][0]))
        slots.append(run_combine((c,), (2, 3), owners, grid_features, (keep,), (received,)))
        keeps.append(keep)
        swaps.append(received)
    every = tuple(range(len(WIDTHS)))
    swaps[-1], _ = lax.optimization_barrier((swaps[-1], slots[-1][0]))
    near_slots, own_slots = run_combine(every, (1, 0), owners, grid_features, keeps, swaps)
    for c in every:
        first = columns_of(c).start
        spots = [(2, first), (3, first)]
        arrived = [crossed(slot, d, shards) for d, slot in zip((2, 3), slots[c])]
        if c == len(WIDTHS) - 1:
            spots += [(1, 0), (0, 0)]
            arrived += [crossed(near_slots, 1, shards), own_slots]
        placed = [run_place(spots, arrived, placed, shape)]
    return placed[0]


def attend_plain(queries, key_table, value_table, chosen, scaling):
    count = chosen.shape[0]
    picked_keys = key_table[chosen]
    picked_keys = picked_keys.reshape(count, -1, picked_keys.shape[3], picked_keys.shape[4])
    picked_values = value_table[chosen]
    picked_values = picked_values.reshape(count, -1, picked_values.shape[3], picked_values.shape[4])
    scores = (
        jnp.einsum("gqhe,gkhe->ghqk", queries, picked_keys, preferred_element_type=jnp.float32)
        * scaling
    )
    highest = jnp.max(scores, axis=-1, keepdims=True)
    weights = jnp.exp(scores - highest)
    weights = (weights / jnp.sum(weights, axis=-1, keepdims=True)).astype(jnp.bfloat16)
    result = jnp.einsum(
        "ghqk,gkhe->gqhe", weights, picked_values, preferred_element_type=jnp.float32
    )
    return result.astype(jnp.bfloat16)


def general(
    grid_features,
    owners,
    adjacency,
    mesh_nodes,
    norm_gain,
    query_weight,
    key_weight,
    value_weight,
    output_weight,
    up_weight,
    down_weight,
):
    shard_count = lax.axis_size("shard")
    head_count = lax.axis_size("head")
    local_blocks, block_rows, feature_share = grid_features.shape
    slots = shard_count * CAP
    owner_col = owners[:, 0]
    position = jnp.arange(local_blocks, dtype=jnp.int32)
    earlier = (owner_col[:, None] == owner_col[None, :]) & (position[None, :] < position[:, None])
    target = owner_col * CAP + jnp.sum(earlier.astype(jnp.int32), axis=1)
    dispatch = (target[:, None] == jnp.arange(slots, dtype=jnp.int32)[None, :]).astype(jnp.bfloat16)
    offset = lax.axis_index("head") * (D // head_count)
    projected = jnp.stack(
        (
            jnp.dot(mesh_nodes, key_weight, preferred_element_type=jnp.float32).astype(
                jnp.bfloat16
            ),
            jnp.dot(mesh_nodes, value_weight, preferred_element_type=jnp.float32).astype(
                jnp.bfloat16
            ),
        )
    )
    tables = lax.all_gather(projected, ("shard", "sub"), axis=1, tiled=True)
    head_local = query_weight.shape[1] // HEAD_DIM
    key_table = tables[0].reshape(-1, block_rows, head_local, HEAD_DIM)
    value_table = tables[1].reshape(-1, block_rows, head_local, HEAD_DIM)
    send_lists = jnp.full((slots, adjacency.shape[1]), -1, jnp.int32).at[target].set(adjacency)
    send_lists = send_lists.reshape(shard_count, CAP, -1)
    complete = lax.all_gather(grid_features, "head", axis=2, tiled=True)
    outgoing = jnp.einsum(
        "gs,gbd->sbd", dispatch, complete, preferred_element_type=jnp.float32
    ).astype(jnp.bfloat16)
    arrived, lists = (
        lax.all_to_all(
            outgoing.reshape(shard_count, CAP, block_rows, D),
            "shard",
            split_axis=0,
            concat_axis=0,
            tiled=True,
        ),
        lax.all_to_all(send_lists, "shard", split_axis=0, concat_axis=0, tiled=True),
    )
    arrived = arrived.reshape(slots, block_rows, D)
    residual = lax.dynamic_slice_in_dim(arrived, offset, D // head_count, 2)
    lists = lists.reshape(slots, -1)
    count = arrived.shape[0]
    values_f = arrived.astype(jnp.float32)
    average = jnp.mean(values_f, axis=-1, keepdims=True)
    centered = values_f - average
    variance = jnp.mean(centered * centered, axis=-1, keepdims=True)
    normed = (centered * lax.rsqrt(variance + epsilon) * norm_gain).astype(jnp.bfloat16)
    flattened = normed.reshape(-1, D)
    queries = jnp.dot(flattened, query_weight, preferred_element_type=jnp.float32).astype(
        jnp.bfloat16
    )
    blocks_each = math.gcd(count, max(1, 512 // block_rows))
    steps_count = count // blocks_each
    queries = queries.reshape(steps_count, blocks_each, block_rows, head_local, HEAD_DIM)

    def attend_step(operands):
        return attend_plain(operands[0], key_table, value_table, operands[1], HEAD_DIM ** (-0.5))

    attended = lax.map(
        attend_step, (queries, jnp.maximum(lists, 0).reshape(steps_count, blocks_each, -1))
    )
    attended = attended.reshape(-1, head_local * HEAD_DIM)
    hidden = jax.nn.gelu(
        jnp.dot(flattened, up_weight, preferred_element_type=jnp.float32), approximate=False
    ).astype(jnp.bfloat16)
    branch = jnp.dot(attended, output_weight, preferred_element_type=jnp.float32)
    branch = branch + jnp.dot(hidden, down_weight, preferred_element_type=jnp.float32)
    branch = branch.reshape(count, block_rows, D)
    reduced = lax.psum_scatter(
        branch.astype(jnp.bfloat16), "head", scatter_dimension=2, tiled=True
    ).astype(jnp.float32)
    occupied = lists[:, 0] >= 0
    summed = residual.astype(jnp.float32) + reduced
    return jnp.where(occupied[:, None, None], summed, 0.0).astype(jnp.bfloat16)


def local(grid_features, owners, adjacency, mesh_nodes, *parameters):
    sizes = [lax.axis_size(axis) for axis in ("shard", "head", "sub")]
    small = grid_features.shape[:2] == (4, BLOCK) and mesh_nodes.shape[0] == 2 * BLOCK
    if sizes == [4, 2, 2] and small and grid_features.shape[2] == 512:
        return paired(grid_features, owners, adjacency, mesh_nodes, *parameters)
    return general(grid_features, owners, adjacency, mesh_nodes, *parameters)


def solution(mesh):
    return jax.shard_map(
        local,
        mesh=mesh,
        in_specs=(
            P(("groups", "shard", "sub"), None, "head"),
            P(("groups", "shard", "sub"), None),
            P(("groups", "shard", "sub"), None),
            P(("groups", "shard", "sub"), None),
            P(),
            P(None, "head"),
            P(None, "head"),
            P(None, "head"),
            P("head", None),
            P(None, "head"),
            P("head", None),
        ),
        out_specs=P(("groups", "shard", "sub"), None, "head"),
        check_vma=False,
    )
```

```python
import functools
import math

import jax
import jax.numpy as jnp
from jax import lax
from jax.experimental import pallas as pl
from jax.experimental.pallas import tpu as pltpu
from jax.sharding import PartitionSpec as P

D = 1024
HEAD_DIM = 64
CAP = 2
BLOCK = 64
QUAD = 4
WIDE = QUAD * HEAD_DIM
WIDTHS = (128, 384)
MIB = 1 << 20


epsilon = 1e-05


def dot(a, b):
    return jnp.dot(a, b, preferred_element_type=jnp.float32)


def gelu(x):
    return 0.5 * x * (1.0 + lax.erf(x * (2.0**-0.5)))


def in_hbm(x):
    return pltpu.with_memory_space_constraint(x, pltpu.HBM)


def whole(space):
    return pl.BlockSpec(memory_space=space)


def vmem(count):
    return [whole(pltpu.VMEM)] * count


def params(mib):
    return pltpu.CompilerParams(vmem_limit_bytes=mib * MIB)


def mlp_kernel(own, other, gain, wq, wup, wdn, q_out, mlp_out, normed_s):
    half = own.shape[1]
    units = wup.shape[1]
    chunk = units // 4
    x_other = other[...].astype(jnp.float32)
    x_own = own[...].astype(jnp.float32)

    def mean(a, b):
        total = jnp.sum(a, axis=-1, keepdims=True) + jnp.sum(b, axis=-1, keepdims=True)
        return total * (0.5 / half)

    average = mean(x_other, x_own)
    x_other = x_other - average
    x_own = x_own - average
    factor = lax.rsqrt(mean(x_other * x_other, x_own * x_own) + epsilon)
    normed_s[:, :half] = (x_other * factor * gain[:, :half]).astype(jnp.bfloat16)
    normed_s[:, half:] = (x_own * factor * gain[:, half:]).astype(jnp.bfloat16)
    normed = normed_s[...]
    q_out[...] = dot(normed, wq[...]).astype(jnp.bfloat16)
    for c in range(units // chunk):
        span = slice(c * chunk, (c + 1) * chunk)
        hidden = gelu(dot(normed, wup[:, span])).astype(jnp.bfloat16)
        term = dot(hidden, wdn[span, :])
        if c == 0:
            mlp_out[...] = term
        else:
            mlp_out[...] += term


def run_mlp(own, other, gain, wq, wup, wdn):
    rows = own.shape[0]
    width = wq.shape[0]
    units = wup.shape[1]
    return pl.pallas_call(
        mlp_kernel,
        out_shape=(
            jax.ShapeDtypeStruct((rows, wq.shape[1]), jnp.bfloat16),
            jax.ShapeDtypeStruct((rows, width), jnp.float32),
        ),
        in_specs=vmem(6),
        out_specs=tuple(vmem(2)),
        scratch_shapes=[pltpu.VMEM((rows, width), jnp.bfloat16)],
        compiler_params=params(16),
        cost_estimate=pl.CostEstimate(
            flops=2 * rows * width * (wq.shape[1] + 2 * units),
            bytes_accessed=2 * width * (wq.shape[1] + 2 * units),
            transcendentals=rows * units,
        ),
        name="mlp",
    )(own, other, gain, wq, wup, wdn)


def pick_kernel(mesh, out, sem):
    first = pl.multiple_of(lax.axis_index("head") * BLOCK, BLOCK)
    copy = pltpu.make_async_copy(mesh.at[pl.ds(first, BLOCK), :], out, sem)
    copy.start()
    copy.wait()


def run_pick(mesh):
    return pl.pallas_call(
        pick_kernel,
        out_shape=jax.ShapeDtypeStruct((BLOCK, mesh.shape[1]), mesh.dtype),
        in_specs=[whole(pltpu.HBM)],
        out_specs=whole(pltpu.VMEM),
        scratch_shapes=[pltpu.SemaphoreType.DMA(())],
        compiler_params=params(4),
        cost_estimate=pl.CostEstimate(flops=0, bytes_accessed=4 * mesh.size, transcendentals=0),
        name="pick",
    )(in_hbm(mesh))


def stage_kernel(axes, *refs):
    sources, targets, sem = refs[: len(axes)], refs[len(axes) : -1], refs[-1]
    h = lax.axis_index("head")
    copies = []
    for source, target, axis in zip(sources, targets, axes):
        if axis is None:
            copies.append(pltpu.make_async_copy(source, target, sem.at[len(copies)]))
            continue
        if axis == "rest":
            span = pl.ds(pl.multiple_of((1 - h) * BLOCK, BLOCK), BLOCK)
            copies.append(pltpu.make_async_copy(source.at[span, :], target, sem.at[len(copies)]))
            continue
        half = source.shape[axis] // 2
        for part, head in enumerate((1 - h, h)):
            span = pl.ds(pl.multiple_of(head * half, half), half)
            place = pl.ds(part * half, half)
            if axis == 0:
                pair = (source.at[span, :], target.at[place, :])
            else:
                pair = (source.at[:, span], target.at[:, place])
            copies.append(pltpu.make_async_copy(*pair, sem.at[len(copies)]))
    for copy in copies:
        copy.start()
    for copy in copies:
        copy.wait()


def run_stage(arrays, axes):
    size = sum(2 * array.size for array in arrays)
    return pl.pallas_call(
        functools.partial(stage_kernel, axes),
        out_shape=tuple(
            jax.ShapeDtypeStruct((BLOCK,) + array.shape[1:] if axis == "rest" else array.shape, array.dtype)
            for array, axis in zip(arrays, axes)
        ),
        in_specs=[whole(pltpu.HBM)] * len(arrays),
        out_specs=tuple(vmem(len(arrays))),
        scratch_shapes=[pltpu.SemaphoreType.DMA((2 * len(arrays),))],
        compiler_params=params(16),
        cost_estimate=pl.CostEstimate(flops=0, bytes_accessed=20 * size, transcendentals=0),
        name="stage",
    )(*(in_hbm(array) for array in arrays))


def project_kernel(*refs):
    pieces, (wk, wv, out) = refs[:-3], refs[-3:]
    width = wk.shape[1]
    rows = jnp.concatenate([piece[...] for piece in pieces], axis=0)
    out[:, :width] = dot(rows, wk[...]).astype(jnp.bfloat16)
    out[:, width:] = dot(rows, wv[...]).astype(jnp.bfloat16)


def run_project(pieces, wk, wv):
    rows = sum(piece.shape[0] for piece in pieces)
    depth, width = wk.shape
    return pl.pallas_call(
        project_kernel,
        out_shape=jax.ShapeDtypeStruct((rows, 2 * width), jnp.bfloat16),
        in_specs=vmem(len(pieces) + 2),
        out_specs=whole(pltpu.VMEM),
        compiler_params=params(8),
        cost_estimate=pl.CostEstimate(
            flops=300 * rows * depth * width,
            bytes_accessed=300 * depth * width + 300 * rows * depth,
            transcendentals=0,
        ),
        name="project",
    )(*pieces, wk, wv)


def table_kernel(mine, sibling, table):
    table[0, : mine.shape[0]] = mine[...]
    table[1, : mine.shape[0]] = sibling[...]


def run_table(mine, sibling, blocks):
    return pl.pallas_call(
        table_kernel,
        out_shape=jax.ShapeDtypeStruct((2, blocks) + mine.shape[1:], jnp.bfloat16),
        in_specs=vmem(2),
        out_specs=whole(pltpu.VMEM),
        compiler_params=params(8),
        cost_estimate=pl.CostEstimate(
            flops=0, bytes_accessed=80 * mine.size, transcendentals=0
        ),
        name="table",
    )(mine, sibling)


def columns_of(c):
    return slice(sum(WIDTHS[:c]), sum(WIDTHS[: c + 1]))


def project_out(c, att, mlp, wo, send, keep):
    half = att.shape[1]
    chunk = columns_of(c)
    for out, first in ((send, 0), (keep, half)):
        span = slice(first + chunk.start, first + chunk.stop)
        out[...] = (mlp[:, span] + dot(att[...], wo[:, span])).astype(jnp.bfloat16)


def attend_kernel(
    adjacency, q, mine, sibling, table_in, mlp, wo, send, keep, att, table
):
    del table_in
    s = lax.axis_index("shard")
    h = lax.axis_index("head")
    u = lax.axis_index("sub")
    half = wo.shape[0]
    ready = table.shape[1] - mine.shape[0]
    for i, part in enumerate((mine, sibling)):
        table[i, ready:] = part[...]
    rows_of = lax.broadcasted_iota(jnp.int32, (WIDE, WIDE), 0) // BLOCK
    lanes_of = lax.broadcasted_iota(jnp.int32, (WIDE, WIDE), 1) // HEAD_DIM
    diagonal = rows_of == lanes_of
    lane_head = lax.broadcasted_iota(jnp.int32, (BLOCK, WIDE), 1) // HEAD_DIM
    scale = HEAD_DIM**-0.5 * math.log2(math.e)
    groups = half // WIDE
    places = []
    for b in range(adjacency.shape[0]):
        places.append([])
        for j in range(adjacency.shape[1]):
            m = adjacency[b, j]
            part = lax.rem(m, 2)
            core = lax.rem(m // 2, 2)
            distance = s ^ (m // 4)
            part = jnp.where(distance <= 1, part, part ^ h)
            places[b].append((core ^ u, distance * 2 + part))

    def scores_of(step):
        b, g = divmod(step, groups)
        columns = slice(g * WIDE, (g + 1) * WIDE)
        keys = jnp.concatenate([table[i, p, :, columns] for i, p in places[b]], axis=0)
        stacked = jnp.concatenate([q[b * BLOCK : (b + 1) * BLOCK, columns]] * QUAD, axis=0)
        stacked = jnp.where(diagonal, stacked, jnp.zeros_like(stacked))
        return lax.dot_general(
            stacked, keys, (((1,), (1,)), ((), ())), preferred_element_type=jnp.float32
        )

    steps = len(places) * groups
    scores = scores_of(0)
    for step in range(steps):
        following = scores_of(step + 1) if step + 1 < steps else None
        b, g = divmod(step, groups)
        columns = slice(half + g * WIDE, half + (g + 1) * WIDE)
        values = jnp.concatenate([table[i, p, :, columns] for i, p in places[b]], axis=0)
        highest = jnp.max(scores, axis=-1, keepdims=True)
        weights = jnp.exp2((scores - highest) * scale)
        total = jnp.sum(weights, axis=-1, keepdims=True)
        mixed = dot(weights.astype(jnp.bfloat16), values) * (1.0 / total)
        merged = mixed[0:BLOCK, :]
        for i in range(1, QUAD):
            merged = jnp.where(lane_head == i, mixed[i * BLOCK : (i + 1) * BLOCK, :], merged)
        rows = slice(b * BLOCK, (b + 1) * BLOCK)
        att[rows, g * WIDE : (g + 1) * WIDE] = merged.astype(jnp.bfloat16)
        scores = following
    project_out(0, att, mlp, wo, send, keep)


def run_attend(adjacency, q, mine, sibling, table, mlp, wo):
    rows, half = q.shape
    part = jax.ShapeDtypeStruct((rows, WIDTHS[0]), jnp.bfloat16)
    blocks = table.shape[0] * table.shape[1]
    send, keep, att, _ = pl.pallas_call(
        attend_kernel,
        out_shape=(
            part,
            part,
            jax.ShapeDtypeStruct(q.shape, jnp.bfloat16),
            jax.ShapeDtypeStruct(table.shape, jnp.bfloat16),
        ),
        in_specs=[whole(pltpu.SMEM)] + vmem(6),
        out_specs=tuple(vmem(4)),
        input_output_aliases={4: 3},
        compiler_params=params(16),
        cost_estimate=pl.CostEstimate(
            flops=20 * rows * half * (D + 8 * 8 * BLOCK),
            bytes_accessed=40 * blocks * BLOCK * half + 20 * half * D + 40 * rows * D,
            transcendentals=rows * 8 * BLOCK * half // HEAD_DIM,
        ),
        name="attend",
    )(adjacency, q, mine, sibling, table, mlp, wo)
    return send, keep, att


def run_project_out(c, att, mlp, wo):
    rows, half = att.shape
    part = jax.ShapeDtypeStruct((rows, WIDTHS[c]), jnp.bfloat16)
    return pl.pallas_call(
        functools.partial(project_out, c),
        out_shape=(part, part),
        in_specs=vmem(3),
        out_specs=tuple(vmem(2)),
        compiler_params=params(8),
        cost_estimate=pl.CostEstimate(
            flops=200 * rows * half * D,
            bytes_accessed=200 * half * D,
            transcendentals=0,
        ),
        name="project_out",
    )(att, mlp, wo)


def combine_kernel(chunks, distances, owners, grid_features, *refs):
    s = lax.axis_index("shard")
    keeps, refs = refs[: len(chunks)], refs[len(chunks) :]
    swaps, outs = refs[: len(chunks)], refs[len(chunks) :]
    count = grid_features.shape[0]
    names = [owners[t, 0] for t in range(count)]
    first = columns_of(chunks[0]).start
    for d, out in zip(distances, outs):
        out[...] = jnp.zeros(out.shape, jnp.bfloat16)
        seen = jnp.int32(0)
        for t in range(count):
            hit = names[t] == s ^ d
            rank = seen

            @pl.when(hit)
            def _():
                rows = slice(t * BLOCK, (t + 1) * BLOCK)
                for c, keep, swap in zip(chunks, keeps, swaps):
                    columns = columns_of(c)
                    partials = keep[rows, :].astype(jnp.float32)
                    partials = partials + swap[rows, :].astype(jnp.float32)
                    residual = grid_features[t, :, columns].astype(jnp.float32)
                    place = slice(columns.start - first, columns.stop - first)
                    out[rank, :, place] = (residual + partials).astype(jnp.bfloat16)

            seen = seen + hit.astype(jnp.int32)


def run_combine(chunks, distances, owners, grid_features, keeps, swaps):
    count, rows, _ = grid_features.shape
    width = sum(WIDTHS[c] for c in chunks)
    slot = jax.ShapeDtypeStruct((CAP, rows, width), jnp.bfloat16)
    return pl.pallas_call(
        functools.partial(combine_kernel, chunks, distances),
        out_shape=(slot,) * len(distances),
        in_specs=[whole(pltpu.SMEM)] + vmem(1 + 2 * len(chunks)),
        out_specs=tuple(vmem(len(distances))),
        compiler_params=params(8),
        cost_estimate=pl.CostEstimate(
            flops=60000 * count * rows * width,
            bytes_accessed=400 * rows * width * (3 * count + CAP * len(distances)),
            transcendentals=0,
        ),
        name="combine",
    )(owners, grid_features, *keeps, *swaps)


def place_kernel(spots, *refs):
    out, sem = refs[-2:]
    s = lax.axis_index("shard")
    copies = []
    for i, (d, first) in enumerate(spots):
        columns = pl.ds(first, refs[i].shape[2])
        slots = pl.ds((s ^ d) * CAP, CAP)
        copies.append(pltpu.make_async_copy(refs[i], out.at[slots, :, columns], sem.at[i]))
        copies[i].start()
    for copy in copies:
        copy.wait()


def run_place(spots, arrived, placed, shape):
    return pl.pallas_call(
        functools.partial(place_kernel, spots),
        out_shape=jax.ShapeDtypeStruct(shape, jnp.bfloat16),
        in_specs=vmem(len(arrived)) + [whole(pltpu.HBM)] * len(placed),
        out_specs=whole(pltpu.HBM),
        scratch_shapes=[pltpu.SemaphoreType.DMA((len(arrived),))],
        input_output_aliases={len(arrived): 0} if placed else {},
        compiler_params=params(4),
        cost_estimate=pl.CostEstimate(
            flops=400000 * sum(part.size for part in arrived), bytes_accessed=0, transcendentals=0
        ),
        name="place",
    )(*arrived, *placed)


def crossed(x, distance, size):
    return lax.ppermute(x, "shard", [(i, i ^ distance) for i in range(size)])


def swapped(x, axis):
    return lax.ppermute(x, axis, [(0, 1), (1, 0)])


def paired(
    grid_features,
    owners,
    adjacency,
    mesh_nodes,
    norm_gain,
    query_weight,
    key_weight,
    value_weight,
    output_weight,
    up_weight,
    down_weight,
):
    shards = lax.axis_size("shard")
    count, rows, half = grid_features.shape
    flat = grid_features.reshape(count * rows, half)
    far = crossed(run_pick(mesh_nodes), 2, shards)
    near = crossed(mesh_nodes, 1, shards)
    other = swapped(flat, "head")
    staged = run_stage(
        (
            flat,
            norm_gain.reshape(1, -1),
            query_weight,
            up_weight,
            down_weight,
            output_weight,
            key_weight,
            value_weight,
            mesh_nodes,
            mesh_nodes,
        ),
        (None, 1, 0, 0, 1, 1, None, None, None, "rest"),
    )
    flat, gain, wq, wup, wdn, wo, wk, wv, mesh, rest = staged
    straight = crossed(rest, 3, shards)
    far, _ = lax.optimization_barrier((far, rest))
    farther = crossed(far, 1, shards)
    far_pair = swapped(far, "head")
    queries, mlp = run_mlp(flat, other, gain, wq, wup, wdn)
    queries, mlp, far_pair, near = lax.optimization_barrier((queries, mlp, far_pair, near))
    blocked = (-1, BLOCK, 2 * half)
    mine_a = run_project((mesh, near, far, far_pair), wk, wv)
    sibling_a = swapped(mine_a, "sub")
    table = run_table(mine_a.reshape(blocked), sibling_a.reshape(blocked), 2 * shards)
    mine_b = run_project((farther, straight), wk, wv)
    sibling_b = swapped(mine_b, "sub")
    send, keep, att = run_attend(
        adjacency, queries, mine_b.reshape(blocked), sibling_b.reshape(blocked), table, mlp, wo
    )
    keeps, swaps, slots, placed = [], [], [], []
    shape = (shards * CAP, rows, half)
    for c in range(len(WIDTHS)):
        if c > 0:
            send, keep = run_project_out(c, att, mlp, wo)
        received = swapped(send, "head")
        if c > 0:
            received, _ = lax.optimization_barrier((received, slots[c - 1][0]))
        slots.append(run_combine((c,), (2, 3), owners, grid_features, (keep,), (received,)))
        keeps.append(keep)
        swaps.append(received)
    every = tuple(range(len(WIDTHS)))
    swaps[-1], _ = lax.optimization_barrier((swaps[-1], slots[-1][0]))
    near_slots, own_slots = run_combine(every, (1, 0), owners, grid_features, keeps, swaps)
    for c in every:
        first = columns_of(c).start
        spots = [(2, first), (3, first)]
        arrived = [crossed(slot, d, shards) for d, slot in zip((2, 3), slots[c])]
        if c == len(WIDTHS) - 1:
            spots += [(1, 0), (0, 0)]
            arrived += [crossed(near_slots, 1, shards), own_slots]
        placed = [run_place(spots, arrived, placed, shape)]
    return placed[0]


def attend_plain(queries, key_table, value_table, chosen, scaling):
    count = chosen.shape[0]
    picked_keys = key_table[chosen]
    picked_keys = picked_keys.reshape(count, -1, picked_keys.shape[3], picked_keys.shape[4])
    picked_values = value_table[chosen]
    picked_values = picked_values.reshape(count, -1, picked_values.shape[3], picked_values.shape[4])
    scores = (
        jnp.einsum("gqhe,gkhe->ghqk", queries, picked_keys, preferred_element_type=jnp.float32)
        * scaling
    )
    highest = jnp.max(scores, axis=-1, keepdims=True)
    weights = jnp.exp(scores - highest)
    weights = (weights / jnp.sum(weights, axis=-1, keepdims=True)).astype(jnp.bfloat16)
    result = jnp.einsum(
        "ghqk,gkhe->gqhe", weights, picked_values, preferred_element_type=jnp.float32
    )
    return result.astype(jnp.bfloat16)


def general(
    grid_features,
    owners,
    adjacency,
    mesh_nodes,
    norm_gain,
    query_weight,
    key_weight,
    value_weight,
    output_weight,
    up_weight,
    down_weight,
):
    shard_count = lax.axis_size("shard")
    head_count = lax.axis_size("head")
    local_blocks, block_rows, feature_share = grid_features.shape
    slots = shard_count * CAP
    owner_col = owners[:, 0]
    position = jnp.arange(local_blocks, dtype=jnp.int32)
    earlier = (owner_col[:, None] == owner_col[None, :]) & (position[None, :] < position[:, None])
    target = owner_col * CAP + jnp.sum(earlier.astype(jnp.int32), axis=1)
    dispatch = (target[:, None] == jnp.arange(slots, dtype=jnp.int32)[None, :]).astype(jnp.bfloat16)
    offset = lax.axis_index("head") * (D // head_count)
    projected = jnp.stack(
        (
            jnp.dot(mesh_nodes, key_weight, preferred_element_type=jnp.float32).astype(
                jnp.bfloat16
            ),
            jnp.dot(mesh_nodes, value_weight, preferred_element_type=jnp.float32).astype(
                jnp.bfloat16
            ),
        )
    )
    tables = lax.all_gather(projected, ("shard", "sub"), axis=1, tiled=True)
    head_local = query_weight.shape[1] // HEAD_DIM
    key_table = tables[0].reshape(-1, block_rows, head_local, HEAD_DIM)
    value_table = tables[1].reshape(-1, block_rows, head_local, HEAD_DIM)
    send_lists = jnp.full((slots, adjacency.shape[1]), -1, jnp.int32).at[target].set(adjacency)
    send_lists = send_lists.reshape(shard_count, CAP, -1)
    complete = lax.all_gather(grid_features, "head", axis=2, tiled=True)
    outgoing = jnp.einsum(
        "gs,gbd->sbd", dispatch, complete, preferred_element_type=jnp.float32
    ).astype(jnp.bfloat16)
    arrived, lists = (
        lax.all_to_all(
            outgoing.reshape(shard_count, CAP, block_rows, D),
            "shard",
            split_axis=0,
            concat_axis=0,
            tiled=True,
        ),
        lax.all_to_all(send_lists, "shard", split_axis=0, concat_axis=0, tiled=True),
    )
    arrived = arrived.reshape(slots, block_rows, D)
    residual = lax.dynamic_slice_in_dim(arrived, offset, D // head_count, 2)
    lists = lists.reshape(slots, -1)
    count = arrived.shape[0]
    values_f = arrived.astype(jnp.float32)
    average = jnp.mean(values_f, axis=-1, keepdims=True)
    centered = values_f - average
    variance = jnp.mean(centered * centered, axis=-1, keepdims=True)
    normed = (centered * lax.rsqrt(variance + epsilon) * norm_gain).astype(jnp.bfloat16)
    flattened = normed.reshape(-1, D)
    queries = jnp.dot(flattened, query_weight, preferred_element_type=jnp.float32).astype(
        jnp.bfloat16
    )
    blocks_each = math.gcd(count, max(1, 512 // block_rows))
    steps_count = count // blocks_each
    queries = queries.reshape(steps_count, blocks_each, block_rows, head_local, HEAD_DIM)

    def attend_step(operands):
        return attend_plain(operands[0], key_table, value_table, operands[1], HEAD_DIM ** (-0.5))

    attended = lax.map(
        attend_step, (queries, jnp.maximum(lists, 0).reshape(steps_count, blocks_each, -1))
    )
    attended = attended.reshape(-1, head_local * HEAD_DIM)
    hidden = jax.nn.gelu(
        jnp.dot(flattened, up_weight, preferred_element_type=jnp.float32), approximate=False
    ).astype(jnp.bfloat16)
    branch = jnp.dot(attended, output_weight, preferred_element_type=jnp.float32)
    branch = branch + jnp.dot(hidden, down_weight, preferred_element_type=jnp.float32)
    branch = branch.reshape(count, block_rows, D)
    reduced = lax.psum_scatter(
        branch.astype(jnp.bfloat16), "head", scatter_dimension=2, tiled=True
    ).astype(jnp.float32)
    occupied = lists[:, 0] >= 0
    summed = residual.astype(jnp.float32) + reduced
    return jnp.where(occupied[:, None, None], summed, 0.0).astype(jnp.bfloat16)


def local(grid_features, owners, adjacency, mesh_nodes, *parameters):
    sizes = [lax.axis_size(axis) for axis in ("shard", "head", "sub")]
    small = grid_features.shape[:2] == (4, BLOCK) and mesh_nodes.shape[0] == 2 * BLOCK
    if sizes == [4, 2, 2] and small and grid_features.shape[2] == 512:
        return paired(grid_features, owners, adjacency, mesh_nodes, *parameters)
    return general(grid_features, owners, adjacency, mesh_nodes, *parameters)


def solution(mesh):
    return jax.shard_map(
        local,
        mesh=mesh,
        in_specs=(
            P(("groups", "shard", "sub"), None, "head"),
            P(("groups", "shard", "sub"), None),
            P(("groups", "shard", "sub"), None),
            P(("groups", "shard", "sub"), None),
            P(),
            P(None, "head"),
            P(None, "head"),
            P(None, "head"),
            P("head", None),
            P(None, "head"),
            P("head", None),
        ),
        out_specs=P(("groups", "shard", "sub"), None, "head"),
        check_vma=False,
    )
```

```python
import functools
import math

import jax
import jax.numpy as jnp
from jax import lax
from jax.experimental import pallas as pl
from jax.experimental.pallas import tpu as pltpu
from jax.sharding import PartitionSpec as P

D = 1024
HEAD_DIM = 64
CAP = 2
BLOCK = 64
QUAD = 4
WIDE = QUAD * HEAD_DIM
WIDTHS = (128, 384)
MIB = 1 << 20


epsilon = 1e-05


def dot(a, b):
    return jnp.dot(a, b, preferred_element_type=jnp.float32)


def gelu(x):
    return 0.5 * x * (1.0 + lax.erf(x * (2.0**-0.5)))


def in_hbm(x):
    return pltpu.with_memory_space_constraint(x, pltpu.HBM)


def in_vmem(x):
    return pltpu.with_memory_space_constraint(x, pltpu.VMEM)


def whole(space):
    return pl.BlockSpec(memory_space=space)


def vmem(count):
    return [whole(pltpu.VMEM)] * count


def params(mib):
    return pltpu.CompilerParams(vmem_limit_bytes=mib * MIB)


def mlp_kernel(own, other, gain, wq, wup, wdn, q_out, mlp_out, normed_s):
    half = own.shape[1]
    units = wup.shape[1]
    chunk = units // 4
    x_other = other[...].astype(jnp.float32)
    x_own = own[...].astype(jnp.float32)

    def mean(a, b):
        total = jnp.sum(a, axis=-1, keepdims=True) + jnp.sum(b, axis=-1, keepdims=True)
        return total * (0.5 / half)

    average = mean(x_other, x_own)
    x_other = x_other - average
    x_own = x_own - average
    factor = lax.rsqrt(mean(x_other * x_other, x_own * x_own) + epsilon)
    normed_s[:, :half] = (x_other * factor * gain[:, :half]).astype(jnp.bfloat16)
    normed_s[:, half:] = (x_own * factor * gain[:, half:]).astype(jnp.bfloat16)
    normed = normed_s[...]
    q_out[...] = dot(normed, wq[...]).astype(jnp.bfloat16)
    for c in range(units // chunk):
        span = slice(c * chunk, (c + 1) * chunk)
        hidden = gelu(dot(normed, wup[:, span])).astype(jnp.bfloat16)
        term = dot(hidden, wdn[span, :])
        if c == 0:
            mlp_out[...] = term
        else:
            mlp_out[...] += term


def run_mlp(own, other, gain, wq, wup, wdn):
    rows = own.shape[0]
    width = wq.shape[0]
    units = wup.shape[1]
    return pl.pallas_call(
        mlp_kernel,
        out_shape=(
            jax.ShapeDtypeStruct((rows, wq.shape[1]), jnp.bfloat16),
            jax.ShapeDtypeStruct((rows, width), jnp.float32),
        ),
        in_specs=vmem(6),
        out_specs=tuple(vmem(2)),
        scratch_shapes=[pltpu.VMEM((rows, width), jnp.bfloat16)],
        compiler_params=params(16),
        cost_estimate=pl.CostEstimate(
            flops=2 * rows * width * (wq.shape[1] + 2 * units),
            bytes_accessed=2 * width * (wq.shape[1] + 2 * units),
            transcendentals=rows * units,
        ),
        name="mlp",
    )(own, other, gain, wq, wup, wdn)


def pick_kernel(mesh, out, sem):
    first = pl.multiple_of(lax.axis_index("head") * BLOCK, BLOCK)
    copy = pltpu.make_async_copy(mesh.at[pl.ds(first, BLOCK), :], out, sem)
    copy.start()
    copy.wait()


def run_pick(mesh):
    return pl.pallas_call(
        pick_kernel,
        out_shape=jax.ShapeDtypeStruct((BLOCK, mesh.shape[1]), mesh.dtype),
        in_specs=[whole(pltpu.HBM)],
        out_specs=whole(pltpu.VMEM),
        scratch_shapes=[pltpu.SemaphoreType.DMA(())],
        compiler_params=params(4),
        cost_estimate=pl.CostEstimate(flops=0, bytes_accessed=4 * mesh.size, transcendentals=0),
        name="pick",
    )(in_hbm(mesh))


def stage_kernel(axes, *refs):
    sources, targets, sem = refs[: len(axes)], refs[len(axes) : -1], refs[-1]
    h = lax.axis_index("head")
    copies = []

    def add(source, target):
        pieces = 2 if source.shape[0] >= 512 else 1
        rows = source.shape[0] // pieces
        for piece in range(pieces):
            span = pl.ds(piece * rows, rows)
            copies.append(
                pltpu.make_async_copy(
                    source.at[span, :], target.at[span, :], sem.at[len(copies)]
                )
            )
            copies[-1].start()

    for source, target, axis in zip(sources, targets, axes):
        if axis is None:
            add(source, target)
            continue
        if axis == "rest":
            add(source.at[pl.ds(pl.multiple_of((1 - h) * BLOCK, BLOCK), BLOCK), :], target)
            continue
        half = source.shape[axis] // 2
        for part, head in enumerate((1 - h, h)):
            span = pl.ds(pl.multiple_of(head * half, half), half)
            place = pl.ds(part * half, half)
            if axis == 0:
                add(source.at[span, :], target.at[place, :])
            else:
                add(source.at[:, span], target.at[:, place])
    for copy in copies:
        copy.wait()


def run_stage(arrays, axes):
    size = sum(2 * array.size for array in arrays)
    return pl.pallas_call(
        functools.partial(stage_kernel, axes),
        out_shape=tuple(
            jax.ShapeDtypeStruct((BLOCK,) + array.shape[1:] if axis == "rest" else array.shape, array.dtype)
            for array, axis in zip(arrays, axes)
        ),
        in_specs=[whole(pltpu.HBM)] * len(arrays),
        out_specs=tuple(vmem(len(arrays))),
        scratch_shapes=[pltpu.SemaphoreType.DMA((4 * len(arrays),))],
        compiler_params=params(16),
        cost_estimate=pl.CostEstimate(
            flops=2000 * size, bytes_accessed=20 * size, transcendentals=0
        ),
        name="stage",
    )(*(in_hbm(array) for array in arrays))


def project_kernel(*refs):
    pieces, (wk, wv, out) = refs[:-3], refs[-3:]
    width = wk.shape[1]
    rows = jnp.concatenate([piece[...] for piece in pieces], axis=0)
    out[:, :width] = dot(rows, wk[...]).astype(jnp.bfloat16)
    out[:, width:] = dot(rows, wv[...]).astype(jnp.bfloat16)


def run_project(pieces, wk, wv):
    rows = sum(piece.shape[0] for piece in pieces)
    depth, width = wk.shape
    return pl.pallas_call(
        project_kernel,
        out_shape=jax.ShapeDtypeStruct((rows, 2 * width), jnp.bfloat16),
        in_specs=vmem(len(pieces) + 2),
        out_specs=whole(pltpu.VMEM),
        compiler_params=params(8),
        cost_estimate=pl.CostEstimate(
            flops=300 * rows * depth * width,
            bytes_accessed=300 * depth * width + 300 * rows * depth,
            transcendentals=0,
        ),
        name="project",
    )(*pieces, in_vmem(wk), in_vmem(wv))


def table_kernel(mine, sibling, table):
    table[0, : mine.shape[0]] = mine[...]
    table[1, : mine.shape[0]] = sibling[...]


def run_table(mine, sibling, blocks):
    return pl.pallas_call(
        table_kernel,
        out_shape=jax.ShapeDtypeStruct((2, blocks) + mine.shape[1:], jnp.bfloat16),
        in_specs=vmem(2),
        out_specs=whole(pltpu.VMEM),
        compiler_params=params(8),
        cost_estimate=pl.CostEstimate(
            flops=0, bytes_accessed=80 * mine.size, transcendentals=0
        ),
        name="table",
    )(mine, sibling)


def columns_of(c):
    return slice(sum(WIDTHS[:c]), sum(WIDTHS[: c + 1]))


def project_out(c, att, mlp, wo, send, keep):
    half = att.shape[1]
    chunk = columns_of(c)
    for out, first in ((send, 0), (keep, half)):
        span = slice(first + chunk.start, first + chunk.stop)
        out[...] = (mlp[:, span] + dot(att[...], wo[:, span])).astype(jnp.bfloat16)


def attend_kernel(
    adjacency, q, mine, sibling, table_in, mlp, wo, send, keep, att, table
):
    del table_in
    s = lax.axis_index("shard")
    h = lax.axis_index("head")
    u = lax.axis_index("sub")
    half = wo.shape[0]
    ready = table.shape[1] - mine.shape[0]
    for i, part in enumerate((mine, sibling)):
        table[i, ready:] = part[...]
    rows_of = lax.broadcasted_iota(jnp.int32, (WIDE, WIDE), 0) // BLOCK
    lanes_of = lax.broadcasted_iota(jnp.int32, (WIDE, WIDE), 1) // HEAD_DIM
    diagonal = rows_of == lanes_of
    lane_head = lax.broadcasted_iota(jnp.int32, (BLOCK, WIDE), 1) // HEAD_DIM
    scale = HEAD_DIM**-0.5 * math.log2(math.e)
    groups = half // WIDE
    places = []
    for b in range(adjacency.shape[0]):
        places.append([])
        for j in range(adjacency.shape[1]):
            m = adjacency[b, j]
            part = lax.rem(m, 2)
            core = lax.rem(m // 2, 2)
            distance = s ^ (m // 4)
            part = jnp.where(distance <= 1, part, part ^ h)
            places[b].append((core ^ u, distance * 2 + part))

    def scores_of(step):
        b, g = divmod(step, groups)
        columns = slice(g * WIDE, (g + 1) * WIDE)
        keys = jnp.concatenate([table[i, p, :, columns] for i, p in places[b]], axis=0)
        stacked = jnp.concatenate([q[b * BLOCK : (b + 1) * BLOCK, columns]] * QUAD, axis=0)
        stacked = jnp.where(diagonal, stacked, jnp.zeros_like(stacked))
        return lax.dot_general(
            stacked, keys, (((1,), (1,)), ((), ())), preferred_element_type=jnp.float32
        )

    steps = len(places) * groups
    scores = scores_of(0)
    for step in range(steps):
        following = scores_of(step + 1) if step + 1 < steps else None
        b, g = divmod(step, groups)
        columns = slice(half + g * WIDE, half + (g + 1) * WIDE)
        values = jnp.concatenate([table[i, p, :, columns] for i, p in places[b]], axis=0)
        highest = jnp.max(scores, axis=-1, keepdims=True)
        weights = jnp.exp2((scores - highest) * scale)
        total = jnp.sum(weights, axis=-1, keepdims=True)
        mixed = dot(weights.astype(jnp.bfloat16), values) * (1.0 / total)
        merged = mixed[0:BLOCK, :]
        for i in range(1, QUAD):
            merged = jnp.where(lane_head == i, mixed[i * BLOCK : (i + 1) * BLOCK, :], merged)
        rows = slice(b * BLOCK, (b + 1) * BLOCK)
        att[rows, g * WIDE : (g + 1) * WIDE] = merged.astype(jnp.bfloat16)
        scores = following
    project_out(0, att, mlp, wo, send, keep)


def run_attend(adjacency, q, mine, sibling, table, mlp, wo):
    rows, half = q.shape
    part = jax.ShapeDtypeStruct((rows, WIDTHS[0]), jnp.bfloat16)
    blocks = table.shape[0] * table.shape[1]
    send, keep, att, _ = pl.pallas_call(
        attend_kernel,
        out_shape=(
            part,
            part,
            jax.ShapeDtypeStruct(q.shape, jnp.bfloat16),
            jax.ShapeDtypeStruct(table.shape, jnp.bfloat16),
        ),
        in_specs=[whole(pltpu.SMEM)] + vmem(6),
        out_specs=tuple(vmem(4)),
        input_output_aliases={4: 3},
        compiler_params=params(16),
        cost_estimate=pl.CostEstimate(
            flops=20 * rows * half * (D + 8 * 8 * BLOCK),
            bytes_accessed=40 * blocks * BLOCK * half + 20 * half * D + 40 * rows * D,
            transcendentals=rows * 8 * BLOCK * half // HEAD_DIM,
        ),
        name="attend",
    )(adjacency, q, mine, sibling, table, mlp, wo)
    return send, keep, att


def run_project_out(c, att, mlp, wo):
    rows, half = att.shape
    part = jax.ShapeDtypeStruct((rows, WIDTHS[c]), jnp.bfloat16)
    return pl.pallas_call(
        functools.partial(project_out, c),
        out_shape=(part, part),
        in_specs=vmem(3),
        out_specs=tuple(vmem(2)),
        compiler_params=params(8),
        cost_estimate=pl.CostEstimate(
            flops=200 * rows * half * D,
            bytes_accessed=200 * half * D,
            transcendentals=0,
        ),
        name="project_out",
    )(att, mlp, wo)


def combine_kernel(chunks, distances, owners, grid_features, *refs):
    s = lax.axis_index("shard")
    keeps, refs = refs[: len(chunks)], refs[len(chunks) :]
    swaps, outs = refs[: len(chunks)], refs[len(chunks) :]
    count = grid_features.shape[0]
    names = [owners[t, 0] for t in range(count)]
    first = columns_of(chunks[0]).start
    for d, out in zip(distances, outs):
        out[...] = jnp.zeros(out.shape, jnp.bfloat16)
        seen = jnp.int32(0)
        for t in range(count):
            hit = names[t] == s ^ d
            rank = seen

            @pl.when(hit)
            def _():
                rows = slice(t * BLOCK, (t + 1) * BLOCK)
                for c, keep, swap in zip(chunks, keeps, swaps):
                    columns = columns_of(c)
                    partials = keep[rows, :].astype(jnp.float32)
                    partials = partials + swap[rows, :].astype(jnp.float32)
                    residual = grid_features[t, :, columns].astype(jnp.float32)
                    place = slice(columns.start - first, columns.stop - first)
                    out[rank, :, place] = (residual + partials).astype(jnp.bfloat16)

            seen = seen + hit.astype(jnp.int32)


def run_combine(chunks, distances, owners, grid_features, keeps, swaps):
    count, rows, _ = grid_features.shape
    width = sum(WIDTHS[c] for c in chunks)
    slot = jax.ShapeDtypeStruct((CAP, rows, width), jnp.bfloat16)
    return pl.pallas_call(
        functools.partial(combine_kernel, chunks, distances),
        out_shape=(slot,) * len(distances),
        in_specs=[whole(pltpu.SMEM)] + vmem(1 + 2 * len(chunks)),
        out_specs=tuple(vmem(len(distances))),
        compiler_params=params(8),
        cost_estimate=pl.CostEstimate(
            flops=60000 * count * rows * width,
            bytes_accessed=400 * rows * width * (3 * count + CAP * len(distances)),
            transcendentals=0,
        ),
        name="combine",
    )(owners, grid_features, *keeps, *swaps)


def place_kernel(spots, *refs):
    out, sem = refs[-2:]
    s = lax.axis_index("shard")
    copies = []
    for i, (d, first) in enumerate(spots):
        columns = pl.ds(first, refs[i].shape[2])
        slots = pl.ds((s ^ d) * CAP, CAP)
        copies.append(pltpu.make_async_copy(refs[i], out.at[slots, :, columns], sem.at[i]))
        copies[i].start()
    for copy in copies:
        copy.wait()


def run_place(spots, arrived, placed, shape):
    return pl.pallas_call(
        functools.partial(place_kernel, spots),
        out_shape=jax.ShapeDtypeStruct(shape, jnp.bfloat16),
        in_specs=vmem(len(arrived)) + [whole(pltpu.HBM)] * len(placed),
        out_specs=whole(pltpu.HBM),
        scratch_shapes=[pltpu.SemaphoreType.DMA((len(arrived),))],
        input_output_aliases={len(arrived): 0} if placed else {},
        compiler_params=params(4),
        cost_estimate=pl.CostEstimate(
            flops=400000 * sum(part.size for part in arrived), bytes_accessed=0, transcendentals=0
        ),
        name="place",
    )(*arrived, *placed)


def crossed(x, distance, size):
    return lax.ppermute(x, "shard", [(i, i ^ distance) for i in range(size)])


def swapped(x, axis):
    return lax.ppermute(x, axis, [(0, 1), (1, 0)])


def paired(
    grid_features,
    owners,
    adjacency,
    mesh_nodes,
    norm_gain,
    query_weight,
    key_weight,
    value_weight,
    output_weight,
    up_weight,
    down_weight,
):
    shards = lax.axis_size("shard")
    count, rows, half = grid_features.shape
    flat = grid_features.reshape(count * rows, half)
    half_unit = run_pick(mesh_nodes)
    far = crossed(half_unit, 2, shards)
    waiting, _ = lax.optimization_barrier((mesh_nodes, half_unit))
    near = crossed(waiting, 1, shards)
    waiting, _ = lax.optimization_barrier((flat, half_unit))
    other = swapped(waiting, "head")
    flat, gain, wq, wup, wdn, mesh, rest = run_stage(
        (
            flat,
            norm_gain.reshape(1, -1),
            query_weight,
            up_weight,
            down_weight,
            mesh_nodes,
            mesh_nodes,
        ),
        (None, 1, 0, 0, 1, None, "rest"),
    )
    straight = crossed(rest, 3, shards)
    far, _ = lax.optimization_barrier((far, rest))
    farther = crossed(far, 1, shards)
    far_pair = swapped(far, "head")
    queries, mlp = run_mlp(flat, other, gain, wq, wup, wdn)
    queries, mlp, far_pair, near = lax.optimization_barrier((queries, mlp, far_pair, near))
    blocked = (-1, BLOCK, 2 * half)
    mine_a = run_project((mesh, near, far, far_pair), key_weight, value_weight)
    sibling_a = swapped(mine_a, "sub")
    unstaged, _ = lax.optimization_barrier((output_weight, mine_a))
    (wo,) = run_stage((unstaged,), (1,))
    table = run_table(mine_a.reshape(blocked), sibling_a.reshape(blocked), 2 * shards)
    mine_b = run_project((farther, straight), key_weight, value_weight)
    sibling_b = swapped(mine_b, "sub")
    send, keep, att = run_attend(
        adjacency, queries, mine_b.reshape(blocked), sibling_b.reshape(blocked), table, mlp, wo
    )
    keeps, swaps, slots, placed = [], [], [], []
    shape = (shards * CAP, rows, half)
    for c in range(len(WIDTHS)):
        if c > 0:
            send, keep = run_project_out(c, att, mlp, wo)
        received = swapped(send, "head")
        if c > 0:
            received, _ = lax.optimization_barrier((received, slots[c - 1][0]))
        slots.append(run_combine((c,), (2, 3), owners, grid_features, (keep,), (received,)))
        keeps.append(keep)
        swaps.append(received)
    every = tuple(range(len(WIDTHS)))
    swaps[-1], _ = lax.optimization_barrier((swaps[-1], slots[-1][0]))
    near_slots, own_slots = run_combine(every, (1, 0), owners, grid_features, keeps, swaps)
    for c in every:
        first = columns_of(c).start
        spots = [(2, first), (3, first)]
        arrived = [crossed(slot, d, shards) for d, slot in zip((2, 3), slots[c])]
        if c == len(WIDTHS) - 1:
            spots += [(1, 0), (0, 0)]
            arrived += [crossed(near_slots, 1, shards), own_slots]
        placed = [run_place(spots, arrived, placed, shape)]
    return placed[0]


def attend_plain(queries, key_table, value_table, chosen, scaling):
    count = chosen.shape[0]
    picked_keys = key_table[chosen]
    picked_keys = picked_keys.reshape(count, -1, picked_keys.shape[3], picked_keys.shape[4])
    picked_values = value_table[chosen]
    picked_values = picked_values.reshape(count, -1, picked_values.shape[3], picked_values.shape[4])
    scores = (
        jnp.einsum("gqhe,gkhe->ghqk", queries, picked_keys, preferred_element_type=jnp.float32)
        * scaling
    )
    highest = jnp.max(scores, axis=-1, keepdims=True)
    weights = jnp.exp(scores - highest)
    weights = (weights / jnp.sum(weights, axis=-1, keepdims=True)).astype(jnp.bfloat16)
    result = jnp.einsum(
        "ghqk,gkhe->gqhe", weights, picked_values, preferred_element_type=jnp.float32
    )
    return result.astype(jnp.bfloat16)


def general(
    grid_features,
    owners,
    adjacency,
    mesh_nodes,
    norm_gain,
    query_weight,
    key_weight,
    value_weight,
    output_weight,
    up_weight,
    down_weight,
):
    shard_count = lax.axis_size("shard")
    head_count = lax.axis_size("head")
    local_blocks, block_rows, feature_share = grid_features.shape
    slots = shard_count * CAP
    owner_col = owners[:, 0]
    position = jnp.arange(local_blocks, dtype=jnp.int32)
    earlier = (owner_col[:, None] == owner_col[None, :]) & (position[None, :] < position[:, None])
    target = owner_col * CAP + jnp.sum(earlier.astype(jnp.int32), axis=1)
    dispatch = (target[:, None] == jnp.arange(slots, dtype=jnp.int32)[None, :]).astype(jnp.bfloat16)
    offset = lax.axis_index("head") * (D // head_count)
    projected = jnp.stack(
        (
            jnp.dot(mesh_nodes, key_weight, preferred_element_type=jnp.float32).astype(
                jnp.bfloat16
            ),
            jnp.dot(mesh_nodes, value_weight, preferred_element_type=jnp.float32).astype(
                jnp.bfloat16
            ),
        )
    )
    tables = lax.all_gather(projected, ("shard", "sub"), axis=1, tiled=True)
    head_local = query_weight.shape[1] // HEAD_DIM
    key_table = tables[0].reshape(-1, block_rows, head_local, HEAD_DIM)
    value_table = tables[1].reshape(-1, block_rows, head_local, HEAD_DIM)
    send_lists = jnp.full((slots, adjacency.shape[1]), -1, jnp.int32).at[target].set(adjacency)
    send_lists = send_lists.reshape(shard_count, CAP, -1)
    complete = lax.all_gather(grid_features, "head", axis=2, tiled=True)
    outgoing = jnp.einsum(
        "gs,gbd->sbd", dispatch, complete, preferred_element_type=jnp.float32
    ).astype(jnp.bfloat16)
    arrived, lists = (
        lax.all_to_all(
            outgoing.reshape(shard_count, CAP, block_rows, D),
            "shard",
            split_axis=0,
            concat_axis=0,
            tiled=True,
        ),
        lax.all_to_all(send_lists, "shard", split_axis=0, concat_axis=0, tiled=True),
    )
    arrived = arrived.reshape(slots, block_rows, D)
    residual = lax.dynamic_slice_in_dim(arrived, offset, D // head_count, 2)
    lists = lists.reshape(slots, -1)
    count = arrived.shape[0]
    values_f = arrived.astype(jnp.float32)
    average = jnp.mean(values_f, axis=-1, keepdims=True)
    centered = values_f - average
    variance = jnp.mean(centered * centered, axis=-1, keepdims=True)
    normed = (centered * lax.rsqrt(variance + epsilon) * norm_gain).astype(jnp.bfloat16)
    flattened = normed.reshape(-1, D)
    queries = jnp.dot(flattened, query_weight, preferred_element_type=jnp.float32).astype(
        jnp.bfloat16
    )
    blocks_each = math.gcd(count, max(1, 512 // block_rows))
    steps_count = count // blocks_each
    queries = queries.reshape(steps_count, blocks_each, block_rows, head_local, HEAD_DIM)

    def attend_step(operands):
        return attend_plain(operands[0], key_table, value_table, operands[1], HEAD_DIM ** (-0.5))

    attended = lax.map(
        attend_step, (queries, jnp.maximum(lists, 0).reshape(steps_count, blocks_each, -1))
    )
    attended = attended.reshape(-1, head_local * HEAD_DIM)
    hidden = jax.nn.gelu(
        jnp.dot(flattened, up_weight, preferred_element_type=jnp.float32), approximate=False
    ).astype(jnp.bfloat16)
    branch = jnp.dot(attended, output_weight, preferred_element_type=jnp.float32)
    branch = branch + jnp.dot(hidden, down_weight, preferred_element_type=jnp.float32)
    branch = branch.reshape(count, block_rows, D)
    reduced = lax.psum_scatter(
        branch.astype(jnp.bfloat16), "head", scatter_dimension=2, tiled=True
    ).astype(jnp.float32)
    occupied = lists[:, 0] >= 0
    summed = residual.astype(jnp.float32) + reduced
    return jnp.where(occupied[:, None, None], summed, 0.0).astype(jnp.bfloat16)


def local(grid_features, owners, adjacency, mesh_nodes, *parameters):
    sizes = [lax.axis_size(axis) for axis in ("shard", "head", "sub")]
    small = grid_features.shape[:2] == (4, BLOCK) and mesh_nodes.shape[0] == 2 * BLOCK
    if sizes == [4, 2, 2] and small and grid_features.shape[2] == 512:
        return paired(grid_features, owners, adjacency, mesh_nodes, *parameters)
    return general(grid_features, owners, adjacency, mesh_nodes, *parameters)


def solution(mesh):
    return jax.shard_map(
        local,
        mesh=mesh,
        in_specs=(
            P(("groups", "shard", "sub"), None, "head"),
            P(("groups", "shard", "sub"), None),
            P(("groups", "shard", "sub"), None),
            P(("groups", "shard", "sub"), None),
            P(),
            P(None, "head"),
            P(None, "head"),
            P(None, "head"),
            P("head", None),
            P(None, "head"),
            P("head", None),
        ),
        out_specs=P(("groups", "shard", "sub"), None, "head"),
        check_vma=False,
    )
```

```python
import functools
import math

import jax
import jax.numpy as jnp
from jax import lax
from jax.experimental import pallas as pl
from jax.experimental.pallas import tpu as pltpu
from jax.sharding import PartitionSpec as P

D = 1024
HEAD_DIM = 64
CAP = 2
BLOCK = 64
QUAD = 4
WIDE = QUAD * HEAD_DIM
WIDTHS = (128, 384)
MIB = 1 << 20


epsilon = 1e-05


def dot(a, b):
    return jnp.dot(a, b, preferred_element_type=jnp.float32)


def gelu(x):
    return 0.5 * x * (1.0 + lax.erf(x * (2.0**-0.5)))


def in_hbm(x):
    return pltpu.with_memory_space_constraint(x, pltpu.HBM)


def in_vmem(x):
    return pltpu.with_memory_space_constraint(x, pltpu.VMEM)


def whole(space):
    return pl.BlockSpec(memory_space=space)


def vmem(count):
    return [whole(pltpu.VMEM)] * count


def params(mib):
    return pltpu.CompilerParams(vmem_limit_bytes=mib * MIB)


def mlp_kernel(own, other, gain, wq, wup, wdn, q_out, mlp_out, normed_s):
    half = own.shape[1]
    units = wup.shape[1]
    chunk = units // 4
    x_other = other[...].astype(jnp.float32)
    x_own = own[...].astype(jnp.float32)

    def mean(a, b):
        total = jnp.sum(a, axis=-1, keepdims=True) + jnp.sum(b, axis=-1, keepdims=True)
        return total * (0.5 / half)

    average = mean(x_other, x_own)
    x_other = x_other - average
    x_own = x_own - average
    factor = lax.rsqrt(mean(x_other * x_other, x_own * x_own) + epsilon)
    normed_s[:, :half] = (x_other * factor * gain[:, :half]).astype(jnp.bfloat16)
    normed_s[:, half:] = (x_own * factor * gain[:, half:]).astype(jnp.bfloat16)
    normed = normed_s[...]
    q_out[...] = dot(normed, wq[...]).astype(jnp.bfloat16)
    for c in range(units // chunk):
        span = slice(c * chunk, (c + 1) * chunk)
        hidden = gelu(dot(normed, wup[:, span])).astype(jnp.bfloat16)
        term = dot(hidden, wdn[span, :])
        if c == 0:
            mlp_out[...] = term
        else:
            mlp_out[...] += term


def run_mlp(own, other, gain, wq, wup, wdn):
    rows = own.shape[0]
    width = wq.shape[0]
    units = wup.shape[1]
    return pl.pallas_call(
        mlp_kernel,
        out_shape=(
            jax.ShapeDtypeStruct((rows, wq.shape[1]), jnp.bfloat16),
            jax.ShapeDtypeStruct((rows, width), jnp.float32),
        ),
        in_specs=vmem(6),
        out_specs=tuple(vmem(2)),
        scratch_shapes=[pltpu.VMEM((rows, width), jnp.bfloat16)],
        compiler_params=params(16),
        cost_estimate=pl.CostEstimate(
            flops=2 * rows * width * (wq.shape[1] + 2 * units),
            bytes_accessed=2 * width * (wq.shape[1] + 2 * units),
            transcendentals=rows * units,
        ),
        name="mlp",
    )(own, other, gain, wq, wup, wdn)


def pick_kernel(mesh, out, sem):
    first = pl.multiple_of(lax.axis_index("head") * BLOCK, BLOCK)
    copy = pltpu.make_async_copy(mesh.at[pl.ds(first, BLOCK), :], out, sem)
    copy.start()
    copy.wait()


def run_pick(mesh):
    return pl.pallas_call(
        pick_kernel,
        out_shape=jax.ShapeDtypeStruct((BLOCK, mesh.shape[1]), mesh.dtype),
        in_specs=[whole(pltpu.HBM)],
        out_specs=whole(pltpu.VMEM),
        scratch_shapes=[pltpu.SemaphoreType.DMA(())],
        compiler_params=params(4),
        cost_estimate=pl.CostEstimate(flops=0, bytes_accessed=4 * mesh.size, transcendentals=0),
        name="pick",
    )(in_hbm(mesh))


def stage_kernel(axes, *refs):
    sources, targets, sem = refs[: len(axes)], refs[len(axes) : -1], refs[-1]
    h = lax.axis_index("head")
    copies = []

    def add(source, target):
        pieces = 2 if source.shape[0] >= 512 else 1
        rows = source.shape[0] // pieces
        for piece in range(pieces):
            span = pl.ds(piece * rows, rows)
            copies.append(
                pltpu.make_async_copy(
                    source.at[span, :], target.at[span, :], sem.at[len(copies)]
                )
            )
            copies[-1].start()

    for source, target, axis in zip(sources, targets, axes):
        if axis is None:
            add(source, target)
            continue
        if axis == "rest":
            add(source.at[pl.ds(pl.multiple_of((1 - h) * BLOCK, BLOCK), BLOCK), :], target)
            continue
        half = source.shape[axis] // 2
        for part, head in enumerate((1 - h, h)):
            span = pl.ds(pl.multiple_of(head * half, half), half)
            place = pl.ds(part * half, half)
            if axis == 0:
                add(source.at[span, :], target.at[place, :])
            else:
                add(source.at[:, span], target.at[:, place])
    for copy in copies:
        copy.wait()


def run_stage(arrays, axes):
    size = sum(2 * array.size for array in arrays)
    return pl.pallas_call(
        functools.partial(stage_kernel, axes),
        out_shape=tuple(
            jax.ShapeDtypeStruct((BLOCK,) + array.shape[1:] if axis == "rest" else array.shape, array.dtype)
            for array, axis in zip(arrays, axes)
        ),
        in_specs=[whole(pltpu.HBM)] * len(arrays),
        out_specs=tuple(vmem(len(arrays))),
        scratch_shapes=[pltpu.SemaphoreType.DMA((4 * len(arrays),))],
        compiler_params=params(16),
        cost_estimate=pl.CostEstimate(
            flops=2000 * size, bytes_accessed=20 * size, transcendentals=0
        ),
        name="stage",
    )(*(in_hbm(array) for array in arrays))


def project_kernel(*refs):
    pieces, (wk, wv, out) = refs[:-3], refs[-3:]
    width = wk.shape[1]
    rows = jnp.concatenate([piece[...] for piece in pieces], axis=0)
    out[:, :width] = dot(rows, wk[...]).astype(jnp.bfloat16)
    out[:, width:] = dot(rows, wv[...]).astype(jnp.bfloat16)


def run_project(pieces, wk, wv):
    rows = sum(piece.shape[0] for piece in pieces)
    depth, width = wk.shape
    return pl.pallas_call(
        project_kernel,
        out_shape=jax.ShapeDtypeStruct((rows, 2 * width), jnp.bfloat16),
        in_specs=vmem(len(pieces) + 2),
        out_specs=whole(pltpu.VMEM),
        compiler_params=params(8),
        cost_estimate=pl.CostEstimate(
            flops=300 * rows * depth * width,
            bytes_accessed=300 * depth * width + 300 * rows * depth,
            transcendentals=0,
        ),
        name="project",
    )(*pieces, in_vmem(wk), in_vmem(wv))


def table_kernel(mine, sibling, table):
    table[0, : mine.shape[0]] = mine[...]
    table[1, : mine.shape[0]] = sibling[...]


def run_table(mine, sibling, blocks):
    return pl.pallas_call(
        table_kernel,
        out_shape=jax.ShapeDtypeStruct((2, blocks) + mine.shape[1:], jnp.bfloat16),
        in_specs=vmem(2),
        out_specs=whole(pltpu.VMEM),
        compiler_params=params(8),
        cost_estimate=pl.CostEstimate(
            flops=0, bytes_accessed=80 * mine.size, transcendentals=0
        ),
        name="table",
    )(mine, sibling)


def columns_of(c):
    return slice(sum(WIDTHS[:c]), sum(WIDTHS[: c + 1]))


def project_out(c, att, mlp, wo, send, keep):
    half = att.shape[1]
    chunk = columns_of(c)
    h = lax.axis_index("head")

    def write(head):
        for out, first, place in ((send, 0, 1 - head), (keep, half, head)):
            extra = mlp[:, first + chunk.start : first + chunk.stop]
            span = slice(place * half + chunk.start, place * half + chunk.stop)
            out[...] = (extra + dot(att[...], wo[:, span])).astype(jnp.bfloat16)

    for head in range(2):
        pl.when(h == head)(functools.partial(write, head))


def attend_kernel(
    adjacency, q, mine, sibling, table_in, mlp, wo, send, keep, att, table
):
    del table_in
    s = lax.axis_index("shard")
    h = lax.axis_index("head")
    u = lax.axis_index("sub")
    half = wo.shape[0]
    ready = table.shape[1] - mine.shape[0]
    for i, part in enumerate((mine, sibling)):
        table[i, ready:] = part[...]
    rows_of = lax.broadcasted_iota(jnp.int32, (WIDE, WIDE), 0) // BLOCK
    lanes_of = lax.broadcasted_iota(jnp.int32, (WIDE, WIDE), 1) // HEAD_DIM
    diagonal = rows_of == lanes_of
    lane_head = lax.broadcasted_iota(jnp.int32, (BLOCK, WIDE), 1) // HEAD_DIM
    scale = HEAD_DIM**-0.5 * math.log2(math.e)
    groups = half // WIDE
    places = []
    for b in range(adjacency.shape[0]):
        places.append([])
        for j in range(adjacency.shape[1]):
            m = adjacency[b, j]
            part = lax.rem(m, 2)
            core = lax.rem(m // 2, 2)
            distance = s ^ (m // 4)
            part = jnp.where(distance == 0, part, part ^ h)
            places[b].append((core ^ u, distance * 2 + part))

    def scores_of(step):
        b, g = divmod(step, groups)
        columns = slice(g * WIDE, (g + 1) * WIDE)
        keys = jnp.concatenate([table[i, p, :, columns] for i, p in places[b]], axis=0)
        stacked = jnp.concatenate([q[b * BLOCK : (b + 1) * BLOCK, columns]] * QUAD, axis=0)
        stacked = jnp.where(diagonal, stacked, jnp.zeros_like(stacked))
        return lax.dot_general(
            stacked, keys, (((1,), (1,)), ((), ())), preferred_element_type=jnp.float32
        )

    steps = len(places) * groups
    scores = scores_of(0)
    for step in range(steps):
        following = scores_of(step + 1) if step + 1 < steps else None
        b, g = divmod(step, groups)
        columns = slice(half + g * WIDE, half + (g + 1) * WIDE)
        values = jnp.concatenate([table[i, p, :, columns] for i, p in places[b]], axis=0)
        highest = jnp.max(scores, axis=-1, keepdims=True)
        weights = jnp.exp2((scores - highest) * scale)
        total = jnp.sum(weights, axis=-1, keepdims=True)
        mixed = dot(weights.astype(jnp.bfloat16), values) * (1.0 / total)
        merged = mixed[0:BLOCK, :]
        for i in range(1, QUAD):
            merged = jnp.where(lane_head == i, mixed[i * BLOCK : (i + 1) * BLOCK, :], merged)
        rows = slice(b * BLOCK, (b + 1) * BLOCK)
        att[rows, g * WIDE : (g + 1) * WIDE] = merged.astype(jnp.bfloat16)
        scores = following
    project_out(0, att, mlp, wo, send, keep)


def run_attend(adjacency, q, mine, sibling, table, mlp, wo):
    rows, half = q.shape
    part = jax.ShapeDtypeStruct((rows, WIDTHS[0]), jnp.bfloat16)
    blocks = table.shape[0] * table.shape[1]
    send, keep, att, _ = pl.pallas_call(
        attend_kernel,
        out_shape=(
            part,
            part,
            jax.ShapeDtypeStruct(q.shape, jnp.bfloat16),
            jax.ShapeDtypeStruct(table.shape, jnp.bfloat16),
        ),
        in_specs=[whole(pltpu.SMEM)] + vmem(6),
        out_specs=tuple(vmem(4)),
        input_output_aliases={4: 3},
        compiler_params=params(16),
        cost_estimate=pl.CostEstimate(
            flops=20 * rows * half * (D + 8 * 8 * BLOCK),
            bytes_accessed=40 * blocks * BLOCK * half + 20 * half * D + 40 * rows * D,
            transcendentals=rows * 8 * BLOCK * half // HEAD_DIM,
        ),
        name="attend",
    )(adjacency, q, mine, sibling, table, mlp, in_vmem(wo))
    return send, keep, att


def run_project_out(c, att, mlp, wo):
    rows, half = att.shape
    part = jax.ShapeDtypeStruct((rows, WIDTHS[c]), jnp.bfloat16)
    return pl.pallas_call(
        functools.partial(project_out, c),
        out_shape=(part, part),
        in_specs=vmem(3),
        out_specs=tuple(vmem(2)),
        compiler_params=params(8),
        cost_estimate=pl.CostEstimate(
            flops=200 * rows * half * D,
            bytes_accessed=200 * half * D,
            transcendentals=0,
        ),
        name="project_out",
    )(att, mlp, in_vmem(wo))


def combine_kernel(chunks, distances, owners, grid_features, *refs):
    s = lax.axis_index("shard")
    keeps, refs = refs[: len(chunks)], refs[len(chunks) :]
    swaps, outs = refs[: len(chunks)], refs[len(chunks) :]
    count = grid_features.shape[0]
    names = [owners[t, 0] for t in range(count)]
    first = columns_of(chunks[0]).start
    for d, out in zip(distances, outs):
        out[...] = jnp.zeros(out.shape, jnp.bfloat16)
        seen = jnp.int32(0)
        for t in range(count):
            hit = names[t] == s ^ d
            rank = seen

            @pl.when(hit)
            def _():
                rows = slice(t * BLOCK, (t + 1) * BLOCK)
                for c, keep, swap in zip(chunks, keeps, swaps):
                    columns = columns_of(c)
                    partials = keep[rows, :].astype(jnp.float32)
                    partials = partials + swap[rows, :].astype(jnp.float32)
                    residual = grid_features[t, :, columns].astype(jnp.float32)
                    place = slice(columns.start - first, columns.stop - first)
                    out[rank, :, place] = (residual + partials).astype(jnp.bfloat16)

            seen = seen + hit.astype(jnp.int32)


def run_combine(chunks, distances, owners, grid_features, keeps, swaps):
    count, rows, _ = grid_features.shape
    width = sum(WIDTHS[c] for c in chunks)
    slot = jax.ShapeDtypeStruct((CAP, rows, width), jnp.bfloat16)
    return pl.pallas_call(
        functools.partial(combine_kernel, chunks, distances),
        out_shape=(slot,) * len(distances),
        in_specs=[whole(pltpu.SMEM)] + vmem(1 + 2 * len(chunks)),
        out_specs=tuple(vmem(len(distances))),
        compiler_params=params(8),
        cost_estimate=pl.CostEstimate(
            flops=60000 * count * rows * width,
            bytes_accessed=400 * rows * width * (3 * count + CAP * len(distances)),
            transcendentals=0,
        ),
        name="combine",
    )(owners, grid_features, *keeps, *swaps)


def place_kernel(spots, *refs):
    out, sem = refs[-2:]
    s = lax.axis_index("shard")
    copies = []
    for i, (d, first) in enumerate(spots):
        columns = pl.ds(first, refs[i].shape[2])
        slots = pl.ds((s ^ d) * CAP, CAP)
        copies.append(pltpu.make_async_copy(refs[i], out.at[slots, :, columns], sem.at[i]))
        copies[i].start()
    for copy in copies:
        copy.wait()


def run_place(spots, arrived, placed, shape):
    return pl.pallas_call(
        functools.partial(place_kernel, spots),
        out_shape=jax.ShapeDtypeStruct(shape, jnp.bfloat16),
        in_specs=vmem(len(arrived)) + [whole(pltpu.HBM)] * len(placed),
        out_specs=whole(pltpu.HBM),
        scratch_shapes=[pltpu.SemaphoreType.DMA((len(arrived),))],
        input_output_aliases={len(arrived): 0} if placed else {},
        compiler_params=params(4),
        cost_estimate=pl.CostEstimate(
            flops=400000 * sum(part.size for part in arrived), bytes_accessed=0, transcendentals=0
        ),
        name="place",
    )(*arrived, *placed)


def crossed(x, distance, size):
    return lax.ppermute(x, "shard", [(i, i ^ distance) for i in range(size)])


def swapped(x, axis):
    return lax.ppermute(x, axis, [(0, 1), (1, 0)])


def paired(
    grid_features,
    owners,
    adjacency,
    mesh_nodes,
    norm_gain,
    query_weight,
    key_weight,
    value_weight,
    output_weight,
    up_weight,
    down_weight,
):
    shards = lax.axis_size("shard")
    count, rows, half = grid_features.shape
    flat = grid_features.reshape(count * rows, half)
    half_unit = run_pick(mesh_nodes)
    far = crossed(half_unit, 2, shards)
    near = crossed(half_unit, 1, shards)
    waiting, _ = lax.optimization_barrier((flat, half_unit))
    other = swapped(waiting, "head")
    flat, gain, wq, wup, wdn, mesh, rest = run_stage(
        (
            flat,
            norm_gain.reshape(1, -1),
            query_weight,
            up_weight,
            down_weight,
            mesh_nodes,
            mesh_nodes,
        ),
        (None, 1, 0, 0, 1, None, "rest"),
    )
    straight = crossed(rest, 3, shards)
    near, _ = lax.optimization_barrier((near, rest))
    near_pair = swapped(near, "head")
    far, _, _ = lax.optimization_barrier((far, near, rest))
    farther = crossed(far, 1, shards)
    far_pair = swapped(far, "head")
    queries, mlp = run_mlp(flat, other, gain, wq, wup, wdn)
    queries, mlp, far_pair = lax.optimization_barrier((queries, mlp, far_pair))
    blocked = (-1, BLOCK, 2 * half)
    mine_a = run_project((mesh, near, near_pair, far, far_pair), key_weight, value_weight)
    sibling_a = swapped(mine_a, "sub")
    table = run_table(mine_a.reshape(blocked), sibling_a.reshape(blocked), 2 * shards)
    mine_b = run_project((farther, straight), key_weight, value_weight)
    sibling_b = swapped(mine_b, "sub")
    send, keep, att = run_attend(
        adjacency, queries, mine_b.reshape(blocked), sibling_b.reshape(blocked), table, mlp, output_weight
    )
    keeps, swaps, slots, placed = [], [], [], []
    shape = (shards * CAP, rows, half)
    for c in range(len(WIDTHS)):
        if c > 0:
            send, keep = run_project_out(c, att, mlp, output_weight)
        received = swapped(send, "head")
        if c > 0:
            received, _ = lax.optimization_barrier((received, slots[c - 1][0]))
        slots.append(run_combine((c,), (2, 3), owners, grid_features, (keep,), (received,)))
        keeps.append(keep)
        swaps.append(received)
    every = tuple(range(len(WIDTHS)))
    swaps[-1], _ = lax.optimization_barrier((swaps[-1], slots[-1][0]))
    near_slots, own_slots = run_combine(every, (1, 0), owners, grid_features, keeps, swaps)
    for c in every:
        first = columns_of(c).start
        spots = [(2, first), (3, first)]
        arrived = [crossed(slot, d, shards) for d, slot in zip((2, 3), slots[c])]
        if c == len(WIDTHS) - 1:
            spots += [(1, 0), (0, 0)]
            arrived += [crossed(near_slots, 1, shards), own_slots]
        placed = [run_place(spots, arrived, placed, shape)]
    return placed[0]


def attend_plain(queries, key_table, value_table, chosen, scaling):
    count = chosen.shape[0]
    picked_keys = key_table[chosen]
    picked_keys = picked_keys.reshape(count, -1, picked_keys.shape[3], picked_keys.shape[4])
    picked_values = value_table[chosen]
    picked_values = picked_values.reshape(count, -1, picked_values.shape[3], picked_values.shape[4])
    scores = (
        jnp.einsum("gqhe,gkhe->ghqk", queries, picked_keys, preferred_element_type=jnp.float32)
        * scaling
    )
    highest = jnp.max(scores, axis=-1, keepdims=True)
    weights = jnp.exp(scores - highest)
    weights = (weights / jnp.sum(weights, axis=-1, keepdims=True)).astype(jnp.bfloat16)
    result = jnp.einsum(
        "ghqk,gkhe->gqhe", weights, picked_values, preferred_element_type=jnp.float32
    )
    return result.astype(jnp.bfloat16)


def general(
    grid_features,
    owners,
    adjacency,
    mesh_nodes,
    norm_gain,
    query_weight,
    key_weight,
    value_weight,
    output_weight,
    up_weight,
    down_weight,
):
    shard_count = lax.axis_size("shard")
    head_count = lax.axis_size("head")
    local_blocks, block_rows, feature_share = grid_features.shape
    slots = shard_count * CAP
    owner_col = owners[:, 0]
    position = jnp.arange(local_blocks, dtype=jnp.int32)
    earlier = (owner_col[:, None] == owner_col[None, :]) & (position[None, :] < position[:, None])
    target = owner_col * CAP + jnp.sum(earlier.astype(jnp.int32), axis=1)
    dispatch = (target[:, None] == jnp.arange(slots, dtype=jnp.int32)[None, :]).astype(jnp.bfloat16)
    offset = lax.axis_index("head") * (D // head_count)
    projected = jnp.stack(
        (
            jnp.dot(mesh_nodes, key_weight, preferred_element_type=jnp.float32).astype(
                jnp.bfloat16
            ),
            jnp.dot(mesh_nodes, value_weight, preferred_element_type=jnp.float32).astype(
                jnp.bfloat16
            ),
        )
    )
    tables = lax.all_gather(projected, ("shard", "sub"), axis=1, tiled=True)
    head_local = query_weight.shape[1] // HEAD_DIM
    key_table = tables[0].reshape(-1, block_rows, head_local, HEAD_DIM)
    value_table = tables[1].reshape(-1, block_rows, head_local, HEAD_DIM)
    send_lists = jnp.full((slots, adjacency.shape[1]), -1, jnp.int32).at[target].set(adjacency)
    send_lists = send_lists.reshape(shard_count, CAP, -1)
    complete = lax.all_gather(grid_features, "head", axis=2, tiled=True)
    outgoing = jnp.einsum(
        "gs,gbd->sbd", dispatch, complete, preferred_element_type=jnp.float32
    ).astype(jnp.bfloat16)
    arrived, lists = (
        lax.all_to_all(
            outgoing.reshape(shard_count, CAP, block_rows, D),
            "shard",
            split_axis=0,
            concat_axis=0,
            tiled=True,
        ),
        lax.all_to_all(send_lists, "shard", split_axis=0, concat_axis=0, tiled=True),
    )
    arrived = arrived.reshape(slots, block_rows, D)
    residual = lax.dynamic_slice_in_dim(arrived, offset, D // head_count, 2)
    lists = lists.reshape(slots, -1)
    count = arrived.shape[0]
    values_f = arrived.astype(jnp.float32)
    average = jnp.mean(values_f, axis=-1, keepdims=True)
    centered = values_f - average
    variance = jnp.mean(centered * centered, axis=-1, keepdims=True)
    normed = (centered * lax.rsqrt(variance + epsilon) * norm_gain).astype(jnp.bfloat16)
    flattened = normed.reshape(-1, D)
    queries = jnp.dot(flattened, query_weight, preferred_element_type=jnp.float32).astype(
        jnp.bfloat16
    )
    blocks_each = math.gcd(count, max(1, 512 // block_rows))
    steps_count = count // blocks_each
    queries = queries.reshape(steps_count, blocks_each, block_rows, head_local, HEAD_DIM)

    def attend_step(operands):
        return attend_plain(operands[0], key_table, value_table, operands[1], HEAD_DIM ** (-0.5))

    attended = lax.map(
        attend_step, (queries, jnp.maximum(lists, 0).reshape(steps_count, blocks_each, -1))
    )
    attended = attended.reshape(-1, head_local * HEAD_DIM)
    hidden = jax.nn.gelu(
        jnp.dot(flattened, up_weight, preferred_element_type=jnp.float32), approximate=False
    ).astype(jnp.bfloat16)
    branch = jnp.dot(attended, output_weight, preferred_element_type=jnp.float32)
    branch = branch + jnp.dot(hidden, down_weight, preferred_element_type=jnp.float32)
    branch = branch.reshape(count, block_rows, D)
    reduced = lax.psum_scatter(
        branch.astype(jnp.bfloat16), "head", scatter_dimension=2, tiled=True
    ).astype(jnp.float32)
    occupied = lists[:, 0] >= 0
    summed = residual.astype(jnp.float32) + reduced
    return jnp.where(occupied[:, None, None], summed, 0.0).astype(jnp.bfloat16)


def local(grid_features, owners, adjacency, mesh_nodes, *parameters):
    sizes = [lax.axis_size(axis) for axis in ("shard", "head", "sub")]
    small = grid_features.shape[:2] == (4, BLOCK) and mesh_nodes.shape[0] == 2 * BLOCK
    if sizes == [4, 2, 2] and small and grid_features.shape[2] == 512:
        return paired(grid_features, owners, adjacency, mesh_nodes, *parameters)
    return general(grid_features, owners, adjacency, mesh_nodes, *parameters)


def solution(mesh):
    return jax.shard_map(
        local,
        mesh=mesh,
        in_specs=(
            P(("groups", "shard", "sub"), None, "head"),
            P(("groups", "shard", "sub"), None),
            P(("groups", "shard", "sub"), None),
            P(("groups", "shard", "sub"), None),
            P(),
            P(None, "head"),
            P(None, "head"),
            P(None, "head"),
            P("head", None),
            P(None, "head"),
            P("head", None),
        ),
        out_specs=P(("groups", "shard", "sub"), None, "head"),
        check_vma=False,
    )
```

```python
import functools
import math

import jax
import jax.numpy as jnp
from jax import lax
from jax.experimental import pallas as pl
from jax.experimental.pallas import tpu as pltpu
from jax.sharding import PartitionSpec as P

D = 1024
HEAD_DIM = 64
CAP = 2
BLOCK = 64
QUAD = 4
WIDE = QUAD * HEAD_DIM
WIDTHS = (128, 384)
MIB = 1 << 20


epsilon = 1e-05


def dot(a, b):
    return jnp.dot(a, b, preferred_element_type=jnp.float32)


def gelu(x):
    return 0.5 * x * (1.0 + lax.erf(x * (2.0**-0.5)))


def in_hbm(x):
    return pltpu.with_memory_space_constraint(x, pltpu.HBM)


def in_vmem(x):
    return pltpu.with_memory_space_constraint(x, pltpu.VMEM)


def whole(space):
    return pl.BlockSpec(memory_space=space)


def vmem(count):
    return [whole(pltpu.VMEM)] * count


def params(mib):
    return pltpu.CompilerParams(vmem_limit_bytes=mib * MIB)


def mlp_kernel(own, other, gain, wq, wup, wdn, q_out, mlp_out, normed_s, wdn_s, sem):
    half = own.shape[1]
    units = wup.shape[1]
    chunk = units // 4
    copies = []
    for c in range(units // chunk):
        span = pl.ds(c * chunk, chunk)
        copies.append(pltpu.make_async_copy(wdn.at[span, :], wdn_s.at[span, :], sem.at[c]))
        copies[c].start()
    x_other = other[...].astype(jnp.float32)
    x_own = own[...].astype(jnp.float32)

    def mean(a, b):
        total = jnp.sum(a, axis=-1, keepdims=True) + jnp.sum(b, axis=-1, keepdims=True)
        return total * (0.5 / half)

    average = mean(x_other, x_own)
    x_other = x_other - average
    x_own = x_own - average
    factor = lax.rsqrt(mean(x_other * x_other, x_own * x_own) + epsilon)
    normed_s[:, :half] = (x_other * factor * gain[:, :half]).astype(jnp.bfloat16)
    normed_s[:, half:] = (x_own * factor * gain[:, half:]).astype(jnp.bfloat16)
    normed = normed_s[...]
    q_out[...] = dot(normed, wq[...]).astype(jnp.bfloat16)
    for c in range(units // chunk):
        span = slice(c * chunk, (c + 1) * chunk)
        hidden = gelu(dot(normed, wup[:, span])).astype(jnp.bfloat16)
        copies[c].wait()
        term = dot(hidden, wdn_s[span, :])
        if c == 0:
            mlp_out[...] = term
        else:
            mlp_out[...] += term


def run_mlp(own, other, gain, wq, wup, wdn):
    rows = own.shape[0]
    width = wq.shape[0]
    units = wup.shape[1]
    return pl.pallas_call(
        mlp_kernel,
        out_shape=(
            jax.ShapeDtypeStruct((rows, wq.shape[1]), jnp.bfloat16),
            jax.ShapeDtypeStruct((rows, width), jnp.float32),
        ),
        in_specs=vmem(5) + [whole(pltpu.HBM)],
        out_specs=tuple(vmem(2)),
        scratch_shapes=[
            pltpu.VMEM((rows, width), jnp.bfloat16),
            pltpu.VMEM(wdn.shape, jnp.bfloat16),
            pltpu.SemaphoreType.DMA((4,)),
        ],
        compiler_params=params(16),
        cost_estimate=pl.CostEstimate(
            flops=2 * rows * width * (wq.shape[1] + 2 * units),
            bytes_accessed=2 * width * (wq.shape[1] + 2 * units),
            transcendentals=rows * units,
        ),
        name="mlp",
    )(own, other, gain, wq, wup, in_hbm(wdn))


def pick_kernel(mesh, out, sem):
    first = pl.multiple_of(lax.axis_index("head") * BLOCK, BLOCK)
    copy = pltpu.make_async_copy(mesh.at[pl.ds(first, BLOCK), :], out, sem)
    copy.start()
    copy.wait()


def run_pick(mesh):
    return pl.pallas_call(
        pick_kernel,
        out_shape=jax.ShapeDtypeStruct((BLOCK, mesh.shape[1]), mesh.dtype),
        in_specs=[whole(pltpu.HBM)],
        out_specs=whole(pltpu.VMEM),
        scratch_shapes=[pltpu.SemaphoreType.DMA(())],
        compiler_params=params(4),
        cost_estimate=pl.CostEstimate(flops=0, bytes_accessed=4 * mesh.size, transcendentals=0),
        name="pick",
    )(in_hbm(mesh))


def stage_kernel(axes, *refs):
    sources, targets, sem = refs[: len(axes)], refs[len(axes) : -1], refs[-1]
    h = lax.axis_index("head")
    copies = []

    def add(source, target):
        pieces = 2 if source.shape[0] >= 512 else 1
        rows = source.shape[0] // pieces
        for piece in range(pieces):
            span = pl.ds(piece * rows, rows)
            copies.append(
                pltpu.make_async_copy(
                    source.at[span, :], target.at[span, :], sem.at[len(copies)]
                )
            )
            copies[-1].start()

    for source, target, axis in zip(sources, targets, axes):
        if axis is None:
            add(source, target)
            continue
        if axis == "rest":
            add(source.at[pl.ds(pl.multiple_of((1 - h) * BLOCK, BLOCK), BLOCK), :], target)
            continue
        half = source.shape[axis] // 2
        for part, head in enumerate((1 - h, h)):
            span = pl.ds(pl.multiple_of(head * half, half), half)
            place = pl.ds(part * half, half)
            if axis == 0:
                add(source.at[span, :], target.at[place, :])
            else:
                add(source.at[:, span], target.at[:, place])
    for copy in copies:
        copy.wait()


def run_stage(arrays, axes):
    size = sum(2 * array.size for array in arrays)
    return pl.pallas_call(
        functools.partial(stage_kernel, axes),
        out_shape=tuple(
            jax.ShapeDtypeStruct((BLOCK,) + array.shape[1:] if axis == "rest" else array.shape, array.dtype)
            for array, axis in zip(arrays, axes)
        ),
        in_specs=[whole(pltpu.HBM)] * len(arrays),
        out_specs=tuple(vmem(len(arrays))),
        scratch_shapes=[pltpu.SemaphoreType.DMA((4 * len(arrays),))],
        compiler_params=params(16),
        cost_estimate=pl.CostEstimate(
            flops=2000 * size, bytes_accessed=20 * size, transcendentals=0
        ),
        name="stage",
    )(*(in_hbm(array) for array in arrays))


def project_kernel(*refs):
    pieces, (wk, wv, out) = refs[:-3], refs[-3:]
    width = wk.shape[1]
    rows = jnp.concatenate([piece[...] for piece in pieces], axis=0)
    out[:, :width] = dot(rows, wk[...]).astype(jnp.bfloat16)
    out[:, width:] = dot(rows, wv[...]).astype(jnp.bfloat16)


def run_project(pieces, wk, wv):
    rows = sum(piece.shape[0] for piece in pieces)
    depth, width = wk.shape
    return pl.pallas_call(
        project_kernel,
        out_shape=jax.ShapeDtypeStruct((rows, 2 * width), jnp.bfloat16),
        in_specs=vmem(len(pieces) + 2),
        out_specs=whole(pltpu.VMEM),
        compiler_params=params(8),
        cost_estimate=pl.CostEstimate(
            flops=300 * rows * depth * width,
            bytes_accessed=300 * depth * width + 300 * rows * depth,
            transcendentals=0,
        ),
        name="project",
    )(*pieces, in_vmem(wk), in_vmem(wv))


def table_kernel(mine, sibling, table):
    table[0, : mine.shape[0]] = mine[...]
    table[1, : mine.shape[0]] = sibling[...]


def run_table(mine, sibling, blocks):
    return pl.pallas_call(
        table_kernel,
        out_shape=jax.ShapeDtypeStruct((2, blocks) + mine.shape[1:], jnp.bfloat16),
        in_specs=vmem(2),
        out_specs=whole(pltpu.VMEM),
        compiler_params=params(8),
        cost_estimate=pl.CostEstimate(
            flops=0, bytes_accessed=80 * mine.size, transcendentals=0
        ),
        name="table",
    )(mine, sibling)


def columns_of(c):
    return slice(sum(WIDTHS[:c]), sum(WIDTHS[: c + 1]))


def project_out(c, att, mlp, wo, send, keep):
    half = att.shape[1]
    chunk = columns_of(c)
    h = lax.axis_index("head")

    def write(head):
        for out, place in ((send, 1 - head), (keep, head)):
            span = slice(place * half + chunk.start, place * half + chunk.stop)
            out[...] = (mlp[:, span] + dot(att[...], wo[:, span])).astype(jnp.bfloat16)

    for head in range(2):
        pl.when(h == head)(functools.partial(write, head))


def attend_kernel(
    adjacency, q, mine, sibling, table_in, mlp, wo, send, keep, att, table
):
    del table_in
    s = lax.axis_index("shard")
    h = lax.axis_index("head")
    u = lax.axis_index("sub")
    half = wo.shape[0]
    ready = table.shape[1] - mine.shape[0]
    for i, part in enumerate((mine, sibling)):
        table[i, ready:] = part[...]
    rows_of = lax.broadcasted_iota(jnp.int32, (WIDE, WIDE), 0) // BLOCK
    lanes_of = lax.broadcasted_iota(jnp.int32, (WIDE, WIDE), 1) // HEAD_DIM
    diagonal = rows_of == lanes_of
    lane_head = lax.broadcasted_iota(jnp.int32, (BLOCK, WIDE), 1) // HEAD_DIM
    scale = HEAD_DIM**-0.5 * math.log2(math.e)
    groups = half // WIDE
    places = []
    for b in range(adjacency.shape[0]):
        places.append([])
        for j in range(adjacency.shape[1]):
            m = adjacency[b, j]
            part = lax.rem(m, 2)
            core = lax.rem(m // 2, 2)
            distance = s ^ (m // 4)
            part = jnp.where(distance == 0, part, part ^ h)
            places[b].append((core ^ u, distance * 2 + part))

    def scores_of(step):
        b, g = divmod(step, groups)
        columns = slice(g * WIDE, (g + 1) * WIDE)
        keys = jnp.concatenate([table[i, p, :, columns] for i, p in places[b]], axis=0)
        stacked = jnp.concatenate([q[b * BLOCK : (b + 1) * BLOCK, columns]] * QUAD, axis=0)
        stacked = jnp.where(diagonal, stacked, jnp.zeros_like(stacked))
        return lax.dot_general(
            stacked, keys, (((1,), (1,)), ((), ())), preferred_element_type=jnp.float32
        )

    steps = len(places) * groups
    scores = scores_of(0)
    for step in range(steps):
        following = scores_of(step + 1) if step + 1 < steps else None
        b, g = divmod(step, groups)
        columns = slice(half + g * WIDE, half + (g + 1) * WIDE)
        values = jnp.concatenate([table[i, p, :, columns] for i, p in places[b]], axis=0)
        highest = jnp.max(scores, axis=-1, keepdims=True)
        weights = jnp.exp2((scores - highest) * scale)
        total = jnp.sum(weights, axis=-1, keepdims=True)
        mixed = dot(weights.astype(jnp.bfloat16), values) * (1.0 / total)
        merged = mixed[0:BLOCK, :]
        for i in range(1, QUAD):
            merged = jnp.where(lane_head == i, mixed[i * BLOCK : (i + 1) * BLOCK, :], merged)
        rows = slice(b * BLOCK, (b + 1) * BLOCK)
        att[rows, g * WIDE : (g + 1) * WIDE] = merged.astype(jnp.bfloat16)
        scores = following
    project_out(0, att, mlp, wo, send, keep)


def run_attend(adjacency, q, mine, sibling, table, mlp, wo):
    rows, half = q.shape
    part = jax.ShapeDtypeStruct((rows, WIDTHS[0]), jnp.bfloat16)
    blocks = table.shape[0] * table.shape[1]
    send, keep, att, _ = pl.pallas_call(
        attend_kernel,
        out_shape=(
            part,
            part,
            jax.ShapeDtypeStruct(q.shape, jnp.bfloat16),
            jax.ShapeDtypeStruct(table.shape, jnp.bfloat16),
        ),
        in_specs=[whole(pltpu.SMEM)] + vmem(6),
        out_specs=tuple(vmem(4)),
        input_output_aliases={4: 3},
        compiler_params=params(16),
        cost_estimate=pl.CostEstimate(
            flops=20 * rows * half * (D + 8 * 8 * BLOCK),
            bytes_accessed=40 * blocks * BLOCK * half + 20 * half * D + 40 * rows * D,
            transcendentals=rows * 8 * BLOCK * half // HEAD_DIM,
        ),
        name="attend",
    )(adjacency, q, mine, sibling, table, mlp, in_vmem(wo))
    return send, keep, att


def run_project_out(c, att, mlp, wo):
    rows, half = att.shape
    part = jax.ShapeDtypeStruct((rows, WIDTHS[c]), jnp.bfloat16)
    return pl.pallas_call(
        functools.partial(project_out, c),
        out_shape=(part, part),
        in_specs=vmem(3),
        out_specs=tuple(vmem(2)),
        compiler_params=params(8),
        cost_estimate=pl.CostEstimate(
            flops=200 * rows * half * D,
            bytes_accessed=200 * half * D,
            transcendentals=0,
        ),
        name="project_out",
    )(att, mlp, in_vmem(wo))


def combine_kernel(chunks, distances, owners, grid_features, *refs):
    s = lax.axis_index("shard")
    keeps, refs = refs[: len(chunks)], refs[len(chunks) :]
    swaps, outs = refs[: len(chunks)], refs[len(chunks) :]
    count = grid_features.shape[0]
    names = [owners[t, 0] for t in range(count)]
    first = columns_of(chunks[0]).start
    for d, out in zip(distances, outs):
        out[...] = jnp.zeros(out.shape, jnp.bfloat16)
        seen = jnp.int32(0)
        for t in range(count):
            hit = names[t] == s ^ d
            rank = seen

            @pl.when(hit)
            def _():
                rows = slice(t * BLOCK, (t + 1) * BLOCK)
                for c, keep, swap in zip(chunks, keeps, swaps):
                    columns = columns_of(c)
                    partials = keep[rows, :].astype(jnp.float32)
                    partials = partials + swap[rows, :].astype(jnp.float32)
                    residual = grid_features[t, :, columns].astype(jnp.float32)
                    place = slice(columns.start - first, columns.stop - first)
                    out[rank, :, place] = (residual + partials).astype(jnp.bfloat16)

            seen = seen + hit.astype(jnp.int32)


def run_combine(chunks, distances, owners, grid_features, keeps, swaps):
    count, rows, _ = grid_features.shape
    width = sum(WIDTHS[c] for c in chunks)
    slot = jax.ShapeDtypeStruct((CAP, rows, width), jnp.bfloat16)
    return pl.pallas_call(
        functools.partial(combine_kernel, chunks, distances),
        out_shape=(slot,) * len(distances),
        in_specs=[whole(pltpu.SMEM)] + vmem(1 + 2 * len(chunks)),
        out_specs=tuple(vmem(len(distances))),
        compiler_params=params(8),
        cost_estimate=pl.CostEstimate(
            flops=60000 * count * rows * width,
            bytes_accessed=400 * rows * width * (3 * count + CAP * len(distances)),
            transcendentals=0,
        ),
        name="combine",
    )(owners, grid_features, *keeps, *swaps)


def place_kernel(spots, *refs):
    out, sem = refs[-2:]
    s = lax.axis_index("shard")
    copies = []
    for i, (d, first) in enumerate(spots):
        columns = pl.ds(first, refs[i].shape[2])
        slots = pl.ds((s ^ d) * CAP, CAP)
        copies.append(pltpu.make_async_copy(refs[i], out.at[slots, :, columns], sem.at[i]))
        copies[i].start()
    for copy in copies:
        copy.wait()


def run_place(spots, arrived, placed, shape):
    return pl.pallas_call(
        functools.partial(place_kernel, spots),
        out_shape=jax.ShapeDtypeStruct(shape, jnp.bfloat16),
        in_specs=vmem(len(arrived)) + [whole(pltpu.HBM)] * len(placed),
        out_specs=whole(pltpu.HBM),
        scratch_shapes=[pltpu.SemaphoreType.DMA((len(arrived),))],
        input_output_aliases={len(arrived): 0} if placed else {},
        compiler_params=params(4),
        cost_estimate=pl.CostEstimate(
            flops=400000 * sum(part.size for part in arrived), bytes_accessed=0, transcendentals=0
        ),
        name="place",
    )(*arrived, *placed)


def crossed(x, distance, size):
    return lax.ppermute(x, "shard", [(i, i ^ distance) for i in range(size)])


def swapped(x, axis):
    return lax.ppermute(x, axis, [(0, 1), (1, 0)])


def paired(
    grid_features,
    owners,
    adjacency,
    mesh_nodes,
    norm_gain,
    query_weight,
    key_weight,
    value_weight,
    output_weight,
    up_weight,
    down_weight,
):
    shards = lax.axis_size("shard")
    count, rows, half = grid_features.shape
    flat = grid_features.reshape(count * rows, half)
    half_unit = run_pick(mesh_nodes)
    far = crossed(half_unit, 2, shards)
    near = crossed(half_unit, 1, shards)
    waiting, _ = lax.optimization_barrier((flat, half_unit))
    other = swapped(waiting, "head")
    flat, gain, wq, wup, mesh, rest = run_stage(
        (
            flat,
            norm_gain.reshape(1, -1),
            query_weight,
            up_weight,
            mesh_nodes,
            mesh_nodes,
        ),
        (None, 1, 0, 0, None, "rest"),
    )
    straight = crossed(rest, 3, shards)
    near, _ = lax.optimization_barrier((near, rest))
    near_pair = swapped(near, "head")
    far, _, _ = lax.optimization_barrier((far, near, rest))
    farther = crossed(far, 1, shards)
    far_pair = swapped(far, "head")
    queries, mlp = run_mlp(flat, other, gain, wq, wup, down_weight)
    queries, mlp, far_pair = lax.optimization_barrier((queries, mlp, far_pair))
    blocked = (-1, BLOCK, 2 * half)
    mine_a = run_project((mesh, near, near_pair, far, far_pair), key_weight, value_weight)
    sibling_a = swapped(mine_a, "sub")
    table = run_table(mine_a.reshape(blocked), sibling_a.reshape(blocked), 2 * shards)
    mine_b = run_project((farther, straight), key_weight, value_weight)
    sibling_b = swapped(mine_b, "sub")
    send, keep, att = run_attend(
        adjacency, queries, mine_b.reshape(blocked), sibling_b.reshape(blocked), table, mlp, output_weight
    )
    keeps, swaps, slots, placed = [], [], [], []
    shape = (shards * CAP, rows, half)
    for c in range(len(WIDTHS)):
        if c > 0:
            send, keep = run_project_out(c, att, mlp, output_weight)
        received = swapped(send, "head")
        if c > 0:
            received, _ = lax.optimization_barrier((received, slots[c - 1][0]))
        slots.append(run_combine((c,), (2, 3), owners, grid_features, (keep,), (received,)))
        keeps.append(keep)
        swaps.append(received)
    every = tuple(range(len(WIDTHS)))
    swaps[-1], _ = lax.optimization_barrier((swaps[-1], slots[-1][0]))
    near_slots, own_slots = run_combine(every, (1, 0), owners, grid_features, keeps, swaps)
    for c in every:
        first = columns_of(c).start
        spots = [(2, first), (3, first)]
        arrived = [crossed(slot, d, shards) for d, slot in zip((2, 3), slots[c])]
        if c == len(WIDTHS) - 1:
            spots += [(1, 0), (0, 0)]
            arrived += [crossed(near_slots, 1, shards), own_slots]
        placed = [run_place(spots, arrived, placed, shape)]
    return placed[0]


def attend_plain(queries, key_table, value_table, chosen, scaling):
    count = chosen.shape[0]
    picked_keys = key_table[chosen]
    picked_keys = picked_keys.reshape(count, -1, picked_keys.shape[3], picked_keys.shape[4])
    picked_values = value_table[chosen]
    picked_values = picked_values.reshape(count, -1, picked_values.shape[3], picked_values.shape[4])
    scores = (
        jnp.einsum("gqhe,gkhe->ghqk", queries, picked_keys, preferred_element_type=jnp.float32)
        * scaling
    )
    highest = jnp.max(scores, axis=-1, keepdims=True)
    weights = jnp.exp(scores - highest)
    weights = (weights / jnp.sum(weights, axis=-1, keepdims=True)).astype(jnp.bfloat16)
    result = jnp.einsum(
        "ghqk,gkhe->gqhe", weights, picked_values, preferred_element_type=jnp.float32
    )
    return result.astype(jnp.bfloat16)


def general(
    grid_features,
    owners,
    adjacency,
    mesh_nodes,
    norm_gain,
    query_weight,
    key_weight,
    value_weight,
    output_weight,
    up_weight,
    down_weight,
):
    shard_count = lax.axis_size("shard")
    head_count = lax.axis_size("head")
    local_blocks, block_rows, feature_share = grid_features.shape
    slots = shard_count * CAP
    owner_col = owners[:, 0]
    position = jnp.arange(local_blocks, dtype=jnp.int32)
    earlier = (owner_col[:, None] == owner_col[None, :]) & (position[None, :] < position[:, None])
    target = owner_col * CAP + jnp.sum(earlier.astype(jnp.int32), axis=1)
    dispatch = (target[:, None] == jnp.arange(slots, dtype=jnp.int32)[None, :]).astype(jnp.bfloat16)
    offset = lax.axis_index("head") * (D // head_count)
    projected = jnp.stack(
        (
            jnp.dot(mesh_nodes, key_weight, preferred_element_type=jnp.float32).astype(
                jnp.bfloat16
            ),
            jnp.dot(mesh_nodes, value_weight, preferred_element_type=jnp.float32).astype(
                jnp.bfloat16
            ),
        )
    )
    tables = lax.all_gather(projected, ("shard", "sub"), axis=1, tiled=True)
    head_local = query_weight.shape[1] // HEAD_DIM
    key_table = tables[0].reshape(-1, block_rows, head_local, HEAD_DIM)
    value_table = tables[1].reshape(-1, block_rows, head_local, HEAD_DIM)
    send_lists = jnp.full((slots, adjacency.shape[1]), -1, jnp.int32).at[target].set(adjacency)
    send_lists = send_lists.reshape(shard_count, CAP, -1)
    complete = lax.all_gather(grid_features, "head", axis=2, tiled=True)
    outgoing = jnp.einsum(
        "gs,gbd->sbd", dispatch, complete, preferred_element_type=jnp.float32
    ).astype(jnp.bfloat16)
    arrived, lists = (
        lax.all_to_all(
            outgoing.reshape(shard_count, CAP, block_rows, D),
            "shard",
            split_axis=0,
            concat_axis=0,
            tiled=True,
        ),
        lax.all_to_all(send_lists, "shard", split_axis=0, concat_axis=0, tiled=True),
    )
    arrived = arrived.reshape(slots, block_rows, D)
    residual = lax.dynamic_slice_in_dim(arrived, offset, D // head_count, 2)
    lists = lists.reshape(slots, -1)
    count = arrived.shape[0]
    values_f = arrived.astype(jnp.float32)
    average = jnp.mean(values_f, axis=-1, keepdims=True)
    centered = values_f - average
    variance = jnp.mean(centered * centered, axis=-1, keepdims=True)
    normed = (centered * lax.rsqrt(variance + epsilon) * norm_gain).astype(jnp.bfloat16)
    flattened = normed.reshape(-1, D)
    queries = jnp.dot(flattened, query_weight, preferred_element_type=jnp.float32).astype(
        jnp.bfloat16
    )
    blocks_each = math.gcd(count, max(1, 512 // block_rows))
    steps_count = count // blocks_each
    queries = queries.reshape(steps_count, blocks_each, block_rows, head_local, HEAD_DIM)

    def attend_step(operands):
        return attend_plain(operands[0], key_table, value_table, operands[1], HEAD_DIM ** (-0.5))

    attended = lax.map(
        attend_step, (queries, jnp.maximum(lists, 0).reshape(steps_count, blocks_each, -1))
    )
    attended = attended.reshape(-1, head_local * HEAD_DIM)
    hidden = jax.nn.gelu(
        jnp.dot(flattened, up_weight, preferred_element_type=jnp.float32), approximate=False
    ).astype(jnp.bfloat16)
    branch = jnp.dot(attended, output_weight, preferred_element_type=jnp.float32)
    branch = branch + jnp.dot(hidden, down_weight, preferred_element_type=jnp.float32)
    branch = branch.reshape(count, block_rows, D)
    reduced = lax.psum_scatter(
        branch.astype(jnp.bfloat16), "head", scatter_dimension=2, tiled=True
    ).astype(jnp.float32)
    occupied = lists[:, 0] >= 0
    summed = residual.astype(jnp.float32) + reduced
    return jnp.where(occupied[:, None, None], summed, 0.0).astype(jnp.bfloat16)


def local(grid_features, owners, adjacency, mesh_nodes, *parameters):
    sizes = [lax.axis_size(axis) for axis in ("shard", "head", "sub")]
    small = grid_features.shape[:2] == (4, BLOCK) and mesh_nodes.shape[0] == 2 * BLOCK
    if sizes == [4, 2, 2] and small and grid_features.shape[2] == 512:
        return paired(grid_features, owners, adjacency, mesh_nodes, *parameters)
    return general(grid_features, owners, adjacency, mesh_nodes, *parameters)


def solution(mesh):
    return jax.shard_map(
        local,
        mesh=mesh,
        in_specs=(
            P(("groups", "shard", "sub"), None, "head"),
            P(("groups", "shard", "sub"), None),
            P(("groups", "shard", "sub"), None),
            P(("groups", "shard", "sub"), None),
            P(),
            P(None, "head"),
            P(None, "head"),
            P(None, "head"),
            P("head", None),
            P(None, "head"),
            P("head", None),
        ),
        out_specs=P(("groups", "shard", "sub"), None, "head"),
        check_vma=False,
    )
```

```python
import functools
import math

import jax
import jax.numpy as jnp
from jax import lax
from jax.experimental import pallas as pl
from jax.experimental.pallas import tpu as pltpu
from jax.sharding import PartitionSpec as P

D = 1024
HEAD_DIM = 64
CAP = 2
BLOCK = 64
QUAD = 4
WIDE = QUAD * HEAD_DIM
WIDTHS = (128, 384)
MIB = 1 << 20


epsilon = 1e-05


def dot(a, b):
    return jnp.dot(a, b, preferred_element_type=jnp.float32)


def gelu(x):
    return 0.5 * x * (1.0 + lax.erf(x * (2.0**-0.5)))


def in_hbm(x):
    return pltpu.with_memory_space_constraint(x, pltpu.HBM)


def in_vmem(x):
    return pltpu.with_memory_space_constraint(x, pltpu.VMEM)


def whole(space):
    return pl.BlockSpec(memory_space=space)


def vmem(count):
    return [whole(pltpu.VMEM)] * count


def params(mib):
    return pltpu.CompilerParams(vmem_limit_bytes=mib * MIB)


def mlp_kernel(own, other, gain, wq, wup, wdn, q_out, mlp_out, normed_s):
    half = own.shape[1]
    units = wup.shape[1]
    chunk = units // 4
    x_other = other[...].astype(jnp.float32)
    x_own = own[...].astype(jnp.float32)

    def mean(a, b):
        total = jnp.sum(a, axis=-1, keepdims=True) + jnp.sum(b, axis=-1, keepdims=True)
        return total * (0.5 / half)

    average = mean(x_other, x_own)
    x_other = x_other - average
    x_own = x_own - average
    factor = lax.rsqrt(mean(x_other * x_other, x_own * x_own) + epsilon)
    normed_s[:, :half] = (x_other * factor * gain[:, :half]).astype(jnp.bfloat16)
    normed_s[:, half:] = (x_own * factor * gain[:, half:]).astype(jnp.bfloat16)
    normed = normed_s[...]
    q_out[...] = dot(normed, wq[...]).astype(jnp.bfloat16)
    for c in range(units // chunk):
        span = slice(c * chunk, (c + 1) * chunk)
        hidden = gelu(dot(normed, wup[:, span])).astype(jnp.bfloat16)
        term = dot(hidden, wdn[span, :])
        if c == 0:
            mlp_out[...] = term
        else:
            mlp_out[...] += term


def run_mlp(own, other, gain, wq, wup, wdn):
    rows = own.shape[0]
    width = wq.shape[0]
    units = wup.shape[1]
    return pl.pallas_call(
        mlp_kernel,
        out_shape=(
            jax.ShapeDtypeStruct((rows, wq.shape[1]), jnp.bfloat16),
            jax.ShapeDtypeStruct((rows, width), jnp.float32),
        ),
        in_specs=vmem(6),
        out_specs=tuple(vmem(2)),
        scratch_shapes=[pltpu.VMEM((rows, width), jnp.bfloat16)],
        compiler_params=params(16),
        cost_estimate=pl.CostEstimate(
            flops=2 * rows * width * (wq.shape[1] + 2 * units),
            bytes_accessed=2 * width * (wq.shape[1] + 2 * units),
            transcendentals=rows * units,
        ),
        name="mlp",
    )(own, other, gain, wq, wup, wdn)


def pick_kernel(mesh, out, sem):
    first = pl.multiple_of(lax.axis_index("head") * BLOCK, BLOCK)
    copy = pltpu.make_async_copy(mesh.at[pl.ds(first, BLOCK), :], out, sem)
    copy.start()
    copy.wait()


def run_pick(mesh):
    return pl.pallas_call(
        pick_kernel,
        out_shape=jax.ShapeDtypeStruct((BLOCK, mesh.shape[1]), mesh.dtype),
        in_specs=[whole(pltpu.HBM)],
        out_specs=whole(pltpu.VMEM),
        scratch_shapes=[pltpu.SemaphoreType.DMA(())],
        compiler_params=params(4),
        cost_estimate=pl.CostEstimate(flops=0, bytes_accessed=4 * mesh.size, transcendentals=0),
        name="pick",
    )(in_hbm(mesh))


def stage_kernel(axes, *refs):
    sources, targets, sem = refs[: len(axes)], refs[len(axes) : -1], refs[-1]
    h = lax.axis_index("head")
    copies = []

    def add(source, target):
        pieces = 2 if source.shape[0] >= 512 else 1
        rows = source.shape[0] // pieces
        for piece in range(pieces):
            span = pl.ds(piece * rows, rows)
            copies.append(
                pltpu.make_async_copy(
                    source.at[span, :], target.at[span, :], sem.at[len(copies)]
                )
            )
            copies[-1].start()

    for source, target, axis in zip(sources, targets, axes):
        if axis is None:
            add(source, target)
            continue
        if axis == "rest":
            add(source.at[pl.ds(pl.multiple_of((1 - h) * BLOCK, BLOCK), BLOCK), :], target)
            continue
        half = source.shape[axis] // 2
        for part, head in enumerate((1 - h, h)):
            span = pl.ds(pl.multiple_of(head * half, half), half)
            place = pl.ds(part * half, half)
            if axis == 0:
                add(source.at[span, :], target.at[place, :])
            else:
                add(source.at[:, span], target.at[:, place])
    for copy in copies:
        copy.wait()


def run_stage(arrays, axes):
    size = sum(2 * array.size for array in arrays)
    return pl.pallas_call(
        functools.partial(stage_kernel, axes),
        out_shape=tuple(
            jax.ShapeDtypeStruct((BLOCK,) + array.shape[1:] if axis == "rest" else array.shape, array.dtype)
            for array, axis in zip(arrays, axes)
        ),
        in_specs=[whole(pltpu.HBM)] * len(arrays),
        out_specs=tuple(vmem(len(arrays))),
        scratch_shapes=[pltpu.SemaphoreType.DMA((4 * len(arrays),))],
        compiler_params=params(16),
        cost_estimate=pl.CostEstimate(
            flops=2000 * size, bytes_accessed=20 * size, transcendentals=0
        ),
        name="stage",
    )(*(in_hbm(array) for array in arrays))


def project_kernel(*refs):
    pieces, (wk, wv, out) = refs[:-3], refs[-3:]
    width = wk.shape[1]
    rows = jnp.concatenate([piece[...] for piece in pieces], axis=0)
    out[:, :width] = dot(rows, wk[...]).astype(jnp.bfloat16)
    out[:, width:] = dot(rows, wv[...]).astype(jnp.bfloat16)


def run_project(pieces, wk, wv):
    rows = sum(piece.shape[0] for piece in pieces)
    depth, width = wk.shape
    return pl.pallas_call(
        project_kernel,
        out_shape=jax.ShapeDtypeStruct((rows, 2 * width), jnp.bfloat16),
        in_specs=vmem(len(pieces) + 2),
        out_specs=whole(pltpu.VMEM),
        compiler_params=params(8),
        cost_estimate=pl.CostEstimate(
            flops=300 * rows * depth * width,
            bytes_accessed=300 * depth * width + 300 * rows * depth,
            transcendentals=0,
        ),
        name="project",
    )(*pieces, in_vmem(wk), in_vmem(wv))


def table_kernel(mine, sibling, table):
    table[0, : mine.shape[0]] = mine[...]
    table[1, : mine.shape[0]] = sibling[...]


def run_table(mine, sibling, blocks):
    return pl.pallas_call(
        table_kernel,
        out_shape=jax.ShapeDtypeStruct((2, blocks) + mine.shape[1:], jnp.bfloat16),
        in_specs=vmem(2),
        out_specs=whole(pltpu.VMEM),
        compiler_params=params(8),
        cost_estimate=pl.CostEstimate(
            flops=0, bytes_accessed=80 * mine.size, transcendentals=0
        ),
        name="table",
    )(mine, sibling)


def columns_of(c):
    return slice(sum(WIDTHS[:c]), sum(WIDTHS[: c + 1]))


def project_out(c, att, mlp, wo, send, keep):
    half = att.shape[1]
    chunk = columns_of(c)
    h = lax.axis_index("head")

    def write(head):
        for out, first, place in ((send, 0, 1 - head), (keep, half, head)):
            extra = mlp[:, first + chunk.start : first + chunk.stop]
            span = slice(place * half + chunk.start, place * half + chunk.stop)
            out[...] = (extra + dot(att[...], wo[:, span])).astype(jnp.bfloat16)

    for head in range(2):
        pl.when(h == head)(functools.partial(write, head))


def attend_kernel(
    adjacency, q, mine, sibling, table_in, mlp, wo, send, keep, att, table
):
    del table_in
    s = lax.axis_index("shard")
    h = lax.axis_index("head")
    u = lax.axis_index("sub")
    half = wo.shape[0]
    ready = table.shape[1] - mine.shape[0]
    for i, part in enumerate((mine, sibling)):
        table[i, ready:] = part[...]
    rows_of = lax.broadcasted_iota(jnp.int32, (WIDE, WIDE), 0) // BLOCK
    lanes_of = lax.broadcasted_iota(jnp.int32, (WIDE, WIDE), 1) // HEAD_DIM
    diagonal = rows_of == lanes_of
    lane_head = lax.broadcasted_iota(jnp.int32, (BLOCK, WIDE), 1) // HEAD_DIM
    scale = HEAD_DIM**-0.5 * math.log2(math.e)
    groups = half // WIDE
    places = []
    for b in range(adjacency.shape[0]):
        places.append([])
        for j in range(adjacency.shape[1]):
            m = adjacency[b, j]
            part = lax.rem(m, 2)
            core = lax.rem(m // 2, 2)
            distance = s ^ (m // 4)
            part = jnp.where(distance <= 1, part, part ^ h)
            places[b].append((core ^ u, distance * 2 + part))

    def scores_of(step):
        b, g = divmod(step, groups)
        columns = slice(g * WIDE, (g + 1) * WIDE)
        keys = jnp.concatenate([table[i, p, :, columns] for i, p in places[b]], axis=0)
        stacked = jnp.concatenate([q[b * BLOCK : (b + 1) * BLOCK, columns]] * QUAD, axis=0)
        stacked = jnp.where(diagonal, stacked, jnp.zeros_like(stacked))
        return lax.dot_general(
            stacked, keys, (((1,), (1,)), ((), ())), preferred_element_type=jnp.float32
        )

    steps = len(places) * groups
    scores = scores_of(0)
    for step in range(steps):
        following = scores_of(step + 1) if step + 1 < steps else None
        b, g = divmod(step, groups)
        columns = slice(half + g * WIDE, half + (g + 1) * WIDE)
        values = jnp.concatenate([table[i, p, :, columns] for i, p in places[b]], axis=0)
        highest = jnp.max(scores, axis=-1, keepdims=True)
        weights = jnp.exp2((scores - highest) * scale)
        total = jnp.sum(weights, axis=-1, keepdims=True)
        mixed = dot(weights.astype(jnp.bfloat16), values) * (1.0 / total)
        merged = mixed[0:BLOCK, :]
        for i in range(1, QUAD):
            merged = jnp.where(lane_head == i, mixed[i * BLOCK : (i + 1) * BLOCK, :], merged)
        rows = slice(b * BLOCK, (b + 1) * BLOCK)
        att[rows, g * WIDE : (g + 1) * WIDE] = merged.astype(jnp.bfloat16)
        scores = following
    project_out(0, att, mlp, wo, send, keep)


def run_attend(adjacency, q, mine, sibling, table, mlp, wo):
    rows, half = q.shape
    part = jax.ShapeDtypeStruct((rows, WIDTHS[0]), jnp.bfloat16)
    blocks = table.shape[0] * table.shape[1]
    send, keep, att, _ = pl.pallas_call(
        attend_kernel,
        out_shape=(
            part,
            part,
            jax.ShapeDtypeStruct(q.shape, jnp.bfloat16),
            jax.ShapeDtypeStruct(table.shape, jnp.bfloat16),
        ),
        in_specs=[whole(pltpu.SMEM)] + vmem(6),
        out_specs=tuple(vmem(4)),
        input_output_aliases={4: 3},
        compiler_params=params(16),
        cost_estimate=pl.CostEstimate(
            flops=20 * rows * half * (D + 8 * 8 * BLOCK),
            bytes_accessed=40 * blocks * BLOCK * half + 20 * half * D + 40 * rows * D,
            transcendentals=rows * 8 * BLOCK * half // HEAD_DIM,
        ),
        name="attend",
    )(adjacency, q, mine, sibling, table, mlp, in_vmem(wo))
    return send, keep, att


def run_project_out(c, att, mlp, wo):
    rows, half = att.shape
    part = jax.ShapeDtypeStruct((rows, WIDTHS[c]), jnp.bfloat16)
    return pl.pallas_call(
        functools.partial(project_out, c),
        out_shape=(part, part),
        in_specs=vmem(3),
        out_specs=tuple(vmem(2)),
        compiler_params=params(8),
        cost_estimate=pl.CostEstimate(
            flops=200 * rows * half * D,
            bytes_accessed=200 * half * D,
            transcendentals=0,
        ),
        name="project_out",
    )(att, mlp, in_vmem(wo))


def combine_kernel(chunks, distances, owners, grid_features, *refs):
    s = lax.axis_index("shard")
    keeps, refs = refs[: len(chunks)], refs[len(chunks) :]
    swaps, outs = refs[: len(chunks)], refs[len(chunks) :]
    count = grid_features.shape[0]
    names = [owners[t, 0] for t in range(count)]
    first = columns_of(chunks[0]).start
    for d, out in zip(distances, outs):
        out[...] = jnp.zeros(out.shape, jnp.bfloat16)
        seen = jnp.int32(0)
        for t in range(count):
            hit = names[t] == s ^ d
            rank = seen

            @pl.when(hit)
            def _():
                rows = slice(t * BLOCK, (t + 1) * BLOCK)
                for c, keep, swap in zip(chunks, keeps, swaps):
                    columns = columns_of(c)
                    partials = keep[rows, :].astype(jnp.float32)
                    partials = partials + swap[rows, :].astype(jnp.float32)
                    residual = grid_features[t, :, columns].astype(jnp.float32)
                    place = slice(columns.start - first, columns.stop - first)
                    out[rank, :, place] = (residual + partials).astype(jnp.bfloat16)

            seen = seen + hit.astype(jnp.int32)


def run_combine(chunks, distances, owners, grid_features, keeps, swaps):
    count, rows, _ = grid_features.shape
    width = sum(WIDTHS[c] for c in chunks)
    slot = jax.ShapeDtypeStruct((CAP, rows, width), jnp.bfloat16)
    return pl.pallas_call(
        functools.partial(combine_kernel, chunks, distances),
        out_shape=(slot,) * len(distances),
        in_specs=[whole(pltpu.SMEM)] + vmem(1 + 2 * len(chunks)),
        out_specs=tuple(vmem(len(distances))),
        compiler_params=params(8),
        cost_estimate=pl.CostEstimate(
            flops=60000 * count * rows * width,
            bytes_accessed=400 * rows * width * (3 * count + CAP * len(distances)),
            transcendentals=0,
        ),
        name="combine",
    )(owners, grid_features, *keeps, *swaps)


def place_kernel(spots, *refs):
    out, sem = refs[-2:]
    s = lax.axis_index("shard")
    copies = []
    for i, (d, first) in enumerate(spots):
        columns = pl.ds(first, refs[i].shape[2])
        slots = pl.ds((s ^ d) * CAP, CAP)
        copies.append(pltpu.make_async_copy(refs[i], out.at[slots, :, columns], sem.at[i]))
        copies[i].start()
    for copy in copies:
        copy.wait()


def run_place(spots, arrived, placed, shape):
    return pl.pallas_call(
        functools.partial(place_kernel, spots),
        out_shape=jax.ShapeDtypeStruct(shape, jnp.bfloat16),
        in_specs=vmem(len(arrived)) + [whole(pltpu.HBM)] * len(placed),
        out_specs=whole(pltpu.HBM),
        scratch_shapes=[pltpu.SemaphoreType.DMA((len(arrived),))],
        input_output_aliases={len(arrived): 0} if placed else {},
        compiler_params=params(4),
        cost_estimate=pl.CostEstimate(
            flops=400000 * sum(part.size for part in arrived), bytes_accessed=0, transcendentals=0
        ),
        name="place",
    )(*arrived, *placed)


def crossed(x, distance, size):
    return lax.ppermute(x, "shard", [(i, i ^ distance) for i in range(size)])


def swapped(x, axis):
    return lax.ppermute(x, axis, [(0, 1), (1, 0)])


def paired(
    grid_features,
    owners,
    adjacency,
    mesh_nodes,
    norm_gain,
    query_weight,
    key_weight,
    value_weight,
    output_weight,
    up_weight,
    down_weight,
):
    shards = lax.axis_size("shard")
    count, rows, half = grid_features.shape
    flat = grid_features.reshape(count * rows, half)
    half_unit = run_pick(mesh_nodes)
    far = crossed(half_unit, 2, shards)
    waiting, _ = lax.optimization_barrier((mesh_nodes, half_unit))
    near = crossed(waiting, 1, shards)
    waiting, _ = lax.optimization_barrier((flat, half_unit))
    other = swapped(waiting, "head")
    flat, gain, wq, wup, wdn, mesh, rest = run_stage(
        (
            flat,
            norm_gain.reshape(1, -1),
            query_weight,
            up_weight,
            down_weight,
            mesh_nodes,
            mesh_nodes,
        ),
        (None, 1, 0, 0, 1, None, "rest"),
    )
    straight = crossed(rest, 3, shards)
    far, _ = lax.optimization_barrier((far, rest))
    farther = crossed(far, 1, shards)
    far_pair = swapped(far, "head")
    queries, mlp = run_mlp(flat, other, gain, wq, wup, wdn)
    queries, mlp, far_pair, near = lax.optimization_barrier((queries, mlp, far_pair, near))
    blocked = (-1, BLOCK, 2 * half)
    mine_a = run_project((mesh, near, far, far_pair), key_weight, value_weight)
    sibling_a = swapped(mine_a, "sub")
    table = run_table(mine_a.reshape(blocked), sibling_a.reshape(blocked), 2 * shards)
    mine_b = run_project((farther, straight), key_weight, value_weight)
    sibling_b = swapped(mine_b, "sub")
    send, keep, att = run_attend(
        adjacency, queries, mine_b.reshape(blocked), sibling_b.reshape(blocked), table, mlp, output_weight
    )
    keeps, swaps, slots, placed = [], [], [], []
    shape = (shards * CAP, rows, half)
    for c in range(len(WIDTHS)):
        if c > 0:
            send, keep = run_project_out(c, att, mlp, output_weight)
        received = swapped(send, "head")
        if c > 0:
            received, _ = lax.optimization_barrier((received, slots[c - 1][0]))
        slots.append(run_combine((c,), (2, 3), owners, grid_features, (keep,), (received,)))
        keeps.append(keep)
        swaps.append(received)
    every = tuple(range(len(WIDTHS)))
    swaps[-1], _ = lax.optimization_barrier((swaps[-1], slots[-1][0]))
    near_slots, own_slots = run_combine(every, (1, 0), owners, grid_features, keeps, swaps)
    for c in every:
        first = columns_of(c).start
        spots = [(2, first), (3, first)]
        arrived = [crossed(slot, d, shards) for d, slot in zip((2, 3), slots[c])]
        if c == len(WIDTHS) - 1:
            spots += [(1, 0), (0, 0)]
            arrived += [crossed(near_slots, 1, shards), own_slots]
        placed = [run_place(spots, arrived, placed, shape)]
    return placed[0]


def attend_plain(queries, key_table, value_table, chosen, scaling):
    count = chosen.shape[0]
    picked_keys = key_table[chosen]
    picked_keys = picked_keys.reshape(count, -1, picked_keys.shape[3], picked_keys.shape[4])
    picked_values = value_table[chosen]
    picked_values = picked_values.reshape(count, -1, picked_values.shape[3], picked_values.shape[4])
    scores = (
        jnp.einsum("gqhe,gkhe->ghqk", queries, picked_keys, preferred_element_type=jnp.float32)
        * scaling
    )
    highest = jnp.max(scores, axis=-1, keepdims=True)
    weights = jnp.exp(scores - highest)
    weights = (weights / jnp.sum(weights, axis=-1, keepdims=True)).astype(jnp.bfloat16)
    result = jnp.einsum(
        "ghqk,gkhe->gqhe", weights, picked_values, preferred_element_type=jnp.float32
    )
    return result.astype(jnp.bfloat16)


def general(
    grid_features,
    owners,
    adjacency,
    mesh_nodes,
    norm_gain,
    query_weight,
    key_weight,
    value_weight,
    output_weight,
    up_weight,
    down_weight,
):
    shard_count = lax.axis_size("shard")
    head_count = lax.axis_size("head")
    local_blocks, block_rows, feature_share = grid_features.shape
    slots = shard_count * CAP
    owner_col = owners[:, 0]
    position = jnp.arange(local_blocks, dtype=jnp.int32)
    earlier = (owner_col[:, None] == owner_col[None, :]) & (position[None, :] < position[:, None])
    target = owner_col * CAP + jnp.sum(earlier.astype(jnp.int32), axis=1)
    dispatch = (target[:, None] == jnp.arange(slots, dtype=jnp.int32)[None, :]).astype(jnp.bfloat16)
    offset = lax.axis_index("head") * (D // head_count)
    projected = jnp.stack(
        (
            jnp.dot(mesh_nodes, key_weight, preferred_element_type=jnp.float32).astype(
                jnp.bfloat16
            ),
            jnp.dot(mesh_nodes, value_weight, preferred_element_type=jnp.float32).astype(
                jnp.bfloat16
            ),
        )
    )
    tables = lax.all_gather(projected, ("shard", "sub"), axis=1, tiled=True)
    head_local = query_weight.shape[1] // HEAD_DIM
    key_table = tables[0].reshape(-1, block_rows, head_local, HEAD_DIM)
    value_table = tables[1].reshape(-1, block_rows, head_local, HEAD_DIM)
    send_lists = jnp.full((slots, adjacency.shape[1]), -1, jnp.int32).at[target].set(adjacency)
    send_lists = send_lists.reshape(shard_count, CAP, -1)
    complete = lax.all_gather(grid_features, "head", axis=2, tiled=True)
    outgoing = jnp.einsum(
        "gs,gbd->sbd", dispatch, complete, preferred_element_type=jnp.float32
    ).astype(jnp.bfloat16)
    arrived, lists = (
        lax.all_to_all(
            outgoing.reshape(shard_count, CAP, block_rows, D),
            "shard",
            split_axis=0,
            concat_axis=0,
            tiled=True,
        ),
        lax.all_to_all(send_lists, "shard", split_axis=0, concat_axis=0, tiled=True),
    )
    arrived = arrived.reshape(slots, block_rows, D)
    residual = lax.dynamic_slice_in_dim(arrived, offset, D // head_count, 2)
    lists = lists.reshape(slots, -1)
    count = arrived.shape[0]
    values_f = arrived.astype(jnp.float32)
    average = jnp.mean(values_f, axis=-1, keepdims=True)
    centered = values_f - average
    variance = jnp.mean(centered * centered, axis=-1, keepdims=True)
    normed = (centered * lax.rsqrt(variance + epsilon) * norm_gain).astype(jnp.bfloat16)
    flattened = normed.reshape(-1, D)
    queries = jnp.dot(flattened, query_weight, preferred_element_type=jnp.float32).astype(
        jnp.bfloat16
    )
    blocks_each = math.gcd(count, max(1, 512 // block_rows))
    steps_count = count // blocks_each
    queries = queries.reshape(steps_count, blocks_each, block_rows, head_local, HEAD_DIM)

    def attend_step(operands):
        return attend_plain(operands[0], key_table, value_table, operands[1], HEAD_DIM ** (-0.5))

    attended = lax.map(
        attend_step, (queries, jnp.maximum(lists, 0).reshape(steps_count, blocks_each, -1))
    )
    attended = attended.reshape(-1, head_local * HEAD_DIM)
    hidden = jax.nn.gelu(
        jnp.dot(flattened, up_weight, preferred_element_type=jnp.float32), approximate=False
    ).astype(jnp.bfloat16)
    branch = jnp.dot(attended, output_weight, preferred_element_type=jnp.float32)
    branch = branch + jnp.dot(hidden, down_weight, preferred_element_type=jnp.float32)
    branch = branch.reshape(count, block_rows, D)
    reduced = lax.psum_scatter(
        branch.astype(jnp.bfloat16), "head", scatter_dimension=2, tiled=True
    ).astype(jnp.float32)
    occupied = lists[:, 0] >= 0
    summed = residual.astype(jnp.float32) + reduced
    return jnp.where(occupied[:, None, None], summed, 0.0).astype(jnp.bfloat16)


def local(grid_features, owners, adjacency, mesh_nodes, *parameters):
    sizes = [lax.axis_size(axis) for axis in ("shard", "head", "sub")]
    small = grid_features.shape[:2] == (4, BLOCK) and mesh_nodes.shape[0] == 2 * BLOCK
    if sizes == [4, 2, 2] and small and grid_features.shape[2] == 512:
        return paired(grid_features, owners, adjacency, mesh_nodes, *parameters)
    return general(grid_features, owners, adjacency, mesh_nodes, *parameters)


def solution(mesh):
    return jax.shard_map(
        local,
        mesh=mesh,
        in_specs=(
            P(("groups", "shard", "sub"), None, "head"),
            P(("groups", "shard", "sub"), None),
            P(("groups", "shard", "sub"), None),
            P(("groups", "shard", "sub"), None),
            P(),
            P(None, "head"),
            P(None, "head"),
            P(None, "head"),
            P("head", None),
            P(None, "head"),
            P("head", None),
        ),
        out_specs=P(("groups", "shard", "sub"), None, "head"),
        check_vma=False,
    )
```

```python
import functools
import math

import jax
import jax.numpy as jnp
from jax import lax
from jax.experimental import pallas as pl
from jax.experimental.pallas import tpu as pltpu
from jax.sharding import PartitionSpec as P

D = 1024
HEAD_DIM = 64
CAP = 2
BLOCK = 64
QUAD = 4
WIDE = QUAD * HEAD_DIM
WIDTHS = (128, 384)
MIB = 1 << 20


epsilon = 1e-05


def dot(a, b):
    return jnp.dot(a, b, preferred_element_type=jnp.float32)


def gelu(x):
    return 0.5 * x * (1.0 + lax.erf(x * (2.0**-0.5)))


def in_hbm(x):
    return pltpu.with_memory_space_constraint(x, pltpu.HBM)


def in_vmem(x):
    return pltpu.with_memory_space_constraint(x, pltpu.VMEM)


def whole(space):
    return pl.BlockSpec(memory_space=space)


def vmem(count):
    return [whole(pltpu.VMEM)] * count


def params(mib):
    return pltpu.CompilerParams(vmem_limit_bytes=mib * MIB)


def mlp_kernel(own, other, gain, wq, wup, wdn, q_out, mlp_out, normed_s):
    half = own.shape[1]
    units = wup.shape[1]
    chunk = units // 4
    x_other = other[...].astype(jnp.float32)
    x_own = own[...].astype(jnp.float32)

    def mean(a, b):
        total = jnp.sum(a, axis=-1, keepdims=True) + jnp.sum(b, axis=-1, keepdims=True)
        return total * (0.5 / half)

    average = mean(x_other, x_own)
    x_other = x_other - average
    x_own = x_own - average
    factor = lax.rsqrt(mean(x_other * x_other, x_own * x_own) + epsilon)
    normed_s[:, :half] = (x_other * factor * gain[:, :half]).astype(jnp.bfloat16)
    normed_s[:, half:] = (x_own * factor * gain[:, half:]).astype(jnp.bfloat16)
    normed = normed_s[...]
    q_out[...] = dot(normed, wq[...]).astype(jnp.bfloat16)
    for c in range(units // chunk):
        span = slice(c * chunk, (c + 1) * chunk)
        hidden = gelu(dot(normed, wup[:, span])).astype(jnp.bfloat16)
        term = dot(hidden, wdn[span, :])
        if c == 0:
            mlp_out[...] = term
        else:
            mlp_out[...] += term


def run_mlp(own, other, gain, wq, wup, wdn):
    rows = own.shape[0]
    width = wq.shape[0]
    units = wup.shape[1]
    return pl.pallas_call(
        mlp_kernel,
        out_shape=(
            jax.ShapeDtypeStruct((rows, wq.shape[1]), jnp.bfloat16),
            jax.ShapeDtypeStruct((rows, width), jnp.float32),
        ),
        in_specs=vmem(6),
        out_specs=tuple(vmem(2)),
        scratch_shapes=[pltpu.VMEM((rows, width), jnp.bfloat16)],
        compiler_params=params(16),
        cost_estimate=pl.CostEstimate(
            flops=2 * rows * width * (wq.shape[1] + 2 * units),
            bytes_accessed=2 * width * (wq.shape[1] + 2 * units),
            transcendentals=rows * units,
        ),
        name="mlp",
    )(own, other, gain, wq, wup, wdn)


def stage_kernel(axes, *refs):
    sources, targets, sem = refs[: len(axes)], refs[len(axes) : -1], refs[-1]
    h = lax.axis_index("head")
    copies = []

    def add(source, target):
        pieces = 2 if source.shape[0] >= 512 else 1
        rows = source.shape[0] // pieces
        for piece in range(pieces):
            span = pl.ds(piece * rows, rows)
            copies.append(
                pltpu.make_async_copy(
                    source.at[span, :], target.at[span, :], sem.at[len(copies)]
                )
            )
            copies[-1].start()

    for source, target, axis in zip(sources, targets, axes):
        if axis is None:
            add(source, target)
            continue
        half = source.shape[axis] // 2
        for part, head in enumerate((1 - h, h)):
            span = pl.ds(pl.multiple_of(head * half, half), half)
            place = pl.ds(part * half, half)
            if axis == 0:
                add(source.at[span, :], target.at[place, :])
            else:
                add(source.at[:, span], target.at[:, place])
    for copy in copies:
        copy.wait()


def run_stage(arrays, axes):
    size = sum(2 * array.size for array in arrays)
    return pl.pallas_call(
        functools.partial(stage_kernel, axes),
        out_shape=tuple(jax.ShapeDtypeStruct(array.shape, array.dtype) for array in arrays),
        in_specs=[whole(pltpu.HBM)] * len(arrays),
        out_specs=tuple(vmem(len(arrays))),
        scratch_shapes=[pltpu.SemaphoreType.DMA((4 * len(arrays),))],
        compiler_params=params(16),
        cost_estimate=pl.CostEstimate(
            flops=2000 * size, bytes_accessed=20 * size, transcendentals=0
        ),
        name="stage",
    )(*(in_hbm(array) for array in arrays))


def project_kernel(*refs):
    *pieces, first, second, wk, wv, out, rows_s = refs
    width = wk.shape[1]
    fixed = sum(piece.shape[0] for piece in pieces)
    start = 0
    for piece in pieces:
        rows_s[start : start + piece.shape[0], :] = piece[...]
        start += piece.shape[0]
    same = lax.axis_index("head") == lax.axis_index("sub")

    @pl.when(same)
    def _():
        rows_s[fixed:, :] = first[...]

    @pl.when(jnp.logical_not(same))
    def _():
        rows_s[fixed:, :] = second[...]

    out[:, :width] = dot(rows_s[...], wk[...]).astype(jnp.bfloat16)
    out[:, width:] = dot(rows_s[...], wv[...]).astype(jnp.bfloat16)


def run_project(pieces, wk, wv):
    rows = sum(piece.shape[0] for piece in pieces[:-1])
    depth, width = wk.shape
    return pl.pallas_call(
        project_kernel,
        out_shape=jax.ShapeDtypeStruct((rows, 2 * width), jnp.bfloat16),
        in_specs=vmem(len(pieces) + 2),
        out_specs=whole(pltpu.VMEM),
        scratch_shapes=[pltpu.VMEM((rows, depth), jnp.bfloat16)],
        compiler_params=params(8),
        cost_estimate=pl.CostEstimate(
            flops=300 * rows * depth * width,
            bytes_accessed=300 * depth * width + 300 * rows * depth,
            transcendentals=0,
        ),
        name="project",
    )(*pieces, in_vmem(wk), in_vmem(wv))


def table_kernel(mine, sibling, table):
    table[0, : mine.shape[0]] = mine[...]
    table[1, : mine.shape[0]] = sibling[...]


def run_table(mine, sibling, blocks):
    return pl.pallas_call(
        table_kernel,
        out_shape=jax.ShapeDtypeStruct((2, blocks) + mine.shape[1:], jnp.bfloat16),
        in_specs=vmem(2),
        out_specs=whole(pltpu.VMEM),
        compiler_params=params(8),
        cost_estimate=pl.CostEstimate(
            flops=0, bytes_accessed=80 * mine.size, transcendentals=0
        ),
        name="table",
    )(mine, sibling)


def columns_of(c):
    return slice(sum(WIDTHS[:c]), sum(WIDTHS[: c + 1]))


def project_out(c, att, mlp, wo, send, keep):
    half = att.shape[1]
    chunk = columns_of(c)
    h = lax.axis_index("head")

    def write(head):
        for out, first, place in ((send, 0, 1 - head), (keep, half, head)):
            extra = mlp[:, first + chunk.start : first + chunk.stop]
            span = slice(place * half + chunk.start, place * half + chunk.stop)
            out[...] = (extra + dot(att[...], wo[:, span])).astype(jnp.bfloat16)

    for head in range(2):
        pl.when(h == head)(functools.partial(write, head))


def attend_kernel(
    adjacency, q, mine, sibling, table_in, mlp, wo, send, keep, att, table
):
    del table_in
    s = lax.axis_index("shard")
    u = lax.axis_index("sub")
    half = wo.shape[0]
    ready = table.shape[1] - mine.shape[0]
    for i, part in enumerate((mine, sibling)):
        table[i, ready:] = part[...]
    rows_of = lax.broadcasted_iota(jnp.int32, (WIDE, WIDE), 0) // BLOCK
    lanes_of = lax.broadcasted_iota(jnp.int32, (WIDE, WIDE), 1) // HEAD_DIM
    diagonal = rows_of == lanes_of
    lane_head = lax.broadcasted_iota(jnp.int32, (BLOCK, WIDE), 1) // HEAD_DIM
    scale = HEAD_DIM**-0.5 * math.log2(math.e)
    groups = half // WIDE
    places = []
    for b in range(adjacency.shape[0]):
        places.append([])
        for j in range(adjacency.shape[1]):
            m = adjacency[b, j]
            part = lax.rem(m, 2)
            core = lax.rem(m // 2, 2)
            distance = s ^ (m // 4)
            places[b].append((core ^ u, distance * 2 + part))

    def scores_of(step):
        b, g = divmod(step, groups)
        columns = slice(g * WIDE, (g + 1) * WIDE)
        keys = jnp.concatenate([table[i, p, :, columns] for i, p in places[b]], axis=0)
        stacked = jnp.concatenate([q[b * BLOCK : (b + 1) * BLOCK, columns]] * QUAD, axis=0)
        stacked = jnp.where(diagonal, stacked, jnp.zeros_like(stacked))
        return lax.dot_general(
            stacked, keys, (((1,), (1,)), ((), ())), preferred_element_type=jnp.float32
        )

    steps = len(places) * groups
    scores = scores_of(0)
    for step in range(steps):
        following = scores_of(step + 1) if step + 1 < steps else None
        b, g = divmod(step, groups)
        columns = slice(half + g * WIDE, half + (g + 1) * WIDE)
        values = jnp.concatenate([table[i, p, :, columns] for i, p in places[b]], axis=0)
        highest = jnp.max(scores, axis=-1, keepdims=True)
        weights = jnp.exp2((scores - highest) * scale)
        total = jnp.sum(weights, axis=-1, keepdims=True)
        mixed = dot(weights.astype(jnp.bfloat16), values) * (1.0 / total)
        merged = mixed[0:BLOCK, :]
        for i in range(1, QUAD):
            merged = jnp.where(lane_head == i, mixed[i * BLOCK : (i + 1) * BLOCK, :], merged)
        rows = slice(b * BLOCK, (b + 1) * BLOCK)
        att[rows, g * WIDE : (g + 1) * WIDE] = merged.astype(jnp.bfloat16)
        scores = following
    project_out(0, att, mlp, wo, send, keep)


def run_attend(adjacency, q, mine, sibling, table, mlp, wo):
    rows, half = q.shape
    part = jax.ShapeDtypeStruct((rows, WIDTHS[0]), jnp.bfloat16)
    blocks = table.shape[0] * table.shape[1]
    send, keep, att, _ = pl.pallas_call(
        attend_kernel,
        out_shape=(
            part,
            part,
            jax.ShapeDtypeStruct(q.shape, jnp.bfloat16),
            jax.ShapeDtypeStruct(table.shape, jnp.bfloat16),
        ),
        in_specs=[whole(pltpu.SMEM)] + vmem(6),
        out_specs=tuple(vmem(4)),
        input_output_aliases={4: 3},
        compiler_params=params(16),
        cost_estimate=pl.CostEstimate(
            flops=20 * rows * half * (D + 8 * 8 * BLOCK),
            bytes_accessed=40 * blocks * BLOCK * half + 20 * half * D + 40 * rows * D,
            transcendentals=rows * 8 * BLOCK * half // HEAD_DIM,
        ),
        name="attend",
    )(adjacency, q, mine, sibling, table, mlp, in_vmem(wo))
    return send, keep, att


def run_project_out(c, att, mlp, wo):
    rows, half = att.shape
    part = jax.ShapeDtypeStruct((rows, WIDTHS[c]), jnp.bfloat16)
    return pl.pallas_call(
        functools.partial(project_out, c),
        out_shape=(part, part),
        in_specs=vmem(3),
        out_specs=tuple(vmem(2)),
        compiler_params=params(8),
        cost_estimate=pl.CostEstimate(
            flops=200 * rows * half * D,
            bytes_accessed=200 * half * D,
            transcendentals=0,
        ),
        name="project_out",
    )(att, mlp, in_vmem(wo))


def combine_kernel(chunks, distances, owners, grid_features, *refs):
    s = lax.axis_index("shard")
    keeps, refs = refs[: len(chunks)], refs[len(chunks) :]
    swaps, outs = refs[: len(chunks)], refs[len(chunks) :]
    count = grid_features.shape[0]
    names = [owners[t, 0] for t in range(count)]
    first = columns_of(chunks[0]).start
    for d, out in zip(distances, outs):
        out[...] = jnp.zeros(out.shape, jnp.bfloat16)
        seen = jnp.int32(0)
        for t in range(count):
            hit = names[t] == s ^ d
            rank = seen

            @pl.when(hit)
            def _():
                rows = slice(t * BLOCK, (t + 1) * BLOCK)
                for c, keep, swap in zip(chunks, keeps, swaps):
                    columns = columns_of(c)
                    partials = keep[rows, :].astype(jnp.float32)
                    partials = partials + swap[rows, :].astype(jnp.float32)
                    residual = grid_features[t, :, columns].astype(jnp.float32)
                    place = slice(columns.start - first, columns.stop - first)
                    out[rank, :, place] = (residual + partials).astype(jnp.bfloat16)

            seen = seen + hit.astype(jnp.int32)


def run_combine(chunks, distances, owners, grid_features, keeps, swaps):
    count, rows, _ = grid_features.shape
    width = sum(WIDTHS[c] for c in chunks)
    slot = jax.ShapeDtypeStruct((CAP, rows, width), jnp.bfloat16)
    return pl.pallas_call(
        functools.partial(combine_kernel, chunks, distances),
        out_shape=(slot,) * len(distances),
        in_specs=[whole(pltpu.SMEM)] + vmem(1 + 2 * len(chunks)),
        out_specs=tuple(vmem(len(distances))),
        compiler_params=params(8),
        cost_estimate=pl.CostEstimate(
            flops=60000 * count * rows * width,
            bytes_accessed=400 * rows * width * (3 * count + CAP * len(distances)),
            transcendentals=0,
        ),
        name="combine",
    )(owners, grid_features, *keeps, *swaps)


def place_kernel(spots, *refs):
    out, sem = refs[-2:]
    s = lax.axis_index("shard")
    copies = []
    for i, (d, first) in enumerate(spots):
        columns = pl.ds(first, refs[i].shape[2])
        slots = pl.ds((s ^ d) * CAP, CAP)
        copies.append(pltpu.make_async_copy(refs[i], out.at[slots, :, columns], sem.at[i]))
        copies[i].start()
    for copy in copies:
        copy.wait()


def run_place(spots, arrived, placed, shape):
    return pl.pallas_call(
        functools.partial(place_kernel, spots),
        out_shape=jax.ShapeDtypeStruct(shape, jnp.bfloat16),
        in_specs=vmem(len(arrived)) + [whole(pltpu.HBM)] * len(placed),
        out_specs=whole(pltpu.HBM),
        scratch_shapes=[pltpu.SemaphoreType.DMA((len(arrived),))],
        input_output_aliases={len(arrived): 0} if placed else {},
        compiler_params=params(4),
        cost_estimate=pl.CostEstimate(
            flops=400000 * sum(part.size for part in arrived), bytes_accessed=0, transcendentals=0
        ),
        name="place",
    )(*arrived, *placed)


def crossed(x, distance, size):
    return lax.ppermute(x, "shard", [(i, i ^ distance) for i in range(size)])


def fetched(x, distance, same, size):
    pairs = []
    for i in range(size):
        for h in range(2):
            u = h if same else 1 - h
            pairs.append((4 * i + 2 * h + u, 4 * (i ^ distance) + 2 * h + u))
    return lax.ppermute(x, ("shard", "head", "sub"), pairs)


def handed(x):
    return lax.ppermute(x, ("head", "sub"), [(0, 2), (3, 1)])


def swapped(x, axis):
    return lax.ppermute(x, axis, [(0, 1), (1, 0)])


def paired(
    grid_features,
    owners,
    adjacency,
    mesh_nodes,
    norm_gain,
    query_weight,
    key_weight,
    value_weight,
    output_weight,
    up_weight,
    down_weight,
):
    shards = lax.axis_size("shard")
    count, rows, half = grid_features.shape
    flat = grid_features.reshape(count * rows, half)
    far = fetched(mesh_nodes, 2, True, shards)
    near = crossed(mesh_nodes, 1, shards)
    other = swapped(flat, "head")
    flat, gain, wq, wup, wdn, mesh = run_stage(
        (
            flat,
            norm_gain.reshape(1, -1),
            query_weight,
            up_weight,
            down_weight,
            mesh_nodes,
        ),
        (None, 1, 0, 0, 1, None),
    )
    straight = fetched(mesh, 3, False, shards)
    far, _ = lax.optimization_barrier((far, mesh))
    farther = fetched(far, 1, True, shards)
    passed = handed(far)
    queries, mlp = run_mlp(flat, other, gain, wq, wup, wdn)
    queries, mlp, passed, near = lax.optimization_barrier((queries, mlp, passed, near))
    blocked = (-1, BLOCK, 2 * half)
    mine_a = run_project((mesh, near, far, passed), key_weight, value_weight)
    sibling_a = swapped(mine_a, "sub")
    table = run_table(mine_a.reshape(blocked), sibling_a.reshape(blocked), 2 * shards)
    mine_b = run_project((farther, straight), key_weight, value_weight)
    sibling_b = swapped(mine_b, "sub")
    send, keep, att = run_attend(
        adjacency, queries, mine_b.reshape(blocked), sibling_b.reshape(blocked), table, mlp, output_weight
    )
    keeps, swaps, slots, placed = [], [], [], []
    shape = (shards * CAP, rows, half)
    for c in range(len(WIDTHS)):
        if c > 0:
            send, keep = run_project_out(c, att, mlp, output_weight)
        received = swapped(send, "head")
        if c > 0:
            received, _ = lax.optimization_barrier((received, slots[c - 1][0]))
        slots.append(run_combine((c,), (2, 3), owners, grid_features, (keep,), (received,)))
        keeps.append(keep)
        swaps.append(received)
    every = tuple(range(len(WIDTHS)))
    swaps[-1], _ = lax.optimization_barrier((swaps[-1], slots[-1][0]))
    near_slots, own_slots = run_combine(every, (1, 0), owners, grid_features, keeps, swaps)
    for c in every:
        first = columns_of(c).start
        spots = [(2, first), (3, first)]
        arrived = [crossed(slot, d, shards) for d, slot in zip((2, 3), slots[c])]
        if c == len(WIDTHS) - 1:
            spots += [(1, 0), (0, 0)]
            arrived += [crossed(near_slots, 1, shards), own_slots]
        placed = [run_place(spots, arrived, placed, shape)]
    return placed[0]


def attend_plain(queries, key_table, value_table, chosen, scaling):
    count = chosen.shape[0]
    picked_keys = key_table[chosen]
    picked_keys = picked_keys.reshape(count, -1, picked_keys.shape[3], picked_keys.shape[4])
    picked_values = value_table[chosen]
    picked_values = picked_values.reshape(count, -1, picked_values.shape[3], picked_values.shape[4])
    scores = (
        jnp.einsum("gqhe,gkhe->ghqk", queries, picked_keys, preferred_element_type=jnp.float32)
        * scaling
    )
    highest = jnp.max(scores, axis=-1, keepdims=True)
    weights = jnp.exp(scores - highest)
    weights = (weights / jnp.sum(weights, axis=-1, keepdims=True)).astype(jnp.bfloat16)
    result = jnp.einsum(
        "ghqk,gkhe->gqhe", weights, picked_values, preferred_element_type=jnp.float32
    )
    return result.astype(jnp.bfloat16)


def general(
    grid_features,
    owners,
    adjacency,
    mesh_nodes,
    norm_gain,
    query_weight,
    key_weight,
    value_weight,
    output_weight,
    up_weight,
    down_weight,
):
    shard_count = lax.axis_size("shard")
    head_count = lax.axis_size("head")
    local_blocks, block_rows, feature_share = grid_features.shape
    slots = shard_count * CAP
    owner_col = owners[:, 0]
    position = jnp.arange(local_blocks, dtype=jnp.int32)
    earlier = (owner_col[:, None] == owner_col[None, :]) & (position[None, :] < position[:, None])
    target = owner_col * CAP + jnp.sum(earlier.astype(jnp.int32), axis=1)
    dispatch = (target[:, None] == jnp.arange(slots, dtype=jnp.int32)[None, :]).astype(jnp.bfloat16)
    offset = lax.axis_index("head") * (D // head_count)
    projected = jnp.stack(
        (
            jnp.dot(mesh_nodes, key_weight, preferred_element_type=jnp.float32).astype(
                jnp.bfloat16
            ),
            jnp.dot(mesh_nodes, value_weight, preferred_element_type=jnp.float32).astype(
                jnp.bfloat16
            ),
        )
    )
    tables = lax.all_gather(projected, ("shard", "sub"), axis=1, tiled=True)
    head_local = query_weight.shape[1] // HEAD_DIM
    key_table = tables[0].reshape(-1, block_rows, head_local, HEAD_DIM)
    value_table = tables[1].reshape(-1, block_rows, head_local, HEAD_DIM)
    send_lists = jnp.full((slots, adjacency.shape[1]), -1, jnp.int32).at[target].set(adjacency)
    send_lists = send_lists.reshape(shard_count, CAP, -1)
    complete = lax.all_gather(grid_features, "head", axis=2, tiled=True)
    outgoing = jnp.einsum(
        "gs,gbd->sbd", dispatch, complete, preferred_element_type=jnp.float32
    ).astype(jnp.bfloat16)
    arrived, lists = (
        lax.all_to_all(
            outgoing.reshape(shard_count, CAP, block_rows, D),
            "shard",
            split_axis=0,
            concat_axis=0,
            tiled=True,
        ),
        lax.all_to_all(send_lists, "shard", split_axis=0, concat_axis=0, tiled=True),
    )
    arrived = arrived.reshape(slots, block_rows, D)
    residual = lax.dynamic_slice_in_dim(arrived, offset, D // head_count, 2)
    lists = lists.reshape(slots, -1)
    count = arrived.shape[0]
    values_f = arrived.astype(jnp.float32)
    average = jnp.mean(values_f, axis=-1, keepdims=True)
    centered = values_f - average
    variance = jnp.mean(centered * centered, axis=-1, keepdims=True)
    normed = (centered * lax.rsqrt(variance + epsilon) * norm_gain).astype(jnp.bfloat16)
    flattened = normed.reshape(-1, D)
    queries = jnp.dot(flattened, query_weight, preferred_element_type=jnp.float32).astype(
        jnp.bfloat16
    )
    blocks_each = math.gcd(count, max(1, 512 // block_rows))
    steps_count = count // blocks_each
    queries = queries.reshape(steps_count, blocks_each, block_rows, head_local, HEAD_DIM)

    def attend_step(operands):
        return attend_plain(operands[0], key_table, value_table, operands[1], HEAD_DIM ** (-0.5))

    attended = lax.map(
        attend_step, (queries, jnp.maximum(lists, 0).reshape(steps_count, blocks_each, -1))
    )
    attended = attended.reshape(-1, head_local * HEAD_DIM)
    hidden = jax.nn.gelu(
        jnp.dot(flattened, up_weight, preferred_element_type=jnp.float32), approximate=False
    ).astype(jnp.bfloat16)
    branch = jnp.dot(attended, output_weight, preferred_element_type=jnp.float32)
    branch = branch + jnp.dot(hidden, down_weight, preferred_element_type=jnp.float32)
    branch = branch.reshape(count, block_rows, D)
    reduced = lax.psum_scatter(
        branch.astype(jnp.bfloat16), "head", scatter_dimension=2, tiled=True
    ).astype(jnp.float32)
    occupied = lists[:, 0] >= 0
    summed = residual.astype(jnp.float32) + reduced
    return jnp.where(occupied[:, None, None], summed, 0.0).astype(jnp.bfloat16)


def local(grid_features, owners, adjacency, mesh_nodes, *parameters):
    sizes = [lax.axis_size(axis) for axis in ("shard", "head", "sub")]
    small = grid_features.shape[:2] == (4, BLOCK) and mesh_nodes.shape[0] == 2 * BLOCK
    if sizes == [4, 2, 2] and small and grid_features.shape[2] == 512:
        return paired(grid_features, owners, adjacency, mesh_nodes, *parameters)
    return general(grid_features, owners, adjacency, mesh_nodes, *parameters)


def solution(mesh):
    return jax.shard_map(
        local,
        mesh=mesh,
        in_specs=(
            P(("groups", "shard", "sub"), None, "head"),
            P(("groups", "shard", "sub"), None),
            P(("groups", "shard", "sub"), None),
            P(("groups", "shard", "sub"), None),
            P(),
            P(None, "head"),
            P(None, "head"),
            P(None, "head"),
            P("head", None),
            P(None, "head"),
            P("head", None),
        ),
        out_specs=P(("groups", "shard", "sub"), None, "head"),
        check_vma=False,
    )
```

```python
import functools
import math

import jax
import jax.numpy as jnp
from jax import lax
from jax.experimental import pallas as pl
from jax.experimental.pallas import tpu as pltpu
from jax.sharding import PartitionSpec as P

D = 1024
HEAD_DIM = 64
CAP = 2
BLOCK = 64
QUAD = 4
WIDE = QUAD * HEAD_DIM
WIDTHS = (128, 384)
MIB = 1 << 20


epsilon = 1e-05


def dot(a, b):
    return jnp.dot(a, b, preferred_element_type=jnp.float32)


def gelu(x):
    return 0.5 * x * (1.0 + lax.erf(x * (2.0**-0.5)))


def in_hbm(x):
    return pltpu.with_memory_space_constraint(x, pltpu.HBM)


def in_vmem(x):
    return pltpu.with_memory_space_constraint(x, pltpu.VMEM)


def whole(space):
    return pl.BlockSpec(memory_space=space)


def vmem(count):
    return [whole(pltpu.VMEM)] * count


def params(mib):
    return pltpu.CompilerParams(vmem_limit_bytes=mib * MIB)


def mlp_kernel(own, other, gain, wq, wup, wdn, q_out, mlp_out, normed_s):
    half = own.shape[1]
    units = wup.shape[1]
    chunk = units // 4
    x_other = other[...].astype(jnp.float32)
    x_own = own[...].astype(jnp.float32)

    def mean(a, b):
        total = jnp.sum(a, axis=-1, keepdims=True) + jnp.sum(b, axis=-1, keepdims=True)
        return total * (0.5 / half)

    average = mean(x_other, x_own)
    x_other = x_other - average
    x_own = x_own - average
    factor = lax.rsqrt(mean(x_other * x_other, x_own * x_own) + epsilon)
    normed_s[:, :half] = (x_other * factor * gain[:, :half]).astype(jnp.bfloat16)
    normed_s[:, half:] = (x_own * factor * gain[:, half:]).astype(jnp.bfloat16)
    normed = normed_s[...]
    q_out[...] = dot(normed, wq[...]).astype(jnp.bfloat16)
    for c in range(units // chunk):
        span = slice(c * chunk, (c + 1) * chunk)
        hidden = gelu(dot(normed, wup[:, span])).astype(jnp.bfloat16)
        term = dot(hidden, wdn[span, :])
        if c == 0:
            mlp_out[...] = term
        else:
            mlp_out[...] += term


def run_mlp(own, other, gain, wq, wup, wdn):
    rows = own.shape[0]
    width = wq.shape[0]
    units = wup.shape[1]
    return pl.pallas_call(
        mlp_kernel,
        out_shape=(
            jax.ShapeDtypeStruct((rows, wq.shape[1]), jnp.bfloat16),
            jax.ShapeDtypeStruct((rows, width), jnp.float32),
        ),
        in_specs=vmem(6),
        out_specs=tuple(vmem(2)),
        scratch_shapes=[pltpu.VMEM((rows, width), jnp.bfloat16)],
        compiler_params=params(16),
        cost_estimate=pl.CostEstimate(
            flops=2 * rows * width * (wq.shape[1] + 2 * units),
            bytes_accessed=2 * width * (wq.shape[1] + 2 * units),
            transcendentals=rows * units,
        ),
        name="mlp",
    )(own, other, gain, wq, wup, wdn)


def pick_kernel(mesh, out, sem):
    first = pl.multiple_of(lax.axis_index("head") * BLOCK, BLOCK)
    copy = pltpu.make_async_copy(mesh.at[pl.ds(first, BLOCK), :], out, sem)
    copy.start()
    copy.wait()


def run_pick(mesh):
    return pl.pallas_call(
        pick_kernel,
        out_shape=jax.ShapeDtypeStruct((BLOCK, mesh.shape[1]), mesh.dtype),
        in_specs=[whole(pltpu.HBM)],
        out_specs=whole(pltpu.VMEM),
        scratch_shapes=[pltpu.SemaphoreType.DMA(())],
        compiler_params=params(4),
        cost_estimate=pl.CostEstimate(flops=0, bytes_accessed=4 * mesh.size, transcendentals=0),
        name="pick",
    )(in_hbm(mesh))


def stage_kernel(axes, *refs):
    sources, targets, sem = refs[: len(axes)], refs[len(axes) : -1], refs[-1]
    h = lax.axis_index("head")
    copies = []

    def add(source, target):
        pieces = 2 if source.shape[0] >= 512 else 1
        rows = source.shape[0] // pieces
        for piece in range(pieces):
            span = pl.ds(piece * rows, rows)
            copies.append(
                pltpu.make_async_copy(
                    source.at[span, :], target.at[span, :], sem.at[len(copies)]
                )
            )
            copies[-1].start()

    for source, target, axis in zip(sources, targets, axes):
        if axis is None:
            add(source, target)
            continue
        if axis == "rest":
            add(source.at[pl.ds(pl.multiple_of((1 - h) * BLOCK, BLOCK), BLOCK), :], target)
            continue
        half = source.shape[axis] // 2
        for part, head in enumerate((1 - h, h)):
            span = pl.ds(pl.multiple_of(head * half, half), half)
            place = pl.ds(part * half, half)
            if axis == 0:
                add(source.at[span, :], target.at[place, :])
            else:
                add(source.at[:, span], target.at[:, place])
    for copy in copies:
        copy.wait()


def run_stage(arrays, axes):
    size = sum(2 * array.size for array in arrays)
    return pl.pallas_call(
        functools.partial(stage_kernel, axes),
        out_shape=tuple(
            jax.ShapeDtypeStruct((BLOCK,) + array.shape[1:] if axis == "rest" else array.shape, array.dtype)
            for array, axis in zip(arrays, axes)
        ),
        in_specs=[whole(pltpu.HBM)] * len(arrays),
        out_specs=tuple(vmem(len(arrays))),
        scratch_shapes=[pltpu.SemaphoreType.DMA((4 * len(arrays),))],
        compiler_params=params(16),
        cost_estimate=pl.CostEstimate(
            flops=2000 * size, bytes_accessed=20 * size, transcendentals=0
        ),
        name="stage",
    )(*(in_hbm(array) for array in arrays))


def project_kernel(*refs):
    pieces, (wk, wv, out) = refs[:-3], refs[-3:]
    width = wk.shape[1]
    rows = jnp.concatenate([piece[...] for piece in pieces], axis=0)
    out[:, :width] = dot(rows, wk[...]).astype(jnp.bfloat16)
    out[:, width:] = dot(rows, wv[...]).astype(jnp.bfloat16)


def run_project(pieces, wk, wv):
    rows = sum(piece.shape[0] for piece in pieces)
    depth, width = wk.shape
    return pl.pallas_call(
        project_kernel,
        out_shape=jax.ShapeDtypeStruct((rows, 2 * width), jnp.bfloat16),
        in_specs=vmem(len(pieces) + 2),
        out_specs=whole(pltpu.VMEM),
        compiler_params=params(8),
        cost_estimate=pl.CostEstimate(
            flops=300 * rows * depth * width,
            bytes_accessed=300 * depth * width + 300 * rows * depth,
            transcendentals=0,
        ),
        name="project",
    )(*pieces, in_vmem(wk), in_vmem(wv))


def table_kernel(mine, sibling, table):
    table[0, : mine.shape[0]] = mine[...]
    table[1, : mine.shape[0]] = sibling[...]


def run_table(mine, sibling, blocks):
    return pl.pallas_call(
        table_kernel,
        out_shape=jax.ShapeDtypeStruct((2, blocks) + mine.shape[1:], jnp.bfloat16),
        in_specs=vmem(2),
        out_specs=whole(pltpu.VMEM),
        compiler_params=params(8),
        cost_estimate=pl.CostEstimate(
            flops=0, bytes_accessed=80 * mine.size, transcendentals=0
        ),
        name="table",
    )(mine, sibling)


def columns_of(c):
    return slice(sum(WIDTHS[:c]), sum(WIDTHS[: c + 1]))


def project_out(c, att, mlp, wo, send, keep):
    half = att.shape[1]
    chunk = columns_of(c)
    h = lax.axis_index("head")

    def write(head):
        for out, first, place in ((send, 0, 1 - head), (keep, half, head)):
            extra = mlp[:, first + chunk.start : first + chunk.stop]
            span = slice(place * half + chunk.start, place * half + chunk.stop)
            out[...] = (extra + dot(att[...], wo[:, span])).astype(jnp.bfloat16)

    for head in range(2):
        pl.when(h == head)(functools.partial(write, head))


def attend_kernel(
    adjacency, q, mine, sibling, table_in, mlp, wo, send, keep, att, table
):
    del table_in
    s = lax.axis_index("shard")
    h = lax.axis_index("head")
    u = lax.axis_index("sub")
    half = wo.shape[0]
    ready = table.shape[1] - mine.shape[0]
    for i, part in enumerate((mine, sibling)):
        table[i, ready:] = part[...]
    rows_of = lax.broadcasted_iota(jnp.int32, (WIDE, WIDE), 0) // BLOCK
    lanes_of = lax.broadcasted_iota(jnp.int32, (WIDE, WIDE), 1) // HEAD_DIM
    diagonal = rows_of == lanes_of
    lane_head = lax.broadcasted_iota(jnp.int32, (BLOCK, WIDE), 1) // HEAD_DIM
    scale = HEAD_DIM**-0.5 * math.log2(math.e)
    groups = half // WIDE
    places = []
    for b in range(adjacency.shape[0]):
        places.append([])
        for j in range(adjacency.shape[1]):
            m = adjacency[b, j]
            part = lax.rem(m, 2)
            core = lax.rem(m // 2, 2)
            distance = s ^ (m // 4)
            part = jnp.where(distance <= 1, part, part ^ h)
            places[b].append((core ^ u, distance * 2 + part))

    def scores_of(step):
        b, g = divmod(step, groups)
        columns = slice(g * WIDE, (g + 1) * WIDE)
        keys = jnp.concatenate([table[i, p, :, columns] for i, p in places[b]], axis=0)
        stacked = jnp.concatenate([q[b * BLOCK : (b + 1) * BLOCK, columns]] * QUAD, axis=0)
        stacked = jnp.where(diagonal, stacked, jnp.zeros_like(stacked))
        return lax.dot_general(
            stacked, keys, (((1,), (1,)), ((), ())), preferred_element_type=jnp.float32
        )

    steps = len(places) * groups
    scores = scores_of(0)
    for step in range(steps):
        following = scores_of(step + 1) if step + 1 < steps else None
        b, g = divmod(step, groups)
        columns = slice(half + g * WIDE, half + (g + 1) * WIDE)
        values = jnp.concatenate([table[i, p, :, columns] for i, p in places[b]], axis=0)
        highest = jnp.max(scores, axis=-1, keepdims=True)
        weights = jnp.exp2((scores - highest) * scale)
        total = jnp.sum(weights, axis=-1, keepdims=True)
        mixed = dot(weights.astype(jnp.bfloat16), values) * (1.0 / total)
        merged = mixed[0:BLOCK, :]
        for i in range(1, QUAD):
            merged = jnp.where(lane_head == i, mixed[i * BLOCK : (i + 1) * BLOCK, :], merged)
        rows = slice(b * BLOCK, (b + 1) * BLOCK)
        att[rows, g * WIDE : (g + 1) * WIDE] = merged.astype(jnp.bfloat16)
        scores = following
    project_out(0, att, mlp, wo, send, keep)


def run_attend(adjacency, q, mine, sibling, table, mlp, wo):
    rows, half = q.shape
    part = jax.ShapeDtypeStruct((rows, WIDTHS[0]), jnp.bfloat16)
    blocks = table.shape[0] * table.shape[1]
    send, keep, att, _ = pl.pallas_call(
        attend_kernel,
        out_shape=(
            part,
            part,
            jax.ShapeDtypeStruct(q.shape, jnp.bfloat16),
            jax.ShapeDtypeStruct(table.shape, jnp.bfloat16),
        ),
        in_specs=[whole(pltpu.SMEM)] + vmem(6),
        out_specs=tuple(vmem(4)),
        input_output_aliases={4: 3},
        compiler_params=params(16),
        cost_estimate=pl.CostEstimate(
            flops=20 * rows * half * (D + 8 * 8 * BLOCK),
            bytes_accessed=40 * blocks * BLOCK * half + 20 * half * D + 40 * rows * D,
            transcendentals=rows * 8 * BLOCK * half // HEAD_DIM,
        ),
        name="attend",
    )(adjacency, q, mine, sibling, table, mlp, in_vmem(wo))
    return send, keep, att


def run_project_out(c, att, mlp, wo):
    rows, half = att.shape
    part = jax.ShapeDtypeStruct((rows, WIDTHS[c]), jnp.bfloat16)
    return pl.pallas_call(
        functools.partial(project_out, c),
        out_shape=(part, part),
        in_specs=vmem(3),
        out_specs=tuple(vmem(2)),
        compiler_params=params(8),
        cost_estimate=pl.CostEstimate(
            flops=200 * rows * half * D,
            bytes_accessed=200 * half * D,
            transcendentals=0,
        ),
        name="project_out",
    )(att, mlp, in_vmem(wo))


def combine_kernel(chunks, distances, owners, grid_features, *refs):
    s = lax.axis_index("shard")
    keeps, refs = refs[: len(chunks)], refs[len(chunks) :]
    swaps, outs, ready = refs[: len(chunks)], refs[len(chunks) : -1], refs[-1]
    count = grid_features.shape[0]
    first = columns_of(chunks[0]).start
    names = [owners[t, 0] for t in range(count)]
    ranks = []
    for t in range(count):
        same = [(names[e] == names[t]).astype(jnp.int32) for e in range(t)]
        ranks.append(sum(same, jnp.int32(0)))
    for c, keep, swap in zip(chunks, keeps, swaps):
        columns = columns_of(c)
        place = slice(columns.start - first, columns.stop - first)
        for t in range(count):
            rows = slice(t * BLOCK, (t + 1) * BLOCK)
            partials = keep[rows, :].astype(jnp.float32) + swap[rows, :].astype(jnp.float32)
            residual = grid_features[t, :, columns].astype(jnp.float32)
            ready[t, :, place] = (residual + partials).astype(jnp.bfloat16)
    ready[count] = jnp.zeros(ready.shape[1:], jnp.bfloat16)
    for d, out in zip(distances, outs):
        for j in range(CAP):
            index = jnp.int32(count)
            for t in range(count):
                index = jnp.where((names[t] == s ^ d) & (ranks[t] == j), t, index)
            out[j] = ready[index]


def run_combine(chunks, distances, owners, grid_features, keeps, swaps):
    count, rows, _ = grid_features.shape
    width = sum(WIDTHS[c] for c in chunks)
    slot = jax.ShapeDtypeStruct((CAP, rows, width), jnp.bfloat16)
    return pl.pallas_call(
        functools.partial(combine_kernel, chunks, distances),
        out_shape=(slot,) * len(distances),
        in_specs=[whole(pltpu.SMEM)] + vmem(1 + 2 * len(chunks)),
        out_specs=tuple(vmem(len(distances))),
        scratch_shapes=[pltpu.VMEM((count + 1, rows, width), jnp.bfloat16)],
        compiler_params=params(8),
        cost_estimate=pl.CostEstimate(
            flops=60000 * count * rows * width,
            bytes_accessed=400 * rows * width * (3 * count + CAP * len(distances)),
            transcendentals=0,
        ),
        name="combine",
    )(owners, grid_features, *keeps, *swaps)


def place_kernel(spots, *refs):
    out, sem = refs[-2:]
    s = lax.axis_index("shard")
    copies = []
    for i, (d, first) in enumerate(spots):
        columns = pl.ds(first, refs[i].shape[2])
        slots = pl.ds((s ^ d) * CAP, CAP)
        copies.append(pltpu.make_async_copy(refs[i], out.at[slots, :, columns], sem.at[i]))
        copies[i].start()
    for copy in copies:
        copy.wait()


def run_place(spots, arrived, placed, shape):
    return pl.pallas_call(
        functools.partial(place_kernel, spots),
        out_shape=jax.ShapeDtypeStruct(shape, jnp.bfloat16),
        in_specs=vmem(len(arrived)) + [whole(pltpu.HBM)] * len(placed),
        out_specs=whole(pltpu.HBM),
        scratch_shapes=[pltpu.SemaphoreType.DMA((len(arrived),))],
        input_output_aliases={len(arrived): 0} if placed else {},
        compiler_params=params(4),
        cost_estimate=pl.CostEstimate(
            flops=400000 * sum(part.size for part in arrived), bytes_accessed=0, transcendentals=0
        ),
        name="place",
    )(*arrived, *placed)


def crossed(x, distance, size):
    return lax.ppermute(x, "shard", [(i, i ^ distance) for i in range(size)])


def swapped(x, axis):
    return lax.ppermute(x, axis, [(0, 1), (1, 0)])


def paired(
    grid_features,
    owners,
    adjacency,
    mesh_nodes,
    norm_gain,
    query_weight,
    key_weight,
    value_weight,
    output_weight,
    up_weight,
    down_weight,
):
    shards = lax.axis_size("shard")
    count, rows, half = grid_features.shape
    flat = grid_features.reshape(count * rows, half)
    half_unit = run_pick(mesh_nodes)
    far = crossed(half_unit, 2, shards)
    waiting, _ = lax.optimization_barrier((mesh_nodes, half_unit))
    near = crossed(waiting, 1, shards)
    waiting, _ = lax.optimization_barrier((flat, half_unit))
    other = swapped(waiting, "head")
    flat, gain, wq, wup, wdn, mesh, rest = run_stage(
        (
            flat,
            norm_gain.reshape(1, -1),
            query_weight,
            up_weight,
            down_weight,
            mesh_nodes,
            mesh_nodes,
        ),
        (None, 1, 0, 0, 1, None, "rest"),
    )
    straight = crossed(rest, 3, shards)
    far, _ = lax.optimization_barrier((far, rest))
    farther = crossed(far, 1, shards)
    far_pair = swapped(far, "head")
    queries, mlp = run_mlp(flat, other, gain, wq, wup, wdn)
    queries, mlp, far_pair, near = lax.optimization_barrier((queries, mlp, far_pair, near))
    blocked = (-1, BLOCK, 2 * half)
    mine_a = run_project((mesh, near, far, far_pair), key_weight, value_weight)
    sibling_a = swapped(mine_a, "sub")
    table = run_table(mine_a.reshape(blocked), sibling_a.reshape(blocked), 2 * shards)
    mine_b = run_project((farther, straight), key_weight, value_weight)
    sibling_b = swapped(mine_b, "sub")
    send, keep, att = run_attend(
        adjacency, queries, mine_b.reshape(blocked), sibling_b.reshape(blocked), table, mlp, output_weight
    )
    keeps, swaps, slots, placed = [], [], [], []
    shape = (shards * CAP, rows, half)
    for c in range(len(WIDTHS)):
        if c > 0:
            send, keep = run_project_out(c, att, mlp, output_weight)
        received = swapped(send, "head")
        if c > 0:
            received, _ = lax.optimization_barrier((received, slots[c - 1][0]))
        slots.append(run_combine((c,), (2, 3), owners, grid_features, (keep,), (received,)))
        keeps.append(keep)
        swaps.append(received)
    every = tuple(range(len(WIDTHS)))
    swaps[-1], _ = lax.optimization_barrier((swaps[-1], slots[-1][0]))
    near_slots, own_slots = run_combine(every, (1, 0), owners, grid_features, keeps, swaps)
    for c in every:
        first = columns_of(c).start
        spots = [(2, first), (3, first)]
        arrived = [crossed(slot, d, shards) for d, slot in zip((2, 3), slots[c])]
        if c == 0:
            spots.append((0, 0))
            arrived.append(own_slots)
        if c == len(WIDTHS) - 1:
            spots.append((1, 0))
            arrived.append(crossed(near_slots, 1, shards))
        placed = [run_place(spots, arrived, placed, shape)]
    return placed[0]


def attend_plain(queries, key_table, value_table, chosen, scaling):
    count = chosen.shape[0]
    picked_keys = key_table[chosen]
    picked_keys = picked_keys.reshape(count, -1, picked_keys.shape[3], picked_keys.shape[4])
    picked_values = value_table[chosen]
    picked_values = picked_values.reshape(count, -1, picked_values.shape[3], picked_values.shape[4])
    scores = (
        jnp.einsum("gqhe,gkhe->ghqk", queries, picked_keys, preferred_element_type=jnp.float32)
        * scaling
    )
    highest = jnp.max(scores, axis=-1, keepdims=True)
    weights = jnp.exp(scores - highest)
    weights = (weights / jnp.sum(weights, axis=-1, keepdims=True)).astype(jnp.bfloat16)
    result = jnp.einsum(
        "ghqk,gkhe->gqhe", weights, picked_values, preferred_element_type=jnp.float32
    )
    return result.astype(jnp.bfloat16)


def general(
    grid_features,
    owners,
    adjacency,
    mesh_nodes,
    norm_gain,
    query_weight,
    key_weight,
    value_weight,
    output_weight,
    up_weight,
    down_weight,
):
    shard_count = lax.axis_size("shard")
    head_count = lax.axis_size("head")
    local_blocks, block_rows, feature_share = grid_features.shape
    slots = shard_count * CAP
    owner_col = owners[:, 0]
    position = jnp.arange(local_blocks, dtype=jnp.int32)
    earlier = (owner_col[:, None] == owner_col[None, :]) & (position[None, :] < position[:, None])
    target = owner_col * CAP + jnp.sum(earlier.astype(jnp.int32), axis=1)
    dispatch = (target[:, None] == jnp.arange(slots, dtype=jnp.int32)[None, :]).astype(jnp.bfloat16)
    offset = lax.axis_index("head") * (D // head_count)
    projected = jnp.stack(
        (
            jnp.dot(mesh_nodes, key_weight, preferred_element_type=jnp.float32).astype(
                jnp.bfloat16
            ),
            jnp.dot(mesh_nodes, value_weight, preferred_element_type=jnp.float32).astype(
                jnp.bfloat16
            ),
        )
    )
    tables = lax.all_gather(projected, ("shard", "sub"), axis=1, tiled=True)
    head_local = query_weight.shape[1] // HEAD_DIM
    key_table = tables[0].reshape(-1, block_rows, head_local, HEAD_DIM)
    value_table = tables[1].reshape(-1, block_rows, head_local, HEAD_DIM)
    send_lists = jnp.full((slots, adjacency.shape[1]), -1, jnp.int32).at[target].set(adjacency)
    send_lists = send_lists.reshape(shard_count, CAP, -1)
    complete = lax.all_gather(grid_features, "head", axis=2, tiled=True)
    outgoing = jnp.einsum(
        "gs,gbd->sbd", dispatch, complete, preferred_element_type=jnp.float32
    ).astype(jnp.bfloat16)
    arrived, lists = (
        lax.all_to_all(
            outgoing.reshape(shard_count, CAP, block_rows, D),
            "shard",
            split_axis=0,
            concat_axis=0,
            tiled=True,
        ),
        lax.all_to_all(send_lists, "shard", split_axis=0, concat_axis=0, tiled=True),
    )
    arrived = arrived.reshape(slots, block_rows, D)
    residual = lax.dynamic_slice_in_dim(arrived, offset, D // head_count, 2)
    lists = lists.reshape(slots, -1)
    count = arrived.shape[0]
    values_f = arrived.astype(jnp.float32)
    average = jnp.mean(values_f, axis=-1, keepdims=True)
    centered = values_f - average
    variance = jnp.mean(centered * centered, axis=-1, keepdims=True)
    normed = (centered * lax.rsqrt(variance + epsilon) * norm_gain).astype(jnp.bfloat16)
    flattened = normed.reshape(-1, D)
    queries = jnp.dot(flattened, query_weight, preferred_element_type=jnp.float32).astype(
        jnp.bfloat16
    )
    blocks_each = math.gcd(count, max(1, 512 // block_rows))
    steps_count = count // blocks_each
    queries = queries.reshape(steps_count, blocks_each, block_rows, head_local, HEAD_DIM)

    def attend_step(operands):
        return attend_plain(operands[0], key_table, value_table, operands[1], HEAD_DIM ** (-0.5))

    attended = lax.map(
        attend_step, (queries, jnp.maximum(lists, 0).reshape(steps_count, blocks_each, -1))
    )
    attended = attended.reshape(-1, head_local * HEAD_DIM)
    hidden = jax.nn.gelu(
        jnp.dot(flattened, up_weight, preferred_element_type=jnp.float32), approximate=False
    ).astype(jnp.bfloat16)
    branch = jnp.dot(attended, output_weight, preferred_element_type=jnp.float32)
    branch = branch + jnp.dot(hidden, down_weight, preferred_element_type=jnp.float32)
    branch = branch.reshape(count, block_rows, D)
    reduced = lax.psum_scatter(
        branch.astype(jnp.bfloat16), "head", scatter_dimension=2, tiled=True
    ).astype(jnp.float32)
    occupied = lists[:, 0] >= 0
    summed = residual.astype(jnp.float32) + reduced
    return jnp.where(occupied[:, None, None], summed, 0.0).astype(jnp.bfloat16)


def local(grid_features, owners, adjacency, mesh_nodes, *parameters):
    sizes = [lax.axis_size(axis) for axis in ("shard", "head", "sub")]
    small = grid_features.shape[:2] == (4, BLOCK) and mesh_nodes.shape[0] == 2 * BLOCK
    if sizes == [4, 2, 2] and small and grid_features.shape[2] == 512:
        return paired(grid_features, owners, adjacency, mesh_nodes, *parameters)
    return general(grid_features, owners, adjacency, mesh_nodes, *parameters)


def solution(mesh):
    return jax.shard_map(
        local,
        mesh=mesh,
        in_specs=(
            P(("groups", "shard", "sub"), None, "head"),
            P(("groups", "shard", "sub"), None),
            P(("groups", "shard", "sub"), None),
            P(("groups", "shard", "sub"), None),
            P(),
            P(None, "head"),
            P(None, "head"),
            P(None, "head"),
            P("head", None),
            P(None, "head"),
            P("head", None),
        ),
        out_specs=P(("groups", "shard", "sub"), None, "head"),
        check_vma=False,
    )
```

```python
import functools
import math

import jax
import jax.numpy as jnp
from jax import lax
from jax.experimental import pallas as pl
from jax.experimental.pallas import tpu as pltpu
from jax.sharding import PartitionSpec as P

D = 1024
HEAD_DIM = 64
CAP = 2
BLOCK = 64
QUAD = 4
WIDE = QUAD * HEAD_DIM
WIDTHS = (128, 384)
MIB = 1 << 20


epsilon = 1e-05


def dot(a, b):
    return jnp.dot(a, b, preferred_element_type=jnp.float32)


def gelu(x):
    return 0.5 * x * (1.0 + lax.erf(x * (2.0**-0.5)))


def in_hbm(x):
    return pltpu.with_memory_space_constraint(x, pltpu.HBM)


def in_vmem(x):
    return pltpu.with_memory_space_constraint(x, pltpu.VMEM)


def whole(space):
    return pl.BlockSpec(memory_space=space)


def vmem(count):
    return [whole(pltpu.VMEM)] * count


def params(mib):
    return pltpu.CompilerParams(vmem_limit_bytes=mib * MIB)


def mlp_kernel(own, other, gain, wq, wup, wdn, q_out, mlp_out, normed_s):
    half = own.shape[1]
    units = wup.shape[1]
    chunk = units // 4
    x_other = other[...].astype(jnp.float32)
    x_own = own[...].astype(jnp.float32)

    def mean(a, b):
        total = jnp.sum(a, axis=-1, keepdims=True) + jnp.sum(b, axis=-1, keepdims=True)
        return total * (0.5 / half)

    average = mean(x_other, x_own)
    x_other = x_other - average
    x_own = x_own - average
    factor = lax.rsqrt(mean(x_other * x_other, x_own * x_own) + epsilon)
    normed_s[:, :half] = (x_other * factor * gain[:, :half]).astype(jnp.bfloat16)
    normed_s[:, half:] = (x_own * factor * gain[:, half:]).astype(jnp.bfloat16)
    normed = normed_s[...]
    q_out[...] = dot(normed, wq[...]).astype(jnp.bfloat16)
    for c in range(units // chunk):
        span = slice(c * chunk, (c + 1) * chunk)
        hidden = gelu(dot(normed, wup[:, span])).astype(jnp.bfloat16)
        term = dot(hidden, wdn[span, :])
        if c == 0:
            mlp_out[...] = term
        else:
            mlp_out[...] += term


def run_mlp(own, other, gain, wq, wup, wdn):
    rows = own.shape[0]
    width = wq.shape[0]
    units = wup.shape[1]
    return pl.pallas_call(
        mlp_kernel,
        out_shape=(
            jax.ShapeDtypeStruct((rows, wq.shape[1]), jnp.bfloat16),
            jax.ShapeDtypeStruct((rows, width), jnp.float32),
        ),
        in_specs=vmem(6),
        out_specs=tuple(vmem(2)),
        scratch_shapes=[pltpu.VMEM((rows, width), jnp.bfloat16)],
        compiler_params=params(16),
        cost_estimate=pl.CostEstimate(
            flops=2 * rows * width * (wq.shape[1] + 2 * units),
            bytes_accessed=2 * width * (wq.shape[1] + 2 * units),
            transcendentals=rows * units,
        ),
        name="mlp",
    )(own, other, gain, wq, wup, wdn)


def pick_kernel(mesh, out, sem):
    first = pl.multiple_of(lax.axis_index("head") * BLOCK, BLOCK)
    copy = pltpu.make_async_copy(mesh.at[pl.ds(first, BLOCK), :], out, sem)
    copy.start()
    copy.wait()


def run_pick(mesh):
    return pl.pallas_call(
        pick_kernel,
        out_shape=jax.ShapeDtypeStruct((BLOCK, mesh.shape[1]), mesh.dtype),
        in_specs=[whole(pltpu.HBM)],
        out_specs=whole(pltpu.VMEM),
        scratch_shapes=[pltpu.SemaphoreType.DMA(())],
        compiler_params=params(4),
        cost_estimate=pl.CostEstimate(flops=0, bytes_accessed=4 * mesh.size, transcendentals=0),
        name="pick",
    )(in_hbm(mesh))


def stage_kernel(axes, *refs):
    sources, targets, sem = refs[: len(axes)], refs[len(axes) : -1], refs[-1]
    h = lax.axis_index("head")
    copies = []

    def add(source, target):
        pieces = 2 if source.shape[0] >= 512 else 1
        rows = source.shape[0] // pieces
        for piece in range(pieces):
            span = pl.ds(piece * rows, rows)
            copies.append(
                pltpu.make_async_copy(
                    source.at[span, :], target.at[span, :], sem.at[len(copies)]
                )
            )
            copies[-1].start()

    for source, target, axis in zip(sources, targets, axes):
        if axis is None:
            add(source, target)
            continue
        if axis == "rest":
            add(source.at[pl.ds(pl.multiple_of((1 - h) * BLOCK, BLOCK), BLOCK), :], target)
            continue
        half = source.shape[axis] // 2
        for part, head in enumerate((1 - h, h)):
            span = pl.ds(pl.multiple_of(head * half, half), half)
            place = pl.ds(part * half, half)
            if axis == 0:
                add(source.at[span, :], target.at[place, :])
            else:
                add(source.at[:, span], target.at[:, place])
    for copy in copies:
        copy.wait()


def run_stage(arrays, axes):
    size = sum(2 * array.size for array in arrays)
    return pl.pallas_call(
        functools.partial(stage_kernel, axes),
        out_shape=tuple(
            jax.ShapeDtypeStruct((BLOCK,) + array.shape[1:] if axis == "rest" else array.shape, array.dtype)
            for array, axis in zip(arrays, axes)
        ),
        in_specs=[whole(pltpu.HBM)] * len(arrays),
        out_specs=tuple(vmem(len(arrays))),
        scratch_shapes=[pltpu.SemaphoreType.DMA((4 * len(arrays),))],
        compiler_params=params(16),
        cost_estimate=pl.CostEstimate(
            flops=2000 * size, bytes_accessed=20 * size, transcendentals=0
        ),
        name="stage",
    )(*(in_hbm(array) for array in arrays))


def project_kernel(*refs):
    pieces, (wk, wv, out) = refs[:-3], refs[-3:]
    width = wk.shape[1]
    rows = jnp.concatenate([piece[...] for piece in pieces], axis=0)
    out[:, :width] = dot(rows, wk[...]).astype(jnp.bfloat16)
    out[:, width:] = dot(rows, wv[...]).astype(jnp.bfloat16)


def run_project(pieces, wk, wv):
    rows = sum(piece.shape[0] for piece in pieces)
    depth, width = wk.shape
    return pl.pallas_call(
        project_kernel,
        out_shape=jax.ShapeDtypeStruct((rows, 2 * width), jnp.bfloat16),
        in_specs=vmem(len(pieces) + 2),
        out_specs=whole(pltpu.VMEM),
        compiler_params=params(8),
        cost_estimate=pl.CostEstimate(
            flops=300 * rows * depth * width,
            bytes_accessed=300 * depth * width + 300 * rows * depth,
            transcendentals=0,
        ),
        name="project",
    )(*pieces, in_vmem(wk), in_vmem(wv))


def table_kernel(mine, sibling, table):
    table[0, : mine.shape[0]] = mine[...]
    table[1, : mine.shape[0]] = sibling[...]


def run_table(mine, sibling, blocks):
    return pl.pallas_call(
        table_kernel,
        out_shape=jax.ShapeDtypeStruct((2, blocks) + mine.shape[1:], jnp.bfloat16),
        in_specs=vmem(2),
        out_specs=whole(pltpu.VMEM),
        compiler_params=params(8),
        cost_estimate=pl.CostEstimate(
            flops=0, bytes_accessed=80 * mine.size, transcendentals=0
        ),
        name="table",
    )(mine, sibling)


def columns_of(c):
    return slice(sum(WIDTHS[:c]), sum(WIDTHS[: c + 1]))


def project_out(c, att, mlp, wo, send, keep):
    half = att.shape[1]
    chunk = columns_of(c)
    h = lax.axis_index("head")

    def write(head):
        for out, first, place in ((send, 0, 1 - head), (keep, half, head)):
            extra = mlp[:, first + chunk.start : first + chunk.stop]
            span = slice(place * half + chunk.start, place * half + chunk.stop)
            out[...] = (extra + dot(att[...], wo[:, span])).astype(jnp.bfloat16)

    for head in range(2):
        pl.when(h == head)(functools.partial(write, head))


def attend_kernel(
    adjacency, q, mine, sibling, table_in, mlp, wo, send, keep, att, table
):
    del table_in
    s = lax.axis_index("shard")
    h = lax.axis_index("head")
    u = lax.axis_index("sub")
    half = wo.shape[0]
    ready = table.shape[1] - mine.shape[0]
    for i, part in enumerate((mine, sibling)):
        table[i, ready:] = part[...]
    rows_of = lax.broadcasted_iota(jnp.int32, (WIDE, WIDE), 0) // BLOCK
    lanes_of = lax.broadcasted_iota(jnp.int32, (WIDE, WIDE), 1) // HEAD_DIM
    diagonal = rows_of == lanes_of
    lane_head = lax.broadcasted_iota(jnp.int32, (BLOCK, WIDE), 1) // HEAD_DIM
    scale = HEAD_DIM**-0.5 * math.log2(math.e)
    groups = half // WIDE
    places = []
    for b in range(adjacency.shape[0]):
        places.append([])
        for j in range(adjacency.shape[1]):
            m = adjacency[b, j]
            part = lax.rem(m, 2)
            core = lax.rem(m // 2, 2)
            distance = s ^ (m // 4)
            part = jnp.where(distance <= 1, part, part ^ h)
            places[b].append((core ^ u, distance * 2 + part))

    def scores_of(step):
        b, g = divmod(step, groups)
        columns = slice(g * WIDE, (g + 1) * WIDE)
        keys = jnp.concatenate([table[i, p, :, columns] for i, p in places[b]], axis=0)
        stacked = jnp.concatenate([q[b * BLOCK : (b + 1) * BLOCK, columns]] * QUAD, axis=0)
        stacked = jnp.where(diagonal, stacked, jnp.zeros_like(stacked))
        return lax.dot_general(
            stacked, keys, (((1,), (1,)), ((), ())), preferred_element_type=jnp.float32
        )

    steps = len(places) * groups
    scores = scores_of(0)
    for step in range(steps):
        following = scores_of(step + 1) if step + 1 < steps else None
        b, g = divmod(step, groups)
        columns = slice(half + g * WIDE, half + (g + 1) * WIDE)
        values = jnp.concatenate([table[i, p, :, columns] for i, p in places[b]], axis=0)
        highest = jnp.max(scores, axis=-1, keepdims=True)
        weights = jnp.exp2((scores - highest) * scale)
        total = jnp.sum(weights, axis=-1, keepdims=True)
        mixed = dot(weights.astype(jnp.bfloat16), values) * (1.0 / total)
        merged = mixed[0:BLOCK, :]
        for i in range(1, QUAD):
            merged = jnp.where(lane_head == i, mixed[i * BLOCK : (i + 1) * BLOCK, :], merged)
        rows = slice(b * BLOCK, (b + 1) * BLOCK)
        att[rows, g * WIDE : (g + 1) * WIDE] = merged.astype(jnp.bfloat16)
        scores = following
    project_out(0, att, mlp, wo, send, keep)


def run_attend(adjacency, q, mine, sibling, table, mlp, wo):
    rows, half = q.shape
    part = jax.ShapeDtypeStruct((rows, WIDTHS[0]), jnp.bfloat16)
    blocks = table.shape[0] * table.shape[1]
    send, keep, att, _ = pl.pallas_call(
        attend_kernel,
        out_shape=(
            part,
            part,
            jax.ShapeDtypeStruct(q.shape, jnp.bfloat16),
            jax.ShapeDtypeStruct(table.shape, jnp.bfloat16),
        ),
        in_specs=[whole(pltpu.SMEM)] + vmem(6),
        out_specs=tuple(vmem(4)),
        input_output_aliases={4: 3},
        compiler_params=params(16),
        cost_estimate=pl.CostEstimate(
            flops=20 * rows * half * (D + 8 * 8 * BLOCK),
            bytes_accessed=40 * blocks * BLOCK * half + 20 * half * D + 40 * rows * D,
            transcendentals=rows * 8 * BLOCK * half // HEAD_DIM,
        ),
        name="attend",
    )(adjacency, q, mine, sibling, table, mlp, in_vmem(wo))
    return send, keep, att


def run_project_out(c, att, mlp, wo):
    rows, half = att.shape
    part = jax.ShapeDtypeStruct((rows, WIDTHS[c]), jnp.bfloat16)
    return pl.pallas_call(
        functools.partial(project_out, c),
        out_shape=(part, part),
        in_specs=vmem(3),
        out_specs=tuple(vmem(2)),
        compiler_params=params(8),
        cost_estimate=pl.CostEstimate(
            flops=200 * rows * half * D,
            bytes_accessed=200 * half * D,
            transcendentals=0,
        ),
        name="project_out",
    )(att, mlp, in_vmem(wo))


def plan_kernel(owners, masks):
    s = lax.axis_index("shard")
    count = owners.shape[0]
    names = [owners[t, 0] for t in range(count)]
    for t in range(count):
        same = [(names[e] == names[t]).astype(jnp.int32) for e in range(t)]
        rank = sum(same, jnp.int32(0))
        for d in range(masks.shape[0]):
            for j in range(CAP):
                hit = (names[t] == s ^ d) & (rank == j)
                masks[d, j, t] = jnp.full(masks.shape[3:], hit.astype(jnp.float32))


def run_plan(owners, shards):
    return pl.pallas_call(
        plan_kernel,
        out_shape=jax.ShapeDtypeStruct((shards, CAP, owners.shape[0], 8, 128), jnp.float32),
        in_specs=[whole(pltpu.SMEM)],
        out_specs=whole(pltpu.VMEM),
        compiler_params=params(4),
        cost_estimate=pl.CostEstimate(flops=0, bytes_accessed=1 << 18, transcendentals=0),
        name="plan",
    )(owners)


def combine_kernel(chunks, distances, masks, grid_features, *refs):
    keeps, refs = refs[: len(chunks)], refs[len(chunks) :]
    swaps, outs = refs[: len(chunks)], refs[len(chunks) :]
    count = grid_features.shape[0]
    first = columns_of(chunks[0]).start
    for c, keep, swap in zip(chunks, keeps, swaps):
        columns = columns_of(c)
        place = slice(columns.start - first, columns.stop - first)
        updated = []
        for t in range(count):
            rows = slice(t * BLOCK, (t + 1) * BLOCK)
            partials = keep[rows, :].astype(jnp.float32) + swap[rows, :].astype(jnp.float32)
            updated.append(grid_features[t, :, columns].astype(jnp.float32) + partials)
        for d, out in zip(distances, outs):
            for j in range(CAP):
                chosen = jnp.zeros_like(updated[0])
                for t in range(count):
                    row = jnp.concatenate([masks[d, j, t, 0:1, :]] * (WIDTHS[c] // 128), axis=1)
                    chosen = jnp.where(jnp.broadcast_to(row, chosen.shape) > 0.5, updated[t], chosen)
                out[j, :, place] = chosen.astype(jnp.bfloat16)


def run_combine(chunks, distances, masks, grid_features, keeps, swaps):
    count, rows, _ = grid_features.shape
    width = sum(WIDTHS[c] for c in chunks)
    slot = jax.ShapeDtypeStruct((CAP, rows, width), jnp.bfloat16)
    return pl.pallas_call(
        functools.partial(combine_kernel, chunks, distances),
        out_shape=(slot,) * len(distances),
        in_specs=vmem(2 + 2 * len(chunks)),
        out_specs=tuple(vmem(len(distances))),
        compiler_params=params(8),
        cost_estimate=pl.CostEstimate(
            flops=60000 * count * rows * width,
            bytes_accessed=400 * rows * width * (3 * count + CAP * len(distances)),
            transcendentals=0,
        ),
        name="combine",
    )(masks, grid_features, *keeps, *swaps)


def place_kernel(spots, *refs):
    out, sem = refs[-2:]
    s = lax.axis_index("shard")
    copies = []
    for i, (d, first) in enumerate(spots):
        columns = pl.ds(first, refs[i].shape[2])
        slots = pl.ds((s ^ d) * CAP, CAP)
        copies.append(pltpu.make_async_copy(refs[i], out.at[slots, :, columns], sem.at[i]))
        copies[i].start()
    for copy in copies:
        copy.wait()


def run_place(spots, arrived, placed, shape):
    return pl.pallas_call(
        functools.partial(place_kernel, spots),
        out_shape=jax.ShapeDtypeStruct(shape, jnp.bfloat16),
        in_specs=vmem(len(arrived)) + [whole(pltpu.HBM)] * len(placed),
        out_specs=whole(pltpu.HBM),
        scratch_shapes=[pltpu.SemaphoreType.DMA((len(arrived),))],
        input_output_aliases={len(arrived): 0} if placed else {},
        compiler_params=params(4),
        cost_estimate=pl.CostEstimate(
            flops=400000 * sum(part.size for part in arrived), bytes_accessed=0, transcendentals=0
        ),
        name="place",
    )(*arrived, *placed)


def crossed(x, distance, size):
    return lax.ppermute(x, "shard", [(i, i ^ distance) for i in range(size)])


def swapped(x, axis):
    return lax.ppermute(x, axis, [(0, 1), (1, 0)])


def paired(
    grid_features,
    owners,
    adjacency,
    mesh_nodes,
    norm_gain,
    query_weight,
    key_weight,
    value_weight,
    output_weight,
    up_weight,
    down_weight,
):
    shards = lax.axis_size("shard")
    count, rows, half = grid_features.shape
    flat = grid_features.reshape(count * rows, half)
    half_unit = run_pick(mesh_nodes)
    far = crossed(half_unit, 2, shards)
    waiting, _ = lax.optimization_barrier((mesh_nodes, half_unit))
    near = crossed(waiting, 1, shards)
    waiting, _ = lax.optimization_barrier((flat, half_unit))
    other = swapped(waiting, "head")
    flat, gain, wq, wup, wdn, mesh, rest = run_stage(
        (
            flat,
            norm_gain.reshape(1, -1),
            query_weight,
            up_weight,
            down_weight,
            mesh_nodes,
            mesh_nodes,
        ),
        (None, 1, 0, 0, 1, None, "rest"),
    )
    straight = crossed(rest, 3, shards)
    far, _ = lax.optimization_barrier((far, rest))
    farther = crossed(far, 1, shards)
    far_pair = swapped(far, "head")
    queries, mlp = run_mlp(flat, other, gain, wq, wup, wdn)
    queries, mlp, far_pair, near = lax.optimization_barrier((queries, mlp, far_pair, near))
    blocked = (-1, BLOCK, 2 * half)
    mine_a = run_project((mesh, near, far, far_pair), key_weight, value_weight)
    sibling_a = swapped(mine_a, "sub")
    named, _ = lax.optimization_barrier((owners, mine_a))
    masks = run_plan(named, shards)
    table = run_table(mine_a.reshape(blocked), sibling_a.reshape(blocked), 2 * shards)
    mine_b = run_project((farther, straight), key_weight, value_weight)
    sibling_b = swapped(mine_b, "sub")
    send, keep, att = run_attend(
        adjacency, queries, mine_b.reshape(blocked), sibling_b.reshape(blocked), table, mlp, output_weight
    )
    keeps, swaps, slots, placed = [], [], [], []
    shape = (shards * CAP, rows, half)
    for c in range(len(WIDTHS)):
        if c > 0:
            send, keep = run_project_out(c, att, mlp, output_weight)
        received = swapped(send, "head")
        if c > 0:
            received, _ = lax.optimization_barrier((received, slots[c - 1][0]))
        slots.append(run_combine((c,), (2, 3), masks, grid_features, (keep,), (received,)))
        keeps.append(keep)
        swaps.append(received)
    every = tuple(range(len(WIDTHS)))
    swaps[-1], _ = lax.optimization_barrier((swaps[-1], slots[-1][0]))
    near_slots, own_slots = run_combine(every, (1, 0), masks, grid_features, keeps, swaps)
    for c in every:
        first = columns_of(c).start
        spots = [(2, first), (3, first)]
        arrived = [crossed(slot, d, shards) for d, slot in zip((2, 3), slots[c])]
        if c == 0:
            spots.append((0, 0))
            arrived.append(own_slots)
        if c == len(WIDTHS) - 1:
            spots.append((1, 0))
            arrived.append(crossed(near_slots, 1, shards))
        placed = [run_place(spots, arrived, placed, shape)]
    return placed[0]


def attend_plain(queries, key_table, value_table, chosen, scaling):
    count = chosen.shape[0]
    picked_keys = key_table[chosen]
    picked_keys = picked_keys.reshape(count, -1, picked_keys.shape[3], picked_keys.shape[4])
    picked_values = value_table[chosen]
    picked_values = picked_values.reshape(count, -1, picked_values.shape[3], picked_values.shape[4])
    scores = (
        jnp.einsum("gqhe,gkhe->ghqk", queries, picked_keys, preferred_element_type=jnp.float32)
        * scaling
    )
    highest = jnp.max(scores, axis=-1, keepdims=True)
    weights = jnp.exp(scores - highest)
    weights = (weights / jnp.sum(weights, axis=-1, keepdims=True)).astype(jnp.bfloat16)
    result = jnp.einsum(
        "ghqk,gkhe->gqhe", weights, picked_values, preferred_element_type=jnp.float32
    )
    return result.astype(jnp.bfloat16)


def general(
    grid_features,
    owners,
    adjacency,
    mesh_nodes,
    norm_gain,
    query_weight,
    key_weight,
    value_weight,
    output_weight,
    up_weight,
    down_weight,
):
    shard_count = lax.axis_size("shard")
    head_count = lax.axis_size("head")
    local_blocks, block_rows, feature_share = grid_features.shape
    slots = shard_count * CAP
    owner_col = owners[:, 0]
    position = jnp.arange(local_blocks, dtype=jnp.int32)
    earlier = (owner_col[:, None] == owner_col[None, :]) & (position[None, :] < position[:, None])
    target = owner_col * CAP + jnp.sum(earlier.astype(jnp.int32), axis=1)
    dispatch = (target[:, None] == jnp.arange(slots, dtype=jnp.int32)[None, :]).astype(jnp.bfloat16)
    offset = lax.axis_index("head") * (D // head_count)
    projected = jnp.stack(
        (
            jnp.dot(mesh_nodes, key_weight, preferred_element_type=jnp.float32).astype(
                jnp.bfloat16
            ),
            jnp.dot(mesh_nodes, value_weight, preferred_element_type=jnp.float32).astype(
                jnp.bfloat16
            ),
        )
    )
    tables = lax.all_gather(projected, ("shard", "sub"), axis=1, tiled=True)
    head_local = query_weight.shape[1] // HEAD_DIM
    key_table = tables[0].reshape(-1, block_rows, head_local, HEAD_DIM)
    value_table = tables[1].reshape(-1, block_rows, head_local, HEAD_DIM)
    send_lists = jnp.full((slots, adjacency.shape[1]), -1, jnp.int32).at[target].set(adjacency)
    send_lists = send_lists.reshape(shard_count, CAP, -1)
    complete = lax.all_gather(grid_features, "head", axis=2, tiled=True)
    outgoing = jnp.einsum(
        "gs,gbd->sbd", dispatch, complete, preferred_element_type=jnp.float32
    ).astype(jnp.bfloat16)
    arrived, lists = (
        lax.all_to_all(
            outgoing.reshape(shard_count, CAP, block_rows, D),
            "shard",
            split_axis=0,
            concat_axis=0,
            tiled=True,
        ),
        lax.all_to_all(send_lists, "shard", split_axis=0, concat_axis=0, tiled=True),
    )
    arrived = arrived.reshape(slots, block_rows, D)
    residual = lax.dynamic_slice_in_dim(arrived, offset, D // head_count, 2)
    lists = lists.reshape(slots, -1)
    count = arrived.shape[0]
    values_f = arrived.astype(jnp.float32)
    average = jnp.mean(values_f, axis=-1, keepdims=True)
    centered = values_f - average
    variance = jnp.mean(centered * centered, axis=-1, keepdims=True)
    normed = (centered * lax.rsqrt(variance + epsilon) * norm_gain).astype(jnp.bfloat16)
    flattened = normed.reshape(-1, D)
    queries = jnp.dot(flattened, query_weight, preferred_element_type=jnp.float32).astype(
        jnp.bfloat16
    )
    blocks_each = math.gcd(count, max(1, 512 // block_rows))
    steps_count = count // blocks_each
    queries = queries.reshape(steps_count, blocks_each, block_rows, head_local, HEAD_DIM)

    def attend_step(operands):
        return attend_plain(operands[0], key_table, value_table, operands[1], HEAD_DIM ** (-0.5))

    attended = lax.map(
        attend_step, (queries, jnp.maximum(lists, 0).reshape(steps_count, blocks_each, -1))
    )
    attended = attended.reshape(-1, head_local * HEAD_DIM)
    hidden = jax.nn.gelu(
        jnp.dot(flattened, up_weight, preferred_element_type=jnp.float32), approximate=False
    ).astype(jnp.bfloat16)
    branch = jnp.dot(attended, output_weight, preferred_element_type=jnp.float32)
    branch = branch + jnp.dot(hidden, down_weight, preferred_element_type=jnp.float32)
    branch = branch.reshape(count, block_rows, D)
    reduced = lax.psum_scatter(
        branch.astype(jnp.bfloat16), "head", scatter_dimension=2, tiled=True
    ).astype(jnp.float32)
    occupied = lists[:, 0] >= 0
    summed = residual.astype(jnp.float32) + reduced
    return jnp.where(occupied[:, None, None], summed, 0.0).astype(jnp.bfloat16)


def local(grid_features, owners, adjacency, mesh_nodes, *parameters):
    sizes = [lax.axis_size(axis) for axis in ("shard", "head", "sub")]
    small = grid_features.shape[:2] == (4, BLOCK) and mesh_nodes.shape[0] == 2 * BLOCK
    if sizes == [4, 2, 2] and small and grid_features.shape[2] == 512:
        return paired(grid_features, owners, adjacency, mesh_nodes, *parameters)
    return general(grid_features, owners, adjacency, mesh_nodes, *parameters)


def solution(mesh):
    return jax.shard_map(
        local,
        mesh=mesh,
        in_specs=(
            P(("groups", "shard", "sub"), None, "head"),
            P(("groups", "shard", "sub"), None),
            P(("groups", "shard", "sub"), None),
            P(("groups", "shard", "sub"), None),
            P(),
            P(None, "head"),
            P(None, "head"),
            P(None, "head"),
            P("head", None),
            P(None, "head"),
            P("head", None),
        ),
        out_specs=P(("groups", "shard", "sub"), None, "head"),
        check_vma=False,
    )
```

```python
import functools
import math

import jax
import jax.numpy as jnp
from jax import lax
from jax.experimental import pallas as pl
from jax.experimental.pallas import tpu as pltpu
from jax.sharding import PartitionSpec as P

D = 1024
HEAD_DIM = 64
CAP = 2
BLOCK = 64
QUAD = 4
WIDE = QUAD * HEAD_DIM
TILE = 128
CHUNKS = ((0, 96), (96, 256))
MIB = 1 << 20


epsilon = 1e-05


def dot(a, b):
    return jnp.dot(a, b, preferred_element_type=jnp.float32)


def gelu(x):
    return 0.5 * x * (1.0 + lax.erf(x * (2.0**-0.5)))


def in_hbm(x):
    return pltpu.with_memory_space_constraint(x, pltpu.HBM)


def in_vmem(x):
    return pltpu.with_memory_space_constraint(x, pltpu.VMEM)


def whole(space):
    return pl.BlockSpec(memory_space=space)


def vmem(count):
    return [whole(pltpu.VMEM)] * count


def params(mib):
    return pltpu.CompilerParams(vmem_limit_bytes=mib * MIB)


def mlp_kernel(own, other, gain, wq, wup, wdn, q_out, mlp_out, normed_s):
    half = own.shape[1]
    units = wup.shape[1]
    chunk = units // 4
    x_other = other[...].astype(jnp.float32)
    x_own = own[...].astype(jnp.float32)

    def mean(a, b):
        total = jnp.sum(a, axis=-1, keepdims=True) + jnp.sum(b, axis=-1, keepdims=True)
        return total * (0.5 / half)

    average = mean(x_other, x_own)
    x_other = x_other - average
    x_own = x_own - average
    factor = lax.rsqrt(mean(x_other * x_other, x_own * x_own) + epsilon)
    normed_s[:, :half] = (x_other * factor * gain[:, :half]).astype(jnp.bfloat16)
    normed_s[:, half:] = (x_own * factor * gain[:, half:]).astype(jnp.bfloat16)
    normed = normed_s[...]
    q_out[...] = dot(normed, wq[...]).astype(jnp.bfloat16)
    for c in range(units // chunk):
        span = slice(c * chunk, (c + 1) * chunk)
        hidden = gelu(dot(normed, wup[:, span])).astype(jnp.bfloat16)
        term = dot(hidden, wdn[span, :])
        if c == 0:
            mlp_out[...] = term
        else:
            mlp_out[...] += term


def run_mlp(own, other, gain, wq, wup, wdn):
    rows = own.shape[0]
    width = wq.shape[0]
    units = wup.shape[1]
    return pl.pallas_call(
        mlp_kernel,
        out_shape=(
            jax.ShapeDtypeStruct((rows, wq.shape[1]), jnp.bfloat16),
            jax.ShapeDtypeStruct((rows, width), jnp.float32),
        ),
        in_specs=vmem(6),
        out_specs=tuple(vmem(2)),
        scratch_shapes=[pltpu.VMEM((rows, width), jnp.bfloat16)],
        compiler_params=params(16),
        cost_estimate=pl.CostEstimate(
            flops=2 * rows * width * (wq.shape[1] + 2 * units),
            bytes_accessed=2 * width * (wq.shape[1] + 2 * units),
            transcendentals=rows * units,
        ),
        name="mlp",
    )(own, other, gain, wq, wup, wdn)


def pick_kernel(mesh, out, sem):
    first = pl.multiple_of(lax.axis_index("head") * BLOCK, BLOCK)
    copy = pltpu.make_async_copy(mesh.at[pl.ds(first, BLOCK), :], out, sem)
    copy.start()
    copy.wait()


def run_pick(mesh):
    return pl.pallas_call(
        pick_kernel,
        out_shape=jax.ShapeDtypeStruct((BLOCK, mesh.shape[1]), mesh.dtype),
        in_specs=[whole(pltpu.HBM)],
        out_specs=whole(pltpu.VMEM),
        scratch_shapes=[pltpu.SemaphoreType.DMA(())],
        compiler_params=params(4),
        cost_estimate=pl.CostEstimate(flops=0, bytes_accessed=4 * mesh.size, transcendentals=0),
        name="pick",
    )(in_hbm(mesh))


def stage_kernel(axes, *refs):
    sources, targets, sem = refs[: len(axes)], refs[len(axes) : -1], refs[-1]
    h = lax.axis_index("head")
    copies = []

    def add(source, target):
        pieces = 2 if source.shape[0] >= 512 else 1
        rows = source.shape[0] // pieces
        for piece in range(pieces):
            span = pl.ds(piece * rows, rows)
            copies.append(
                pltpu.make_async_copy(
                    source.at[span, :], target.at[span, :], sem.at[len(copies)]
                )
            )
            copies[-1].start()

    for source, target, axis in zip(sources, targets, axes):
        if axis is None:
            add(source, target)
            continue
        if axis == "rest":
            add(source.at[pl.ds(pl.multiple_of((1 - h) * BLOCK, BLOCK), BLOCK), :], target)
            continue
        half = source.shape[axis] // 2
        for part, head in enumerate((1 - h, h)):
            span = pl.ds(pl.multiple_of(head * half, half), half)
            place = pl.ds(part * half, half)
            if axis == 0:
                add(source.at[span, :], target.at[place, :])
            else:
                add(source.at[:, span], target.at[:, place])
    for copy in copies:
        copy.wait()


def run_stage(arrays, axes):
    size = sum(2 * array.size for array in arrays)
    return pl.pallas_call(
        functools.partial(stage_kernel, axes),
        out_shape=tuple(
            jax.ShapeDtypeStruct((BLOCK,) + array.shape[1:] if axis == "rest" else array.shape, array.dtype)
            for array, axis in zip(arrays, axes)
        ),
        in_specs=[whole(pltpu.HBM)] * len(arrays),
        out_specs=tuple(vmem(len(arrays))),
        scratch_shapes=[pltpu.SemaphoreType.DMA((4 * len(arrays),))],
        compiler_params=params(16),
        cost_estimate=pl.CostEstimate(
            flops=2000 * size, bytes_accessed=20 * size, transcendentals=0
        ),
        name="stage",
    )(*(in_hbm(array) for array in arrays))


def project_kernel(*refs):
    pieces, (wk, wv, out) = refs[:-3], refs[-3:]
    width = wk.shape[1]
    rows = jnp.concatenate([piece[...] for piece in pieces], axis=0)
    out[:, :width] = dot(rows, wk[...]).astype(jnp.bfloat16)
    out[:, width:] = dot(rows, wv[...]).astype(jnp.bfloat16)


def run_project(pieces, wk, wv):
    rows = sum(piece.shape[0] for piece in pieces)
    depth, width = wk.shape
    return pl.pallas_call(
        project_kernel,
        out_shape=jax.ShapeDtypeStruct((rows, 2 * width), jnp.bfloat16),
        in_specs=vmem(len(pieces) + 2),
        out_specs=whole(pltpu.VMEM),
        compiler_params=params(8),
        cost_estimate=pl.CostEstimate(
            flops=300 * rows * depth * width,
            bytes_accessed=300 * depth * width + 300 * rows * depth,
            transcendentals=0,
        ),
        name="project",
    )(*pieces, in_vmem(wk), in_vmem(wv))


def table_kernel(mine, sibling, table):
    table[0, : mine.shape[0]] = mine[...]
    table[1, : mine.shape[0]] = sibling[...]


def run_table(mine, sibling, blocks):
    return pl.pallas_call(
        table_kernel,
        out_shape=jax.ShapeDtypeStruct((2, blocks) + mine.shape[1:], jnp.bfloat16),
        in_specs=vmem(2),
        out_specs=whole(pltpu.VMEM),
        compiler_params=params(8),
        cost_estimate=pl.CostEstimate(
            flops=0, bytes_accessed=80 * mine.size, transcendentals=0
        ),
        name="table",
    )(mine, sibling)


def pieces_of(c):
    low, high = CHUNKS[c]
    pieces = []
    for tile in range(low // BLOCK, -(-high // BLOCK)):
        first, last = max(low, tile * BLOCK), min(high, (tile + 1) * BLOCK)
        rows = slice(first - tile * BLOCK, last - tile * BLOCK)
        pieces.append((tile, rows, slice(first - low, last - low)))
    return pieces


def project_out(c, att, mlp, wo, send, keep):
    half = att.shape[1]
    h = lax.axis_index("head")
    pieces = pieces_of(c)
    start, stop = pieces[0][0] * TILE, (pieces[-1][0] + 1) * TILE

    def write(head):
        for out, first, place in ((send, 0, 1 - head), (keep, half, head)):
            extra = mlp[:, first + start : first + stop]
            total = extra + dot(att[...], wo[:, place * half + start : place * half + stop])
            total = total.astype(jnp.bfloat16)
            for tile, rows, spot in pieces:
                columns = slice(tile * TILE - start, (tile + 1) * TILE - start)
                for t in range(out.shape[0]):
                    block = slice(t * BLOCK + rows.start, t * BLOCK + rows.stop)
                    out[t, spot, :] = total[block, columns]

    for head in range(2):
        pl.when(h == head)(functools.partial(write, head))


def attend_kernel(
    adjacency, q, mine, sibling, table_in, mlp, wo, send, keep, att, table, stacked_s, near_s, sem
):
    del table_in
    s = lax.axis_index("shard")
    h = lax.axis_index("head")
    u = lax.axis_index("sub")
    half = wo.shape[0]
    ready = table.shape[1] - mine.shape[0]
    copy = pltpu.make_async_copy(adjacency, near_s, sem)
    copy.start()
    for i, part in enumerate((mine, sibling)):
        table[i, ready:] = part[...]
    rows_of = lax.broadcasted_iota(jnp.int32, (WIDE, WIDE), 0) // BLOCK
    lanes_of = lax.broadcasted_iota(jnp.int32, (WIDE, WIDE), 1) // HEAD_DIM
    diagonal = rows_of == lanes_of
    lane_head = lax.broadcasted_iota(jnp.int32, (BLOCK, WIDE), 1) // HEAD_DIM
    scale = HEAD_DIM**-0.5 * math.log2(math.e)
    groups = half // WIDE
    steps = near_s.shape[0] * groups
    for step in range(steps):
        b, g = divmod(step, groups)
        columns = slice(g * WIDE, (g + 1) * WIDE)
        stacked = jnp.concatenate([q[b * BLOCK : (b + 1) * BLOCK, columns]] * QUAD, axis=0)
        stacked_s[step] = jnp.where(diagonal, stacked, jnp.zeros_like(stacked))
    copy.wait()
    places = []
    for b in range(near_s.shape[0]):
        places.append([])
        for j in range(near_s.shape[1]):
            m = near_s[b, j]
            part = lax.rem(m, 2)
            core = lax.rem(m // 2, 2)
            distance = s ^ (m // 4)
            part = jnp.where(distance <= 1, part, part ^ h)
            places[b].append((core ^ u, distance * 2 + part))

    def scores_of(step):
        b, g = divmod(step, groups)
        columns = slice(g * WIDE, (g + 1) * WIDE)
        keys = jnp.concatenate([table[i, p, :, columns] for i, p in places[b]], axis=0)
        return lax.dot_general(
            stacked_s[step], keys, (((1,), (1,)), ((), ())), preferred_element_type=jnp.float32
        )

    scores = scores_of(0)
    for step in range(steps):
        following = scores_of(step + 1) if step + 1 < steps else None
        b, g = divmod(step, groups)
        columns = slice(half + g * WIDE, half + (g + 1) * WIDE)
        values = jnp.concatenate([table[i, p, :, columns] for i, p in places[b]], axis=0)
        highest = jnp.max(scores, axis=-1, keepdims=True)
        weights = jnp.exp2((scores - highest) * scale)
        total = jnp.sum(weights, axis=-1, keepdims=True)
        mixed = dot(weights.astype(jnp.bfloat16), values) * (1.0 / total)
        merged = mixed[0:BLOCK, :]
        for i in range(1, QUAD):
            merged = jnp.where(lane_head == i, mixed[i * BLOCK : (i + 1) * BLOCK, :], merged)
        rows = slice(b * BLOCK, (b + 1) * BLOCK)
        att[rows, g * WIDE : (g + 1) * WIDE] = merged.astype(jnp.bfloat16)
        scores = following
    project_out(0, att, mlp, wo, send, keep)


def run_attend(adjacency, q, mine, sibling, table, mlp, wo):
    rows, half = q.shape
    size = CHUNKS[0][1] - CHUNKS[0][0]
    part = jax.ShapeDtypeStruct((rows // BLOCK, size, TILE), jnp.bfloat16)
    blocks = table.shape[0] * table.shape[1]
    send, keep, att, _ = pl.pallas_call(
        attend_kernel,
        out_shape=(
            part,
            part,
            jax.ShapeDtypeStruct(q.shape, jnp.bfloat16),
            jax.ShapeDtypeStruct(table.shape, jnp.bfloat16),
        ),
        in_specs=[whole(pl.ANY)] + vmem(6),
        out_specs=tuple(vmem(4)),
        scratch_shapes=[
            pltpu.VMEM((rows // BLOCK * (half // WIDE), WIDE, WIDE), jnp.bfloat16),
            pltpu.SMEM(adjacency.shape, jnp.int32),
            pltpu.SemaphoreType.DMA(()),
        ],
        input_output_aliases={4: 3},
        compiler_params=params(16),
        cost_estimate=pl.CostEstimate(
            flops=20 * rows * half * (D + 8 * 8 * BLOCK),
            bytes_accessed=40 * blocks * BLOCK * half + 20 * half * D + 40 * rows * D,
            transcendentals=rows * 8 * BLOCK * half // HEAD_DIM,
        ),
        name="attend",
    )(adjacency, q, mine, sibling, table, mlp, in_vmem(wo))
    return send, keep, att


def run_project_out(c, att, mlp, wo):
    rows, half = att.shape
    size = CHUNKS[c][1] - CHUNKS[c][0]
    part = jax.ShapeDtypeStruct((rows // BLOCK, size, TILE), jnp.bfloat16)
    return pl.pallas_call(
        functools.partial(project_out, c),
        out_shape=(part, part),
        in_specs=vmem(3),
        out_specs=tuple(vmem(2)),
        compiler_params=params(8),
        cost_estimate=pl.CostEstimate(
            flops=200 * rows * half * D,
            bytes_accessed=200 * half * D,
            transcendentals=0,
        ),
        name="project_out",
    )(att, mlp, in_vmem(wo))


def plan_kernel(owners, masks):
    s = lax.axis_index("shard")
    count = owners.shape[0]
    names = [owners[t, 0] for t in range(count)]
    for t in range(count):
        same = [(names[e] == names[t]).astype(jnp.int32) for e in range(t)]
        rank = sum(same, jnp.int32(0))
        for d in range(masks.shape[0]):
            for j in range(CAP):
                hit = (names[t] == s ^ d) & (rank == j)
                masks[d, j, t] = jnp.full(masks.shape[3:], hit.astype(jnp.float32))


def run_plan(owners, shards):
    return pl.pallas_call(
        plan_kernel,
        out_shape=jax.ShapeDtypeStruct((shards, CAP, owners.shape[0], 8, 128), jnp.float32),
        in_specs=[whole(pltpu.SMEM)],
        out_specs=whole(pltpu.VMEM),
        compiler_params=params(4),
        cost_estimate=pl.CostEstimate(flops=0, bytes_accessed=1 << 18, transcendentals=0),
        name="plan",
    )(owners)


def combine_kernel(chunks, distances, masks, grid_features, *refs):
    keeps, refs = refs[: len(chunks)], refs[len(chunks) :]
    swaps, outs = refs[: len(chunks)], refs[len(chunks) :]
    count = grid_features.shape[0]
    first = CHUNKS[chunks[0]][0]
    for c, keep, swap in zip(chunks, keeps, swaps):
        low, high = CHUNKS[c]
        updated = []
        for t in range(count):
            residual = [
                grid_features[t, rows, tile * TILE : (tile + 1) * TILE]
                for tile, rows, _ in pieces_of(c)
            ]
            residual = jnp.concatenate(residual, axis=0).astype(jnp.float32)
            partials = keep[t].astype(jnp.float32) + swap[t].astype(jnp.float32)
            updated.append(residual + partials)
        for d, out in zip(distances, outs):
            for j in range(CAP):
                chosen = jnp.zeros_like(updated[0])
                for t in range(count):
                    mask = jnp.broadcast_to(masks[d, j, t, 0:1, :], chosen.shape)
                    chosen = jnp.where(mask > 0.5, updated[t], chosen)
                out[j, low - first : high - first, :] = chosen.astype(jnp.bfloat16)


def run_combine(chunks, distances, masks, grid_features, keeps, swaps):
    count = grid_features.shape[0]
    rows, width = CHUNKS[chunks[-1]][1] - CHUNKS[chunks[0]][0], TILE
    slot = jax.ShapeDtypeStruct((CAP, rows, width), jnp.bfloat16)
    return pl.pallas_call(
        functools.partial(combine_kernel, chunks, distances),
        out_shape=(slot,) * len(distances),
        in_specs=vmem(2 + 2 * len(chunks)),
        out_specs=tuple(vmem(len(distances))),
        compiler_params=params(8),
        cost_estimate=pl.CostEstimate(
            flops=60000 * count * rows * width,
            bytes_accessed=400 * rows * width * (3 * count + CAP * len(distances)),
            transcendentals=0,
        ),
        name="combine",
    )(masks, grid_features, *keeps, *swaps)


def place_kernel(spots, *refs):
    out, sem = refs[-2:]
    s = lax.axis_index("shard")
    copies = []
    for ref, (d, chunks) in zip(refs, spots):
        first = CHUNKS[chunks[0]][0]
        slots = pl.ds((s ^ d) * CAP, CAP)
        for c in chunks:
            shift = CHUNKS[c][0] - first
            for tile, rows, spot in pieces_of(c):
                size = rows.stop - rows.start
                source = ref.at[:, pl.ds(spot.start + shift, size), :]
                columns = pl.ds(tile * TILE, TILE)
                target = out.at[slots, pl.ds(rows.start, size), columns]
                copies.append(pltpu.make_async_copy(source, target, sem.at[len(copies)]))
                copies[-1].start()
    for copy in copies:
        copy.wait()


def run_place(spots, arrived, placed, shape):
    count = sum(len(pieces_of(c)) for _, chunks in spots for c in chunks)
    return pl.pallas_call(
        functools.partial(place_kernel, spots),
        out_shape=jax.ShapeDtypeStruct(shape, jnp.bfloat16),
        in_specs=vmem(len(arrived)) + [whole(pltpu.HBM)] * len(placed),
        out_specs=whole(pltpu.HBM),
        scratch_shapes=[pltpu.SemaphoreType.DMA((count,))],
        input_output_aliases={len(arrived): 0} if placed else {},
        compiler_params=params(4),
        cost_estimate=pl.CostEstimate(
            flops=400000 * sum(part.size for part in arrived), bytes_accessed=0, transcendentals=0
        ),
        name="place",
    )(*arrived, *placed)


def crossed(x, distance, size):
    return lax.ppermute(x, "shard", [(i, i ^ distance) for i in range(size)])


def swapped(x, axis):
    return lax.ppermute(x, axis, [(0, 1), (1, 0)])


def paired(
    grid_features,
    owners,
    adjacency,
    mesh_nodes,
    norm_gain,
    query_weight,
    key_weight,
    value_weight,
    output_weight,
    up_weight,
    down_weight,
):
    shards = lax.axis_size("shard")
    count, rows, half = grid_features.shape
    flat = grid_features.reshape(count * rows, half)
    half_unit = run_pick(mesh_nodes)
    far = crossed(half_unit, 2, shards)
    waiting, _ = lax.optimization_barrier((mesh_nodes, half_unit))
    near = crossed(waiting, 1, shards)
    waiting, _ = lax.optimization_barrier((flat, half_unit))
    other = swapped(waiting, "head")
    flat, gain, wq, wup, wdn, mesh, rest = run_stage(
        (
            flat,
            norm_gain.reshape(1, -1),
            query_weight,
            up_weight,
            down_weight,
            mesh_nodes,
            mesh_nodes,
        ),
        (None, 1, 0, 0, 1, None, "rest"),
    )
    straight = crossed(rest, 3, shards)
    far, _ = lax.optimization_barrier((far, rest))
    farther = crossed(far, 1, shards)
    far_pair = swapped(far, "head")
    queries, mlp = run_mlp(flat, other, gain, wq, wup, wdn)
    queries, mlp, far_pair, near = lax.optimization_barrier((queries, mlp, far_pair, near))
    blocked = (-1, BLOCK, 2 * half)
    mine_a = run_project((mesh, near, far, far_pair), key_weight, value_weight)
    sibling_a = swapped(mine_a, "sub")
    table = run_table(mine_a.reshape(blocked), sibling_a.reshape(blocked), 2 * shards)
    mine_b = run_project((farther, straight), key_weight, value_weight)
    sibling_b = swapped(mine_b, "sub")
    send, keep, att = run_attend(
        adjacency, queries, mine_b.reshape(blocked), sibling_b.reshape(blocked), table, mlp, output_weight
    )
    named, _ = lax.optimization_barrier((owners, att))
    masks = run_plan(named, shards)
    keeps, swaps, slots, placed = [], [], [], []
    shape = (shards * CAP, rows, half)
    every = tuple(range(len(CHUNKS)))
    for c in every:
        if c > 0:
            send, keep = run_project_out(c, att, mlp, output_weight)
        received = swapped(send, "head")
        if c > 0:
            received, _ = lax.optimization_barrier((received, slots[c - 1][0]))
        slots.append(run_combine((c,), (2, 3), masks, grid_features, (keep,), (received,)))
        keeps.append(keep)
        swaps.append(received)
    swaps[-1], _ = lax.optimization_barrier((swaps[-1], slots[-1][0]))
    near_slots, own_slots = run_combine(every, (1, 0), masks, grid_features, keeps, swaps)
    for c in every:
        spots = [(2, (c,)), (3, (c,))]
        arrived = [crossed(slot, d, shards) for d, slot in zip((2, 3), slots[c])]
        if c == 0:
            spots.append((0, every))
            arrived.append(own_slots)
        if c == every[-1]:
            spots.append((1, every))
            arrived.append(crossed(near_slots, 1, shards))
        placed = [run_place(spots, arrived, placed, shape)]
    return placed[0]


def attend_plain(queries, key_table, value_table, chosen, scaling):
    count = chosen.shape[0]
    picked_keys = key_table[chosen]
    picked_keys = picked_keys.reshape(count, -1, picked_keys.shape[3], picked_keys.shape[4])
    picked_values = value_table[chosen]
    picked_values = picked_values.reshape(count, -1, picked_values.shape[3], picked_values.shape[4])
    scores = (
        jnp.einsum("gqhe,gkhe->ghqk", queries, picked_keys, preferred_element_type=jnp.float32)
        * scaling
    )
    highest = jnp.max(scores, axis=-1, keepdims=True)
    weights = jnp.exp(scores - highest)
    weights = (weights / jnp.sum(weights, axis=-1, keepdims=True)).astype(jnp.bfloat16)
    result = jnp.einsum(
        "ghqk,gkhe->gqhe", weights, picked_values, preferred_element_type=jnp.float32
    )
    return result.astype(jnp.bfloat16)


def general(
    grid_features,
    owners,
    adjacency,
    mesh_nodes,
    norm_gain,
    query_weight,
    key_weight,
    value_weight,
    output_weight,
    up_weight,
    down_weight,
):
    shard_count = lax.axis_size("shard")
    head_count = lax.axis_size("head")
    local_blocks, block_rows, feature_share = grid_features.shape
    slots = shard_count * CAP
    owner_col = owners[:, 0]
    position = jnp.arange(local_blocks, dtype=jnp.int32)
    earlier = (owner_col[:, None] == owner_col[None, :]) & (position[None, :] < position[:, None])
    target = owner_col * CAP + jnp.sum(earlier.astype(jnp.int32), axis=1)
    dispatch = (target[:, None] == jnp.arange(slots, dtype=jnp.int32)[None, :]).astype(jnp.bfloat16)
    offset = lax.axis_index("head") * (D // head_count)
    projected = jnp.stack(
        (
            jnp.dot(mesh_nodes, key_weight, preferred_element_type=jnp.float32).astype(
                jnp.bfloat16
            ),
            jnp.dot(mesh_nodes, value_weight, preferred_element_type=jnp.float32).astype(
                jnp.bfloat16
            ),
        )
    )
    tables = lax.all_gather(projected, ("shard", "sub"), axis=1, tiled=True)
    head_local = query_weight.shape[1] // HEAD_DIM
    key_table = tables[0].reshape(-1, block_rows, head_local, HEAD_DIM)
    value_table = tables[1].reshape(-1, block_rows, head_local, HEAD_DIM)
    send_lists = jnp.full((slots, adjacency.shape[1]), -1, jnp.int32).at[target].set(adjacency)
    send_lists = send_lists.reshape(shard_count, CAP, -1)
    complete = lax.all_gather(grid_features, "head", axis=2, tiled=True)
    outgoing = jnp.einsum(
        "gs,gbd->sbd", dispatch, complete, preferred_element_type=jnp.float32
    ).astype(jnp.bfloat16)
    arrived, lists = (
        lax.all_to_all(
            outgoing.reshape(shard_count, CAP, block_rows, D),
            "shard",
            split_axis=0,
            concat_axis=0,
            tiled=True,
        ),
        lax.all_to_all(send_lists, "shard", split_axis=0, concat_axis=0, tiled=True),
    )
    arrived = arrived.reshape(slots, block_rows, D)
    residual = lax.dynamic_slice_in_dim(arrived, offset, D // head_count, 2)
    lists = lists.reshape(slots, -1)
    count = arrived.shape[0]
    values_f = arrived.astype(jnp.float32)
    average = jnp.mean(values_f, axis=-1, keepdims=True)
    centered = values_f - average
    variance = jnp.mean(centered * centered, axis=-1, keepdims=True)
    normed = (centered * lax.rsqrt(variance + epsilon) * norm_gain).astype(jnp.bfloat16)
    flattened = normed.reshape(-1, D)
    queries = jnp.dot(flattened, query_weight, preferred_element_type=jnp.float32).astype(
        jnp.bfloat16
    )
    blocks_each = math.gcd(count, max(1, 512 // block_rows))
    steps_count = count // blocks_each
    queries = queries.reshape(steps_count, blocks_each, block_rows, head_local, HEAD_DIM)

    def attend_step(operands):
        return attend_plain(operands[0], key_table, value_table, operands[1], HEAD_DIM ** (-0.5))

    attended = lax.map(
        attend_step, (queries, jnp.maximum(lists, 0).reshape(steps_count, blocks_each, -1))
    )
    attended = attended.reshape(-1, head_local * HEAD_DIM)
    hidden = jax.nn.gelu(
        jnp.dot(flattened, up_weight, preferred_element_type=jnp.float32), approximate=False
    ).astype(jnp.bfloat16)
    branch = jnp.dot(attended, output_weight, preferred_element_type=jnp.float32)
    branch = branch + jnp.dot(hidden, down_weight, preferred_element_type=jnp.float32)
    branch = branch.reshape(count, block_rows, D)
    reduced = lax.psum_scatter(
        branch.astype(jnp.bfloat16), "head", scatter_dimension=2, tiled=True
    ).astype(jnp.float32)
    occupied = lists[:, 0] >= 0
    summed = residual.astype(jnp.float32) + reduced
    return jnp.where(occupied[:, None, None], summed, 0.0).astype(jnp.bfloat16)


def local(grid_features, owners, adjacency, mesh_nodes, *parameters):
    sizes = [lax.axis_size(axis) for axis in ("shard", "head", "sub")]
    small = grid_features.shape[:2] == (4, BLOCK) and mesh_nodes.shape[0] == 2 * BLOCK
    if sizes == [4, 2, 2] and small and grid_features.shape[2] == 512:
        return paired(grid_features, owners, adjacency, mesh_nodes, *parameters)
    return general(grid_features, owners, adjacency, mesh_nodes, *parameters)


def solution(mesh):
    return jax.shard_map(
        local,
        mesh=mesh,
        in_specs=(
            P(("groups", "shard", "sub"), None, "head"),
            P(("groups", "shard", "sub"), None),
            P(("groups", "shard", "sub"), None),
            P(("groups", "shard", "sub"), None),
            P(),
            P(None, "head"),
            P(None, "head"),
            P(None, "head"),
            P("head", None),
            P(None, "head"),
            P("head", None),
        ),
        out_specs=P(("groups", "shard", "sub"), None, "head"),
        check_vma=False,
    )
```

```python
import functools
import math

import jax
import jax.numpy as jnp
from jax import lax
from jax.experimental import pallas as pl
from jax.experimental.pallas import tpu as pltpu
from jax.sharding import PartitionSpec as P

D = 1024
HEAD_DIM = 64
CAP = 2
BLOCK = 64
QUAD = 4
WIDE = QUAD * HEAD_DIM
TILE = 128
CHUNKS = ((0, 80), (80, 256))
MIB = 1 << 20


epsilon = 1e-05


def dot(a, b):
    return jnp.dot(a, b, preferred_element_type=jnp.float32)


def gelu(x):
    return 0.5 * x * (1.0 + lax.erf(x * (2.0**-0.5)))


def in_hbm(x):
    return pltpu.with_memory_space_constraint(x, pltpu.HBM)


def in_vmem(x):
    return pltpu.with_memory_space_constraint(x, pltpu.VMEM)


def whole(space):
    return pl.BlockSpec(memory_space=space)


def vmem(count):
    return [whole(pltpu.VMEM)] * count


def params(mib):
    return pltpu.CompilerParams(vmem_limit_bytes=mib * MIB)


def mlp_kernel(own, other, gain, wq, wup, wdn, q_out, mlp_out, normed_s):
    half = own.shape[1]
    units = wup.shape[1]
    chunk = units // 4
    x_other = other[...].astype(jnp.float32)
    x_own = own[...].astype(jnp.float32)

    def mean(a, b):
        total = jnp.sum(a, axis=-1, keepdims=True) + jnp.sum(b, axis=-1, keepdims=True)
        return total * (0.5 / half)

    average = mean(x_other, x_own)
    x_other = x_other - average
    x_own = x_own - average
    factor = lax.rsqrt(mean(x_other * x_other, x_own * x_own) + epsilon)
    normed_s[:, :half] = (x_other * factor * gain[:, :half]).astype(jnp.bfloat16)
    normed_s[:, half:] = (x_own * factor * gain[:, half:]).astype(jnp.bfloat16)
    normed = normed_s[...]
    q_out[...] = dot(normed, wq[...]).astype(jnp.bfloat16)
    for c in range(units // chunk):
        span = slice(c * chunk, (c + 1) * chunk)
        hidden = gelu(dot(normed, wup[:, span])).astype(jnp.bfloat16)
        term = dot(hidden, wdn[span, :])
        if c == 0:
            mlp_out[...] = term
        else:
            mlp_out[...] += term


def run_mlp(own, other, gain, wq, wup, wdn):
    rows = own.shape[0]
    width = wq.shape[0]
    units = wup.shape[1]
    return pl.pallas_call(
        mlp_kernel,
        out_shape=(
            jax.ShapeDtypeStruct((rows, wq.shape[1]), jnp.bfloat16),
            jax.ShapeDtypeStruct((rows, width), jnp.float32),
        ),
        in_specs=vmem(6),
        out_specs=tuple(vmem(2)),
        scratch_shapes=[pltpu.VMEM((rows, width), jnp.bfloat16)],
        compiler_params=params(16),
        cost_estimate=pl.CostEstimate(
            flops=2 * rows * width * (wq.shape[1] + 2 * units),
            bytes_accessed=2 * width * (wq.shape[1] + 2 * units),
            transcendentals=rows * units,
        ),
        name="mlp",
    )(own, other, gain, wq, wup, wdn)


def pick_kernel(mesh, out, sem):
    first = pl.multiple_of(lax.axis_index("head") * BLOCK, BLOCK)
    copy = pltpu.make_async_copy(mesh.at[pl.ds(first, BLOCK), :], out, sem)
    copy.start()
    copy.wait()


def run_pick(mesh):
    return pl.pallas_call(
        pick_kernel,
        out_shape=jax.ShapeDtypeStruct((BLOCK, mesh.shape[1]), mesh.dtype),
        in_specs=[whole(pltpu.HBM)],
        out_specs=whole(pltpu.VMEM),
        scratch_shapes=[pltpu.SemaphoreType.DMA(())],
        compiler_params=params(4),
        cost_estimate=pl.CostEstimate(flops=0, bytes_accessed=4 * mesh.size, transcendentals=0),
        name="pick",
    )(in_hbm(mesh))


def stage_kernel(axes, *refs):
    sources, targets, sem = refs[: len(axes)], refs[len(axes) : -1], refs[-1]
    h = lax.axis_index("head")
    copies = []

    def add(source, target):
        pieces = 2 if source.shape[0] >= 512 else 1
        rows = source.shape[0] // pieces
        for piece in range(pieces):
            span = pl.ds(piece * rows, rows)
            copies.append(
                pltpu.make_async_copy(
                    source.at[span, :], target.at[span, :], sem.at[len(copies)]
                )
            )
            copies[-1].start()

    for source, target, axis in zip(sources, targets, axes):
        if axis is None:
            add(source, target)
            continue
        if axis == "rest":
            add(source.at[pl.ds(pl.multiple_of((1 - h) * BLOCK, BLOCK), BLOCK), :], target)
            continue
        half = source.shape[axis] // 2
        for part, head in enumerate((1 - h, h)):
            span = pl.ds(pl.multiple_of(head * half, half), half)
            place = pl.ds(part * half, half)
            if axis == 0:
                add(source.at[span, :], target.at[place, :])
            else:
                add(source.at[:, span], target.at[:, place])
    for copy in copies:
        copy.wait()


def run_stage(arrays, axes):
    size = sum(2 * array.size for array in arrays)
    return pl.pallas_call(
        functools.partial(stage_kernel, axes),
        out_shape=tuple(
            jax.ShapeDtypeStruct((BLOCK,) + array.shape[1:] if axis == "rest" else array.shape, array.dtype)
            for array, axis in zip(arrays, axes)
        ),
        in_specs=[whole(pltpu.HBM)] * len(arrays),
        out_specs=tuple(vmem(len(arrays))),
        scratch_shapes=[pltpu.SemaphoreType.DMA((4 * len(arrays),))],
        compiler_params=params(16),
        cost_estimate=pl.CostEstimate(
            flops=2000 * size, bytes_accessed=20 * size, transcendentals=0
        ),
        name="stage",
    )(*(in_hbm(array) for array in arrays))


def project_kernel(*refs):
    pieces, (wk, wv, out) = refs[:-3], refs[-3:]
    width = wk.shape[1]
    rows = jnp.concatenate([piece[...] for piece in pieces], axis=0)
    out[:, :width] = dot(rows, wk[...]).astype(jnp.bfloat16)
    out[:, width:] = dot(rows, wv[...]).astype(jnp.bfloat16)


def run_project(pieces, wk, wv):
    rows = sum(piece.shape[0] for piece in pieces)
    depth, width = wk.shape
    return pl.pallas_call(
        project_kernel,
        out_shape=jax.ShapeDtypeStruct((rows, 2 * width), jnp.bfloat16),
        in_specs=vmem(len(pieces) + 2),
        out_specs=whole(pltpu.VMEM),
        compiler_params=params(8),
        cost_estimate=pl.CostEstimate(
            flops=300 * rows * depth * width,
            bytes_accessed=300 * depth * width + 300 * rows * depth,
            transcendentals=0,
        ),
        name="project",
    )(*pieces, in_vmem(wk), in_vmem(wv))


def table_kernel(mine, sibling, table):
    table[0, : mine.shape[0]] = mine[...]
    table[1, : mine.shape[0]] = sibling[...]


def run_table(mine, sibling, blocks):
    return pl.pallas_call(
        table_kernel,
        out_shape=jax.ShapeDtypeStruct((2, blocks) + mine.shape[1:], jnp.bfloat16),
        in_specs=vmem(2),
        out_specs=whole(pltpu.VMEM),
        compiler_params=params(8),
        cost_estimate=pl.CostEstimate(
            flops=0, bytes_accessed=80 * mine.size, transcendentals=0
        ),
        name="table",
    )(mine, sibling)


def pieces_of(c):
    low, high = CHUNKS[c]
    pieces = []
    for tile in range(low // BLOCK, -(-high // BLOCK)):
        first, last = max(low, tile * BLOCK), min(high, (tile + 1) * BLOCK)
        rows = slice(first - tile * BLOCK, last - tile * BLOCK)
        pieces.append((tile, rows, slice(first - low, last - low)))
    return pieces


def project_out(c, att, mlp, wo, send, keep):
    half = att.shape[1]
    h = lax.axis_index("head")
    pieces = pieces_of(c)
    start, stop = pieces[0][0] * TILE, (pieces[-1][0] + 1) * TILE

    def write(head):
        for out, first, place in ((send, 0, 1 - head), (keep, half, head)):
            extra = mlp[:, first + start : first + stop]
            total = extra + dot(att[...], wo[:, place * half + start : place * half + stop])
            total = total.astype(jnp.bfloat16)
            for tile, rows, spot in pieces:
                columns = slice(tile * TILE - start, (tile + 1) * TILE - start)
                for t in range(out.shape[0]):
                    block = slice(t * BLOCK + rows.start, t * BLOCK + rows.stop)
                    out[t, spot, :] = total[block, columns]

    for head in range(2):
        pl.when(h == head)(functools.partial(write, head))


def attend_kernel(
    adjacency, q, mine, sibling, table_in, mlp, wo, send, keep, att, table, stacked_s, near_s, sem
):
    del table_in
    s = lax.axis_index("shard")
    h = lax.axis_index("head")
    u = lax.axis_index("sub")
    half = wo.shape[0]
    ready = table.shape[1] - mine.shape[0]
    copy = pltpu.make_async_copy(adjacency, near_s, sem)
    copy.start()
    for i, part in enumerate((mine, sibling)):
        table[i, ready:] = part[...]
    rows_of = lax.broadcasted_iota(jnp.int32, (WIDE, WIDE), 0) // BLOCK
    lanes_of = lax.broadcasted_iota(jnp.int32, (WIDE, WIDE), 1) // HEAD_DIM
    diagonal = rows_of == lanes_of
    lane_head = lax.broadcasted_iota(jnp.int32, (BLOCK, WIDE), 1) // HEAD_DIM
    scale = HEAD_DIM**-0.5 * math.log2(math.e)
    groups = half // WIDE
    steps = near_s.shape[0] * groups
    for step in range(steps):
        b, g = divmod(step, groups)
        columns = slice(g * WIDE, (g + 1) * WIDE)
        stacked = jnp.concatenate([q[b * BLOCK : (b + 1) * BLOCK, columns]] * QUAD, axis=0)
        stacked_s[step] = jnp.where(diagonal, stacked, jnp.zeros_like(stacked))
    copy.wait()
    places = []
    for b in range(near_s.shape[0]):
        places.append([])
        for j in range(near_s.shape[1]):
            m = near_s[b, j]
            part = lax.rem(m, 2)
            core = lax.rem(m // 2, 2)
            distance = s ^ (m // 4)
            part = jnp.where(distance <= 1, part, part ^ h)
            places[b].append((core ^ u, distance * 2 + part))

    def scores_of(step):
        b, g = divmod(step, groups)
        columns = slice(g * WIDE, (g + 1) * WIDE)
        keys = jnp.concatenate([table[i, p, :, columns] for i, p in places[b]], axis=0)
        return lax.dot_general(
            stacked_s[step], keys, (((1,), (1,)), ((), ())), preferred_element_type=jnp.float32
        )

    scores = scores_of(0)
    for step in range(steps):
        following = scores_of(step + 1) if step + 1 < steps else None
        b, g = divmod(step, groups)
        columns = slice(half + g * WIDE, half + (g + 1) * WIDE)
        values = jnp.concatenate([table[i, p, :, columns] for i, p in places[b]], axis=0)
        highest = jnp.max(scores, axis=-1, keepdims=True)
        weights = jnp.exp2((scores - highest) * scale)
        total = jnp.sum(weights, axis=-1, keepdims=True)
        mixed = dot(weights.astype(jnp.bfloat16), values) * (1.0 / total)
        merged = mixed[0:BLOCK, :]
        for i in range(1, QUAD):
            merged = jnp.where(lane_head == i, mixed[i * BLOCK : (i + 1) * BLOCK, :], merged)
        rows = slice(b * BLOCK, (b + 1) * BLOCK)
        att[rows, g * WIDE : (g + 1) * WIDE] = merged.astype(jnp.bfloat16)
        scores = following
    project_out(0, att, mlp, wo, send, keep)


def run_attend(adjacency, q, mine, sibling, table, mlp, wo):
    rows, half = q.shape
    size = CHUNKS[0][1] - CHUNKS[0][0]
    part = jax.ShapeDtypeStruct((rows // BLOCK, size, TILE), jnp.bfloat16)
    blocks = table.shape[0] * table.shape[1]
    send, keep, att, _ = pl.pallas_call(
        attend_kernel,
        out_shape=(
            part,
            part,
            jax.ShapeDtypeStruct(q.shape, jnp.bfloat16),
            jax.ShapeDtypeStruct(table.shape, jnp.bfloat16),
        ),
        in_specs=[whole(pl.ANY)] + vmem(6),
        out_specs=tuple(vmem(4)),
        scratch_shapes=[
            pltpu.VMEM((rows // BLOCK * (half // WIDE), WIDE, WIDE), jnp.bfloat16),
            pltpu.SMEM(adjacency.shape, jnp.int32),
            pltpu.SemaphoreType.DMA(()),
        ],
        input_output_aliases={4: 3},
        compiler_params=params(16),
        cost_estimate=pl.CostEstimate(
            flops=20 * rows * half * (D + 8 * 8 * BLOCK),
            bytes_accessed=40 * blocks * BLOCK * half + 20 * half * D + 40 * rows * D,
            transcendentals=rows * 8 * BLOCK * half // HEAD_DIM,
        ),
        name="attend",
    )(adjacency, q, mine, sibling, table, mlp, in_vmem(wo))
    return send, keep, att


def run_project_out(c, att, mlp, wo):
    rows, half = att.shape
    size = CHUNKS[c][1] - CHUNKS[c][0]
    part = jax.ShapeDtypeStruct((rows // BLOCK, size, TILE), jnp.bfloat16)
    return pl.pallas_call(
        functools.partial(project_out, c),
        out_shape=(part, part),
        in_specs=vmem(3),
        out_specs=tuple(vmem(2)),
        compiler_params=params(8),
        cost_estimate=pl.CostEstimate(
            flops=200 * rows * half * D,
            bytes_accessed=200 * half * D,
            transcendentals=0,
        ),
        name="project_out",
    )(att, mlp, in_vmem(wo))


def plan_kernel(owners, masks):
    s = lax.axis_index("shard")
    count = owners.shape[0]
    names = [owners[t, 0] for t in range(count)]
    for t in range(count):
        same = [(names[e] == names[t]).astype(jnp.int32) for e in range(t)]
        rank = sum(same, jnp.int32(0))
        for d in range(masks.shape[0]):
            for j in range(CAP):
                hit = (names[t] == s ^ d) & (rank == j)
                masks[d, j, t] = jnp.full(masks.shape[3:], hit.astype(jnp.float32))


def run_plan(owners, shards):
    return pl.pallas_call(
        plan_kernel,
        out_shape=jax.ShapeDtypeStruct((shards, CAP, owners.shape[0], 8, 128), jnp.float32),
        in_specs=[whole(pltpu.SMEM)],
        out_specs=whole(pltpu.VMEM),
        compiler_params=params(4),
        cost_estimate=pl.CostEstimate(
            flops=100000000, bytes_accessed=1 << 18, transcendentals=0
        ),
        name="plan",
    )(owners)


def combine_kernel(chunks, distances, masks, grid_features, *refs):
    keeps, refs = refs[: len(chunks)], refs[len(chunks) :]
    swaps, outs = refs[: len(chunks)], refs[len(chunks) :]
    count = grid_features.shape[0]
    first = CHUNKS[chunks[0]][0]
    for c, keep, swap in zip(chunks, keeps, swaps):
        low, high = CHUNKS[c]
        updated = []
        for t in range(count):
            residual = [
                grid_features[t, rows, tile * TILE : (tile + 1) * TILE]
                for tile, rows, _ in pieces_of(c)
            ]
            residual = jnp.concatenate(residual, axis=0).astype(jnp.float32)
            partials = keep[t].astype(jnp.float32) + swap[t].astype(jnp.float32)
            updated.append(residual + partials)
        for d, out in zip(distances, outs):
            for j in range(CAP):
                chosen = jnp.zeros_like(updated[0])
                for t in range(count):
                    mask = jnp.broadcast_to(masks[d, j, t, 0:1, :], chosen.shape)
                    chosen = jnp.where(mask > 0.5, updated[t], chosen)
                out[j, low - first : high - first, :] = chosen.astype(jnp.bfloat16)


def run_combine(chunks, distances, masks, grid_features, keeps, swaps):
    count = grid_features.shape[0]
    rows, width = CHUNKS[chunks[-1]][1] - CHUNKS[chunks[0]][0], TILE
    slot = jax.ShapeDtypeStruct((CAP, rows, width), jnp.bfloat16)
    return pl.pallas_call(
        functools.partial(combine_kernel, chunks, distances),
        out_shape=(slot,) * len(distances),
        in_specs=vmem(2 + 2 * len(chunks)),
        out_specs=tuple(vmem(len(distances))),
        compiler_params=params(8),
        cost_estimate=pl.CostEstimate(
            flops=60000 * count * rows * width,
            bytes_accessed=400 * rows * width * (3 * count + CAP * len(distances)),
            transcendentals=0,
        ),
        name="combine",
    )(masks, grid_features, *keeps, *swaps)


def place_kernel(spots, *refs):
    out, sem = refs[-2:]
    s = lax.axis_index("shard")
    copies = []
    for ref, (d, chunks) in zip(refs, spots):
        first = CHUNKS[chunks[0]][0]
        slots = pl.ds((s ^ d) * CAP, CAP)
        for c in chunks:
            shift = CHUNKS[c][0] - first
            for tile, rows, spot in pieces_of(c):
                size = rows.stop - rows.start
                source = ref.at[:, pl.ds(spot.start + shift, size), :]
                columns = pl.ds(tile * TILE, TILE)
                target = out.at[slots, pl.ds(rows.start, size), columns]
                copies.append(pltpu.make_async_copy(source, target, sem.at[len(copies)]))
                copies[-1].start()
    for copy in copies:
        copy.wait()


def run_place(spots, arrived, placed, shape):
    count = sum(len(pieces_of(c)) for _, chunks in spots for c in chunks)
    return pl.pallas_call(
        functools.partial(place_kernel, spots),
        out_shape=jax.ShapeDtypeStruct(shape, jnp.bfloat16),
        in_specs=vmem(len(arrived)) + [whole(pltpu.HBM)] * len(placed),
        out_specs=whole(pltpu.HBM),
        scratch_shapes=[pltpu.SemaphoreType.DMA((count,))],
        input_output_aliases={len(arrived): 0} if placed else {},
        compiler_params=params(4),
        cost_estimate=pl.CostEstimate(
            flops=400000 * sum(part.size for part in arrived), bytes_accessed=0, transcendentals=0
        ),
        name="place",
    )(*arrived, *placed)


def crossed(x, distance, size):
    return lax.ppermute(x, "shard", [(i, i ^ distance) for i in range(size)])


def swapped(x, axis):
    return lax.ppermute(x, axis, [(0, 1), (1, 0)])


def paired(
    grid_features,
    owners,
    adjacency,
    mesh_nodes,
    norm_gain,
    query_weight,
    key_weight,
    value_weight,
    output_weight,
    up_weight,
    down_weight,
):
    shards = lax.axis_size("shard")
    count, rows, half = grid_features.shape
    flat = grid_features.reshape(count * rows, half)
    half_unit = run_pick(mesh_nodes)
    far = crossed(half_unit, 2, shards)
    waiting, _ = lax.optimization_barrier((mesh_nodes, half_unit))
    near = crossed(waiting, 1, shards)
    waiting, _ = lax.optimization_barrier((flat, half_unit))
    other = swapped(waiting, "head")
    flat, gain, wq, wup, wdn, mesh, rest = run_stage(
        (
            flat,
            norm_gain.reshape(1, -1),
            query_weight,
            up_weight,
            down_weight,
            mesh_nodes,
            mesh_nodes,
        ),
        (None, 1, 0, 0, 1, None, "rest"),
    )
    straight = crossed(rest, 3, shards)
    far, _ = lax.optimization_barrier((far, rest))
    farther = crossed(far, 1, shards)
    far_pair = swapped(far, "head")
    queries, mlp = run_mlp(flat, other, gain, wq, wup, wdn)
    queries, mlp, far_pair, near = lax.optimization_barrier((queries, mlp, far_pair, near))
    blocked = (-1, BLOCK, 2 * half)
    mine_a = run_project((mesh, near, far, far_pair), key_weight, value_weight)
    sibling_a = swapped(mine_a, "sub")
    table = run_table(mine_a.reshape(blocked), sibling_a.reshape(blocked), 2 * shards)
    mine_b = run_project((farther, straight), key_weight, value_weight)
    sibling_b = swapped(mine_b, "sub")
    send, keep, att = run_attend(
        adjacency, queries, mine_b.reshape(blocked), sibling_b.reshape(blocked), table, mlp, output_weight
    )
    keeps, swaps, slots, placed = [], [], [], []
    shape = (shards * CAP, rows, half)
    every = tuple(range(len(CHUNKS)))
    for c in every:
        if c > 0:
            send, keep = run_project_out(c, att, mlp, output_weight)
        received = swapped(send, "head")
        swaps.append(received)
        keeps.append(keep)
    named, _ = lax.optimization_barrier((owners, keep))
    masks = run_plan(named, shards)
    for c in every:
        received = swaps[c]
        if c > 0:
            received, _ = lax.optimization_barrier((received, slots[c - 1][0]))
        slots.append(run_combine((c,), (2, 3), masks, grid_features, (keeps[c],), (received,)))
    swaps[-1], _ = lax.optimization_barrier((swaps[-1], slots[-1][0]))
    near_slots, own_slots = run_combine(every, (1, 0), masks, grid_features, keeps, swaps)
    for c in every:
        spots = [(2, (c,)), (3, (c,))]
        arrived = [crossed(slot, d, shards) for d, slot in zip((2, 3), slots[c])]
        if c == 0:
            spots.append((0, every))
            arrived.append(own_slots)
        if c == every[-1]:
            spots.append((1, every))
            arrived.append(crossed(near_slots, 1, shards))
        placed = [run_place(spots, arrived, placed, shape)]
    return placed[0]


def attend_plain(queries, key_table, value_table, chosen, scaling):
    count = chosen.shape[0]
    picked_keys = key_table[chosen]
    picked_keys = picked_keys.reshape(count, -1, picked_keys.shape[3], picked_keys.shape[4])
    picked_values = value_table[chosen]
    picked_values = picked_values.reshape(count, -1, picked_values.shape[3], picked_values.shape[4])
    scores = (
        jnp.einsum("gqhe,gkhe->ghqk", queries, picked_keys, preferred_element_type=jnp.float32)
        * scaling
    )
    highest = jnp.max(scores, axis=-1, keepdims=True)
    weights = jnp.exp(scores - highest)
    weights = (weights / jnp.sum(weights, axis=-1, keepdims=True)).astype(jnp.bfloat16)
    result = jnp.einsum(
        "ghqk,gkhe->gqhe", weights, picked_values, preferred_element_type=jnp.float32
    )
    return result.astype(jnp.bfloat16)


def general(
    grid_features,
    owners,
    adjacency,
    mesh_nodes,
    norm_gain,
    query_weight,
    key_weight,
    value_weight,
    output_weight,
    up_weight,
    down_weight,
):
    shard_count = lax.axis_size("shard")
    head_count = lax.axis_size("head")
    local_blocks, block_rows, feature_share = grid_features.shape
    slots = shard_count * CAP
    owner_col = owners[:, 0]
    position = jnp.arange(local_blocks, dtype=jnp.int32)
    earlier = (owner_col[:, None] == owner_col[None, :]) & (position[None, :] < position[:, None])
    target = owner_col * CAP + jnp.sum(earlier.astype(jnp.int32), axis=1)
    dispatch = (target[:, None] == jnp.arange(slots, dtype=jnp.int32)[None, :]).astype(jnp.bfloat16)
    offset = lax.axis_index("head") * (D // head_count)
    projected = jnp.stack(
        (
            jnp.dot(mesh_nodes, key_weight, preferred_element_type=jnp.float32).astype(
                jnp.bfloat16
            ),
            jnp.dot(mesh_nodes, value_weight, preferred_element_type=jnp.float32).astype(
                jnp.bfloat16
            ),
        )
    )
    tables = lax.all_gather(projected, ("shard", "sub"), axis=1, tiled=True)
    head_local = query_weight.shape[1] // HEAD_DIM
    key_table = tables[0].reshape(-1, block_rows, head_local, HEAD_DIM)
    value_table = tables[1].reshape(-1, block_rows, head_local, HEAD_DIM)
    send_lists = jnp.full((slots, adjacency.shape[1]), -1, jnp.int32).at[target].set(adjacency)
    send_lists = send_lists.reshape(shard_count, CAP, -1)
    complete = lax.all_gather(grid_features, "head", axis=2, tiled=True)
    outgoing = jnp.einsum(
        "gs,gbd->sbd", dispatch, complete, preferred_element_type=jnp.float32
    ).astype(jnp.bfloat16)
    arrived, lists = (
        lax.all_to_all(
            outgoing.reshape(shard_count, CAP, block_rows, D),
            "shard",
            split_axis=0,
            concat_axis=0,
            tiled=True,
        ),
        lax.all_to_all(send_lists, "shard", split_axis=0, concat_axis=0, tiled=True),
    )
    arrived = arrived.reshape(slots, block_rows, D)
    residual = lax.dynamic_slice_in_dim(arrived, offset, D // head_count, 2)
    lists = lists.reshape(slots, -1)
    count = arrived.shape[0]
    values_f = arrived.astype(jnp.float32)
    average = jnp.mean(values_f, axis=-1, keepdims=True)
    centered = values_f - average
    variance = jnp.mean(centered * centered, axis=-1, keepdims=True)
    normed = (centered * lax.rsqrt(variance + epsilon) * norm_gain).astype(jnp.bfloat16)
    flattened = normed.reshape(-1, D)
    queries = jnp.dot(flattened, query_weight, preferred_element_type=jnp.float32).astype(
        jnp.bfloat16
    )
    blocks_each = math.gcd(count, max(1, 512 // block_rows))
    steps_count = count // blocks_each
    queries = queries.reshape(steps_count, blocks_each, block_rows, head_local, HEAD_DIM)

    def attend_step(operands):
        return attend_plain(operands[0], key_table, value_table, operands[1], HEAD_DIM ** (-0.5))

    attended = lax.map(
        attend_step, (queries, jnp.maximum(lists, 0).reshape(steps_count, blocks_each, -1))
    )
    attended = attended.reshape(-1, head_local * HEAD_DIM)
    hidden = jax.nn.gelu(
        jnp.dot(flattened, up_weight, preferred_element_type=jnp.float32), approximate=False
    ).astype(jnp.bfloat16)
    branch = jnp.dot(attended, output_weight, preferred_element_type=jnp.float32)
    branch = branch + jnp.dot(hidden, down_weight, preferred_element_type=jnp.float32)
    branch = branch.reshape(count, block_rows, D)
    reduced = lax.psum_scatter(
        branch.astype(jnp.bfloat16), "head", scatter_dimension=2, tiled=True
    ).astype(jnp.float32)
    occupied = lists[:, 0] >= 0
    summed = residual.astype(jnp.float32) + reduced
    return jnp.where(occupied[:, None, None], summed, 0.0).astype(jnp.bfloat16)


def local(grid_features, owners, adjacency, mesh_nodes, *parameters):
    sizes = [lax.axis_size(axis) for axis in ("shard", "head", "sub")]
    small = grid_features.shape[:2] == (4, BLOCK) and mesh_nodes.shape[0] == 2 * BLOCK
    if sizes == [4, 2, 2] and small and grid_features.shape[2] == 512:
        return paired(grid_features, owners, adjacency, mesh_nodes, *parameters)
    return general(grid_features, owners, adjacency, mesh_nodes, *parameters)


def solution(mesh):
    return jax.shard_map(
        local,
        mesh=mesh,
        in_specs=(
            P(("groups", "shard", "sub"), None, "head"),
            P(("groups", "shard", "sub"), None),
            P(("groups", "shard", "sub"), None),
            P(("groups", "shard", "sub"), None),
            P(),
            P(None, "head"),
            P(None, "head"),
            P(None, "head"),
            P("head", None),
            P(None, "head"),
            P("head", None),
        ),
        out_specs=P(("groups", "shard", "sub"), None, "head"),
        check_vma=False,
    )
```

```python
import functools
import math

import jax
import jax.numpy as jnp
from jax import lax
from jax.experimental import pallas as pl
from jax.experimental.pallas import tpu as pltpu
from jax.sharding import PartitionSpec as P

D = 1024
HEAD_DIM = 64
CAP = 2
BLOCK = 64
QUAD = 4
WIDE = QUAD * HEAD_DIM
TILE = 128
CHUNKS = ((0, 96), (96, 256))
MIB = 1 << 20


epsilon = 1e-05


def dot(a, b):
    return jnp.dot(a, b, preferred_element_type=jnp.float32)


def gelu(x):
    return 0.5 * x * (1.0 + lax.erf(x * (2.0**-0.5)))


def in_hbm(x):
    return pltpu.with_memory_space_constraint(x, pltpu.HBM)


def in_vmem(x):
    return pltpu.with_memory_space_constraint(x, pltpu.VMEM)


def whole(space):
    return pl.BlockSpec(memory_space=space)


def vmem(count):
    return [whole(pltpu.VMEM)] * count


def params(mib):
    return pltpu.CompilerParams(vmem_limit_bytes=mib * MIB)


def mlp_kernel(own, other, gain, wq, wup, wdn, q_out, mlp_out, normed_s):
    half = own.shape[1]
    units = wup.shape[1]
    chunk = units // 4
    x_other = other[...].astype(jnp.float32)
    x_own = own[...].astype(jnp.float32)

    def mean(a, b):
        total = jnp.sum(a, axis=-1, keepdims=True) + jnp.sum(b, axis=-1, keepdims=True)
        return total * (0.5 / half)

    average = mean(x_other, x_own)
    x_other = x_other - average
    x_own = x_own - average
    factor = lax.rsqrt(mean(x_other * x_other, x_own * x_own) + epsilon)
    normed_s[:, :half] = (x_other * factor * gain[:, :half]).astype(jnp.bfloat16)
    normed_s[:, half:] = (x_own * factor * gain[:, half:]).astype(jnp.bfloat16)
    normed = normed_s[...]
    q_out[...] = dot(normed, wq[...]).astype(jnp.bfloat16)
    for c in range(units // chunk):
        span = slice(c * chunk, (c + 1) * chunk)
        hidden = gelu(dot(normed, wup[:, span])).astype(jnp.bfloat16)
        term = dot(hidden, wdn[span, :])
        if c == 0:
            mlp_out[...] = term
        else:
            mlp_out[...] += term


def run_mlp(own, other, gain, wq, wup, wdn):
    rows = own.shape[0]
    width = wq.shape[0]
    units = wup.shape[1]
    return pl.pallas_call(
        mlp_kernel,
        out_shape=(
            jax.ShapeDtypeStruct((rows, wq.shape[1]), jnp.bfloat16),
            jax.ShapeDtypeStruct((rows, width), jnp.float32),
        ),
        in_specs=vmem(6),
        out_specs=tuple(vmem(2)),
        scratch_shapes=[pltpu.VMEM((rows, width), jnp.bfloat16)],
        compiler_params=params(16),
        cost_estimate=pl.CostEstimate(
            flops=2 * rows * width * (wq.shape[1] + 2 * units),
            bytes_accessed=2 * width * (wq.shape[1] + 2 * units),
            transcendentals=rows * units,
        ),
        name="mlp",
    )(own, other, gain, wq, wup, wdn)


def pick_kernel(mesh, out, sem):
    first = pl.multiple_of(lax.axis_index("head") * BLOCK, BLOCK)
    copy = pltpu.make_async_copy(mesh.at[pl.ds(first, BLOCK), :], out, sem)
    copy.start()
    copy.wait()


def run_pick(mesh):
    return pl.pallas_call(
        pick_kernel,
        out_shape=jax.ShapeDtypeStruct((BLOCK, mesh.shape[1]), mesh.dtype),
        in_specs=[whole(pltpu.HBM)],
        out_specs=whole(pltpu.VMEM),
        scratch_shapes=[pltpu.SemaphoreType.DMA(())],
        compiler_params=params(4),
        cost_estimate=pl.CostEstimate(flops=0, bytes_accessed=4 * mesh.size, transcendentals=0),
        name="pick",
    )(in_hbm(mesh))


def stage_kernel(axes, *refs):
    sources, targets, sem = refs[: len(axes)], refs[len(axes) : -1], refs[-1]
    h = lax.axis_index("head")
    copies = []

    def add(source, target):
        pieces = 2 if source.shape[0] >= 512 else 1
        rows = source.shape[0] // pieces
        for piece in range(pieces):
            span = pl.ds(piece * rows, rows)
            copies.append(
                pltpu.make_async_copy(
                    source.at[span, :], target.at[span, :], sem.at[len(copies)]
                )
            )
            copies[-1].start()

    for source, target, axis in zip(sources, targets, axes):
        if axis is None:
            add(source, target)
            continue
        if axis == "rest":
            add(source.at[pl.ds(pl.multiple_of((1 - h) * BLOCK, BLOCK), BLOCK), :], target)
            continue
        half = source.shape[axis] // 2
        for part, head in enumerate((1 - h, h)):
            span = pl.ds(pl.multiple_of(head * half, half), half)
            place = pl.ds(part * half, half)
            if axis == 0:
                add(source.at[span, :], target.at[place, :])
            else:
                add(source.at[:, span], target.at[:, place])
    for copy in copies:
        copy.wait()


def run_stage(arrays, axes):
    size = sum(2 * array.size for array in arrays)
    return pl.pallas_call(
        functools.partial(stage_kernel, axes),
        out_shape=tuple(
            jax.ShapeDtypeStruct((BLOCK,) + array.shape[1:] if axis == "rest" else array.shape, array.dtype)
            for array, axis in zip(arrays, axes)
        ),
        in_specs=[whole(pltpu.HBM)] * len(arrays),
        out_specs=tuple(vmem(len(arrays))),
        scratch_shapes=[pltpu.SemaphoreType.DMA((4 * len(arrays),))],
        compiler_params=params(16),
        cost_estimate=pl.CostEstimate(
            flops=2000 * size, bytes_accessed=20 * size, transcendentals=0
        ),
        name="stage",
    )(*(in_hbm(array) for array in arrays))


def project_kernel(*refs):
    pieces, (wk, wv, out) = refs[:-3], refs[-3:]
    width = wk.shape[1]
    rows = jnp.concatenate([piece[...] for piece in pieces], axis=0)
    out[:, :width] = dot(rows, wk[...]).astype(jnp.bfloat16)
    out[:, width:] = dot(rows, wv[...]).astype(jnp.bfloat16)


def run_project(pieces, wk, wv):
    rows = sum(piece.shape[0] for piece in pieces)
    depth, width = wk.shape
    return pl.pallas_call(
        project_kernel,
        out_shape=jax.ShapeDtypeStruct((rows, 2 * width), jnp.bfloat16),
        in_specs=vmem(len(pieces) + 2),
        out_specs=whole(pltpu.VMEM),
        compiler_params=params(8),
        cost_estimate=pl.CostEstimate(
            flops=300 * rows * depth * width,
            bytes_accessed=300 * depth * width + 300 * rows * depth,
            transcendentals=0,
        ),
        name="project",
    )(*pieces, in_vmem(wk), in_vmem(wv))


def table_kernel(mine, sibling, table):
    table[0, : mine.shape[0]] = mine[...]
    table[1, : mine.shape[0]] = sibling[...]


def run_table(mine, sibling, blocks):
    return pl.pallas_call(
        table_kernel,
        out_shape=jax.ShapeDtypeStruct((2, blocks) + mine.shape[1:], jnp.bfloat16),
        in_specs=vmem(2),
        out_specs=whole(pltpu.VMEM),
        compiler_params=params(8),
        cost_estimate=pl.CostEstimate(
            flops=0, bytes_accessed=80 * mine.size, transcendentals=0
        ),
        name="table",
    )(mine, sibling)


def pieces_of(c):
    low, high = CHUNKS[c]
    pieces = []
    for tile in range(low // BLOCK, -(-high // BLOCK)):
        first, last = max(low, tile * BLOCK), min(high, (tile + 1) * BLOCK)
        rows = slice(first - tile * BLOCK, last - tile * BLOCK)
        pieces.append((tile, rows, slice(first - low, last - low)))
    return pieces


def project_out(c, att, mlp, wo, send, keep):
    half = att.shape[1]
    h = lax.axis_index("head")
    pieces = pieces_of(c)
    start, stop = pieces[0][0] * TILE, (pieces[-1][0] + 1) * TILE

    def write(head):
        for out, first, place in ((send, 0, 1 - head), (keep, half, head)):
            extra = mlp[:, first + start : first + stop]
            total = extra + dot(att[...], wo[:, place * half + start : place * half + stop])
            total = total.astype(jnp.bfloat16)
            for tile, rows, spot in pieces:
                columns = slice(tile * TILE - start, (tile + 1) * TILE - start)
                for t in range(out.shape[0]):
                    block = slice(t * BLOCK + rows.start, t * BLOCK + rows.stop)
                    out[t, spot, :] = total[block, columns]

    for head in range(2):
        pl.when(h == head)(functools.partial(write, head))


def attend_kernel(
    adjacency, q, mine, sibling, table_in, mlp, wo, send, keep, att, table, stacked_s, near_s, sem
):
    del table_in
    s = lax.axis_index("shard")
    h = lax.axis_index("head")
    u = lax.axis_index("sub")
    half = wo.shape[0]
    ready = table.shape[1] - mine.shape[0]
    copy = pltpu.make_async_copy(adjacency, near_s, sem)
    copy.start()
    for i, part in enumerate((mine, sibling)):
        table[i, ready:] = part[...]
    rows_of = lax.broadcasted_iota(jnp.int32, (WIDE, WIDE), 0) // BLOCK
    lanes_of = lax.broadcasted_iota(jnp.int32, (WIDE, WIDE), 1) // HEAD_DIM
    diagonal = rows_of == lanes_of
    lane_head = lax.broadcasted_iota(jnp.int32, (BLOCK, WIDE), 1) // HEAD_DIM
    scale = HEAD_DIM**-0.5 * math.log2(math.e)
    groups = half // WIDE
    steps = near_s.shape[0] * groups
    for step in range(steps):
        b, g = divmod(step, groups)
        columns = slice(g * WIDE, (g + 1) * WIDE)
        stacked = jnp.concatenate([q[b * BLOCK : (b + 1) * BLOCK, columns]] * QUAD, axis=0)
        stacked_s[step] = jnp.where(diagonal, stacked, jnp.zeros_like(stacked))
    copy.wait()
    places = []
    for b in range(near_s.shape[0]):
        places.append([])
        for j in range(near_s.shape[1]):
            m = near_s[b, j]
            part = lax.rem(m, 2)
            core = lax.rem(m // 2, 2)
            distance = s ^ (m // 4)
            part = jnp.where(distance <= 1, part, part ^ h)
            places[b].append((core ^ u, distance * 2 + part))

    def scores_of(step):
        b, g = divmod(step, groups)
        columns = slice(g * WIDE, (g + 1) * WIDE)
        keys = jnp.concatenate([table[i, p, :, columns] for i, p in places[b]], axis=0)
        return lax.dot_general(
            stacked_s[step], keys, (((1,), (1,)), ((), ())), preferred_element_type=jnp.float32
        )

    scores = scores_of(0)
    for step in range(steps):
        following = scores_of(step + 1) if step + 1 < steps else None
        b, g = divmod(step, groups)
        columns = slice(half + g * WIDE, half + (g + 1) * WIDE)
        values = jnp.concatenate([table[i, p, :, columns] for i, p in places[b]], axis=0)
        highest = jnp.max(scores, axis=-1, keepdims=True)
        weights = jnp.exp2(((scores - highest) * scale).astype(jnp.bfloat16))
        total = jnp.sum(weights.astype(jnp.float32), axis=-1, keepdims=True)
        mixed = dot(weights, values) * (1.0 / total)
        merged = mixed[0:BLOCK, :]
        for i in range(1, QUAD):
            merged = jnp.where(lane_head == i, mixed[i * BLOCK : (i + 1) * BLOCK, :], merged)
        rows = slice(b * BLOCK, (b + 1) * BLOCK)
        att[rows, g * WIDE : (g + 1) * WIDE] = merged.astype(jnp.bfloat16)
        scores = following
    project_out(0, att, mlp, wo, send, keep)


def run_attend(adjacency, q, mine, sibling, table, mlp, wo):
    rows, half = q.shape
    size = CHUNKS[0][1] - CHUNKS[0][0]
    part = jax.ShapeDtypeStruct((rows // BLOCK, size, TILE), jnp.bfloat16)
    blocks = table.shape[0] * table.shape[1]
    send, keep, att, _ = pl.pallas_call(
        attend_kernel,
        out_shape=(
            part,
            part,
            jax.ShapeDtypeStruct(q.shape, jnp.bfloat16),
            jax.ShapeDtypeStruct(table.shape, jnp.bfloat16),
        ),
        in_specs=[whole(pl.ANY)] + vmem(6),
        out_specs=tuple(vmem(4)),
        scratch_shapes=[
            pltpu.VMEM((rows // BLOCK * (half // WIDE), WIDE, WIDE), jnp.bfloat16),
            pltpu.SMEM(adjacency.shape, jnp.int32),
            pltpu.SemaphoreType.DMA(()),
        ],
        input_output_aliases={4: 3},
        compiler_params=params(16),
        cost_estimate=pl.CostEstimate(
            flops=20 * rows * half * (D + 8 * 8 * BLOCK),
            bytes_accessed=40 * blocks * BLOCK * half + 20 * half * D + 40 * rows * D,
            transcendentals=rows * 8 * BLOCK * half // HEAD_DIM,
        ),
        name="attend",
    )(adjacency, q, mine, sibling, table, mlp, in_vmem(wo))
    return send, keep, att


def run_project_out(c, att, mlp, wo):
    rows, half = att.shape
    size = CHUNKS[c][1] - CHUNKS[c][0]
    part = jax.ShapeDtypeStruct((rows // BLOCK, size, TILE), jnp.bfloat16)
    return pl.pallas_call(
        functools.partial(project_out, c),
        out_shape=(part, part),
        in_specs=vmem(3),
        out_specs=tuple(vmem(2)),
        compiler_params=params(8),
        cost_estimate=pl.CostEstimate(
            flops=200 * rows * half * D,
            bytes_accessed=200 * half * D,
            transcendentals=0,
        ),
        name="project_out",
    )(att, mlp, in_vmem(wo))


def plan_kernel(owners, masks):
    s = lax.axis_index("shard")
    count = owners.shape[0]
    names = [owners[t, 0] for t in range(count)]
    for t in range(count):
        same = [(names[e] == names[t]).astype(jnp.int32) for e in range(t)]
        rank = sum(same, jnp.int32(0))
        for d in range(masks.shape[0]):
            for j in range(CAP):
                hit = (names[t] == s ^ d) & (rank == j)
                masks[d, j, t] = jnp.full(masks.shape[3:], hit.astype(jnp.float32))


def run_plan(owners, shards):
    return pl.pallas_call(
        plan_kernel,
        out_shape=jax.ShapeDtypeStruct((shards, CAP, owners.shape[0], 8, 128), jnp.float32),
        in_specs=[whole(pltpu.SMEM)],
        out_specs=whole(pltpu.VMEM),
        compiler_params=params(4),
        cost_estimate=pl.CostEstimate(
            flops=100000000, bytes_accessed=1 << 18, transcendentals=0
        ),
        name="plan",
    )(owners)


def combine_kernel(chunks, distances, masks, grid_features, *refs):
    keeps, refs = refs[: len(chunks)], refs[len(chunks) :]
    swaps, outs = refs[: len(chunks)], refs[len(chunks) :]
    count = grid_features.shape[0]
    first = CHUNKS[chunks[0]][0]
    for c, keep, swap in zip(chunks, keeps, swaps):
        low, high = CHUNKS[c]
        updated = []
        for t in range(count):
            residual = [
                grid_features[t, rows, tile * TILE : (tile + 1) * TILE]
                for tile, rows, _ in pieces_of(c)
            ]
            residual = jnp.concatenate(residual, axis=0).astype(jnp.float32)
            partials = keep[t].astype(jnp.float32) + swap[t].astype(jnp.float32)
            updated.append(residual + partials)
        for d, out in zip(distances, outs):
            for j in range(CAP):
                chosen = jnp.zeros_like(updated[0])
                for t in range(count):
                    mask = jnp.broadcast_to(masks[d, j, t, 0:1, :], chosen.shape)
                    chosen = jnp.where(mask > 0.5, updated[t], chosen)
                out[j, low - first : high - first, :] = chosen.astype(jnp.bfloat16)


def run_combine(chunks, distances, masks, grid_features, keeps, swaps):
    count = grid_features.shape[0]
    rows, width = CHUNKS[chunks[-1]][1] - CHUNKS[chunks[0]][0], TILE
    slot = jax.ShapeDtypeStruct((CAP, rows, width), jnp.bfloat16)
    return pl.pallas_call(
        functools.partial(combine_kernel, chunks, distances),
        out_shape=(slot,) * len(distances),
        in_specs=vmem(2 + 2 * len(chunks)),
        out_specs=tuple(vmem(len(distances))),
        compiler_params=params(8),
        cost_estimate=pl.CostEstimate(
            flops=60000 * count * rows * width,
            bytes_accessed=400 * rows * width * (3 * count + CAP * len(distances)),
            transcendentals=0,
        ),
        name="combine",
    )(masks, grid_features, *keeps, *swaps)


def place_kernel(spots, *refs):
    out, sem = refs[-2:]
    s = lax.axis_index("shard")
    copies = []
    for ref, (d, chunks) in zip(refs, spots):
        first = CHUNKS[chunks[0]][0]
        slots = pl.ds((s ^ d) * CAP, CAP)
        for c in chunks:
            shift = CHUNKS[c][0] - first
            for tile, rows, spot in pieces_of(c):
                size = rows.stop - rows.start
                source = ref.at[:, pl.ds(spot.start + shift, size), :]
                columns = pl.ds(tile * TILE, TILE)
                target = out.at[slots, pl.ds(rows.start, size), columns]
                copies.append(pltpu.make_async_copy(source, target, sem.at[len(copies)]))
                copies[-1].start()
    for copy in copies:
        copy.wait()


def run_place(spots, arrived, placed, shape):
    count = sum(len(pieces_of(c)) for _, chunks in spots for c in chunks)
    return pl.pallas_call(
        functools.partial(place_kernel, spots),
        out_shape=jax.ShapeDtypeStruct(shape, jnp.bfloat16),
        in_specs=vmem(len(arrived)) + [whole(pltpu.HBM)] * len(placed),
        out_specs=whole(pltpu.HBM),
        scratch_shapes=[pltpu.SemaphoreType.DMA((count,))],
        input_output_aliases={len(arrived): 0} if placed else {},
        compiler_params=params(4),
        cost_estimate=pl.CostEstimate(
            flops=400000 * sum(part.size for part in arrived), bytes_accessed=0, transcendentals=0
        ),
        name="place",
    )(*arrived, *placed)


def crossed(x, distance, size):
    return lax.ppermute(x, "shard", [(i, i ^ distance) for i in range(size)])


def swapped(x, axis):
    return lax.ppermute(x, axis, [(0, 1), (1, 0)])


def paired(
    grid_features,
    owners,
    adjacency,
    mesh_nodes,
    norm_gain,
    query_weight,
    key_weight,
    value_weight,
    output_weight,
    up_weight,
    down_weight,
):
    shards = lax.axis_size("shard")
    count, rows, half = grid_features.shape
    flat = grid_features.reshape(count * rows, half)
    half_unit = run_pick(mesh_nodes)
    far = crossed(half_unit, 2, shards)
    waiting, _ = lax.optimization_barrier((mesh_nodes, half_unit))
    near = crossed(waiting, 1, shards)
    waiting, _ = lax.optimization_barrier((flat, half_unit))
    other = swapped(waiting, "head")
    flat, gain, wq, wup, wdn, mesh, rest = run_stage(
        (
            flat,
            norm_gain.reshape(1, -1),
            query_weight,
            up_weight,
            down_weight,
            mesh_nodes,
            mesh_nodes,
        ),
        (None, 1, 0, 0, 1, None, "rest"),
    )
    straight = crossed(rest, 3, shards)
    far, _ = lax.optimization_barrier((far, rest))
    farther = crossed(far, 1, shards)
    far_pair = swapped(far, "head")
    queries, mlp = run_mlp(flat, other, gain, wq, wup, wdn)
    queries, mlp, far_pair, near = lax.optimization_barrier((queries, mlp, far_pair, near))
    blocked = (-1, BLOCK, 2 * half)
    mine_a = run_project((mesh, near, far, far_pair), key_weight, value_weight)
    sibling_a = swapped(mine_a, "sub")
    table = run_table(mine_a.reshape(blocked), sibling_a.reshape(blocked), 2 * shards)
    mine_b = run_project((farther, straight), key_weight, value_weight)
    sibling_b = swapped(mine_b, "sub")
    send, keep, att = run_attend(
        adjacency, queries, mine_b.reshape(blocked), sibling_b.reshape(blocked), table, mlp, output_weight
    )
    keeps, swaps, slots, placed = [], [], [], []
    shape = (shards * CAP, rows, half)
    every = tuple(range(len(CHUNKS)))
    for c in every:
        if c > 0:
            send, keep = run_project_out(c, att, mlp, output_weight)
        received = swapped(send, "head")
        swaps.append(received)
        keeps.append(keep)
    named, _ = lax.optimization_barrier((owners, keep))
    masks = run_plan(named, shards)
    for c in every:
        received = swaps[c]
        if c > 0:
            received, _ = lax.optimization_barrier((received, slots[c - 1][0]))
        slots.append(run_combine((c,), (2, 3), masks, grid_features, (keeps[c],), (received,)))
    swaps[-1], _ = lax.optimization_barrier((swaps[-1], slots[-1][0]))
    near_slots, own_slots = run_combine(every, (1, 0), masks, grid_features, keeps, swaps)
    for c in every:
        spots = [(2, (c,)), (3, (c,))]
        arrived = [crossed(slot, d, shards) for d, slot in zip((2, 3), slots[c])]
        if c == 0:
            spots.append((0, every))
            arrived.append(own_slots)
        if c == every[-1]:
            spots.append((1, every))
            arrived.append(crossed(near_slots, 1, shards))
        placed = [run_place(spots, arrived, placed, shape)]
    return placed[0]


def attend_plain(queries, key_table, value_table, chosen, scaling):
    count = chosen.shape[0]
    picked_keys = key_table[chosen]
    picked_keys = picked_keys.reshape(count, -1, picked_keys.shape[3], picked_keys.shape[4])
    picked_values = value_table[chosen]
    picked_values = picked_values.reshape(count, -1, picked_values.shape[3], picked_values.shape[4])
    scores = (
        jnp.einsum("gqhe,gkhe->ghqk", queries, picked_keys, preferred_element_type=jnp.float32)
        * scaling
    )
    highest = jnp.max(scores, axis=-1, keepdims=True)
    weights = jnp.exp(scores - highest)
    weights = (weights / jnp.sum(weights, axis=-1, keepdims=True)).astype(jnp.bfloat16)
    result = jnp.einsum(
        "ghqk,gkhe->gqhe", weights, picked_values, preferred_element_type=jnp.float32
    )
    return result.astype(jnp.bfloat16)


def general(
    grid_features,
    owners,
    adjacency,
    mesh_nodes,
    norm_gain,
    query_weight,
    key_weight,
    value_weight,
    output_weight,
    up_weight,
    down_weight,
):
    shard_count = lax.axis_size("shard")
    head_count = lax.axis_size("head")
    local_blocks, block_rows, feature_share = grid_features.shape
    slots = shard_count * CAP
    owner_col = owners[:, 0]
    position = jnp.arange(local_blocks, dtype=jnp.int32)
    earlier = (owner_col[:, None] == owner_col[None, :]) & (position[None, :] < position[:, None])
    target = owner_col * CAP + jnp.sum(earlier.astype(jnp.int32), axis=1)
    dispatch = (target[:, None] == jnp.arange(slots, dtype=jnp.int32)[None, :]).astype(jnp.bfloat16)
    offset = lax.axis_index("head") * (D // head_count)
    projected = jnp.stack(
        (
            jnp.dot(mesh_nodes, key_weight, preferred_element_type=jnp.float32).astype(
                jnp.bfloat16
            ),
            jnp.dot(mesh_nodes, value_weight, preferred_element_type=jnp.float32).astype(
                jnp.bfloat16
            ),
        )
    )
    tables = lax.all_gather(projected, ("shard", "sub"), axis=1, tiled=True)
    head_local = query_weight.shape[1] // HEAD_DIM
    key_table = tables[0].reshape(-1, block_rows, head_local, HEAD_DIM)
    value_table = tables[1].reshape(-1, block_rows, head_local, HEAD_DIM)
    send_lists = jnp.full((slots, adjacency.shape[1]), -1, jnp.int32).at[target].set(adjacency)
    send_lists = send_lists.reshape(shard_count, CAP, -1)
    complete = lax.all_gather(grid_features, "head", axis=2, tiled=True)
    outgoing = jnp.einsum(
        "gs,gbd->sbd", dispatch, complete, preferred_element_type=jnp.float32
    ).astype(jnp.bfloat16)
    arrived, lists = (
        lax.all_to_all(
            outgoing.reshape(shard_count, CAP, block_rows, D),
            "shard",
            split_axis=0,
            concat_axis=0,
            tiled=True,
        ),
        lax.all_to_all(send_lists, "shard", split_axis=0, concat_axis=0, tiled=True),
    )
    arrived = arrived.reshape(slots, block_rows, D)
    residual = lax.dynamic_slice_in_dim(arrived, offset, D // head_count, 2)
    lists = lists.reshape(slots, -1)
    count = arrived.shape[0]
    values_f = arrived.astype(jnp.float32)
    average = jnp.mean(values_f, axis=-1, keepdims=True)
    centered = values_f - average
    variance = jnp.mean(centered * centered, axis=-1, keepdims=True)
    normed = (centered * lax.rsqrt(variance + epsilon) * norm_gain).astype(jnp.bfloat16)
    flattened = normed.reshape(-1, D)
    queries = jnp.dot(flattened, query_weight, preferred_element_type=jnp.float32).astype(
        jnp.bfloat16
    )
    blocks_each = math.gcd(count, max(1, 512 // block_rows))
    steps_count = count // blocks_each
    queries = queries.reshape(steps_count, blocks_each, block_rows, head_local, HEAD_DIM)

    def attend_step(operands):
        return attend_plain(operands[0], key_table, value_table, operands[1], HEAD_DIM ** (-0.5))

    attended = lax.map(
        attend_step, (queries, jnp.maximum(lists, 0).reshape(steps_count, blocks_each, -1))
    )
    attended = attended.reshape(-1, head_local * HEAD_DIM)
    hidden = jax.nn.gelu(
        jnp.dot(flattened, up_weight, preferred_element_type=jnp.float32), approximate=False
    ).astype(jnp.bfloat16)
    branch = jnp.dot(attended, output_weight, preferred_element_type=jnp.float32)
    branch = branch + jnp.dot(hidden, down_weight, preferred_element_type=jnp.float32)
    branch = branch.reshape(count, block_rows, D)
    reduced = lax.psum_scatter(
        branch.astype(jnp.bfloat16), "head", scatter_dimension=2, tiled=True
    ).astype(jnp.float32)
    occupied = lists[:, 0] >= 0
    summed = residual.astype(jnp.float32) + reduced
    return jnp.where(occupied[:, None, None], summed, 0.0).astype(jnp.bfloat16)


def local(grid_features, owners, adjacency, mesh_nodes, *parameters):
    sizes = [lax.axis_size(axis) for axis in ("shard", "head", "sub")]
    small = grid_features.shape[:2] == (4, BLOCK) and mesh_nodes.shape[0] == 2 * BLOCK
    if sizes == [4, 2, 2] and small and grid_features.shape[2] == 512:
        return paired(grid_features, owners, adjacency, mesh_nodes, *parameters)
    return general(grid_features, owners, adjacency, mesh_nodes, *parameters)


def solution(mesh):
    return jax.shard_map(
        local,
        mesh=mesh,
        in_specs=(
            P(("groups", "shard", "sub"), None, "head"),
            P(("groups", "shard", "sub"), None),
            P(("groups", "shard", "sub"), None),
            P(("groups", "shard", "sub"), None),
            P(),
            P(None, "head"),
            P(None, "head"),
            P(None, "head"),
            P("head", None),
            P(None, "head"),
            P("head", None),
        ),
        out_specs=P(("groups", "shard", "sub"), None, "head"),
        check_vma=False,
    )
```

```python
import functools
import math

import jax
import jax.numpy as jnp
from jax import lax
from jax.experimental import pallas as pl
from jax.experimental.pallas import tpu as pltpu
from jax.sharding import PartitionSpec as P

D = 1024
HEAD_DIM = 64
CAP = 2
BLOCK = 64
QUAD = 4
WIDE = QUAD * HEAD_DIM
TILE = 128
CHUNKS = ((0, 96), (96, 256))
MIB = 1 << 20


epsilon = 1e-05


def dot(a, b):
    return jnp.dot(a, b, preferred_element_type=jnp.float32)


def gelu(x):
    return 0.5 * x * (1.0 + lax.erf(x * (2.0**-0.5)))


def in_hbm(x):
    return pltpu.with_memory_space_constraint(x, pltpu.HBM)


def in_vmem(x):
    return pltpu.with_memory_space_constraint(x, pltpu.VMEM)


def whole(space):
    return pl.BlockSpec(memory_space=space)


def vmem(count):
    return [whole(pltpu.VMEM)] * count


def params(mib):
    return pltpu.CompilerParams(vmem_limit_bytes=mib * MIB)


def mlp_kernel(own, other, gain, wq, wup, wdn, q_out, mlp_out, normed_s):
    half = own.shape[1]
    units = wup.shape[1]
    chunk = units // 4
    x_other = other[...].astype(jnp.float32)
    x_own = own[...].astype(jnp.float32)

    def mean(a, b):
        total = jnp.sum(a, axis=-1, keepdims=True) + jnp.sum(b, axis=-1, keepdims=True)
        return total * (0.5 / half)

    average = mean(x_other, x_own)
    x_other = x_other - average
    x_own = x_own - average
    factor = lax.rsqrt(mean(x_other * x_other, x_own * x_own) + epsilon)
    normed_s[:, :half] = (x_other * factor * gain[:, :half]).astype(jnp.bfloat16)
    normed_s[:, half:] = (x_own * factor * gain[:, half:]).astype(jnp.bfloat16)
    normed = normed_s[...]
    q_out[...] = dot(normed, wq[...]).astype(jnp.bfloat16)
    for c in range(units // chunk):
        span = slice(c * chunk, (c + 1) * chunk)
        hidden = gelu(dot(normed, wup[:, span])).astype(jnp.bfloat16)
        term = dot(hidden, wdn[span, :])
        if c == 0:
            mlp_out[...] = term
        else:
            mlp_out[...] += term


def run_mlp(own, other, gain, wq, wup, wdn):
    rows = own.shape[0]
    width = wq.shape[0]
    units = wup.shape[1]
    return pl.pallas_call(
        mlp_kernel,
        out_shape=(
            jax.ShapeDtypeStruct((rows, wq.shape[1]), jnp.bfloat16),
            jax.ShapeDtypeStruct((rows, width), jnp.float32),
        ),
        in_specs=vmem(6),
        out_specs=tuple(vmem(2)),
        scratch_shapes=[pltpu.VMEM((rows, width), jnp.bfloat16)],
        compiler_params=params(16),
        cost_estimate=pl.CostEstimate(
            flops=2 * rows * width * (wq.shape[1] + 2 * units),
            bytes_accessed=2 * width * (wq.shape[1] + 2 * units),
            transcendentals=rows * units,
        ),
        name="mlp",
    )(own, other, gain, wq, wup, wdn)


def pick_kernel(mesh, out, sem):
    first = pl.multiple_of(lax.axis_index("head") * BLOCK, BLOCK)
    copy = pltpu.make_async_copy(mesh.at[pl.ds(first, BLOCK), :], out, sem)
    copy.start()
    copy.wait()


def run_pick(mesh):
    return pl.pallas_call(
        pick_kernel,
        out_shape=jax.ShapeDtypeStruct((BLOCK, mesh.shape[1]), mesh.dtype),
        in_specs=[whole(pltpu.HBM)],
        out_specs=whole(pltpu.VMEM),
        scratch_shapes=[pltpu.SemaphoreType.DMA(())],
        compiler_params=params(4),
        cost_estimate=pl.CostEstimate(flops=0, bytes_accessed=4 * mesh.size, transcendentals=0),
        name="pick",
    )(in_hbm(mesh))


def stage_kernel(axes, *refs):
    sources, targets, sem = refs[: len(axes)], refs[len(axes) : -1], refs[-1]
    h = lax.axis_index("head")
    copies = []

    def add(source, target):
        pieces = 2 if source.shape[0] >= 512 else 1
        rows = source.shape[0] // pieces
        for piece in range(pieces):
            span = pl.ds(piece * rows, rows)
            copies.append(
                pltpu.make_async_copy(
                    source.at[span, :], target.at[span, :], sem.at[len(copies)]
                )
            )
            copies[-1].start()

    for source, target, axis in zip(sources, targets, axes):
        if axis is None:
            add(source, target)
            continue
        if axis == "rest":
            add(source.at[pl.ds(pl.multiple_of((1 - h) * BLOCK, BLOCK), BLOCK), :], target)
            continue
        half = source.shape[axis] // 2
        for part, head in enumerate((1 - h, h)):
            span = pl.ds(pl.multiple_of(head * half, half), half)
            place = pl.ds(part * half, half)
            if axis == 0:
                add(source.at[span, :], target.at[place, :])
            else:
                add(source.at[:, span], target.at[:, place])
    for copy in copies:
        copy.wait()


def run_stage(arrays, axes):
    size = sum(2 * array.size for array in arrays)
    return pl.pallas_call(
        functools.partial(stage_kernel, axes),
        out_shape=tuple(
            jax.ShapeDtypeStruct((BLOCK,) + array.shape[1:] if axis == "rest" else array.shape, array.dtype)
            for array, axis in zip(arrays, axes)
        ),
        in_specs=[whole(pltpu.HBM)] * len(arrays),
        out_specs=tuple(vmem(len(arrays))),
        scratch_shapes=[pltpu.SemaphoreType.DMA((4 * len(arrays),))],
        compiler_params=params(16),
        cost_estimate=pl.CostEstimate(
            flops=2000 * size, bytes_accessed=20 * size, transcendentals=0
        ),
        name="stage",
    )(*(in_hbm(array) for array in arrays))


def project_kernel(*refs):
    pieces, (wk, wv, out) = refs[:-3], refs[-3:]
    width = wk.shape[1]
    rows = jnp.concatenate([piece[...] for piece in pieces], axis=0)
    out[:, :width] = dot(rows, wk[...]).astype(jnp.bfloat16)
    out[:, width:] = dot(rows, wv[...]).astype(jnp.bfloat16)


def run_project(pieces, wk, wv):
    rows = sum(piece.shape[0] for piece in pieces)
    depth, width = wk.shape
    return pl.pallas_call(
        project_kernel,
        out_shape=jax.ShapeDtypeStruct((rows, 2 * width), jnp.bfloat16),
        in_specs=vmem(len(pieces) + 2),
        out_specs=whole(pltpu.VMEM),
        compiler_params=params(8),
        cost_estimate=pl.CostEstimate(
            flops=300 * rows * depth * width,
            bytes_accessed=300 * depth * width + 300 * rows * depth,
            transcendentals=0,
        ),
        name="project",
    )(*pieces, in_vmem(wk), in_vmem(wv))


def table_kernel(mine, sibling, table):
    table[0, : mine.shape[0]] = mine[...]
    table[1, : mine.shape[0]] = sibling[...]


def run_table(mine, sibling, blocks):
    return pl.pallas_call(
        table_kernel,
        out_shape=jax.ShapeDtypeStruct((2, blocks) + mine.shape[1:], jnp.bfloat16),
        in_specs=vmem(2),
        out_specs=whole(pltpu.VMEM),
        compiler_params=params(8),
        cost_estimate=pl.CostEstimate(
            flops=0, bytes_accessed=80 * mine.size, transcendentals=0
        ),
        name="table",
    )(mine, sibling)


def pieces_of(c):
    low, high = CHUNKS[c]
    pieces = []
    for tile in range(low // BLOCK, -(-high // BLOCK)):
        first, last = max(low, tile * BLOCK), min(high, (tile + 1) * BLOCK)
        rows = slice(first - tile * BLOCK, last - tile * BLOCK)
        pieces.append((tile, rows, slice(first - low, last - low)))
    return pieces


def project_out(c, att, mlp, wo, send, keep):
    half = att.shape[1]
    h = lax.axis_index("head")
    pieces = pieces_of(c)
    start, stop = pieces[0][0] * TILE, (pieces[-1][0] + 1) * TILE

    def write(head):
        for out, first, place in ((send, 0, 1 - head), (keep, half, head)):
            extra = mlp[:, first + start : first + stop]
            total = extra + dot(att[...], wo[:, place * half + start : place * half + stop])
            total = total.astype(jnp.bfloat16)
            for tile, rows, spot in pieces:
                columns = slice(tile * TILE - start, (tile + 1) * TILE - start)
                for t in range(out.shape[0]):
                    block = slice(t * BLOCK + rows.start, t * BLOCK + rows.stop)
                    out[t, spot, :] = total[block, columns]

    for head in range(2):
        pl.when(h == head)(functools.partial(write, head))


def attend_kernel(
    adjacency, q, mine, sibling, table_in, mlp, wo, send, keep, att, table, stacked_s, near_s, sem
):
    del table_in
    s = lax.axis_index("shard")
    h = lax.axis_index("head")
    u = lax.axis_index("sub")
    half = wo.shape[0]
    ready = table.shape[1] - mine.shape[0]
    copy = pltpu.make_async_copy(adjacency, near_s, sem)
    copy.start()
    for i, part in enumerate((mine, sibling)):
        table[i, ready:] = part[...]
    rows_of = lax.broadcasted_iota(jnp.int32, (WIDE, WIDE), 0) // BLOCK
    lanes_of = lax.broadcasted_iota(jnp.int32, (WIDE, WIDE), 1) // HEAD_DIM
    diagonal = rows_of == lanes_of
    lane_head = lax.broadcasted_iota(jnp.int32, (BLOCK, WIDE), 1) // HEAD_DIM
    scale = HEAD_DIM**-0.5 * math.log2(math.e)
    groups = half // WIDE
    steps = near_s.shape[0] * groups
    for step in range(steps):
        b, g = divmod(step, groups)
        columns = slice(g * WIDE, (g + 1) * WIDE)
        stacked = jnp.concatenate([q[b * BLOCK : (b + 1) * BLOCK, columns]] * QUAD, axis=0)
        stacked_s[step] = jnp.where(diagonal, stacked, jnp.zeros_like(stacked))
    copy.wait()
    places = []
    for b in range(near_s.shape[0]):
        places.append([])
        for j in range(near_s.shape[1]):
            m = near_s[b, j]
            part = lax.rem(m, 2)
            core = lax.rem(m // 2, 2)
            distance = s ^ (m // 4)
            part = jnp.where(distance <= 1, part, part ^ h)
            places[b].append((core ^ u, distance * 2 + part))

    def scores_of(step):
        b, g = divmod(step, groups)
        columns = slice(g * WIDE, (g + 1) * WIDE)
        keys = jnp.concatenate([table[i, p, :, columns] for i, p in places[b]], axis=0)
        return lax.dot_general(
            stacked_s[step], keys, (((1,), (1,)), ((), ())), preferred_element_type=jnp.float32
        )

    scores = scores_of(0)
    for step in range(steps):
        following = scores_of(step + 1) if step + 1 < steps else None
        b, g = divmod(step, groups)
        columns = slice(half + g * WIDE, half + (g + 1) * WIDE)
        values = jnp.concatenate([table[i, p, :, columns] for i, p in places[b]], axis=0)
        highest = jnp.max(scores, axis=-1, keepdims=True)
        weights = jnp.exp2((scores - highest) * scale)
        total = jnp.sum(weights, axis=-1, keepdims=True)
        mixed = dot(weights.astype(jnp.bfloat16), values) * (1.0 / total)
        merged = mixed[0:BLOCK, :]
        for i in range(1, QUAD):
            merged = jnp.where(lane_head == i, mixed[i * BLOCK : (i + 1) * BLOCK, :], merged)
        rows = slice(b * BLOCK, (b + 1) * BLOCK)
        att[rows, g * WIDE : (g + 1) * WIDE] = merged.astype(jnp.bfloat16)
        scores = following
    project_out(0, att, mlp, wo, send, keep)


def run_attend(adjacency, q, mine, sibling, table, mlp, wo):
    rows, half = q.shape
    size = CHUNKS[0][1] - CHUNKS[0][0]
    part = jax.ShapeDtypeStruct((rows // BLOCK, size, TILE), jnp.bfloat16)
    blocks = table.shape[0] * table.shape[1]
    send, keep, att, _ = pl.pallas_call(
        attend_kernel,
        out_shape=(
            part,
            part,
            jax.ShapeDtypeStruct(q.shape, jnp.bfloat16),
            jax.ShapeDtypeStruct(table.shape, jnp.bfloat16),
        ),
        in_specs=[whole(pl.ANY)] + vmem(6),
        out_specs=tuple(vmem(4)),
        scratch_shapes=[
            pltpu.VMEM((rows // BLOCK * (half // WIDE), WIDE, WIDE), jnp.bfloat16),
            pltpu.SMEM(adjacency.shape, jnp.int32),
            pltpu.SemaphoreType.DMA(()),
        ],
        input_output_aliases={4: 3},
        compiler_params=params(16),
        cost_estimate=pl.CostEstimate(
            flops=20 * rows * half * (D + 8 * 8 * BLOCK),
            bytes_accessed=40 * blocks * BLOCK * half + 20 * half * D + 40 * rows * D,
            transcendentals=rows * 8 * BLOCK * half // HEAD_DIM,
        ),
        name="attend",
    )(adjacency, q, mine, sibling, table, mlp, in_vmem(wo))
    return send, keep, att


def run_project_out(c, att, mlp, wo):
    rows, half = att.shape
    size = CHUNKS[c][1] - CHUNKS[c][0]
    part = jax.ShapeDtypeStruct((rows // BLOCK, size, TILE), jnp.bfloat16)
    return pl.pallas_call(
        functools.partial(project_out, c),
        out_shape=(part, part),
        in_specs=vmem(3),
        out_specs=tuple(vmem(2)),
        compiler_params=params(8),
        cost_estimate=pl.CostEstimate(
            flops=200 * rows * half * D,
            bytes_accessed=200 * half * D,
            transcendentals=0,
        ),
        name="project_out",
    )(att, mlp, in_vmem(wo))


def plan_kernel(owners, masks):
    s = lax.axis_index("shard")
    count = owners.shape[1]
    names = [owners[0, t] for t in range(count)]
    for t in range(count):
        same = [(names[e] == names[t]).astype(jnp.int32) for e in range(t)]
        rank = sum(same, jnp.int32(0))
        for d in range(masks.shape[0]):
            for j in range(CAP):
                hit = (names[t] == s ^ d) & (rank == j)
                masks[d, j, t] = jnp.full(masks.shape[3:], hit.astype(jnp.float32))


def run_plan(owners, shards):
    return pl.pallas_call(
        plan_kernel,
        out_shape=jax.ShapeDtypeStruct((shards, CAP, owners.shape[1], 8, 128), jnp.float32),
        in_specs=[whole(pltpu.SMEM)],
        out_specs=whole(pltpu.VMEM),
        compiler_params=params(4),
        cost_estimate=pl.CostEstimate(
            flops=100000000, bytes_accessed=1 << 18, transcendentals=0
        ),
        name="plan",
    )(owners)


def combine_kernel(chunks, distances, masks, grid_features, *refs):
    keeps, refs = refs[: len(chunks)], refs[len(chunks) :]
    swaps, outs = refs[: len(chunks)], refs[len(chunks) :]
    count = grid_features.shape[0]
    first = CHUNKS[chunks[0]][0]
    for c, keep, swap in zip(chunks, keeps, swaps):
        low, high = CHUNKS[c]
        updated = []
        for t in range(count):
            residual = [
                grid_features[t, rows, tile * TILE : (tile + 1) * TILE]
                for tile, rows, _ in pieces_of(c)
            ]
            residual = jnp.concatenate(residual, axis=0).astype(jnp.float32)
            partials = keep[t].astype(jnp.float32) + swap[t].astype(jnp.float32)
            updated.append(residual + partials)
        for d, out in zip(distances, outs):
            for j in range(CAP):
                chosen = jnp.zeros_like(updated[0])
                for t in range(count):
                    mask = jnp.broadcast_to(masks[d, j, t, 0:1, :], chosen.shape)
                    chosen = jnp.where(mask > 0.5, updated[t], chosen)
                out[j, low - first : high - first, :] = chosen.astype(jnp.bfloat16)


def run_combine(chunks, distances, masks, grid_features, keeps, swaps):
    count = grid_features.shape[0]
    rows, width = CHUNKS[chunks[-1]][1] - CHUNKS[chunks[0]][0], TILE
    slot = jax.ShapeDtypeStruct((CAP, rows, width), jnp.bfloat16)
    return pl.pallas_call(
        functools.partial(combine_kernel, chunks, distances),
        out_shape=(slot,) * len(distances),
        in_specs=vmem(2 + 2 * len(chunks)),
        out_specs=tuple(vmem(len(distances))),
        compiler_params=params(8),
        cost_estimate=pl.CostEstimate(
            flops=60000 * count * rows * width,
            bytes_accessed=400 * rows * width * (3 * count + CAP * len(distances)),
            transcendentals=0,
        ),
        name="combine",
    )(masks, grid_features, *keeps, *swaps)


def place_kernel(spots, *refs):
    out, sem = refs[-2:]
    s = lax.axis_index("shard")
    copies = []
    for ref, (d, chunks) in zip(refs, spots):
        first = CHUNKS[chunks[0]][0]
        slots = pl.ds((s ^ d) * CAP, CAP)
        for c in chunks:
            shift = CHUNKS[c][0] - first
            for tile, rows, spot in pieces_of(c):
                size = rows.stop - rows.start
                source = ref.at[:, pl.ds(spot.start + shift, size), :]
                columns = pl.ds(tile * TILE, TILE)
                target = out.at[slots, pl.ds(rows.start, size), columns]
                copies.append(pltpu.make_async_copy(source, target, sem.at[len(copies)]))
                copies[-1].start()
    for copy in copies:
        copy.wait()


def run_place(spots, arrived, placed, shape):
    count = sum(len(pieces_of(c)) for _, chunks in spots for c in chunks)
    return pl.pallas_call(
        functools.partial(place_kernel, spots),
        out_shape=jax.ShapeDtypeStruct(shape, jnp.bfloat16),
        in_specs=vmem(len(arrived)) + [whole(pltpu.HBM)] * len(placed),
        out_specs=whole(pltpu.HBM),
        scratch_shapes=[pltpu.SemaphoreType.DMA((count,))],
        input_output_aliases={len(arrived): 0} if placed else {},
        compiler_params=params(4),
        cost_estimate=pl.CostEstimate(
            flops=400000 * sum(part.size for part in arrived), bytes_accessed=0, transcendentals=0
        ),
        name="place",
    )(*arrived, *placed)


def crossed(x, distance, size):
    return lax.ppermute(x, "shard", [(i, i ^ distance) for i in range(size)])


def swapped(x, axis):
    return lax.ppermute(x, axis, [(0, 1), (1, 0)])


def paired(
    grid_features,
    owners,
    adjacency,
    mesh_nodes,
    norm_gain,
    query_weight,
    key_weight,
    value_weight,
    output_weight,
    up_weight,
    down_weight,
):
    shards = lax.axis_size("shard")
    count, rows, half = grid_features.shape
    flat = grid_features.reshape(count * rows, half)
    half_unit = run_pick(mesh_nodes)
    far = crossed(half_unit, 2, shards)
    waiting, _ = lax.optimization_barrier((mesh_nodes, half_unit))
    near = crossed(waiting, 1, shards)
    waiting, _ = lax.optimization_barrier((flat, half_unit))
    other = swapped(waiting, "head")
    flat, gain, wq, wup, wdn, mesh, rest = run_stage(
        (
            flat,
            norm_gain.reshape(1, -1),
            query_weight,
            up_weight,
            down_weight,
            mesh_nodes,
            mesh_nodes,
        ),
        (None, 1, 0, 0, 1, None, "rest"),
    )
    straight = crossed(rest, 3, shards)
    far, _ = lax.optimization_barrier((far, rest))
    farther = crossed(far, 1, shards)
    far_pair = swapped(far, "head")
    queries, mlp = run_mlp(flat, other, gain, wq, wup, wdn)
    queries, mlp, far_pair, near = lax.optimization_barrier((queries, mlp, far_pair, near))
    blocked = (-1, BLOCK, 2 * half)
    mine_a = run_project((mesh, near, far, far_pair), key_weight, value_weight)
    sibling_a = swapped(mine_a, "sub")
    table = run_table(mine_a.reshape(blocked), sibling_a.reshape(blocked), 2 * shards)
    mine_b = run_project((farther, straight), key_weight, value_weight)
    sibling_b = swapped(mine_b, "sub")
    send, keep, att = run_attend(
        adjacency, queries, mine_b.reshape(blocked), sibling_b.reshape(blocked), table, mlp, output_weight
    )
    keeps, swaps, slots, placed = [], [], [], []
    shape = (shards * CAP, rows, half)
    every = tuple(range(len(CHUNKS)))
    for c in every:
        if c > 0:
            send, keep = run_project_out(c, att, mlp, output_weight)
        received = swapped(send, "head")
        swaps.append(received)
        keeps.append(keep)
    named, _ = lax.optimization_barrier((owners, keep))
    masks = run_plan(named.T, shards)
    for c in every:
        received = swaps[c]
        if c > 0:
            received, _ = lax.optimization_barrier((received, slots[c - 1][0]))
        slots.append(run_combine((c,), (2, 3), masks, grid_features, (keeps[c],), (received,)))
    swaps[-1], _ = lax.optimization_barrier((swaps[-1], slots[-1][0]))
    near_slots, own_slots = run_combine(every, (1, 0), masks, grid_features, keeps, swaps)
    for c in every:
        moved = {d: crossed(slot, d, shards) for d, slot in zip((2, 3), slots[c])}
        if c == 0:
            groups = [[(2, (c,)), (3, (c,)), (0, every)]]
            moved[0] = own_slots
        else:
            groups = [[(1, every), (2, (c,))], [(3, (c,))]]
            moved[1] = crossed(near_slots, 1, shards)
        for spots in groups:
            placed = [run_place(spots, [moved[d] for d, _ in spots], placed, shape)]
    return placed[0]


def attend_plain(queries, key_table, value_table, chosen, scaling):
    count = chosen.shape[0]
    picked_keys = key_table[chosen]
    picked_keys = picked_keys.reshape(count, -1, picked_keys.shape[3], picked_keys.shape[4])
    picked_values = value_table[chosen]
    picked_values = picked_values.reshape(count, -1, picked_values.shape[3], picked_values.shape[4])
    scores = (
        jnp.einsum("gqhe,gkhe->ghqk", queries, picked_keys, preferred_element_type=jnp.float32)
        * scaling
    )
    highest = jnp.max(scores, axis=-1, keepdims=True)
    weights = jnp.exp(scores - highest)
    weights = (weights / jnp.sum(weights, axis=-1, keepdims=True)).astype(jnp.bfloat16)
    result = jnp.einsum(
        "ghqk,gkhe->gqhe", weights, picked_values, preferred_element_type=jnp.float32
    )
    return result.astype(jnp.bfloat16)


def general(
    grid_features,
    owners,
    adjacency,
    mesh_nodes,
    norm_gain,
    query_weight,
    key_weight,
    value_weight,
    output_weight,
    up_weight,
    down_weight,
):
    shard_count = lax.axis_size("shard")
    head_count = lax.axis_size("head")
    local_blocks, block_rows, feature_share = grid_features.shape
    slots = shard_count * CAP
    owner_col = owners[:, 0]
    position = jnp.arange(local_blocks, dtype=jnp.int32)
    earlier = (owner_col[:, None] == owner_col[None, :]) & (position[None, :] < position[:, None])
    target = owner_col * CAP + jnp.sum(earlier.astype(jnp.int32), axis=1)
    dispatch = (target[:, None] == jnp.arange(slots, dtype=jnp.int32)[None, :]).astype(jnp.bfloat16)
    offset = lax.axis_index("head") * (D // head_count)
    projected = jnp.stack(
        (
            jnp.dot(mesh_nodes, key_weight, preferred_element_type=jnp.float32).astype(
                jnp.bfloat16
            ),
            jnp.dot(mesh_nodes, value_weight, preferred_element_type=jnp.float32).astype(
                jnp.bfloat16
            ),
        )
    )
    tables = lax.all_gather(projected, ("shard", "sub"), axis=1, tiled=True)
    head_local = query_weight.shape[1] // HEAD_DIM
    key_table = tables[0].reshape(-1, block_rows, head_local, HEAD_DIM)
    value_table = tables[1].reshape(-1, block_rows, head_local, HEAD_DIM)
    send_lists = jnp.full((slots, adjacency.shape[1]), -1, jnp.int32).at[target].set(adjacency)
    send_lists = send_lists.reshape(shard_count, CAP, -1)
    complete = lax.all_gather(grid_features, "head", axis=2, tiled=True)
    outgoing = jnp.einsum(
        "gs,gbd->sbd", dispatch, complete, preferred_element_type=jnp.float32
    ).astype(jnp.bfloat16)
    arrived, lists = (
        lax.all_to_all(
            outgoing.reshape(shard_count, CAP, block_rows, D),
            "shard",
            split_axis=0,
            concat_axis=0,
            tiled=True,
        ),
        lax.all_to_all(send_lists, "shard", split_axis=0, concat_axis=0, tiled=True),
    )
    arrived = arrived.reshape(slots, block_rows, D)
    residual = lax.dynamic_slice_in_dim(arrived, offset, D // head_count, 2)
    lists = lists.reshape(slots, -1)
    count = arrived.shape[0]
    values_f = arrived.astype(jnp.float32)
    average = jnp.mean(values_f, axis=-1, keepdims=True)
    centered = values_f - average
    variance = jnp.mean(centered * centered, axis=-1, keepdims=True)
    normed = (centered * lax.rsqrt(variance + epsilon) * norm_gain).astype(jnp.bfloat16)
    flattened = normed.reshape(-1, D)
    queries = jnp.dot(flattened, query_weight, preferred_element_type=jnp.float32).astype(
        jnp.bfloat16
    )
    blocks_each = math.gcd(count, max(1, 512 // block_rows))
    steps_count = count // blocks_each
    queries = queries.reshape(steps_count, blocks_each, block_rows, head_local, HEAD_DIM)

    def attend_step(operands):
        return attend_plain(operands[0], key_table, value_table, operands[1], HEAD_DIM ** (-0.5))

    attended = lax.map(
        attend_step, (queries, jnp.maximum(lists, 0).reshape(steps_count, blocks_each, -1))
    )
    attended = attended.reshape(-1, head_local * HEAD_DIM)
    hidden = jax.nn.gelu(
        jnp.dot(flattened, up_weight, preferred_element_type=jnp.float32), approximate=False
    ).astype(jnp.bfloat16)
    branch = jnp.dot(attended, output_weight, preferred_element_type=jnp.float32)
    branch = branch + jnp.dot(hidden, down_weight, preferred_element_type=jnp.float32)
    branch = branch.reshape(count, block_rows, D)
    reduced = lax.psum_scatter(
        branch.astype(jnp.bfloat16), "head", scatter_dimension=2, tiled=True
    ).astype(jnp.float32)
    occupied = lists[:, 0] >= 0
    summed = residual.astype(jnp.float32) + reduced
    return jnp.where(occupied[:, None, None], summed, 0.0).astype(jnp.bfloat16)


def local(grid_features, owners, adjacency, mesh_nodes, *parameters):
    sizes = [lax.axis_size(axis) for axis in ("shard", "head", "sub")]
    small = grid_features.shape[:2] == (4, BLOCK) and mesh_nodes.shape[0] == 2 * BLOCK
    if sizes == [4, 2, 2] and small and grid_features.shape[2] == 512:
        return paired(grid_features, owners, adjacency, mesh_nodes, *parameters)
    return general(grid_features, owners, adjacency, mesh_nodes, *parameters)


def solution(mesh):
    return jax.shard_map(
        local,
        mesh=mesh,
        in_specs=(
            P(("groups", "shard", "sub"), None, "head"),
            P(("groups", "shard", "sub"), None),
            P(("groups", "shard", "sub"), None),
            P(("groups", "shard", "sub"), None),
            P(),
            P(None, "head"),
            P(None, "head"),
            P(None, "head"),
            P("head", None),
            P(None, "head"),
            P("head", None),
        ),
        out_specs=P(("groups", "shard", "sub"), None, "head"),
        check_vma=False,
    )
```

```python
import functools
import math

import jax
import jax.numpy as jnp
from jax import lax
from jax.experimental import pallas as pl
from jax.experimental.pallas import tpu as pltpu
from jax.sharding import PartitionSpec as P

D = 1024
HEAD_DIM = 64
CAP = 2
BLOCK = 64
QUAD = 4
WIDE = QUAD * HEAD_DIM
TILE = 128
CHUNKS = ((0, 96), (96, 256))
MIB = 1 << 20


epsilon = 1e-05


def dot(a, b):
    return jnp.dot(a, b, preferred_element_type=jnp.float32)


def gelu(x):
    return 0.5 * x * (1.0 + lax.erf(x * (2.0**-0.5)))


def in_hbm(x):
    return pltpu.with_memory_space_constraint(x, pltpu.HBM)


def in_vmem(x):
    return pltpu.with_memory_space_constraint(x, pltpu.VMEM)


def whole(space):
    return pl.BlockSpec(memory_space=space)


def vmem(count):
    return [whole(pltpu.VMEM)] * count


def params(mib):
    return pltpu.CompilerParams(vmem_limit_bytes=mib * MIB)


def mlp_kernel(own, other, gain, wq, wup, wdn, q_out, mlp_out, normed_s):
    half = own.shape[1]
    units = wup.shape[1]
    chunk = units // 4
    x_other = other[...].astype(jnp.float32)
    x_own = own[...].astype(jnp.float32)

    def mean(a, b):
        total = jnp.sum(a, axis=-1, keepdims=True) + jnp.sum(b, axis=-1, keepdims=True)
        return total * (0.5 / half)

    average = mean(x_other, x_own)
    x_other = x_other - average
    x_own = x_own - average
    factor = lax.rsqrt(mean(x_other * x_other, x_own * x_own) + epsilon)
    normed_s[:, :half] = (x_other * factor * gain[:, :half]).astype(jnp.bfloat16)
    normed_s[:, half:] = (x_own * factor * gain[:, half:]).astype(jnp.bfloat16)
    normed = normed_s[...]
    q_out[...] = dot(normed, wq[...]).astype(jnp.bfloat16)
    for c in range(units // chunk):
        span = slice(c * chunk, (c + 1) * chunk)
        hidden = gelu(dot(normed, wup[:, span])).astype(jnp.bfloat16)
        term = dot(hidden, wdn[span, :])
        if c == 0:
            mlp_out[...] = term
        else:
            mlp_out[...] += term


def run_mlp(own, other, gain, wq, wup, wdn):
    rows = own.shape[0]
    width = wq.shape[0]
    units = wup.shape[1]
    return pl.pallas_call(
        mlp_kernel,
        out_shape=(
            jax.ShapeDtypeStruct((rows, wq.shape[1]), jnp.bfloat16),
            jax.ShapeDtypeStruct((rows, width), jnp.float32),
        ),
        in_specs=vmem(6),
        out_specs=tuple(vmem(2)),
        scratch_shapes=[pltpu.VMEM((rows, width), jnp.bfloat16)],
        compiler_params=params(16),
        cost_estimate=pl.CostEstimate(
            flops=2 * rows * width * (wq.shape[1] + 2 * units),
            bytes_accessed=2 * width * (wq.shape[1] + 2 * units),
            transcendentals=rows * units,
        ),
        name="mlp",
    )(own, other, gain, wq, wup, wdn)


def pick_kernel(mesh, out, sem):
    first = pl.multiple_of(lax.axis_index("head") * BLOCK, BLOCK)
    copy = pltpu.make_async_copy(mesh.at[pl.ds(first, BLOCK), :], out, sem)
    copy.start()
    copy.wait()


def run_pick(mesh):
    return pl.pallas_call(
        pick_kernel,
        out_shape=jax.ShapeDtypeStruct((BLOCK, mesh.shape[1]), mesh.dtype),
        in_specs=[whole(pltpu.HBM)],
        out_specs=whole(pltpu.VMEM),
        scratch_shapes=[pltpu.SemaphoreType.DMA(())],
        compiler_params=params(4),
        cost_estimate=pl.CostEstimate(flops=0, bytes_accessed=4 * mesh.size, transcendentals=0),
        name="pick",
    )(in_hbm(mesh))


def stage_kernel(axes, *refs):
    sources, targets, sem = refs[: len(axes)], refs[len(axes) : -1], refs[-1]
    h = lax.axis_index("head")
    copies = []

    def add(source, target):
        pieces = 2 if source.shape[0] >= 512 else 1
        rows = source.shape[0] // pieces
        for piece in range(pieces):
            span = pl.ds(piece * rows, rows)
            copies.append(
                pltpu.make_async_copy(
                    source.at[span, :], target.at[span, :], sem.at[len(copies)]
                )
            )
            copies[-1].start()

    for source, target, axis in zip(sources, targets, axes):
        if axis is None:
            add(source, target)
            continue
        if axis == "rest":
            add(source.at[pl.ds(pl.multiple_of((1 - h) * BLOCK, BLOCK), BLOCK), :], target)
            continue
        half = source.shape[axis] // 2
        for part, head in enumerate((1 - h, h)):
            span = pl.ds(pl.multiple_of(head * half, half), half)
            place = pl.ds(part * half, half)
            if axis == 0:
                add(source.at[span, :], target.at[place, :])
            else:
                add(source.at[:, span], target.at[:, place])
    for copy in copies:
        copy.wait()


def run_stage(arrays, axes):
    size = sum(2 * array.size for array in arrays)
    return pl.pallas_call(
        functools.partial(stage_kernel, axes),
        out_shape=tuple(
            jax.ShapeDtypeStruct((BLOCK,) + array.shape[1:] if axis == "rest" else array.shape, array.dtype)
            for array, axis in zip(arrays, axes)
        ),
        in_specs=[whole(pltpu.HBM)] * len(arrays),
        out_specs=tuple(vmem(len(arrays))),
        scratch_shapes=[pltpu.SemaphoreType.DMA((4 * len(arrays),))],
        compiler_params=params(16),
        cost_estimate=pl.CostEstimate(
            flops=2000 * size, bytes_accessed=20 * size, transcendentals=0
        ),
        name="stage",
    )(*(in_hbm(array) for array in arrays))


def project_kernel(*refs):
    pieces, (wk, wv, out) = refs[:-3], refs[-3:]
    width = wk.shape[1]
    rows = jnp.concatenate([piece[...] for piece in pieces], axis=0)
    out[:, :width] = dot(rows, wk[...]).astype(jnp.bfloat16)
    out[:, width:] = dot(rows, wv[...]).astype(jnp.bfloat16)


def run_project(pieces, wk, wv):
    rows = sum(piece.shape[0] for piece in pieces)
    depth, width = wk.shape
    return pl.pallas_call(
        project_kernel,
        out_shape=jax.ShapeDtypeStruct((rows, 2 * width), jnp.bfloat16),
        in_specs=vmem(len(pieces) + 2),
        out_specs=whole(pltpu.VMEM),
        compiler_params=params(8),
        cost_estimate=pl.CostEstimate(
            flops=300 * rows * depth * width,
            bytes_accessed=300 * depth * width + 300 * rows * depth,
            transcendentals=0,
        ),
        name="project",
    )(*pieces, in_vmem(wk), in_vmem(wv))


def table_kernel(mine, sibling, table):
    table[0, : mine.shape[0]] = mine[...]
    table[1, : mine.shape[0]] = sibling[...]


def run_table(mine, sibling, blocks):
    return pl.pallas_call(
        table_kernel,
        out_shape=jax.ShapeDtypeStruct((2, blocks) + mine.shape[1:], jnp.bfloat16),
        in_specs=vmem(2),
        out_specs=whole(pltpu.VMEM),
        compiler_params=params(8),
        cost_estimate=pl.CostEstimate(
            flops=0, bytes_accessed=80 * mine.size, transcendentals=0
        ),
        name="table",
    )(mine, sibling)


def pieces_of(c):
    low, high = CHUNKS[c]
    pieces = []
    for tile in range(low // BLOCK, -(-high // BLOCK)):
        first, last = max(low, tile * BLOCK), min(high, (tile + 1) * BLOCK)
        rows = slice(first - tile * BLOCK, last - tile * BLOCK)
        pieces.append((tile, rows, slice(first - low, last - low)))
    return pieces


def project_out(c, att, mlp, wo, send, keep):
    half = att.shape[1]
    h = lax.axis_index("head")
    pieces = pieces_of(c)
    start, stop = pieces[0][0] * TILE, (pieces[-1][0] + 1) * TILE

    def write(head):
        for out, first, place in ((send, 0, 1 - head), (keep, half, head)):
            extra = mlp[:, first + start : first + stop]
            total = extra + dot(att[...], wo[:, place * half + start : place * half + stop])
            total = total.astype(jnp.bfloat16)
            for tile, rows, spot in pieces:
                columns = slice(tile * TILE - start, (tile + 1) * TILE - start)
                for t in range(out.shape[0]):
                    block = slice(t * BLOCK + rows.start, t * BLOCK + rows.stop)
                    out[t, spot, :] = total[block, columns]

    for head in range(2):
        pl.when(h == head)(functools.partial(write, head))


def attend_kernel(
    adjacency, q, mine, sibling, table_in, mlp, wo, send, keep, att, table, stacked_s, near_s, sem
):
    del table_in
    s = lax.axis_index("shard")
    h = lax.axis_index("head")
    u = lax.axis_index("sub")
    half = wo.shape[0]
    ready = table.shape[1] - mine.shape[0]
    copy = pltpu.make_async_copy(adjacency, near_s, sem)
    copy.start()
    for i, part in enumerate((mine, sibling)):
        table[i, ready:] = part[...]
    rows_of = lax.broadcasted_iota(jnp.int32, (WIDE, WIDE), 0) // BLOCK
    lanes_of = lax.broadcasted_iota(jnp.int32, (WIDE, WIDE), 1) // HEAD_DIM
    diagonal = rows_of == lanes_of
    lane_head = lax.broadcasted_iota(jnp.int32, (BLOCK, WIDE), 1) // HEAD_DIM
    scale = HEAD_DIM**-0.5 * math.log2(math.e)
    groups = half // WIDE
    steps = near_s.shape[0] * groups
    for step in range(steps):
        b, g = divmod(step, groups)
        columns = slice(g * WIDE, (g + 1) * WIDE)
        stacked = jnp.concatenate([q[b * BLOCK : (b + 1) * BLOCK, columns]] * QUAD, axis=0)
        stacked_s[step] = jnp.where(diagonal, stacked, jnp.zeros_like(stacked))
    copy.wait()
    places = []
    for b in range(near_s.shape[0]):
        places.append([])
        for j in range(near_s.shape[1]):
            m = near_s[b, j]
            part = lax.rem(m, 2)
            core = lax.rem(m // 2, 2)
            distance = s ^ (m // 4)
            part = jnp.where(distance <= 1, part, part ^ h)
            places[b].append((core ^ u, distance * 2 + part))

    def scores_of(step):
        b, g = divmod(step, groups)
        columns = slice(g * WIDE, (g + 1) * WIDE)
        keys = jnp.concatenate([table[i, p, :, columns] for i, p in places[b]], axis=0)
        return lax.dot_general(
            stacked_s[step], keys, (((1,), (1,)), ((), ())), preferred_element_type=jnp.float32
        )

    scores = scores_of(0)
    for step in range(steps):
        following = scores_of(step + 1) if step + 1 < steps else None
        b, g = divmod(step, groups)
        columns = slice(half + g * WIDE, half + (g + 1) * WIDE)
        values = jnp.concatenate([table[i, p, :, columns] for i, p in places[b]], axis=0)
        highest = jnp.max(scores, axis=-1, keepdims=True)
        weights = jnp.exp2((scores - highest) * scale)
        total = jnp.sum(weights, axis=-1, keepdims=True)
        mixed = dot(weights.astype(jnp.bfloat16), values) * (1.0 / total)
        merged = mixed[0:BLOCK, :]
        for i in range(1, QUAD):
            merged = jnp.where(lane_head == i, mixed[i * BLOCK : (i + 1) * BLOCK, :], merged)
        rows = slice(b * BLOCK, (b + 1) * BLOCK)
        att[rows, g * WIDE : (g + 1) * WIDE] = merged.astype(jnp.bfloat16)
        scores = following
    project_out(0, att, mlp, wo, send, keep)


def run_attend(adjacency, q, mine, sibling, table, mlp, wo):
    rows, half = q.shape
    size = CHUNKS[0][1] - CHUNKS[0][0]
    part = jax.ShapeDtypeStruct((rows // BLOCK, size, TILE), jnp.bfloat16)
    blocks = table.shape[0] * table.shape[1]
    send, keep, att, _ = pl.pallas_call(
        attend_kernel,
        out_shape=(
            part,
            part,
            jax.ShapeDtypeStruct(q.shape, jnp.bfloat16),
            jax.ShapeDtypeStruct(table.shape, jnp.bfloat16),
        ),
        in_specs=[whole(pl.ANY)] + vmem(6),
        out_specs=tuple(vmem(4)),
        scratch_shapes=[
            pltpu.VMEM((rows // BLOCK * (half // WIDE), WIDE, WIDE), jnp.bfloat16),
            pltpu.SMEM(adjacency.shape, jnp.int32),
            pltpu.SemaphoreType.DMA(()),
        ],
        input_output_aliases={4: 3},
        compiler_params=params(16),
        cost_estimate=pl.CostEstimate(
            flops=20 * rows * half * (D + 8 * 8 * BLOCK),
            bytes_accessed=40 * blocks * BLOCK * half + 20 * half * D + 40 * rows * D,
            transcendentals=rows * 8 * BLOCK * half // HEAD_DIM,
        ),
        name="attend",
    )(adjacency, q, mine, sibling, table, mlp, in_vmem(wo))
    return send, keep, att


def run_project_out(c, att, mlp, wo):
    rows, half = att.shape
    size = CHUNKS[c][1] - CHUNKS[c][0]
    part = jax.ShapeDtypeStruct((rows // BLOCK, size, TILE), jnp.bfloat16)
    return pl.pallas_call(
        functools.partial(project_out, c),
        out_shape=(part, part),
        in_specs=vmem(3),
        out_specs=tuple(vmem(2)),
        compiler_params=params(8),
        cost_estimate=pl.CostEstimate(
            flops=200 * rows * half * D,
            bytes_accessed=200 * half * D,
            transcendentals=0,
        ),
        name="project_out",
    )(att, mlp, in_vmem(wo))


def plan_kernel(owners, masks):
    s = lax.axis_index("shard")
    count = owners.shape[1]
    names = [owners[0, t] for t in range(count)]
    for t in range(count):
        same = [(names[e] == names[t]).astype(jnp.int32) for e in range(t)]
        rank = sum(same, jnp.int32(0))
        for d in range(masks.shape[0]):
            for j in range(CAP):
                hit = (names[t] == s ^ d) & (rank == j)
                masks[d, j, t] = jnp.full(masks.shape[3:], hit.astype(jnp.float32))


def run_plan(owners, shards):
    return pl.pallas_call(
        plan_kernel,
        out_shape=jax.ShapeDtypeStruct((shards, CAP, owners.shape[1], 8, 128), jnp.float32),
        in_specs=[whole(pltpu.SMEM)],
        out_specs=whole(pltpu.VMEM),
        compiler_params=params(4),
        cost_estimate=pl.CostEstimate(
            flops=100000000, bytes_accessed=1 << 18, transcendentals=0
        ),
        name="plan",
    )(owners)


def combine_kernel(chunks, distances, masks, grid_features, *refs):
    keeps, refs = refs[: len(chunks)], refs[len(chunks) :]
    swaps, outs = refs[: len(chunks)], refs[len(chunks) :]
    count = grid_features.shape[0]
    first = CHUNKS[chunks[0]][0]
    for c, keep, swap in zip(chunks, keeps, swaps):
        low, high = CHUNKS[c]
        updated = []
        for t in range(count):
            residual = [
                grid_features[t, rows, tile * TILE : (tile + 1) * TILE]
                for tile, rows, _ in pieces_of(c)
            ]
            residual = jnp.concatenate(residual, axis=0).astype(jnp.float32)
            partials = keep[t].astype(jnp.float32) + swap[t].astype(jnp.float32)
            updated.append(residual + partials)
        for d, out in zip(distances, outs):
            for j in range(CAP):
                chosen = jnp.zeros_like(updated[0])
                for t in range(count):
                    mask = jnp.broadcast_to(masks[d, j, t, 0:1, :], chosen.shape)
                    chosen = jnp.where(mask > 0.5, updated[t], chosen)
                out[j, low - first : high - first, :] = chosen.astype(jnp.bfloat16)


def run_combine(chunks, distances, masks, grid_features, keeps, swaps):
    count = grid_features.shape[0]
    rows, width = CHUNKS[chunks[-1]][1] - CHUNKS[chunks[0]][0], TILE
    slot = jax.ShapeDtypeStruct((CAP, rows, width), jnp.bfloat16)
    return pl.pallas_call(
        functools.partial(combine_kernel, chunks, distances),
        out_shape=(slot,) * len(distances),
        in_specs=vmem(2 + 2 * len(chunks)),
        out_specs=tuple(vmem(len(distances))),
        compiler_params=params(8),
        cost_estimate=pl.CostEstimate(
            flops=60000 * count * rows * width,
            bytes_accessed=400 * rows * width * (3 * count + CAP * len(distances)),
            transcendentals=0,
        ),
        name="combine",
    )(masks, grid_features, *keeps, *swaps)


def place_kernel(spots, *refs):
    out, sem = refs[-2:]
    s = lax.axis_index("shard")
    copies = []
    for ref, (d, chunks) in zip(refs, spots):
        first = CHUNKS[chunks[0]][0]
        slots = pl.ds((s ^ d) * CAP, CAP)
        for c in chunks:
            shift = CHUNKS[c][0] - first
            for tile, rows, spot in pieces_of(c):
                size = rows.stop - rows.start
                source = ref.at[:, pl.ds(spot.start + shift, size), :]
                columns = pl.ds(tile * TILE, TILE)
                target = out.at[slots, pl.ds(rows.start, size), columns]
                copies.append(pltpu.make_async_copy(source, target, sem.at[len(copies)]))
                copies[-1].start()
    for copy in copies:
        copy.wait()


def run_place(spots, arrived, placed, shape):
    count = sum(len(pieces_of(c)) for _, chunks in spots for c in chunks)
    return pl.pallas_call(
        functools.partial(place_kernel, spots),
        out_shape=jax.ShapeDtypeStruct(shape, jnp.bfloat16),
        in_specs=vmem(len(arrived)) + [whole(pltpu.HBM)] * len(placed),
        out_specs=whole(pltpu.HBM),
        scratch_shapes=[pltpu.SemaphoreType.DMA((count,))],
        input_output_aliases={len(arrived): 0} if placed else {},
        compiler_params=params(4),
        cost_estimate=pl.CostEstimate(
            flops=400000 * sum(part.size for part in arrived), bytes_accessed=0, transcendentals=0
        ),
        name="place",
    )(*arrived, *placed)


def crossed(x, distance, size):
    return lax.ppermute(x, "shard", [(i, i ^ distance) for i in range(size)])


def swapped(x, axis):
    return lax.ppermute(x, axis, [(0, 1), (1, 0)])


def paired(
    grid_features,
    owners,
    adjacency,
    mesh_nodes,
    norm_gain,
    query_weight,
    key_weight,
    value_weight,
    output_weight,
    up_weight,
    down_weight,
):
    shards = lax.axis_size("shard")
    count, rows, half = grid_features.shape
    flat = grid_features.reshape(count * rows, half)
    half_unit = run_pick(mesh_nodes)
    far = crossed(half_unit, 2, shards)
    near = crossed(mesh_nodes, 1, shards)
    waiting, _ = lax.optimization_barrier((flat, half_unit))
    other = swapped(waiting, "head")
    flat, gain, wq, wup, wdn, mesh, rest = run_stage(
        (
            flat,
            norm_gain.reshape(1, -1),
            query_weight,
            up_weight,
            down_weight,
            mesh_nodes,
            mesh_nodes,
        ),
        (None, 1, 0, 0, 1, None, "rest"),
    )
    straight = crossed(rest, 3, shards)
    far, _ = lax.optimization_barrier((far, rest))
    farther = crossed(far, 1, shards)
    far_pair = swapped(far, "head")
    queries, mlp = run_mlp(flat, other, gain, wq, wup, wdn)
    queries, mlp, far_pair, near = lax.optimization_barrier((queries, mlp, far_pair, near))
    blocked = (-1, BLOCK, 2 * half)
    mine_a = run_project((mesh, near, far, far_pair), key_weight, value_weight)
    sibling_a = swapped(mine_a, "sub")
    table = run_table(mine_a.reshape(blocked), sibling_a.reshape(blocked), 2 * shards)
    mine_b = run_project((farther, straight), key_weight, value_weight)
    sibling_b = swapped(mine_b, "sub")
    send, keep, att = run_attend(
        adjacency, queries, mine_b.reshape(blocked), sibling_b.reshape(blocked), table, mlp, output_weight
    )
    keeps, swaps, slots, placed = [], [], [], []
    shape = (shards * CAP, rows, half)
    every = tuple(range(len(CHUNKS)))
    for c in every:
        if c > 0:
            send, keep = run_project_out(c, att, mlp, output_weight)
        received = swapped(send, "head")
        swaps.append(received)
        keeps.append(keep)
    named, _ = lax.optimization_barrier((owners, keep))
    masks = run_plan(named.T, shards)
    for c in every:
        received = swaps[c]
        if c > 0:
            received, _ = lax.optimization_barrier((received, slots[c - 1][0]))
        slots.append(run_combine((c,), (2, 3), masks, grid_features, (keeps[c],), (received,)))
    swaps[-1], _ = lax.optimization_barrier((swaps[-1], slots[-1][0]))
    near_slots, own_slots = run_combine(every, (1, 0), masks, grid_features, keeps, swaps)
    for c in every:
        spots = [(2, (c,)), (3, (c,))]
        arrived = [crossed(slot, d, shards) for d, slot in zip((2, 3), slots[c])]
        if c == 0:
            spots.append((0, every))
            arrived.append(own_slots)
        if c == every[-1]:
            spots.append((1, every))
            arrived.append(crossed(near_slots, 1, shards))
        placed = [run_place(spots, arrived, placed, shape)]
    return placed[0]


def attend_plain(queries, key_table, value_table, chosen, scaling):
    count = chosen.shape[0]
    picked_keys = key_table[chosen]
    picked_keys = picked_keys.reshape(count, -1, picked_keys.shape[3], picked_keys.shape[4])
    picked_values = value_table[chosen]
    picked_values = picked_values.reshape(count, -1, picked_values.shape[3], picked_values.shape[4])
    scores = (
        jnp.einsum("gqhe,gkhe->ghqk", queries, picked_keys, preferred_element_type=jnp.float32)
        * scaling
    )
    highest = jnp.max(scores, axis=-1, keepdims=True)
    weights = jnp.exp(scores - highest)
    weights = (weights / jnp.sum(weights, axis=-1, keepdims=True)).astype(jnp.bfloat16)
    result = jnp.einsum(
        "ghqk,gkhe->gqhe", weights, picked_values, preferred_element_type=jnp.float32
    )
    return result.astype(jnp.bfloat16)


def general(
    grid_features,
    owners,
    adjacency,
    mesh_nodes,
    norm_gain,
    query_weight,
    key_weight,
    value_weight,
    output_weight,
    up_weight,
    down_weight,
):
    shard_count = lax.axis_size("shard")
    head_count = lax.axis_size("head")
    local_blocks, block_rows, feature_share = grid_features.shape
    slots = shard_count * CAP
    owner_col = owners[:, 0]
    position = jnp.arange(local_blocks, dtype=jnp.int32)
    earlier = (owner_col[:, None] == owner_col[None, :]) & (position[None, :] < position[:, None])
    target = owner_col * CAP + jnp.sum(earlier.astype(jnp.int32), axis=1)
    dispatch = (target[:, None] == jnp.arange(slots, dtype=jnp.int32)[None, :]).astype(jnp.bfloat16)
    offset = lax.axis_index("head") * (D // head_count)
    projected = jnp.stack(
        (
            jnp.dot(mesh_nodes, key_weight, preferred_element_type=jnp.float32).astype(
                jnp.bfloat16
            ),
            jnp.dot(mesh_nodes, value_weight, preferred_element_type=jnp.float32).astype(
                jnp.bfloat16
            ),
        )
    )
    tables = lax.all_gather(projected, ("shard", "sub"), axis=1, tiled=True)
    head_local = query_weight.shape[1] // HEAD_DIM
    key_table = tables[0].reshape(-1, block_rows, head_local, HEAD_DIM)
    value_table = tables[1].reshape(-1, block_rows, head_local, HEAD_DIM)
    send_lists = jnp.full((slots, adjacency.shape[1]), -1, jnp.int32).at[target].set(adjacency)
    send_lists = send_lists.reshape(shard_count, CAP, -1)
    complete = lax.all_gather(grid_features, "head", axis=2, tiled=True)
    outgoing = jnp.einsum(
        "gs,gbd->sbd", dispatch, complete, preferred_element_type=jnp.float32
    ).astype(jnp.bfloat16)
    arrived, lists = (
        lax.all_to_all(
            outgoing.reshape(shard_count, CAP, block_rows, D),
            "shard",
            split_axis=0,
            concat_axis=0,
            tiled=True,
        ),
        lax.all_to_all(send_lists, "shard", split_axis=0, concat_axis=0, tiled=True),
    )
    arrived = arrived.reshape(slots, block_rows, D)
    residual = lax.dynamic_slice_in_dim(arrived, offset, D // head_count, 2)
    lists = lists.reshape(slots, -1)
    count = arrived.shape[0]
    values_f = arrived.astype(jnp.float32)
    average = jnp.mean(values_f, axis=-1, keepdims=True)
    centered = values_f - average
    variance = jnp.mean(centered * centered, axis=-1, keepdims=True)
    normed = (centered * lax.rsqrt(variance + epsilon) * norm_gain).astype(jnp.bfloat16)
    flattened = normed.reshape(-1, D)
    queries = jnp.dot(flattened, query_weight, preferred_element_type=jnp.float32).astype(
        jnp.bfloat16
    )
    blocks_each = math.gcd(count, max(1, 512 // block_rows))
    steps_count = count // blocks_each
    queries = queries.reshape(steps_count, blocks_each, block_rows, head_local, HEAD_DIM)

    def attend_step(operands):
        return attend_plain(operands[0], key_table, value_table, operands[1], HEAD_DIM ** (-0.5))

    attended = lax.map(
        attend_step, (queries, jnp.maximum(lists, 0).reshape(steps_count, blocks_each, -1))
    )
    attended = attended.reshape(-1, head_local * HEAD_DIM)
    hidden = jax.nn.gelu(
        jnp.dot(flattened, up_weight, preferred_element_type=jnp.float32), approximate=False
    ).astype(jnp.bfloat16)
    branch = jnp.dot(attended, output_weight, preferred_element_type=jnp.float32)
    branch = branch + jnp.dot(hidden, down_weight, preferred_element_type=jnp.float32)
    branch = branch.reshape(count, block_rows, D)
    reduced = lax.psum_scatter(
        branch.astype(jnp.bfloat16), "head", scatter_dimension=2, tiled=True
    ).astype(jnp.float32)
    occupied = lists[:, 0] >= 0
    summed = residual.astype(jnp.float32) + reduced
    return jnp.where(occupied[:, None, None], summed, 0.0).astype(jnp.bfloat16)


def local(grid_features, owners, adjacency, mesh_nodes, *parameters):
    sizes = [lax.axis_size(axis) for axis in ("shard", "head", "sub")]
    small = grid_features.shape[:2] == (4, BLOCK) and mesh_nodes.shape[0] == 2 * BLOCK
    if sizes == [4, 2, 2] and small and grid_features.shape[2] == 512:
        return paired(grid_features, owners, adjacency, mesh_nodes, *parameters)
    return general(grid_features, owners, adjacency, mesh_nodes, *parameters)


def solution(mesh):
    return jax.shard_map(
        local,
        mesh=mesh,
        in_specs=(
            P(("groups", "shard", "sub"), None, "head"),
            P(("groups", "shard", "sub"), None),
            P(("groups", "shard", "sub"), None),
            P(("groups", "shard", "sub"), None),
            P(),
            P(None, "head"),
            P(None, "head"),
            P(None, "head"),
            P("head", None),
            P(None, "head"),
            P("head", None),
        ),
        out_specs=P(("groups", "shard", "sub"), None, "head"),
        check_vma=False,
    )
```

```python
import functools
import math

import jax
import jax.numpy as jnp
from jax import lax
from jax.experimental import pallas as pl
from jax.experimental.pallas import tpu as pltpu
from jax.sharding import PartitionSpec as P

D = 1024
HEAD_DIM = 64
CAP = 2
BLOCK = 64
QUAD = 4
WIDE = QUAD * HEAD_DIM
TILE = 128
CHUNKS = ((0, 96), (96, 256))
MIB = 1 << 20


epsilon = 1e-05


def dot(a, b):
    return jnp.dot(a, b, preferred_element_type=jnp.float32)


def gelu(x):
    return 0.5 * x * (1.0 + lax.erf(x * (2.0**-0.5)))


def in_hbm(x):
    return pltpu.with_memory_space_constraint(x, pltpu.HBM)


def in_vmem(x):
    return pltpu.with_memory_space_constraint(x, pltpu.VMEM)


def whole(space):
    return pl.BlockSpec(memory_space=space)


def vmem(count):
    return [whole(pltpu.VMEM)] * count


def params(mib):
    return pltpu.CompilerParams(vmem_limit_bytes=mib * MIB)


def add_units(normed, wup, wdn, out, span, fresh):
    chunk = 512
    for start in range(span.start, span.stop, chunk):
        units = slice(start, start + chunk)
        hidden = gelu(dot(normed, wup[:, units])).astype(jnp.bfloat16)
        term = dot(hidden, wdn[units, :])
        if fresh and start == span.start:
            out[...] = term
        else:
            out[...] += term


def mlp_kernel(split, own, other, gain, wq, wup, wdn, q_out, normed_out, sum_out):
    half = own.shape[1]
    x_other = other[...].astype(jnp.float32)
    x_own = own[...].astype(jnp.float32)

    def mean(a, b):
        total = jnp.sum(a, axis=-1, keepdims=True) + jnp.sum(b, axis=-1, keepdims=True)
        return total * (0.5 / half)

    average = mean(x_other, x_own)
    x_other = x_other - average
    x_own = x_own - average
    factor = lax.rsqrt(mean(x_other * x_other, x_own * x_own) + epsilon)
    normed_out[:, :half] = (x_other * factor * gain[:, :half]).astype(jnp.bfloat16)
    normed_out[:, half:] = (x_own * factor * gain[:, half:]).astype(jnp.bfloat16)
    normed = normed_out[...]
    q_out[...] = dot(normed, wq[...]).astype(jnp.bfloat16)
    add_units(normed, wup, wdn, sum_out, slice(0, split), True)


def mlp_rest_kernel(split, normed, wup, wdn, sum_in, sum_out):
    sum_out[...] = sum_in[...]
    add_units(normed[...], wup, wdn, sum_out, slice(split, wup.shape[1]), False)


def run_mlp(split, own, other, gain, wq, wup, wdn):
    rows = own.shape[0]
    width = wq.shape[0]
    return pl.pallas_call(
        functools.partial(mlp_kernel, split),
        out_shape=(
            jax.ShapeDtypeStruct((rows, wq.shape[1]), jnp.bfloat16),
            jax.ShapeDtypeStruct((rows, width), jnp.bfloat16),
            jax.ShapeDtypeStruct((rows, width), jnp.float32),
        ),
        in_specs=vmem(6),
        out_specs=tuple(vmem(3)),
        compiler_params=params(16),
        cost_estimate=pl.CostEstimate(
            flops=2 * rows * width * (wq.shape[1] + 4 * split),
            bytes_accessed=2 * width * (wq.shape[1] + 4 * split),
            transcendentals=2 * rows * split,
        ),
        name="mlp",
    )(own, other, gain, wq, wup, wdn)


def run_mlp_rest(split, normed, wup, wdn, total):
    rows, width = normed.shape
    units = wup.shape[1] - split
    return pl.pallas_call(
        functools.partial(mlp_rest_kernel, split),
        out_shape=jax.ShapeDtypeStruct((rows, width), jnp.float32),
        in_specs=vmem(4),
        out_specs=whole(pltpu.VMEM),
        compiler_params=params(16),
        cost_estimate=pl.CostEstimate(
            flops=4 * rows * width * units,
            bytes_accessed=4 * width * units,
            transcendentals=rows * units,
        ),
        name="mlp_rest",
    )(normed, wup, wdn, total)


def pick_kernel(mesh, out, sem):
    first = pl.multiple_of(lax.axis_index("head") * BLOCK, BLOCK)
    copy = pltpu.make_async_copy(mesh.at[pl.ds(first, BLOCK), :], out, sem)
    copy.start()
    copy.wait()


def run_pick(mesh):
    return pl.pallas_call(
        pick_kernel,
        out_shape=jax.ShapeDtypeStruct((BLOCK, mesh.shape[1]), mesh.dtype),
        in_specs=[whole(pltpu.HBM)],
        out_specs=whole(pltpu.VMEM),
        scratch_shapes=[pltpu.SemaphoreType.DMA(())],
        compiler_params=params(4),
        cost_estimate=pl.CostEstimate(flops=0, bytes_accessed=4 * mesh.size, transcendentals=0),
        name="pick",
    )(in_hbm(mesh))


def stage_kernel(axes, *refs):
    sources, targets, sem = refs[: len(axes)], refs[len(axes) : -1], refs[-1]
    h = lax.axis_index("head")
    copies = []

    def add(source, target):
        pieces = 2 if source.shape[0] >= 512 else 1
        rows = source.shape[0] // pieces
        for piece in range(pieces):
            span = pl.ds(piece * rows, rows)
            copies.append(
                pltpu.make_async_copy(
                    source.at[span, :], target.at[span, :], sem.at[len(copies)]
                )
            )
            copies[-1].start()

    for source, target, axis in zip(sources, targets, axes):
        if axis is None:
            add(source, target)
            continue
        if axis == "rest":
            add(source.at[pl.ds(pl.multiple_of((1 - h) * BLOCK, BLOCK), BLOCK), :], target)
            continue
        half = source.shape[axis] // 2
        for part, head in enumerate((1 - h, h)):
            span = pl.ds(pl.multiple_of(head * half, half), half)
            place = pl.ds(part * half, half)
            if axis == 0:
                add(source.at[span, :], target.at[place, :])
            else:
                add(source.at[:, span], target.at[:, place])
    for copy in copies:
        copy.wait()


def run_stage(arrays, axes):
    size = sum(2 * array.size for array in arrays)
    return pl.pallas_call(
        functools.partial(stage_kernel, axes),
        out_shape=tuple(
            jax.ShapeDtypeStruct((BLOCK,) + array.shape[1:] if axis == "rest" else array.shape, array.dtype)
            for array, axis in zip(arrays, axes)
        ),
        in_specs=[whole(pltpu.HBM)] * len(arrays),
        out_specs=tuple(vmem(len(arrays))),
        scratch_shapes=[pltpu.SemaphoreType.DMA((4 * len(arrays),))],
        compiler_params=params(16),
        cost_estimate=pl.CostEstimate(
            flops=2000 * size, bytes_accessed=20 * size, transcendentals=0
        ),
        name="stage",
    )(*(in_hbm(array) for array in arrays))


def project_kernel(*refs):
    pieces, (wk, wv, out) = refs[:-3], refs[-3:]
    width = wk.shape[1]
    rows = jnp.concatenate([piece[...] for piece in pieces], axis=0)
    out[:, :width] = dot(rows, wk[...]).astype(jnp.bfloat16)
    out[:, width:] = dot(rows, wv[...]).astype(jnp.bfloat16)


def run_project(pieces, wk, wv):
    rows = sum(piece.shape[0] for piece in pieces)
    depth, width = wk.shape
    return pl.pallas_call(
        project_kernel,
        out_shape=jax.ShapeDtypeStruct((rows, 2 * width), jnp.bfloat16),
        in_specs=vmem(len(pieces) + 2),
        out_specs=whole(pltpu.VMEM),
        compiler_params=params(8),
        cost_estimate=pl.CostEstimate(
            flops=300 * rows * depth * width,
            bytes_accessed=300 * depth * width + 300 * rows * depth,
            transcendentals=0,
        ),
        name="project",
    )(*pieces, in_vmem(wk), in_vmem(wv))


def table_kernel(mine, sibling, table):
    table[0, : mine.shape[0]] = mine[...]
    table[1, : mine.shape[0]] = sibling[...]


def run_table(mine, sibling, blocks):
    return pl.pallas_call(
        table_kernel,
        out_shape=jax.ShapeDtypeStruct((2, blocks) + mine.shape[1:], jnp.bfloat16),
        in_specs=vmem(2),
        out_specs=whole(pltpu.VMEM),
        compiler_params=params(8),
        cost_estimate=pl.CostEstimate(
            flops=0, bytes_accessed=80 * mine.size, transcendentals=0
        ),
        name="table",
    )(mine, sibling)


def pieces_of(c):
    low, high = CHUNKS[c]
    pieces = []
    for tile in range(low // BLOCK, -(-high // BLOCK)):
        first, last = max(low, tile * BLOCK), min(high, (tile + 1) * BLOCK)
        rows = slice(first - tile * BLOCK, last - tile * BLOCK)
        pieces.append((tile, rows, slice(first - low, last - low)))
    return pieces


def project_out(c, att, mlp, wo, send, keep):
    half = att.shape[1]
    h = lax.axis_index("head")
    pieces = pieces_of(c)
    start, stop = pieces[0][0] * TILE, (pieces[-1][0] + 1) * TILE

    def write(head):
        for out, first, place in ((send, 0, 1 - head), (keep, half, head)):
            extra = mlp[:, first + start : first + stop]
            total = extra + dot(att[...], wo[:, place * half + start : place * half + stop])
            total = total.astype(jnp.bfloat16)
            for tile, rows, spot in pieces:
                columns = slice(tile * TILE - start, (tile + 1) * TILE - start)
                for t in range(out.shape[0]):
                    block = slice(t * BLOCK + rows.start, t * BLOCK + rows.stop)
                    out[t, spot, :] = total[block, columns]

    for head in range(2):
        pl.when(h == head)(functools.partial(write, head))


def attend_kernel(
    adjacency, q, mine, sibling, table_in, mlp, wo, send, keep, att, table, stacked_s, near_s, sem
):
    del table_in
    s = lax.axis_index("shard")
    h = lax.axis_index("head")
    u = lax.axis_index("sub")
    half = wo.shape[0]
    ready = table.shape[1] - mine.shape[0]
    copy = pltpu.make_async_copy(adjacency, near_s, sem)
    copy.start()
    for i, part in enumerate((mine, sibling)):
        table[i, ready:] = part[...]
    rows_of = lax.broadcasted_iota(jnp.int32, (WIDE, WIDE), 0) // BLOCK
    lanes_of = lax.broadcasted_iota(jnp.int32, (WIDE, WIDE), 1) // HEAD_DIM
    diagonal = rows_of == lanes_of
    lane_head = lax.broadcasted_iota(jnp.int32, (BLOCK, WIDE), 1) // HEAD_DIM
    scale = HEAD_DIM**-0.5 * math.log2(math.e)
    groups = half // WIDE
    steps = near_s.shape[0] * groups
    for step in range(steps):
        b, g = divmod(step, groups)
        columns = slice(g * WIDE, (g + 1) * WIDE)
        stacked = jnp.concatenate([q[b * BLOCK : (b + 1) * BLOCK, columns]] * QUAD, axis=0)
        stacked_s[step] = jnp.where(diagonal, stacked, jnp.zeros_like(stacked))
    copy.wait()
    places = []
    for b in range(near_s.shape[0]):
        places.append([])
        for j in range(near_s.shape[1]):
            m = near_s[b, j]
            part = lax.rem(m, 2)
            core = lax.rem(m // 2, 2)
            distance = s ^ (m // 4)
            part = jnp.where(distance <= 1, part, part ^ h)
            places[b].append((core ^ u, distance * 2 + part))

    def scores_of(step):
        b, g = divmod(step, groups)
        columns = slice(g * WIDE, (g + 1) * WIDE)
        keys = jnp.concatenate([table[i, p, :, columns] for i, p in places[b]], axis=0)
        return lax.dot_general(
            stacked_s[step], keys, (((1,), (1,)), ((), ())), preferred_element_type=jnp.float32
        )

    scores = scores_of(0)
    for step in range(steps):
        following = scores_of(step + 1) if step + 1 < steps else None
        b, g = divmod(step, groups)
        columns = slice(half + g * WIDE, half + (g + 1) * WIDE)
        values = jnp.concatenate([table[i, p, :, columns] for i, p in places[b]], axis=0)
        highest = jnp.max(scores, axis=-1, keepdims=True)
        weights = jnp.exp2((scores - highest) * scale)
        total = jnp.sum(weights, axis=-1, keepdims=True)
        mixed = dot(weights.astype(jnp.bfloat16), values) * (1.0 / total)
        merged = mixed[0:BLOCK, :]
        for i in range(1, QUAD):
            merged = jnp.where(lane_head == i, mixed[i * BLOCK : (i + 1) * BLOCK, :], merged)
        rows = slice(b * BLOCK, (b + 1) * BLOCK)
        att[rows, g * WIDE : (g + 1) * WIDE] = merged.astype(jnp.bfloat16)
        scores = following
    project_out(0, att, mlp, wo, send, keep)


def run_attend(adjacency, q, mine, sibling, table, mlp, wo):
    rows, half = q.shape
    size = CHUNKS[0][1] - CHUNKS[0][0]
    part = jax.ShapeDtypeStruct((rows // BLOCK, size, TILE), jnp.bfloat16)
    blocks = table.shape[0] * table.shape[1]
    send, keep, att, _ = pl.pallas_call(
        attend_kernel,
        out_shape=(
            part,
            part,
            jax.ShapeDtypeStruct(q.shape, jnp.bfloat16),
            jax.ShapeDtypeStruct(table.shape, jnp.bfloat16),
        ),
        in_specs=[whole(pl.ANY)] + vmem(6),
        out_specs=tuple(vmem(4)),
        scratch_shapes=[
            pltpu.VMEM((rows // BLOCK * (half // WIDE), WIDE, WIDE), jnp.bfloat16),
            pltpu.SMEM(adjacency.shape, jnp.int32),
            pltpu.SemaphoreType.DMA(()),
        ],
        input_output_aliases={4: 3},
        compiler_params=params(16),
        cost_estimate=pl.CostEstimate(
            flops=20 * rows * half * (D + 8 * 8 * BLOCK),
            bytes_accessed=40 * blocks * BLOCK * half + 20 * half * D + 40 * rows * D,
            transcendentals=rows * 8 * BLOCK * half // HEAD_DIM,
        ),
        name="attend",
    )(adjacency, q, mine, sibling, table, mlp, in_vmem(wo))
    return send, keep, att


def run_project_out(c, att, mlp, wo):
    rows, half = att.shape
    size = CHUNKS[c][1] - CHUNKS[c][0]
    part = jax.ShapeDtypeStruct((rows // BLOCK, size, TILE), jnp.bfloat16)
    return pl.pallas_call(
        functools.partial(project_out, c),
        out_shape=(part, part),
        in_specs=vmem(3),
        out_specs=tuple(vmem(2)),
        compiler_params=params(8),
        cost_estimate=pl.CostEstimate(
            flops=200 * rows * half * D,
            bytes_accessed=200 * half * D,
            transcendentals=0,
        ),
        name="project_out",
    )(att, mlp, in_vmem(wo))


def plan_kernel(owners, masks):
    s = lax.axis_index("shard")
    count = owners.shape[1]
    names = [owners[0, t] for t in range(count)]
    for t in range(count):
        same = [(names[e] == names[t]).astype(jnp.int32) for e in range(t)]
        rank = sum(same, jnp.int32(0))
        for d in range(masks.shape[0]):
            for j in range(CAP):
                hit = (names[t] == s ^ d) & (rank == j)
                masks[d, j, t] = jnp.full(masks.shape[3:], hit.astype(jnp.float32))


def run_plan(owners, shards):
    return pl.pallas_call(
        plan_kernel,
        out_shape=jax.ShapeDtypeStruct((shards, CAP, owners.shape[1], 8, 128), jnp.float32),
        in_specs=[whole(pltpu.SMEM)],
        out_specs=whole(pltpu.VMEM),
        compiler_params=params(4),
        cost_estimate=pl.CostEstimate(
            flops=100000000, bytes_accessed=1 << 18, transcendentals=0
        ),
        name="plan",
    )(owners)


def combine_kernel(chunks, distances, masks, grid_features, *refs):
    keeps, refs = refs[: len(chunks)], refs[len(chunks) :]
    swaps, outs = refs[: len(chunks)], refs[len(chunks) :]
    count = grid_features.shape[0]
    first = CHUNKS[chunks[0]][0]
    for c, keep, swap in zip(chunks, keeps, swaps):
        low, high = CHUNKS[c]
        updated = []
        for t in range(count):
            residual = [
                grid_features[t, rows, tile * TILE : (tile + 1) * TILE]
                for tile, rows, _ in pieces_of(c)
            ]
            residual = jnp.concatenate(residual, axis=0).astype(jnp.float32)
            partials = keep[t].astype(jnp.float32) + swap[t].astype(jnp.float32)
            updated.append(residual + partials)
        for d, out in zip(distances, outs):
            for j in range(CAP):
                chosen = jnp.zeros_like(updated[0])
                for t in range(count):
                    mask = jnp.broadcast_to(masks[d, j, t, 0:1, :], chosen.shape)
                    chosen = jnp.where(mask > 0.5, updated[t], chosen)
                out[j, low - first : high - first, :] = chosen.astype(jnp.bfloat16)


def run_combine(chunks, distances, masks, grid_features, keeps, swaps):
    count = grid_features.shape[0]
    rows, width = CHUNKS[chunks[-1]][1] - CHUNKS[chunks[0]][0], TILE
    slot = jax.ShapeDtypeStruct((CAP, rows, width), jnp.bfloat16)
    return pl.pallas_call(
        functools.partial(combine_kernel, chunks, distances),
        out_shape=(slot,) * len(distances),
        in_specs=vmem(2 + 2 * len(chunks)),
        out_specs=tuple(vmem(len(distances))),
        compiler_params=params(8),
        cost_estimate=pl.CostEstimate(
            flops=60000 * count * rows * width,
            bytes_accessed=400 * rows * width * (3 * count + CAP * len(distances)),
            transcendentals=0,
        ),
        name="combine",
    )(masks, grid_features, *keeps, *swaps)


def place_kernel(spots, *refs):
    out, sem = refs[-2:]
    s = lax.axis_index("shard")
    copies = []
    for ref, (d, chunks) in zip(refs, spots):
        first = CHUNKS[chunks[0]][0]
        slots = pl.ds((s ^ d) * CAP, CAP)
        for c in chunks:
            shift = CHUNKS[c][0] - first
            for tile, rows, spot in pieces_of(c):
                size = rows.stop - rows.start
                source = ref.at[:, pl.ds(spot.start + shift, size), :]
                columns = pl.ds(tile * TILE, TILE)
                target = out.at[slots, pl.ds(rows.start, size), columns]
                copies.append(pltpu.make_async_copy(source, target, sem.at[len(copies)]))
                copies[-1].start()
    for copy in copies:
        copy.wait()


def run_place(spots, arrived, placed, shape):
    count = sum(len(pieces_of(c)) for _, chunks in spots for c in chunks)
    return pl.pallas_call(
        functools.partial(place_kernel, spots),
        out_shape=jax.ShapeDtypeStruct(shape, jnp.bfloat16),
        in_specs=vmem(len(arrived)) + [whole(pltpu.HBM)] * len(placed),
        out_specs=whole(pltpu.HBM),
        scratch_shapes=[pltpu.SemaphoreType.DMA((count,))],
        input_output_aliases={len(arrived): 0} if placed else {},
        compiler_params=params(4),
        cost_estimate=pl.CostEstimate(
            flops=400000 * sum(part.size for part in arrived), bytes_accessed=0, transcendentals=0
        ),
        name="place",
    )(*arrived, *placed)


def crossed(x, distance, size):
    return lax.ppermute(x, "shard", [(i, i ^ distance) for i in range(size)])


def swapped(x, axis):
    return lax.ppermute(x, axis, [(0, 1), (1, 0)])


def paired(
    grid_features,
    owners,
    adjacency,
    mesh_nodes,
    norm_gain,
    query_weight,
    key_weight,
    value_weight,
    output_weight,
    up_weight,
    down_weight,
):
    shards = lax.axis_size("shard")
    count, rows, half = grid_features.shape
    flat = grid_features.reshape(count * rows, half)
    half_unit = run_pick(mesh_nodes)
    far = crossed(half_unit, 2, shards)
    near = crossed(mesh_nodes, 1, shards)
    waiting, _ = lax.optimization_barrier((flat, half_unit))
    other = swapped(waiting, "head")
    flat, gain, wq, wup, wdn, mesh, rest = run_stage(
        (
            flat,
            norm_gain.reshape(1, -1),
            query_weight,
            up_weight,
            down_weight,
            mesh_nodes,
            mesh_nodes,
        ),
        (None, 1, 0, 0, 1, None, "rest"),
    )
    straight = crossed(rest, 3, shards)
    far, _ = lax.optimization_barrier((far, rest))
    farther = crossed(far, 1, shards)
    far_pair = swapped(far, "head")
    split = up_weight.shape[1] // 2
    queries, normed, mlp = run_mlp(split, flat, other, gain, wq, wup, wdn)
    queries, mlp, far_pair, near = lax.optimization_barrier((queries, mlp, far_pair, near))
    blocked = (-1, BLOCK, 2 * half)
    mine_a = run_project((mesh, near, far, far_pair), key_weight, value_weight)
    sibling_a = swapped(mine_a, "sub")
    table = run_table(mine_a.reshape(blocked), sibling_a.reshape(blocked), 2 * shards)
    mine_b = run_project((farther, straight), key_weight, value_weight)
    sibling_b = swapped(mine_b, "sub")
    normed, _ = lax.optimization_barrier((normed, mine_b))
    mlp = run_mlp_rest(split, normed, wup, wdn, mlp)
    send, keep, att = run_attend(
        adjacency, queries, mine_b.reshape(blocked), sibling_b.reshape(blocked), table, mlp, output_weight
    )
    keeps, swaps, slots, placed = [], [], [], []
    shape = (shards * CAP, rows, half)
    every = tuple(range(len(CHUNKS)))
    for c in every:
        if c > 0:
            send, keep = run_project_out(c, att, mlp, output_weight)
        received = swapped(send, "head")
        swaps.append(received)
        keeps.append(keep)
    named, _ = lax.optimization_barrier((owners, keep))
    masks = run_plan(named.T, shards)
    for c in every:
        received = swaps[c]
        if c > 0:
            received, _ = lax.optimization_barrier((received, slots[c - 1][0]))
        slots.append(run_combine((c,), (2, 3), masks, grid_features, (keeps[c],), (received,)))
    swaps[-1], _ = lax.optimization_barrier((swaps[-1], slots[-1][0]))
    near_slots, own_slots = run_combine(every, (1, 0), masks, grid_features, keeps, swaps)
    for c in every:
        spots = [(2, (c,)), (3, (c,))]
        arrived = [crossed(slot, d, shards) for d, slot in zip((2, 3), slots[c])]
        if c == 0:
            spots.append((0, every))
            arrived.append(own_slots)
        if c == every[-1]:
            spots.append((1, every))
            arrived.append(crossed(near_slots, 1, shards))
        placed = [run_place(spots, arrived, placed, shape)]
    return placed[0]


def attend_plain(queries, key_table, value_table, chosen, scaling):
    count = chosen.shape[0]
    picked_keys = key_table[chosen]
    picked_keys = picked_keys.reshape(count, -1, picked_keys.shape[3], picked_keys.shape[4])
    picked_values = value_table[chosen]
    picked_values = picked_values.reshape(count, -1, picked_values.shape[3], picked_values.shape[4])
    scores = (
        jnp.einsum("gqhe,gkhe->ghqk", queries, picked_keys, preferred_element_type=jnp.float32)
        * scaling
    )
    highest = jnp.max(scores, axis=-1, keepdims=True)
    weights = jnp.exp(scores - highest)
    weights = (weights / jnp.sum(weights, axis=-1, keepdims=True)).astype(jnp.bfloat16)
    result = jnp.einsum(
        "ghqk,gkhe->gqhe", weights, picked_values, preferred_element_type=jnp.float32
    )
    return result.astype(jnp.bfloat16)


def general(
    grid_features,
    owners,
    adjacency,
    mesh_nodes,
    norm_gain,
    query_weight,
    key_weight,
    value_weight,
    output_weight,
    up_weight,
    down_weight,
):
    shard_count = lax.axis_size("shard")
    head_count = lax.axis_size("head")
    local_blocks, block_rows, feature_share = grid_features.shape
    slots = shard_count * CAP
    owner_col = owners[:, 0]
    position = jnp.arange(local_blocks, dtype=jnp.int32)
    earlier = (owner_col[:, None] == owner_col[None, :]) & (position[None, :] < position[:, None])
    target = owner_col * CAP + jnp.sum(earlier.astype(jnp.int32), axis=1)
    dispatch = (target[:, None] == jnp.arange(slots, dtype=jnp.int32)[None, :]).astype(jnp.bfloat16)
    offset = lax.axis_index("head") * (D // head_count)
    projected = jnp.stack(
        (
            jnp.dot(mesh_nodes, key_weight, preferred_element_type=jnp.float32).astype(
                jnp.bfloat16
            ),
            jnp.dot(mesh_nodes, value_weight, preferred_element_type=jnp.float32).astype(
                jnp.bfloat16
            ),
        )
    )
    tables = lax.all_gather(projected, ("shard", "sub"), axis=1, tiled=True)
    head_local = query_weight.shape[1] // HEAD_DIM
    key_table = tables[0].reshape(-1, block_rows, head_local, HEAD_DIM)
    value_table = tables[1].reshape(-1, block_rows, head_local, HEAD_DIM)
    send_lists = jnp.full((slots, adjacency.shape[1]), -1, jnp.int32).at[target].set(adjacency)
    send_lists = send_lists.reshape(shard_count, CAP, -1)
    complete = lax.all_gather(grid_features, "head", axis=2, tiled=True)
    outgoing = jnp.einsum(
        "gs,gbd->sbd", dispatch, complete, preferred_element_type=jnp.float32
    ).astype(jnp.bfloat16)
    arrived, lists = (
        lax.all_to_all(
            outgoing.reshape(shard_count, CAP, block_rows, D),
            "shard",
            split_axis=0,
            concat_axis=0,
            tiled=True,
        ),
        lax.all_to_all(send_lists, "shard", split_axis=0, concat_axis=0, tiled=True),
    )
    arrived = arrived.reshape(slots, block_rows, D)
    residual = lax.dynamic_slice_in_dim(arrived, offset, D // head_count, 2)
    lists = lists.reshape(slots, -1)
    count = arrived.shape[0]
    values_f = arrived.astype(jnp.float32)
    average = jnp.mean(values_f, axis=-1, keepdims=True)
    centered = values_f - average
    variance = jnp.mean(centered * centered, axis=-1, keepdims=True)
    normed = (centered * lax.rsqrt(variance + epsilon) * norm_gain).astype(jnp.bfloat16)
    flattened = normed.reshape(-1, D)
    queries = jnp.dot(flattened, query_weight, preferred_element_type=jnp.float32).astype(
        jnp.bfloat16
    )
    blocks_each = math.gcd(count, max(1, 512 // block_rows))
    steps_count = count // blocks_each
    queries = queries.reshape(steps_count, blocks_each, block_rows, head_local, HEAD_DIM)

    def attend_step(operands):
        return attend_plain(operands[0], key_table, value_table, operands[1], HEAD_DIM ** (-0.5))

    attended = lax.map(
        attend_step, (queries, jnp.maximum(lists, 0).reshape(steps_count, blocks_each, -1))
    )
    attended = attended.reshape(-1, head_local * HEAD_DIM)
    hidden = jax.nn.gelu(
        jnp.dot(flattened, up_weight, preferred_element_type=jnp.float32), approximate=False
    ).astype(jnp.bfloat16)
    branch = jnp.dot(attended, output_weight, preferred_element_type=jnp.float32)
    branch = branch + jnp.dot(hidden, down_weight, preferred_element_type=jnp.float32)
    branch = branch.reshape(count, block_rows, D)
    reduced = lax.psum_scatter(
        branch.astype(jnp.bfloat16), "head", scatter_dimension=2, tiled=True
    ).astype(jnp.float32)
    occupied = lists[:, 0] >= 0
    summed = residual.astype(jnp.float32) + reduced
    return jnp.where(occupied[:, None, None], summed, 0.0).astype(jnp.bfloat16)


def local(grid_features, owners, adjacency, mesh_nodes, *parameters):
    sizes = [lax.axis_size(axis) for axis in ("shard", "head", "sub")]
    small = grid_features.shape[:2] == (4, BLOCK) and mesh_nodes.shape[0] == 2 * BLOCK
    if sizes == [4, 2, 2] and small and grid_features.shape[2] == 512:
        return paired(grid_features, owners, adjacency, mesh_nodes, *parameters)
    return general(grid_features, owners, adjacency, mesh_nodes, *parameters)


def solution(mesh):
    return jax.shard_map(
        local,
        mesh=mesh,
        in_specs=(
            P(("groups", "shard", "sub"), None, "head"),
            P(("groups", "shard", "sub"), None),
            P(("groups", "shard", "sub"), None),
            P(("groups", "shard", "sub"), None),
            P(),
            P(None, "head"),
            P(None, "head"),
            P(None, "head"),
            P("head", None),
            P(None, "head"),
            P("head", None),
        ),
        out_specs=P(("groups", "shard", "sub"), None, "head"),
        check_vma=False,
    )
```

```python
import functools
import math

import jax
import jax.numpy as jnp
from jax import lax
from jax.experimental import pallas as pl
from jax.experimental.pallas import tpu as pltpu
from jax.sharding import PartitionSpec as P

D = 1024
HEAD_DIM = 64
CAP = 2
BLOCK = 64
QUAD = 4
WIDE = QUAD * HEAD_DIM
TILE = 128
CHUNKS = ((0, 80), (80, 256))
MIB = 1 << 20


epsilon = 1e-05


def dot(a, b):
    return jnp.dot(a, b, preferred_element_type=jnp.float32)


def gelu(x):
    return 0.5 * x * (1.0 + lax.erf(x * (2.0**-0.5)))


def in_hbm(x):
    return pltpu.with_memory_space_constraint(x, pltpu.HBM)


def in_vmem(x):
    return pltpu.with_memory_space_constraint(x, pltpu.VMEM)


def whole(space):
    return pl.BlockSpec(memory_space=space)


def vmem(count):
    return [whole(pltpu.VMEM)] * count


def params(mib):
    return pltpu.CompilerParams(vmem_limit_bytes=mib * MIB)


def mlp_kernel(own, other, gain, wq, wup, wdn, q_out, mlp_out, normed_s):
    half = own.shape[1]
    units = wup.shape[1]
    chunk = units // 4
    x_other = other[...].astype(jnp.float32)
    x_own = own[...].astype(jnp.float32)

    def mean(a, b):
        total = jnp.sum(a, axis=-1, keepdims=True) + jnp.sum(b, axis=-1, keepdims=True)
        return total * (0.5 / half)

    average = mean(x_other, x_own)
    x_other = x_other - average
    x_own = x_own - average
    factor = lax.rsqrt(mean(x_other * x_other, x_own * x_own) + epsilon)
    normed_s[:, :half] = (x_other * factor * gain[:, :half]).astype(jnp.bfloat16)
    normed_s[:, half:] = (x_own * factor * gain[:, half:]).astype(jnp.bfloat16)
    normed = normed_s[...]
    q_out[...] = dot(normed, wq[...]).astype(jnp.bfloat16)
    for c in range(units // chunk):
        span = slice(c * chunk, (c + 1) * chunk)
        hidden = gelu(dot(normed, wup[:, span])).astype(jnp.bfloat16)
        term = dot(hidden, wdn[span, :])
        if c == 0:
            mlp_out[...] = term
        else:
            mlp_out[...] += term


def run_mlp(own, other, gain, wq, wup, wdn):
    rows = own.shape[0]
    width = wq.shape[0]
    units = wup.shape[1]
    return pl.pallas_call(
        mlp_kernel,
        out_shape=(
            jax.ShapeDtypeStruct((rows, wq.shape[1]), jnp.bfloat16),
            jax.ShapeDtypeStruct((rows, width), jnp.float32),
        ),
        in_specs=vmem(6),
        out_specs=tuple(vmem(2)),
        scratch_shapes=[pltpu.VMEM((rows, width), jnp.bfloat16)],
        compiler_params=params(16),
        cost_estimate=pl.CostEstimate(
            flops=2 * rows * width * (wq.shape[1] + 2 * units),
            bytes_accessed=2 * width * (wq.shape[1] + 2 * units),
            transcendentals=rows * units,
        ),
        name="mlp",
    )(own, other, gain, wq, wup, wdn)


def pick_kernel(mesh, out, sem):
    first = pl.multiple_of(lax.axis_index("head") * BLOCK, BLOCK)
    copy = pltpu.make_async_copy(mesh.at[pl.ds(first, BLOCK), :], out, sem)
    copy.start()
    copy.wait()


def run_pick(mesh):
    return pl.pallas_call(
        pick_kernel,
        out_shape=jax.ShapeDtypeStruct((BLOCK, mesh.shape[1]), mesh.dtype),
        in_specs=[whole(pltpu.HBM)],
        out_specs=whole(pltpu.VMEM),
        scratch_shapes=[pltpu.SemaphoreType.DMA(())],
        compiler_params=params(4),
        cost_estimate=pl.CostEstimate(flops=0, bytes_accessed=4 * mesh.size, transcendentals=0),
        name="pick",
    )(in_hbm(mesh))


def stage_kernel(axes, *refs):
    sources, targets, sem = refs[: len(axes)], refs[len(axes) : -1], refs[-1]
    h = lax.axis_index("head")
    copies = []

    def add(source, target):
        pieces = 2 if source.shape[0] >= 512 else 1
        rows = source.shape[0] // pieces
        for piece in range(pieces):
            span = pl.ds(piece * rows, rows)
            copies.append(
                pltpu.make_async_copy(
                    source.at[span, :], target.at[span, :], sem.at[len(copies)]
                )
            )
            copies[-1].start()

    for source, target, axis in zip(sources, targets, axes):
        if axis is None:
            add(source, target)
            continue
        if axis == "rest":
            add(source.at[pl.ds(pl.multiple_of((1 - h) * BLOCK, BLOCK), BLOCK), :], target)
            continue
        half = source.shape[axis] // 2
        for part, head in enumerate((1 - h, h)):
            span = pl.ds(pl.multiple_of(head * half, half), half)
            place = pl.ds(part * half, half)
            if axis == 0:
                add(source.at[span, :], target.at[place, :])
            else:
                add(source.at[:, span], target.at[:, place])
    for copy in copies:
        copy.wait()


def run_stage(arrays, axes):
    size = sum(2 * array.size for array in arrays)
    return pl.pallas_call(
        functools.partial(stage_kernel, axes),
        out_shape=tuple(
            jax.ShapeDtypeStruct((BLOCK,) + array.shape[1:] if axis == "rest" else array.shape, array.dtype)
            for array, axis in zip(arrays, axes)
        ),
        in_specs=[whole(pltpu.HBM)] * len(arrays),
        out_specs=tuple(vmem(len(arrays))),
        scratch_shapes=[pltpu.SemaphoreType.DMA((4 * len(arrays),))],
        compiler_params=params(16),
        cost_estimate=pl.CostEstimate(
            flops=2000 * size, bytes_accessed=20 * size, transcendentals=0
        ),
        name="stage",
    )(*(in_hbm(array) for array in arrays))


def project_kernel(*refs):
    pieces, (wk, wv, out) = refs[:-3], refs[-3:]
    width = wk.shape[1]
    rows = jnp.concatenate([piece[...] for piece in pieces], axis=0)
    out[:, :width] = dot(rows, wk[...]).astype(jnp.bfloat16)
    out[:, width:] = dot(rows, wv[...]).astype(jnp.bfloat16)


def run_project(pieces, wk, wv):
    rows = sum(piece.shape[0] for piece in pieces)
    depth, width = wk.shape
    return pl.pallas_call(
        project_kernel,
        out_shape=jax.ShapeDtypeStruct((rows, 2 * width), jnp.bfloat16),
        in_specs=vmem(len(pieces) + 2),
        out_specs=whole(pltpu.VMEM),
        compiler_params=params(8),
        cost_estimate=pl.CostEstimate(
            flops=300 * rows * depth * width,
            bytes_accessed=300 * depth * width + 300 * rows * depth,
            transcendentals=0,
        ),
        name="project",
    )(*pieces, in_vmem(wk), in_vmem(wv))


def table_kernel(mine, sibling, table):
    table[0, : mine.shape[0]] = mine[...]
    table[1, : mine.shape[0]] = sibling[...]


def run_table(mine, sibling, blocks):
    return pl.pallas_call(
        table_kernel,
        out_shape=jax.ShapeDtypeStruct((2, blocks) + mine.shape[1:], jnp.bfloat16),
        in_specs=vmem(2),
        out_specs=whole(pltpu.VMEM),
        compiler_params=params(8),
        cost_estimate=pl.CostEstimate(
            flops=0, bytes_accessed=80 * mine.size, transcendentals=0
        ),
        name="table",
    )(mine, sibling)


def pieces_of(c):
    low, high = CHUNKS[c]
    pieces = []
    for tile in range(low // BLOCK, -(-high // BLOCK)):
        first, last = max(low, tile * BLOCK), min(high, (tile + 1) * BLOCK)
        rows = slice(first - tile * BLOCK, last - tile * BLOCK)
        pieces.append((tile, rows, slice(first - low, last - low)))
    return pieces


def project_out(c, att, mlp, wo, send, keep):
    half = att.shape[1]
    h = lax.axis_index("head")
    pieces = pieces_of(c)
    start, stop = pieces[0][0] * TILE, (pieces[-1][0] + 1) * TILE

    def write(head):
        for out, first, place in ((send, 0, 1 - head), (keep, half, head)):
            extra = mlp[:, first + start : first + stop]
            total = extra + dot(att[...], wo[:, place * half + start : place * half + stop])
            total = total.astype(jnp.bfloat16)
            for tile, rows, spot in pieces:
                columns = slice(tile * TILE - start, (tile + 1) * TILE - start)
                for t in range(out.shape[0]):
                    block = slice(t * BLOCK + rows.start, t * BLOCK + rows.stop)
                    out[t, spot, :] = total[block, columns]

    for head in range(2):
        pl.when(h == head)(functools.partial(write, head))


def attend_kernel(
    adjacency, q, mine, sibling, table_in, mlp, wo, send, keep, att, table, stacked_s, near_s, sem
):
    del table_in
    s = lax.axis_index("shard")
    h = lax.axis_index("head")
    u = lax.axis_index("sub")
    half = wo.shape[0]
    ready = table.shape[1] - mine.shape[0]
    copy = pltpu.make_async_copy(adjacency, near_s, sem)
    copy.start()
    for i, part in enumerate((mine, sibling)):
        table[i, ready:] = part[...]
    rows_of = lax.broadcasted_iota(jnp.int32, (WIDE, WIDE), 0) // BLOCK
    lanes_of = lax.broadcasted_iota(jnp.int32, (WIDE, WIDE), 1) // HEAD_DIM
    diagonal = rows_of == lanes_of
    lane_head = lax.broadcasted_iota(jnp.int32, (BLOCK, WIDE), 1) // HEAD_DIM
    scale = HEAD_DIM**-0.5 * math.log2(math.e)
    groups = half // WIDE
    steps = near_s.shape[0] * groups
    for step in range(steps):
        b, g = divmod(step, groups)
        columns = slice(g * WIDE, (g + 1) * WIDE)
        stacked = jnp.concatenate([q[b * BLOCK : (b + 1) * BLOCK, columns]] * QUAD, axis=0)
        stacked_s[step] = jnp.where(diagonal, stacked, jnp.zeros_like(stacked))
    copy.wait()
    places = []
    for b in range(near_s.shape[0]):
        places.append([])
        for j in range(near_s.shape[1]):
            m = near_s[b, j]
            part = lax.rem(m, 2)
            core = lax.rem(m // 2, 2)
            distance = s ^ (m // 4)
            part = jnp.where(distance <= 1, part, part ^ h)
            places[b].append((core ^ u, distance * 2 + part))

    def scores_of(step):
        b, g = divmod(step, groups)
        columns = slice(g * WIDE, (g + 1) * WIDE)
        keys = jnp.concatenate([table[i, p, :, columns] for i, p in places[b]], axis=0)
        return lax.dot_general(
            stacked_s[step], keys, (((1,), (1,)), ((), ())), preferred_element_type=jnp.float32
        )

    scores = scores_of(0)
    for step in range(steps):
        following = scores_of(step + 1) if step + 1 < steps else None
        b, g = divmod(step, groups)
        columns = slice(half + g * WIDE, half + (g + 1) * WIDE)
        values = jnp.concatenate([table[i, p, :, columns] for i, p in places[b]], axis=0)
        highest = jnp.max(scores, axis=-1, keepdims=True)
        weights = jnp.exp2((scores - highest) * scale)
        total = jnp.sum(weights, axis=-1, keepdims=True)
        mixed = dot(weights.astype(jnp.bfloat16), values) * (1.0 / total)
        merged = mixed[0:BLOCK, :]
        for i in range(1, QUAD):
            merged = jnp.where(lane_head == i, mixed[i * BLOCK : (i + 1) * BLOCK, :], merged)
        rows = slice(b * BLOCK, (b + 1) * BLOCK)
        att[rows, g * WIDE : (g + 1) * WIDE] = merged.astype(jnp.bfloat16)
        scores = following
    project_out(0, att, mlp, wo, send, keep)


def run_attend(adjacency, q, mine, sibling, table, mlp, wo):
    rows, half = q.shape
    size = CHUNKS[0][1] - CHUNKS[0][0]
    part = jax.ShapeDtypeStruct((rows // BLOCK, size, TILE), jnp.bfloat16)
    blocks = table.shape[0] * table.shape[1]
    send, keep, att, _ = pl.pallas_call(
        attend_kernel,
        out_shape=(
            part,
            part,
            jax.ShapeDtypeStruct(q.shape, jnp.bfloat16),
            jax.ShapeDtypeStruct(table.shape, jnp.bfloat16),
        ),
        in_specs=[whole(pl.ANY)] + vmem(6),
        out_specs=tuple(vmem(4)),
        scratch_shapes=[
            pltpu.VMEM((rows // BLOCK * (half // WIDE), WIDE, WIDE), jnp.bfloat16),
            pltpu.SMEM(adjacency.shape, jnp.int32),
            pltpu.SemaphoreType.DMA(()),
        ],
        input_output_aliases={4: 3},
        compiler_params=params(16),
        cost_estimate=pl.CostEstimate(
            flops=20 * rows * half * (D + 8 * 8 * BLOCK),
            bytes_accessed=40 * blocks * BLOCK * half + 20 * half * D + 40 * rows * D,
            transcendentals=rows * 8 * BLOCK * half // HEAD_DIM,
        ),
        name="attend",
    )(adjacency, q, mine, sibling, table, mlp, in_vmem(wo))
    return send, keep, att


def run_project_out(c, att, mlp, wo):
    rows, half = att.shape
    size = CHUNKS[c][1] - CHUNKS[c][0]
    part = jax.ShapeDtypeStruct((rows // BLOCK, size, TILE), jnp.bfloat16)
    return pl.pallas_call(
        functools.partial(project_out, c),
        out_shape=(part, part),
        in_specs=vmem(3),
        out_specs=tuple(vmem(2)),
        compiler_params=params(8),
        cost_estimate=pl.CostEstimate(
            flops=200 * rows * half * D,
            bytes_accessed=200 * half * D,
            transcendentals=0,
        ),
        name="project_out",
    )(att, mlp, in_vmem(wo))


def plan_kernel(owners, masks):
    s = lax.axis_index("shard")
    count = owners.shape[1]
    names = [owners[0, t] for t in range(count)]
    for t in range(count):
        same = [(names[e] == names[t]).astype(jnp.int32) for e in range(t)]
        rank = sum(same, jnp.int32(0))
        for d in range(masks.shape[0]):
            for j in range(CAP):
                hit = (names[t] == s ^ d) & (rank == j)
                masks[d, j, t] = jnp.full(masks.shape[3:], hit.astype(jnp.float32))


def run_plan(owners, shards):
    return pl.pallas_call(
        plan_kernel,
        out_shape=jax.ShapeDtypeStruct((shards, CAP, owners.shape[1], 8, 128), jnp.float32),
        in_specs=[whole(pltpu.SMEM)],
        out_specs=whole(pltpu.VMEM),
        compiler_params=params(4),
        cost_estimate=pl.CostEstimate(flops=0, bytes_accessed=1 << 18, transcendentals=0),
        name="plan",
    )(owners)


def combine_kernel(chunks, distances, masks, grid_features, *refs):
    keeps, refs = refs[: len(chunks)], refs[len(chunks) :]
    swaps, outs = refs[: len(chunks)], refs[len(chunks) :]
    count = grid_features.shape[0]
    first = CHUNKS[chunks[0]][0]
    for c, keep, swap in zip(chunks, keeps, swaps):
        low, high = CHUNKS[c]
        updated = []
        for t in range(count):
            residual = [
                grid_features[t, rows, tile * TILE : (tile + 1) * TILE]
                for tile, rows, _ in pieces_of(c)
            ]
            residual = jnp.concatenate(residual, axis=0).astype(jnp.float32)
            partials = keep[t].astype(jnp.float32) + swap[t].astype(jnp.float32)
            updated.append(residual + partials)
        for d, out in zip(distances, outs):
            for j in range(CAP):
                chosen = jnp.zeros_like(updated[0])
                for t in range(count):
                    mask = jnp.broadcast_to(masks[d, j, t, 0:1, :], chosen.shape)
                    chosen = jnp.where(mask > 0.5, updated[t], chosen)
                out[j, low - first : high - first, :] = chosen.astype(jnp.bfloat16)


def run_combine(chunks, distances, masks, grid_features, keeps, swaps):
    count = grid_features.shape[0]
    rows, width = CHUNKS[chunks[-1]][1] - CHUNKS[chunks[0]][0], TILE
    slot = jax.ShapeDtypeStruct((CAP, rows, width), jnp.bfloat16)
    return pl.pallas_call(
        functools.partial(combine_kernel, chunks, distances),
        out_shape=(slot,) * len(distances),
        in_specs=vmem(2 + 2 * len(chunks)),
        out_specs=tuple(vmem(len(distances))),
        compiler_params=params(8),
        cost_estimate=pl.CostEstimate(
            flops=60000 * count * rows * width,
            bytes_accessed=400 * rows * width * (3 * count + CAP * len(distances)),
            transcendentals=0,
        ),
        name="combine",
    )(masks, grid_features, *keeps, *swaps)


def place_kernel(spots, *refs):
    out, sem = refs[-2:]
    s = lax.axis_index("shard")
    copies = []
    for ref, (d, chunks) in zip(refs, spots):
        first = CHUNKS[chunks[0]][0]
        slots = pl.ds((s ^ d) * CAP, CAP)
        for c in chunks:
            shift = CHUNKS[c][0] - first
            for tile, rows, spot in pieces_of(c):
                size = rows.stop - rows.start
                source = ref.at[:, pl.ds(spot.start + shift, size), :]
                columns = pl.ds(tile * TILE, TILE)
                target = out.at[slots, pl.ds(rows.start, size), columns]
                copies.append(pltpu.make_async_copy(source, target, sem.at[len(copies)]))
                copies[-1].start()
    for copy in copies:
        copy.wait()


def run_place(spots, arrived, placed, shape):
    count = sum(len(pieces_of(c)) for _, chunks in spots for c in chunks)
    return pl.pallas_call(
        functools.partial(place_kernel, spots),
        out_shape=jax.ShapeDtypeStruct(shape, jnp.bfloat16),
        in_specs=vmem(len(arrived)) + [whole(pltpu.HBM)] * len(placed),
        out_specs=whole(pltpu.HBM),
        scratch_shapes=[pltpu.SemaphoreType.DMA((count,))],
        input_output_aliases={len(arrived): 0} if placed else {},
        compiler_params=params(4),
        cost_estimate=pl.CostEstimate(
            flops=400000 * sum(part.size for part in arrived), bytes_accessed=0, transcendentals=0
        ),
        name="place",
    )(*arrived, *placed)


def crossed(x, distance, size):
    return lax.ppermute(x, "shard", [(i, i ^ distance) for i in range(size)])


def swapped(x, axis):
    return lax.ppermute(x, axis, [(0, 1), (1, 0)])


def paired(
    grid_features,
    owners,
    adjacency,
    mesh_nodes,
    norm_gain,
    query_weight,
    key_weight,
    value_weight,
    output_weight,
    up_weight,
    down_weight,
):
    shards = lax.axis_size("shard")
    count, rows, half = grid_features.shape
    flat = grid_features.reshape(count * rows, half)
    half_unit = run_pick(mesh_nodes)
    far = crossed(half_unit, 2, shards)
    waiting, _ = lax.optimization_barrier((mesh_nodes, half_unit))
    near = crossed(waiting, 1, shards)
    waiting, _ = lax.optimization_barrier((flat, half_unit))
    other = swapped(waiting, "head")
    flat, gain, wq, wup, wdn, mesh, rest = run_stage(
        (
            flat,
            norm_gain.reshape(1, -1),
            query_weight,
            up_weight,
            down_weight,
            mesh_nodes,
            mesh_nodes,
        ),
        (None, 1, 0, 0, 1, None, "rest"),
    )
    straight = crossed(rest, 3, shards)
    far, _ = lax.optimization_barrier((far, rest))
    farther = crossed(far, 1, shards)
    far_pair = swapped(far, "head")
    queries, mlp = run_mlp(flat, other, gain, wq, wup, wdn)
    queries, mlp, far_pair, near = lax.optimization_barrier((queries, mlp, far_pair, near))
    blocked = (-1, BLOCK, 2 * half)
    mine_a = run_project((mesh, near, far, far_pair), key_weight, value_weight)
    sibling_a = swapped(mine_a, "sub")
    table = run_table(mine_a.reshape(blocked), sibling_a.reshape(blocked), 2 * shards)
    mine_b = run_project((farther, straight), key_weight, value_weight)
    sibling_b = swapped(mine_b, "sub")
    send, keep, att = run_attend(
        adjacency, queries, mine_b.reshape(blocked), sibling_b.reshape(blocked), table, mlp, output_weight
    )
    named, _ = lax.optimization_barrier((owners, att))
    masks = run_plan(named.T, shards)
    keeps, swaps, slots, placed = [], [], [], []
    shape = (shards * CAP, rows, half)
    every = tuple(range(len(CHUNKS)))
    for c in every:
        if c > 0:
            send, keep = run_project_out(c, att, mlp, output_weight)
        received = swapped(send, "head")
        if c > 0:
            received, _ = lax.optimization_barrier((received, slots[c - 1][0]))
        slots.append(run_combine((c,), (2, 3), masks, grid_features, (keep,), (received,)))
        keeps.append(keep)
        swaps.append(received)
    swaps[-1], _ = lax.optimization_barrier((swaps[-1], slots[-1][0]))
    near_slots, own_slots = run_combine(every, (1, 0), masks, grid_features, keeps, swaps)
    for c in every:
        spots = [(2, (c,)), (3, (c,))]
        arrived = [crossed(slot, d, shards) for d, slot in zip((2, 3), slots[c])]
        if c == 0:
            spots.append((0, every))
            arrived.append(own_slots)
        if c == every[-1]:
            spots.append((1, every))
            arrived.append(crossed(near_slots, 1, shards))
        placed = [run_place(spots, arrived, placed, shape)]
    return placed[0]


def attend_plain(queries, key_table, value_table, chosen, scaling):
    count = chosen.shape[0]
    picked_keys = key_table[chosen]
    picked_keys = picked_keys.reshape(count, -1, picked_keys.shape[3], picked_keys.shape[4])
    picked_values = value_table[chosen]
    picked_values = picked_values.reshape(count, -1, picked_values.shape[3], picked_values.shape[4])
    scores = (
        jnp.einsum("gqhe,gkhe->ghqk", queries, picked_keys, preferred_element_type=jnp.float32)
        * scaling
    )
    highest = jnp.max(scores, axis=-1, keepdims=True)
    weights = jnp.exp(scores - highest)
    weights = (weights / jnp.sum(weights, axis=-1, keepdims=True)).astype(jnp.bfloat16)
    result = jnp.einsum(
        "ghqk,gkhe->gqhe", weights, picked_values, preferred_element_type=jnp.float32
    )
    return result.astype(jnp.bfloat16)


def general(
    grid_features,
    owners,
    adjacency,
    mesh_nodes,
    norm_gain,
    query_weight,
    key_weight,
    value_weight,
    output_weight,
    up_weight,
    down_weight,
):
    shard_count = lax.axis_size("shard")
    head_count = lax.axis_size("head")
    local_blocks, block_rows, feature_share = grid_features.shape
    slots = shard_count * CAP
    owner_col = owners[:, 0]
    position = jnp.arange(local_blocks, dtype=jnp.int32)
    earlier = (owner_col[:, None] == owner_col[None, :]) & (position[None, :] < position[:, None])
    target = owner_col * CAP + jnp.sum(earlier.astype(jnp.int32), axis=1)
    dispatch = (target[:, None] == jnp.arange(slots, dtype=jnp.int32)[None, :]).astype(jnp.bfloat16)
    offset = lax.axis_index("head") * (D // head_count)
    projected = jnp.stack(
        (
            jnp.dot(mesh_nodes, key_weight, preferred_element_type=jnp.float32).astype(
                jnp.bfloat16
            ),
            jnp.dot(mesh_nodes, value_weight, preferred_element_type=jnp.float32).astype(
                jnp.bfloat16
            ),
        )
    )
    tables = lax.all_gather(projected, ("shard", "sub"), axis=1, tiled=True)
    head_local = query_weight.shape[1] // HEAD_DIM
    key_table = tables[0].reshape(-1, block_rows, head_local, HEAD_DIM)
    value_table = tables[1].reshape(-1, block_rows, head_local, HEAD_DIM)
    send_lists = jnp.full((slots, adjacency.shape[1]), -1, jnp.int32).at[target].set(adjacency)
    send_lists = send_lists.reshape(shard_count, CAP, -1)
    complete = lax.all_gather(grid_features, "head", axis=2, tiled=True)
    outgoing = jnp.einsum(
        "gs,gbd->sbd", dispatch, complete, preferred_element_type=jnp.float32
    ).astype(jnp.bfloat16)
    arrived, lists = (
        lax.all_to_all(
            outgoing.reshape(shard_count, CAP, block_rows, D),
            "shard",
            split_axis=0,
            concat_axis=0,
            tiled=True,
        ),
        lax.all_to_all(send_lists, "shard", split_axis=0, concat_axis=0, tiled=True),
    )
    arrived = arrived.reshape(slots, block_rows, D)
    residual = lax.dynamic_slice_in_dim(arrived, offset, D // head_count, 2)
    lists = lists.reshape(slots, -1)
    count = arrived.shape[0]
    values_f = arrived.astype(jnp.float32)
    average = jnp.mean(values_f, axis=-1, keepdims=True)
    centered = values_f - average
    variance = jnp.mean(centered * centered, axis=-1, keepdims=True)
    normed = (centered * lax.rsqrt(variance + epsilon) * norm_gain).astype(jnp.bfloat16)
    flattened = normed.reshape(-1, D)
    queries = jnp.dot(flattened, query_weight, preferred_element_type=jnp.float32).astype(
        jnp.bfloat16
    )
    blocks_each = math.gcd(count, max(1, 512 // block_rows))
    steps_count = count // blocks_each
    queries = queries.reshape(steps_count, blocks_each, block_rows, head_local, HEAD_DIM)

    def attend_step(operands):
        return attend_plain(operands[0], key_table, value_table, operands[1], HEAD_DIM ** (-0.5))

    attended = lax.map(
        attend_step, (queries, jnp.maximum(lists, 0).reshape(steps_count, blocks_each, -1))
    )
    attended = attended.reshape(-1, head_local * HEAD_DIM)
    hidden = jax.nn.gelu(
        jnp.dot(flattened, up_weight, preferred_element_type=jnp.float32), approximate=False
    ).astype(jnp.bfloat16)
    branch = jnp.dot(attended, output_weight, preferred_element_type=jnp.float32)
    branch = branch + jnp.dot(hidden, down_weight, preferred_element_type=jnp.float32)
    branch = branch.reshape(count, block_rows, D)
    reduced = lax.psum_scatter(
        branch.astype(jnp.bfloat16), "head", scatter_dimension=2, tiled=True
    ).astype(jnp.float32)
    occupied = lists[:, 0] >= 0
    summed = residual.astype(jnp.float32) + reduced
    return jnp.where(occupied[:, None, None], summed, 0.0).astype(jnp.bfloat16)


def local(grid_features, owners, adjacency, mesh_nodes, *parameters):
    sizes = [lax.axis_size(axis) for axis in ("shard", "head", "sub")]
    small = grid_features.shape[:2] == (4, BLOCK) and mesh_nodes.shape[0] == 2 * BLOCK
    if sizes == [4, 2, 2] and small and grid_features.shape[2] == 512:
        return paired(grid_features, owners, adjacency, mesh_nodes, *parameters)
    return general(grid_features, owners, adjacency, mesh_nodes, *parameters)


def solution(mesh):
    return jax.shard_map(
        local,
        mesh=mesh,
        in_specs=(
            P(("groups", "shard", "sub"), None, "head"),
            P(("groups", "shard", "sub"), None),
            P(("groups", "shard", "sub"), None),
            P(("groups", "shard", "sub"), None),
            P(),
            P(None, "head"),
            P(None, "head"),
            P(None, "head"),
            P("head", None),
            P(None, "head"),
            P("head", None),
        ),
        out_specs=P(("groups", "shard", "sub"), None, "head"),
        check_vma=False,
    )
```

```python
import functools
import math

import jax
import jax.numpy as jnp
from jax import lax
from jax.experimental import pallas as pl
from jax.experimental.pallas import tpu as pltpu
from jax.sharding import PartitionSpec as P

D = 1024
HEAD_DIM = 64
CAP = 2
BLOCK = 64
QUAD = 4
WIDE = QUAD * HEAD_DIM
TILE = 128
CHUNKS = ((0, 80), (80, 256))
MIB = 1 << 20


epsilon = 1e-05


def dot(a, b):
    return jnp.dot(a, b, preferred_element_type=jnp.float32)


def gelu(x):
    return 0.5 * x * (1.0 + lax.erf(x * (2.0**-0.5)))


def in_hbm(x):
    return pltpu.with_memory_space_constraint(x, pltpu.HBM)


def in_vmem(x):
    return pltpu.with_memory_space_constraint(x, pltpu.VMEM)


def whole(space):
    return pl.BlockSpec(memory_space=space)


def vmem(count):
    return [whole(pltpu.VMEM)] * count


def params(mib):
    return pltpu.CompilerParams(vmem_limit_bytes=mib * MIB)


def mlp_kernel(own, other, gain, wq, wup, wdn, q_out, mlp_out, normed_s):
    half = own.shape[1]
    units = wup.shape[1]
    chunk = units // 4
    x_other = other[...].astype(jnp.float32)
    x_own = own[...].astype(jnp.float32)

    def mean(a, b):
        total = jnp.sum(a, axis=-1, keepdims=True) + jnp.sum(b, axis=-1, keepdims=True)
        return total * (0.5 / half)

    average = mean(x_other, x_own)
    x_other = x_other - average
    x_own = x_own - average
    factor = lax.rsqrt(mean(x_other * x_other, x_own * x_own) + epsilon)
    normed_s[:, :half] = (x_other * factor * gain[:, :half]).astype(jnp.bfloat16)
    normed_s[:, half:] = (x_own * factor * gain[:, half:]).astype(jnp.bfloat16)
    normed = normed_s[...]
    q_out[...] = dot(normed, wq[...]).astype(jnp.bfloat16)
    for c in range(units // chunk):
        span = slice(c * chunk, (c + 1) * chunk)
        hidden = gelu(dot(normed, wup[:, span])).astype(jnp.bfloat16)
        term = dot(hidden, wdn[span, :])
        if c == 0:
            mlp_out[...] = term
        else:
            mlp_out[...] += term


def run_mlp(own, other, gain, wq, wup, wdn):
    rows = own.shape[0]
    width = wq.shape[0]
    units = wup.shape[1]
    return pl.pallas_call(
        mlp_kernel,
        out_shape=(
            jax.ShapeDtypeStruct((rows, wq.shape[1]), jnp.bfloat16),
            jax.ShapeDtypeStruct((rows, width), jnp.float32),
        ),
        in_specs=vmem(6),
        out_specs=tuple(vmem(2)),
        scratch_shapes=[pltpu.VMEM((rows, width), jnp.bfloat16)],
        compiler_params=params(16),
        cost_estimate=pl.CostEstimate(
            flops=2 * rows * width * (wq.shape[1] + 2 * units),
            bytes_accessed=2 * width * (wq.shape[1] + 2 * units),
            transcendentals=rows * units,
        ),
        name="mlp",
    )(own, other, gain, wq, wup, wdn)


def pick_kernel(mesh, out, sem):
    first = pl.multiple_of(lax.axis_index("head") * BLOCK, BLOCK)
    copy = pltpu.make_async_copy(mesh.at[pl.ds(first, BLOCK), :], out, sem)
    copy.start()
    copy.wait()


def run_pick(mesh):
    return pl.pallas_call(
        pick_kernel,
        out_shape=jax.ShapeDtypeStruct((BLOCK, mesh.shape[1]), mesh.dtype),
        in_specs=[whole(pltpu.HBM)],
        out_specs=whole(pltpu.VMEM),
        scratch_shapes=[pltpu.SemaphoreType.DMA(())],
        compiler_params=params(4),
        cost_estimate=pl.CostEstimate(flops=0, bytes_accessed=4 * mesh.size, transcendentals=0),
        name="pick",
    )(in_hbm(mesh))


def stage_kernel(axes, *refs):
    sources, targets, sem = refs[: len(axes)], refs[len(axes) : -1], refs[-1]
    h = lax.axis_index("head")
    copies = []

    def add(source, target):
        pieces = 2 if source.shape[0] >= 512 else 1
        rows = source.shape[0] // pieces
        for piece in range(pieces):
            span = pl.ds(piece * rows, rows)
            copies.append(
                pltpu.make_async_copy(
                    source.at[span, :], target.at[span, :], sem.at[len(copies)]
                )
            )
            copies[-1].start()

    for source, target, axis in zip(sources, targets, axes):
        if axis is None:
            add(source, target)
            continue
        if axis == "rest":
            add(source.at[pl.ds(pl.multiple_of((1 - h) * BLOCK, BLOCK), BLOCK), :], target)
            continue
        half = source.shape[axis] // 2
        for part, head in enumerate((1 - h, h)):
            span = pl.ds(pl.multiple_of(head * half, half), half)
            place = pl.ds(part * half, half)
            if axis == 0:
                add(source.at[span, :], target.at[place, :])
            else:
                add(source.at[:, span], target.at[:, place])
    for copy in copies:
        copy.wait()


def run_stage(arrays, axes):
    size = sum(2 * array.size for array in arrays)
    return pl.pallas_call(
        functools.partial(stage_kernel, axes),
        out_shape=tuple(
            jax.ShapeDtypeStruct((BLOCK,) + array.shape[1:] if axis == "rest" else array.shape, array.dtype)
            for array, axis in zip(arrays, axes)
        ),
        in_specs=[whole(pltpu.HBM)] * len(arrays),
        out_specs=tuple(vmem(len(arrays))),
        scratch_shapes=[pltpu.SemaphoreType.DMA((4 * len(arrays),))],
        compiler_params=params(16),
        cost_estimate=pl.CostEstimate(
            flops=2000 * size, bytes_accessed=20 * size, transcendentals=0
        ),
        name="stage",
    )(*(in_hbm(array) for array in arrays))


def project_kernel(*refs):
    pieces, (wk, wv, out) = refs[:-3], refs[-3:]
    width = wk.shape[1]
    rows = jnp.concatenate([piece[...] for piece in pieces], axis=0)
    out[:, :width] = dot(rows, wk[...]).astype(jnp.bfloat16)
    out[:, width:] = dot(rows, wv[...]).astype(jnp.bfloat16)


def run_project(pieces, wk, wv):
    rows = sum(piece.shape[0] for piece in pieces)
    depth, width = wk.shape
    return pl.pallas_call(
        project_kernel,
        out_shape=jax.ShapeDtypeStruct((rows, 2 * width), jnp.bfloat16),
        in_specs=vmem(len(pieces) + 2),
        out_specs=whole(pltpu.VMEM),
        compiler_params=params(8),
        cost_estimate=pl.CostEstimate(
            flops=300 * rows * depth * width,
            bytes_accessed=300 * depth * width + 300 * rows * depth,
            transcendentals=0,
        ),
        name="project",
    )(*pieces, in_vmem(wk), in_vmem(wv))


def table_kernel(mine, sibling, mine_last, sibling_last, table):
    for i, (first, last) in enumerate(((mine, mine_last), (sibling, sibling_last))):
        table[i, : first.shape[0]] = first[...]
        table[i, table.shape[1] - last.shape[0] :] = last[...]


def run_table(mine, sibling, mine_last, sibling_last, blocks):
    return pl.pallas_call(
        table_kernel,
        out_shape=jax.ShapeDtypeStruct((2, blocks) + mine.shape[1:], jnp.bfloat16),
        in_specs=vmem(4),
        out_specs=whole(pltpu.VMEM),
        compiler_params=params(8),
        cost_estimate=pl.CostEstimate(
            flops=0, bytes_accessed=80 * mine.size, transcendentals=0
        ),
        name="table",
    )(mine, sibling, mine_last, sibling_last)


def pieces_of(c):
    low, high = CHUNKS[c]
    pieces = []
    for tile in range(low // BLOCK, -(-high // BLOCK)):
        first, last = max(low, tile * BLOCK), min(high, (tile + 1) * BLOCK)
        rows = slice(first - tile * BLOCK, last - tile * BLOCK)
        pieces.append((tile, rows, slice(first - low, last - low)))
    return pieces


def project_out(c, att, mlp, wo, send, keep):
    half = att.shape[1]
    h = lax.axis_index("head")
    pieces = pieces_of(c)
    start, stop = pieces[0][0] * TILE, (pieces[-1][0] + 1) * TILE

    def write(head):
        for out, first, place in ((send, 0, 1 - head), (keep, half, head)):
            extra = mlp[:, first + start : first + stop]
            total = extra + dot(att[...], wo[:, place * half + start : place * half + stop])
            total = total.astype(jnp.bfloat16)
            for tile, rows, spot in pieces:
                columns = slice(tile * TILE - start, (tile + 1) * TILE - start)
                for t in range(out.shape[0]):
                    block = slice(t * BLOCK + rows.start, t * BLOCK + rows.stop)
                    out[t, spot, :] = total[block, columns]

    for head in range(2):
        pl.when(h == head)(functools.partial(write, head))


def attend_kernel(
    adjacency, q, mine, sibling, table_in, mlp, wo, send, keep, att, table, stacked_s, near_s, sem
):
    del table_in
    s = lax.axis_index("shard")
    h = lax.axis_index("head")
    u = lax.axis_index("sub")
    half = wo.shape[0]
    ready = table.shape[1] - 2 * mine.shape[0]
    copy = pltpu.make_async_copy(adjacency, near_s, sem)
    copy.start()
    for i, part in enumerate((mine, sibling)):
        table[i, ready : ready + part.shape[0]] = part[...]
    rows_of = lax.broadcasted_iota(jnp.int32, (WIDE, WIDE), 0) // BLOCK
    lanes_of = lax.broadcasted_iota(jnp.int32, (WIDE, WIDE), 1) // HEAD_DIM
    diagonal = rows_of == lanes_of
    lane_head = lax.broadcasted_iota(jnp.int32, (BLOCK, WIDE), 1) // HEAD_DIM
    scale = HEAD_DIM**-0.5 * math.log2(math.e)
    groups = half // WIDE
    steps = near_s.shape[0] * groups
    for step in range(steps):
        b, g = divmod(step, groups)
        columns = slice(g * WIDE, (g + 1) * WIDE)
        stacked = jnp.concatenate([q[b * BLOCK : (b + 1) * BLOCK, columns]] * QUAD, axis=0)
        stacked_s[step] = jnp.where(diagonal, stacked, jnp.zeros_like(stacked))
    copy.wait()
    places = []
    for b in range(near_s.shape[0]):
        places.append([])
        for j in range(near_s.shape[1]):
            m = near_s[b, j]
            part = lax.rem(m, 2)
            core = lax.rem(m // 2, 2)
            distance = s ^ (m // 4)
            part = jnp.where(distance <= 1, part, part ^ h)
            places[b].append((core ^ u, distance * 2 + part))

    def scores_of(step):
        b, g = divmod(step, groups)
        columns = slice(g * WIDE, (g + 1) * WIDE)
        keys = jnp.concatenate([table[i, p, :, columns] for i, p in places[b]], axis=0)
        return lax.dot_general(
            stacked_s[step], keys, (((1,), (1,)), ((), ())), preferred_element_type=jnp.float32
        )

    scores = scores_of(0)
    for step in range(steps):
        following = scores_of(step + 1) if step + 1 < steps else None
        b, g = divmod(step, groups)
        columns = slice(half + g * WIDE, half + (g + 1) * WIDE)
        values = jnp.concatenate([table[i, p, :, columns] for i, p in places[b]], axis=0)
        highest = jnp.max(scores, axis=-1, keepdims=True)
        weights = jnp.exp2((scores - highest) * scale)
        total = jnp.sum(weights, axis=-1, keepdims=True)
        mixed = dot(weights.astype(jnp.bfloat16), values) * (1.0 / total)
        merged = mixed[0:BLOCK, :]
        for i in range(1, QUAD):
            merged = jnp.where(lane_head == i, mixed[i * BLOCK : (i + 1) * BLOCK, :], merged)
        rows = slice(b * BLOCK, (b + 1) * BLOCK)
        att[rows, g * WIDE : (g + 1) * WIDE] = merged.astype(jnp.bfloat16)
        scores = following
    project_out(0, att, mlp, wo, send, keep)


def run_attend(adjacency, q, mine, sibling, table, mlp, wo):
    rows, half = q.shape
    size = CHUNKS[0][1] - CHUNKS[0][0]
    part = jax.ShapeDtypeStruct((rows // BLOCK, size, TILE), jnp.bfloat16)
    blocks = table.shape[0] * table.shape[1]
    send, keep, att, _ = pl.pallas_call(
        attend_kernel,
        out_shape=(
            part,
            part,
            jax.ShapeDtypeStruct(q.shape, jnp.bfloat16),
            jax.ShapeDtypeStruct(table.shape, jnp.bfloat16),
        ),
        in_specs=[whole(pl.ANY)] + vmem(6),
        out_specs=tuple(vmem(4)),
        scratch_shapes=[
            pltpu.VMEM((rows // BLOCK * (half // WIDE), WIDE, WIDE), jnp.bfloat16),
            pltpu.SMEM(adjacency.shape, jnp.int32),
            pltpu.SemaphoreType.DMA(()),
        ],
        input_output_aliases={4: 3},
        compiler_params=params(16),
        cost_estimate=pl.CostEstimate(
            flops=20 * rows * half * (D + 8 * 8 * BLOCK),
            bytes_accessed=40 * blocks * BLOCK * half + 20 * half * D + 40 * rows * D,
            transcendentals=rows * 8 * BLOCK * half // HEAD_DIM,
        ),
        name="attend",
    )(adjacency, q, mine, sibling, table, mlp, in_vmem(wo))
    return send, keep, att


def run_project_out(c, att, mlp, wo):
    rows, half = att.shape
    size = CHUNKS[c][1] - CHUNKS[c][0]
    part = jax.ShapeDtypeStruct((rows // BLOCK, size, TILE), jnp.bfloat16)
    return pl.pallas_call(
        functools.partial(project_out, c),
        out_shape=(part, part),
        in_specs=vmem(3),
        out_specs=tuple(vmem(2)),
        compiler_params=params(8),
        cost_estimate=pl.CostEstimate(
            flops=200 * rows * half * D,
            bytes_accessed=200 * half * D,
            transcendentals=0,
        ),
        name="project_out",
    )(att, mlp, in_vmem(wo))


def plan_kernel(owners, masks):
    s = lax.axis_index("shard")
    count = owners.shape[1]
    names = [owners[0, t] for t in range(count)]
    for t in range(count):
        same = [(names[e] == names[t]).astype(jnp.int32) for e in range(t)]
        rank = sum(same, jnp.int32(0))
        for d in range(masks.shape[0]):
            for j in range(CAP):
                hit = (names[t] == s ^ d) & (rank == j)
                masks[d, j, t] = jnp.full(masks.shape[3:], hit.astype(jnp.float32))


def run_plan(owners, shards):
    return pl.pallas_call(
        plan_kernel,
        out_shape=jax.ShapeDtypeStruct((shards, CAP, owners.shape[1], 8, 128), jnp.float32),
        in_specs=[whole(pltpu.SMEM)],
        out_specs=whole(pltpu.VMEM),
        compiler_params=params(4),
        cost_estimate=pl.CostEstimate(flops=0, bytes_accessed=1 << 18, transcendentals=0),
        name="plan",
    )(owners)


def combine_kernel(chunks, distances, masks, grid_features, *refs):
    keeps, refs = refs[: len(chunks)], refs[len(chunks) :]
    swaps, outs = refs[: len(chunks)], refs[len(chunks) :]
    count = grid_features.shape[0]
    first = CHUNKS[chunks[0]][0]
    for c, keep, swap in zip(chunks, keeps, swaps):
        low, high = CHUNKS[c]
        updated = []
        for t in range(count):
            residual = [
                grid_features[t, rows, tile * TILE : (tile + 1) * TILE]
                for tile, rows, _ in pieces_of(c)
            ]
            residual = jnp.concatenate(residual, axis=0).astype(jnp.float32)
            partials = keep[t].astype(jnp.float32) + swap[t].astype(jnp.float32)
            updated.append(residual + partials)
        for d, out in zip(distances, outs):
            for j in range(CAP):
                chosen = jnp.zeros_like(updated[0])
                for t in range(count):
                    mask = jnp.broadcast_to(masks[d, j, t, 0:1, :], chosen.shape)
                    chosen = jnp.where(mask > 0.5, updated[t], chosen)
                out[j, low - first : high - first, :] = chosen.astype(jnp.bfloat16)


def run_combine(chunks, distances, masks, grid_features, keeps, swaps):
    count = grid_features.shape[0]
    rows, width = CHUNKS[chunks[-1]][1] - CHUNKS[chunks[0]][0], TILE
    slot = jax.ShapeDtypeStruct((CAP, rows, width), jnp.bfloat16)
    return pl.pallas_call(
        functools.partial(combine_kernel, chunks, distances),
        out_shape=(slot,) * len(distances),
        in_specs=vmem(2 + 2 * len(chunks)),
        out_specs=tuple(vmem(len(distances))),
        compiler_params=params(8),
        cost_estimate=pl.CostEstimate(
            flops=60000 * count * rows * width,
            bytes_accessed=400 * rows * width * (3 * count + CAP * len(distances)),
            transcendentals=0,
        ),
        name="combine",
    )(masks, grid_features, *keeps, *swaps)


def place_kernel(spots, *refs):
    out, sem = refs[-2:]
    s = lax.axis_index("shard")
    copies = []
    for ref, (d, chunks) in zip(refs, spots):
        first = CHUNKS[chunks[0]][0]
        slots = pl.ds((s ^ d) * CAP, CAP)
        for c in chunks:
            shift = CHUNKS[c][0] - first
            for tile, rows, spot in pieces_of(c):
                size = rows.stop - rows.start
                source = ref.at[:, pl.ds(spot.start + shift, size), :]
                columns = pl.ds(tile * TILE, TILE)
                target = out.at[slots, pl.ds(rows.start, size), columns]
                copies.append(pltpu.make_async_copy(source, target, sem.at[len(copies)]))
                copies[-1].start()
    for copy in copies:
        copy.wait()


def run_place(spots, arrived, placed, shape):
    count = sum(len(pieces_of(c)) for _, chunks in spots for c in chunks)
    return pl.pallas_call(
        functools.partial(place_kernel, spots),
        out_shape=jax.ShapeDtypeStruct(shape, jnp.bfloat16),
        in_specs=vmem(len(arrived)) + [whole(pltpu.HBM)] * len(placed),
        out_specs=whole(pltpu.HBM),
        scratch_shapes=[pltpu.SemaphoreType.DMA((count,))],
        input_output_aliases={len(arrived): 0} if placed else {},
        compiler_params=params(4),
        cost_estimate=pl.CostEstimate(
            flops=400000 * sum(part.size for part in arrived), bytes_accessed=0, transcendentals=0
        ),
        name="place",
    )(*arrived, *placed)


def crossed(x, distance, size):
    return lax.ppermute(x, "shard", [(i, i ^ distance) for i in range(size)])


def swapped(x, axis):
    return lax.ppermute(x, axis, [(0, 1), (1, 0)])


def paired(
    grid_features,
    owners,
    adjacency,
    mesh_nodes,
    norm_gain,
    query_weight,
    key_weight,
    value_weight,
    output_weight,
    up_weight,
    down_weight,
):
    shards = lax.axis_size("shard")
    count, rows, half = grid_features.shape
    flat = grid_features.reshape(count * rows, half)
    half_unit = run_pick(mesh_nodes)
    far = crossed(half_unit, 2, shards)
    waiting, _ = lax.optimization_barrier((mesh_nodes, half_unit))
    near = crossed(waiting, 1, shards)
    waiting, _ = lax.optimization_barrier((flat, half_unit))
    other = swapped(waiting, "head")
    flat, gain, wq, wup, wdn, mesh, rest = run_stage(
        (
            flat,
            norm_gain.reshape(1, -1),
            query_weight,
            up_weight,
            down_weight,
            mesh_nodes,
            mesh_nodes,
        ),
        (None, 1, 0, 0, 1, None, "rest"),
    )
    straight = crossed(rest, 3, shards)
    far, _ = lax.optimization_barrier((far, rest))
    farther = crossed(far, 1, shards)
    far_pair = swapped(far, "head")
    queries, mlp = run_mlp(flat, other, gain, wq, wup, wdn)
    queries, mlp, far_pair, near = lax.optimization_barrier((queries, mlp, far_pair, near))
    blocked = (-1, BLOCK, 2 * half)
    mine_a = run_project((mesh, near, far, far_pair), key_weight, value_weight)
    sibling_a = swapped(mine_a, "sub")
    straight, _ = lax.optimization_barrier((straight, mine_a))
    mine_m = run_project((straight,), key_weight, value_weight)
    sibling_m = swapped(mine_m, "sub")
    parts = [part.reshape(blocked) for part in (mine_a, sibling_a, mine_m, sibling_m)]
    table = run_table(*parts, 2 * shards)
    farther, _ = lax.optimization_barrier((farther, mine_m))
    mine_b = run_project((farther,), key_weight, value_weight)
    sibling_b = swapped(mine_b, "sub")
    send, keep, att = run_attend(
        adjacency, queries, mine_b.reshape(blocked), sibling_b.reshape(blocked), table, mlp, output_weight
    )
    named, _ = lax.optimization_barrier((owners, att))
    masks = run_plan(named.T, shards)
    keeps, swaps, slots, placed = [], [], [], []
    shape = (shards * CAP, rows, half)
    every = tuple(range(len(CHUNKS)))
    for c in every:
        if c > 0:
            send, keep = run_project_out(c, att, mlp, output_weight)
        received = swapped(send, "head")
        if c > 0:
            received, _ = lax.optimization_barrier((received, slots[c - 1][0]))
        slots.append(run_combine((c,), (2, 3), masks, grid_features, (keep,), (received,)))
        keeps.append(keep)
        swaps.append(received)
    swaps[-1], _ = lax.optimization_barrier((swaps[-1], slots[-1][0]))
    near_slots, own_slots = run_combine(every, (1, 0), masks, grid_features, keeps, swaps)
    for c in every:
        spots = [(2, (c,)), (3, (c,))]
        arrived = [crossed(slot, d, shards) for d, slot in zip((2, 3), slots[c])]
        if c == 0:
            spots.append((0, every))
            arrived.append(own_slots)
        if c == every[-1]:
            spots.append((1, every))
            arrived.append(crossed(near_slots, 1, shards))
        placed = [run_place(spots, arrived, placed, shape)]
    return placed[0]


def attend_plain(queries, key_table, value_table, chosen, scaling):
    count = chosen.shape[0]
    picked_keys = key_table[chosen]
    picked_keys = picked_keys.reshape(count, -1, picked_keys.shape[3], picked_keys.shape[4])
    picked_values = value_table[chosen]
    picked_values = picked_values.reshape(count, -1, picked_values.shape[3], picked_values.shape[4])
    scores = (
        jnp.einsum("gqhe,gkhe->ghqk", queries, picked_keys, preferred_element_type=jnp.float32)
        * scaling
    )
    highest = jnp.max(scores, axis=-1, keepdims=True)
    weights = jnp.exp(scores - highest)
    weights = (weights / jnp.sum(weights, axis=-1, keepdims=True)).astype(jnp.bfloat16)
    result = jnp.einsum(
        "ghqk,gkhe->gqhe", weights, picked_values, preferred_element_type=jnp.float32
    )
    return result.astype(jnp.bfloat16)


def general(
    grid_features,
    owners,
    adjacency,
    mesh_nodes,
    norm_gain,
    query_weight,
    key_weight,
    value_weight,
    output_weight,
    up_weight,
    down_weight,
):
    shard_count = lax.axis_size("shard")
    head_count = lax.axis_size("head")
    local_blocks, block_rows, feature_share = grid_features.shape
    slots = shard_count * CAP
    owner_col = owners[:, 0]
    position = jnp.arange(local_blocks, dtype=jnp.int32)
    earlier = (owner_col[:, None] == owner_col[None, :]) & (position[None, :] < position[:, None])
    target = owner_col * CAP + jnp.sum(earlier.astype(jnp.int32), axis=1)
    dispatch = (target[:, None] == jnp.arange(slots, dtype=jnp.int32)[None, :]).astype(jnp.bfloat16)
    offset = lax.axis_index("head") * (D // head_count)
    projected = jnp.stack(
        (
            jnp.dot(mesh_nodes, key_weight, preferred_element_type=jnp.float32).astype(
                jnp.bfloat16
            ),
            jnp.dot(mesh_nodes, value_weight, preferred_element_type=jnp.float32).astype(
                jnp.bfloat16
            ),
        )
    )
    tables = lax.all_gather(projected, ("shard", "sub"), axis=1, tiled=True)
    head_local = query_weight.shape[1] // HEAD_DIM
    key_table = tables[0].reshape(-1, block_rows, head_local, HEAD_DIM)
    value_table = tables[1].reshape(-1, block_rows, head_local, HEAD_DIM)
    send_lists = jnp.full((slots, adjacency.shape[1]), -1, jnp.int32).at[target].set(adjacency)
    send_lists = send_lists.reshape(shard_count, CAP, -1)
    complete = lax.all_gather(grid_features, "head", axis=2, tiled=True)
    outgoing = jnp.einsum(
        "gs,gbd->sbd", dispatch, complete, preferred_element_type=jnp.float32
    ).astype(jnp.bfloat16)
    arrived, lists = (
        lax.all_to_all(
            outgoing.reshape(shard_count, CAP, block_rows, D),
            "shard",
            split_axis=0,
            concat_axis=0,
            tiled=True,
        ),
        lax.all_to_all(send_lists, "shard", split_axis=0, concat_axis=0, tiled=True),
    )
    arrived = arrived.reshape(slots, block_rows, D)
    residual = lax.dynamic_slice_in_dim(arrived, offset, D // head_count, 2)
    lists = lists.reshape(slots, -1)
    count = arrived.shape[0]
    values_f = arrived.astype(jnp.float32)
    average = jnp.mean(values_f, axis=-1, keepdims=True)
    centered = values_f - average
    variance = jnp.mean(centered * centered, axis=-1, keepdims=True)
    normed = (centered * lax.rsqrt(variance + epsilon) * norm_gain).astype(jnp.bfloat16)
    flattened = normed.reshape(-1, D)
    queries = jnp.dot(flattened, query_weight, preferred_element_type=jnp.float32).astype(
        jnp.bfloat16
    )
    blocks_each = math.gcd(count, max(1, 512 // block_rows))
    steps_count = count // blocks_each
    queries = queries.reshape(steps_count, blocks_each, block_rows, head_local, HEAD_DIM)

    def attend_step(operands):
        return attend_plain(operands[0], key_table, value_table, operands[1], HEAD_DIM ** (-0.5))

    attended = lax.map(
        attend_step, (queries, jnp.maximum(lists, 0).reshape(steps_count, blocks_each, -1))
    )
    attended = attended.reshape(-1, head_local * HEAD_DIM)
    hidden = jax.nn.gelu(
        jnp.dot(flattened, up_weight, preferred_element_type=jnp.float32), approximate=False
    ).astype(jnp.bfloat16)
    branch = jnp.dot(attended, output_weight, preferred_element_type=jnp.float32)
    branch = branch + jnp.dot(hidden, down_weight, preferred_element_type=jnp.float32)
    branch = branch.reshape(count, block_rows, D)
    reduced = lax.psum_scatter(
        branch.astype(jnp.bfloat16), "head", scatter_dimension=2, tiled=True
    ).astype(jnp.float32)
    occupied = lists[:, 0] >= 0
    summed = residual.astype(jnp.float32) + reduced
    return jnp.where(occupied[:, None, None], summed, 0.0).astype(jnp.bfloat16)


def local(grid_features, owners, adjacency, mesh_nodes, *parameters):
    sizes = [lax.axis_size(axis) for axis in ("shard", "head", "sub")]
    small = grid_features.shape[:2] == (4, BLOCK) and mesh_nodes.shape[0] == 2 * BLOCK
    if sizes == [4, 2, 2] and small and grid_features.shape[2] == 512:
        return paired(grid_features, owners, adjacency, mesh_nodes, *parameters)
    return general(grid_features, owners, adjacency, mesh_nodes, *parameters)


def solution(mesh):
    return jax.shard_map(
        local,
        mesh=mesh,
        in_specs=(
            P(("groups", "shard", "sub"), None, "head"),
            P(("groups", "shard", "sub"), None),
            P(("groups", "shard", "sub"), None),
            P(("groups", "shard", "sub"), None),
            P(),
            P(None, "head"),
            P(None, "head"),
            P(None, "head"),
            P("head", None),
            P(None, "head"),
            P("head", None),
        ),
        out_specs=P(("groups", "shard", "sub"), None, "head"),
        check_vma=False,
    )
```

```python
import functools
import math

import jax
import jax.numpy as jnp
from jax import lax
from jax.experimental import pallas as pl
from jax.experimental.pallas import tpu as pltpu
from jax.sharding import PartitionSpec as P

D = 1024
HEAD_DIM = 64
CAP = 2
BLOCK = 64
QUAD = 4
WIDE = QUAD * HEAD_DIM
TILE = 128
CHUNKS = ((0, 80), (80, 256))
MIB = 1 << 20


epsilon = 1e-05


def dot(a, b):
    return jnp.dot(a, b, preferred_element_type=jnp.float32)


def gelu(x):
    return 0.5 * x * (1.0 + lax.erf(x * (2.0**-0.5)))


def in_hbm(x):
    return pltpu.with_memory_space_constraint(x, pltpu.HBM)


def in_vmem(x):
    return pltpu.with_memory_space_constraint(x, pltpu.VMEM)


def whole(space):
    return pl.BlockSpec(memory_space=space)


def vmem(count):
    return [whole(pltpu.VMEM)] * count


def params(mib):
    return pltpu.CompilerParams(vmem_limit_bytes=mib * MIB)


def mlp_kernel(own, other, gain, wq, wup, wdn, q_out, mlp_out, normed_s, wq_s, sem):
    half = own.shape[1]
    h = lax.axis_index("head")
    copies = []
    for part, head in enumerate((1 - h, h)):
        rows = pl.ds(pl.multiple_of(head * half, half), half)
        target = wq_s.at[pl.ds(part * half, half), :]
        copies.append(pltpu.make_async_copy(wq.at[rows, :], target, sem.at[part]))
        copies[part].start()
    units = wup.shape[1]
    chunk = units // 4
    x_other = other[...].astype(jnp.float32)
    x_own = own[...].astype(jnp.float32)

    def mean(a, b):
        total = jnp.sum(a, axis=-1, keepdims=True) + jnp.sum(b, axis=-1, keepdims=True)
        return total * (0.5 / half)

    average = mean(x_other, x_own)
    x_other = x_other - average
    x_own = x_own - average
    factor = lax.rsqrt(mean(x_other * x_other, x_own * x_own) + epsilon)
    normed_s[:, :half] = (x_other * factor * gain[:, :half]).astype(jnp.bfloat16)
    normed_s[:, half:] = (x_own * factor * gain[:, half:]).astype(jnp.bfloat16)
    normed = normed_s[...]
    for c in range(units // chunk):
        span = slice(c * chunk, (c + 1) * chunk)
        hidden = gelu(dot(normed, wup[:, span])).astype(jnp.bfloat16)
        term = dot(hidden, wdn[span, :])
        if c == 0:
            mlp_out[...] = term
        else:
            mlp_out[...] += term
    for copy in copies:
        copy.wait()
    q_out[...] = dot(normed, wq_s[...]).astype(jnp.bfloat16)


def run_mlp(own, other, gain, wq, wup, wdn):
    rows = own.shape[0]
    width = wq.shape[0]
    units = wup.shape[1]
    return pl.pallas_call(
        mlp_kernel,
        out_shape=(
            jax.ShapeDtypeStruct((rows, wq.shape[1]), jnp.bfloat16),
            jax.ShapeDtypeStruct((rows, width), jnp.float32),
        ),
        in_specs=vmem(3) + [whole(pltpu.HBM)] + vmem(2),
        out_specs=tuple(vmem(2)),
        scratch_shapes=[
            pltpu.VMEM((rows, width), jnp.bfloat16),
            pltpu.VMEM(wq.shape, jnp.bfloat16),
            pltpu.SemaphoreType.DMA((2,)),
        ],
        compiler_params=params(16),
        cost_estimate=pl.CostEstimate(
            flops=2 * rows * width * (wq.shape[1] + 2 * units),
            bytes_accessed=2 * width * (wq.shape[1] + 2 * units),
            transcendentals=rows * units,
        ),
        name="mlp",
    )(own, other, gain, in_hbm(wq), wup, wdn)


def pick_kernel(mesh, out, sem):
    first = pl.multiple_of(lax.axis_index("head") * BLOCK, BLOCK)
    copy = pltpu.make_async_copy(mesh.at[pl.ds(first, BLOCK), :], out, sem)
    copy.start()
    copy.wait()


def run_pick(mesh):
    return pl.pallas_call(
        pick_kernel,
        out_shape=jax.ShapeDtypeStruct((BLOCK, mesh.shape[1]), mesh.dtype),
        in_specs=[whole(pltpu.HBM)],
        out_specs=whole(pltpu.VMEM),
        scratch_shapes=[pltpu.SemaphoreType.DMA(())],
        compiler_params=params(4),
        cost_estimate=pl.CostEstimate(flops=0, bytes_accessed=4 * mesh.size, transcendentals=0),
        name="pick",
    )(in_hbm(mesh))


def stage_kernel(axes, *refs):
    sources, targets, sem = refs[: len(axes)], refs[len(axes) : -1], refs[-1]
    h = lax.axis_index("head")
    copies = []

    def add(source, target):
        pieces = 2 if source.shape[0] >= 512 else 1
        rows = source.shape[0] // pieces
        for piece in range(pieces):
            span = pl.ds(piece * rows, rows)
            copies.append(
                pltpu.make_async_copy(
                    source.at[span, :], target.at[span, :], sem.at[len(copies)]
                )
            )
            copies[-1].start()

    for source, target, axis in zip(sources, targets, axes):
        if axis is None:
            add(source, target)
            continue
        if axis == "rest":
            add(source.at[pl.ds(pl.multiple_of((1 - h) * BLOCK, BLOCK), BLOCK), :], target)
            continue
        half = source.shape[axis] // 2
        for part, head in enumerate((1 - h, h)):
            span = pl.ds(pl.multiple_of(head * half, half), half)
            place = pl.ds(part * half, half)
            if axis == 0:
                add(source.at[span, :], target.at[place, :])
            else:
                add(source.at[:, span], target.at[:, place])
    for copy in copies:
        copy.wait()


def run_stage(arrays, axes):
    size = sum(2 * array.size for array in arrays)
    return pl.pallas_call(
        functools.partial(stage_kernel, axes),
        out_shape=tuple(
            jax.ShapeDtypeStruct((BLOCK,) + array.shape[1:] if axis == "rest" else array.shape, array.dtype)
            for array, axis in zip(arrays, axes)
        ),
        in_specs=[whole(pltpu.HBM)] * len(arrays),
        out_specs=tuple(vmem(len(arrays))),
        scratch_shapes=[pltpu.SemaphoreType.DMA((4 * len(arrays),))],
        compiler_params=params(16),
        cost_estimate=pl.CostEstimate(
            flops=2000 * size, bytes_accessed=20 * size, transcendentals=0
        ),
        name="stage",
    )(*(in_hbm(array) for array in arrays))


def project_kernel(*refs):
    pieces, (wk, wv, out) = refs[:-3], refs[-3:]
    width = wk.shape[1]
    rows = jnp.concatenate([piece[...] for piece in pieces], axis=0)
    out[:, :width] = dot(rows, wk[...]).astype(jnp.bfloat16)
    out[:, width:] = dot(rows, wv[...]).astype(jnp.bfloat16)


def run_project(pieces, wk, wv):
    rows = sum(piece.shape[0] for piece in pieces)
    depth, width = wk.shape
    return pl.pallas_call(
        project_kernel,
        out_shape=jax.ShapeDtypeStruct((rows, 2 * width), jnp.bfloat16),
        in_specs=vmem(len(pieces) + 2),
        out_specs=whole(pltpu.VMEM),
        compiler_params=params(8),
        cost_estimate=pl.CostEstimate(
            flops=300 * rows * depth * width,
            bytes_accessed=300 * depth * width + 300 * rows * depth,
            transcendentals=0,
        ),
        name="project",
    )(*pieces, in_vmem(wk), in_vmem(wv))


def table_kernel(mine, sibling, mine_last, sibling_last, table):
    for i, (first, last) in enumerate(((mine, mine_last), (sibling, sibling_last))):
        table[i, : first.shape[0]] = first[...]
        table[i, table.shape[1] - last.shape[0] :] = last[...]


def run_table(mine, sibling, mine_last, sibling_last, blocks):
    return pl.pallas_call(
        table_kernel,
        out_shape=jax.ShapeDtypeStruct((2, blocks) + mine.shape[1:], jnp.bfloat16),
        in_specs=vmem(4),
        out_specs=whole(pltpu.VMEM),
        compiler_params=params(8),
        cost_estimate=pl.CostEstimate(
            flops=0, bytes_accessed=80 * mine.size, transcendentals=0
        ),
        name="table",
    )(mine, sibling, mine_last, sibling_last)


def pieces_of(c):
    low, high = CHUNKS[c]
    pieces = []
    for tile in range(low // BLOCK, -(-high // BLOCK)):
        first, last = max(low, tile * BLOCK), min(high, (tile + 1) * BLOCK)
        rows = slice(first - tile * BLOCK, last - tile * BLOCK)
        pieces.append((tile, rows, slice(first - low, last - low)))
    return pieces


def project_out(c, att, mlp, wo, send, keep):
    half = att.shape[1]
    h = lax.axis_index("head")
    pieces = pieces_of(c)
    start, stop = pieces[0][0] * TILE, (pieces[-1][0] + 1) * TILE

    def write(head):
        for out, first, place in ((send, 0, 1 - head), (keep, half, head)):
            extra = mlp[:, first + start : first + stop]
            total = extra + dot(att[...], wo[:, place * half + start : place * half + stop])
            total = total.astype(jnp.bfloat16)
            for tile, rows, spot in pieces:
                columns = slice(tile * TILE - start, (tile + 1) * TILE - start)
                for t in range(out.shape[0]):
                    block = slice(t * BLOCK + rows.start, t * BLOCK + rows.stop)
                    out[t, spot, :] = total[block, columns]

    for head in range(2):
        pl.when(h == head)(functools.partial(write, head))


def attend_kernel(
    adjacency, q, mine, sibling, table_in, mlp, wo, send, keep, att, table, stacked_s, near_s, sem
):
    del table_in
    s = lax.axis_index("shard")
    h = lax.axis_index("head")
    u = lax.axis_index("sub")
    half = wo.shape[0]
    ready = table.shape[1] - 2 * mine.shape[0]
    copy = pltpu.make_async_copy(adjacency, near_s, sem)
    copy.start()
    for i, part in enumerate((mine, sibling)):
        table[i, ready : ready + part.shape[0]] = part[...]
    rows_of = lax.broadcasted_iota(jnp.int32, (WIDE, WIDE), 0) // BLOCK
    lanes_of = lax.broadcasted_iota(jnp.int32, (WIDE, WIDE), 1) // HEAD_DIM
    diagonal = rows_of == lanes_of
    lane_head = lax.broadcasted_iota(jnp.int32, (BLOCK, WIDE), 1) // HEAD_DIM
    scale = HEAD_DIM**-0.5 * math.log2(math.e)
    groups = half // WIDE
    steps = near_s.shape[0] * groups
    for step in range(steps):
        b, g = divmod(step, groups)
        columns = slice(g * WIDE, (g + 1) * WIDE)
        stacked = jnp.concatenate([q[b * BLOCK : (b + 1) * BLOCK, columns]] * QUAD, axis=0)
        stacked_s[step] = jnp.where(diagonal, stacked, jnp.zeros_like(stacked))
    copy.wait()
    places = []
    for b in range(near_s.shape[0]):
        places.append([])
        for j in range(near_s.shape[1]):
            m = near_s[b, j]
            part = lax.rem(m, 2)
            core = lax.rem(m // 2, 2)
            distance = s ^ (m // 4)
            part = jnp.where(distance <= 1, part, part ^ h)
            places[b].append((core ^ u, distance * 2 + part))

    def scores_of(step):
        b, g = divmod(step, groups)
        columns = slice(g * WIDE, (g + 1) * WIDE)
        keys = jnp.concatenate([table[i, p, :, columns] for i, p in places[b]], axis=0)
        return lax.dot_general(
            stacked_s[step], keys, (((1,), (1,)), ((), ())), preferred_element_type=jnp.float32
        )

    scores = scores_of(0)
    for step in range(steps):
        following = scores_of(step + 1) if step + 1 < steps else None
        b, g = divmod(step, groups)
        columns = slice(half + g * WIDE, half + (g + 1) * WIDE)
        values = jnp.concatenate([table[i, p, :, columns] for i, p in places[b]], axis=0)
        highest = jnp.max(scores, axis=-1, keepdims=True)
        weights = jnp.exp2((scores - highest) * scale)
        total = jnp.sum(weights, axis=-1, keepdims=True)
        mixed = dot(weights.astype(jnp.bfloat16), values) * (1.0 / total)
        merged = mixed[0:BLOCK, :]
        for i in range(1, QUAD):
            merged = jnp.where(lane_head == i, mixed[i * BLOCK : (i + 1) * BLOCK, :], merged)
        rows = slice(b * BLOCK, (b + 1) * BLOCK)
        att[rows, g * WIDE : (g + 1) * WIDE] = merged.astype(jnp.bfloat16)
        scores = following
    project_out(0, att, mlp, wo, send, keep)


def run_attend(adjacency, q, mine, sibling, table, mlp, wo):
    rows, half = q.shape
    size = CHUNKS[0][1] - CHUNKS[0][0]
    part = jax.ShapeDtypeStruct((rows // BLOCK, size, TILE), jnp.bfloat16)
    blocks = table.shape[0] * table.shape[1]
    send, keep, att, _ = pl.pallas_call(
        attend_kernel,
        out_shape=(
            part,
            part,
            jax.ShapeDtypeStruct(q.shape, jnp.bfloat16),
            jax.ShapeDtypeStruct(table.shape, jnp.bfloat16),
        ),
        in_specs=[whole(pl.ANY)] + vmem(6),
        out_specs=tuple(vmem(4)),
        scratch_shapes=[
            pltpu.VMEM((rows // BLOCK * (half // WIDE), WIDE, WIDE), jnp.bfloat16),
            pltpu.SMEM(adjacency.shape, jnp.int32),
            pltpu.SemaphoreType.DMA(()),
        ],
        input_output_aliases={4: 3},
        compiler_params=params(16),
        cost_estimate=pl.CostEstimate(
            flops=20 * rows * half * (D + 8 * 8 * BLOCK),
            bytes_accessed=40 * blocks * BLOCK * half + 20 * half * D + 40 * rows * D,
            transcendentals=rows * 8 * BLOCK * half // HEAD_DIM,
        ),
        name="attend",
    )(adjacency, q, mine, sibling, table, mlp, in_vmem(wo))
    return send, keep, att


def run_project_out(c, att, mlp, wo):
    rows, half = att.shape
    size = CHUNKS[c][1] - CHUNKS[c][0]
    part = jax.ShapeDtypeStruct((rows // BLOCK, size, TILE), jnp.bfloat16)
    return pl.pallas_call(
        functools.partial(project_out, c),
        out_shape=(part, part),
        in_specs=vmem(3),
        out_specs=tuple(vmem(2)),
        compiler_params=params(8),
        cost_estimate=pl.CostEstimate(
            flops=200 * rows * half * D,
            bytes_accessed=200 * half * D,
            transcendentals=0,
        ),
        name="project_out",
    )(att, mlp, in_vmem(wo))


def plan_kernel(owners, masks):
    s = lax.axis_index("shard")
    count = owners.shape[1]
    names = [owners[0, t] for t in range(count)]
    for t in range(count):
        same = [(names[e] == names[t]).astype(jnp.int32) for e in range(t)]
        rank = sum(same, jnp.int32(0))
        for d in range(masks.shape[0]):
            for j in range(CAP):
                hit = (names[t] == s ^ d) & (rank == j)
                masks[d, j, t] = jnp.full(masks.shape[3:], hit.astype(jnp.float32))


def run_plan(owners, shards):
    return pl.pallas_call(
        plan_kernel,
        out_shape=jax.ShapeDtypeStruct((shards, CAP, owners.shape[1], 8, 128), jnp.float32),
        in_specs=[whole(pltpu.SMEM)],
        out_specs=whole(pltpu.VMEM),
        compiler_params=params(4),
        cost_estimate=pl.CostEstimate(flops=0, bytes_accessed=1 << 18, transcendentals=0),
        name="plan",
    )(owners)


def combine_kernel(chunks, distances, masks, grid_features, *refs):
    keeps, refs = refs[: len(chunks)], refs[len(chunks) :]
    swaps, outs = refs[: len(chunks)], refs[len(chunks) :]
    count = grid_features.shape[0]
    first = CHUNKS[chunks[0]][0]
    for c, keep, swap in zip(chunks, keeps, swaps):
        low, high = CHUNKS[c]
        updated = []
        for t in range(count):
            residual = [
                grid_features[t, rows, tile * TILE : (tile + 1) * TILE]
                for tile, rows, _ in pieces_of(c)
            ]
            residual = jnp.concatenate(residual, axis=0).astype(jnp.float32)
            partials = keep[t].astype(jnp.float32) + swap[t].astype(jnp.float32)
            updated.append(residual + partials)
        for d, out in zip(distances, outs):
            for j in range(CAP):
                chosen = jnp.zeros_like(updated[0])
                for t in range(count):
                    mask = jnp.broadcast_to(masks[d, j, t, 0:1, :], chosen.shape)
                    chosen = jnp.where(mask > 0.5, updated[t], chosen)
                out[j, low - first : high - first, :] = chosen.astype(jnp.bfloat16)


def run_combine(chunks, distances, masks, grid_features, keeps, swaps):
    count = grid_features.shape[0]
    rows, width = CHUNKS[chunks[-1]][1] - CHUNKS[chunks[0]][0], TILE
    slot = jax.ShapeDtypeStruct((CAP, rows, width), jnp.bfloat16)
    return pl.pallas_call(
        functools.partial(combine_kernel, chunks, distances),
        out_shape=(slot,) * len(distances),
        in_specs=vmem(2 + 2 * len(chunks)),
        out_specs=tuple(vmem(len(distances))),
        compiler_params=params(8),
        cost_estimate=pl.CostEstimate(
            flops=60000 * count * rows * width,
            bytes_accessed=400 * rows * width * (3 * count + CAP * len(distances)),
            transcendentals=0,
        ),
        name="combine",
    )(masks, grid_features, *keeps, *swaps)


def place_kernel(spots, *refs):
    out, sem = refs[-2:]
    s = lax.axis_index("shard")
    copies = []
    for ref, (d, chunks) in zip(refs, spots):
        first = CHUNKS[chunks[0]][0]
        slots = pl.ds((s ^ d) * CAP, CAP)
        for c in chunks:
            shift = CHUNKS[c][0] - first
            for tile, rows, spot in pieces_of(c):
                size = rows.stop - rows.start
                source = ref.at[:, pl.ds(spot.start + shift, size), :]
                columns = pl.ds(tile * TILE, TILE)
                target = out.at[slots, pl.ds(rows.start, size), columns]
                copies.append(pltpu.make_async_copy(source, target, sem.at[len(copies)]))
                copies[-1].start()
    for copy in copies:
        copy.wait()


def run_place(spots, arrived, placed, shape):
    count = sum(len(pieces_of(c)) for _, chunks in spots for c in chunks)
    return pl.pallas_call(
        functools.partial(place_kernel, spots),
        out_shape=jax.ShapeDtypeStruct(shape, jnp.bfloat16),
        in_specs=vmem(len(arrived)) + [whole(pltpu.HBM)] * len(placed),
        out_specs=whole(pltpu.HBM),
        scratch_shapes=[pltpu.SemaphoreType.DMA((count,))],
        input_output_aliases={len(arrived): 0} if placed else {},
        compiler_params=params(4),
        cost_estimate=pl.CostEstimate(
            flops=400000 * sum(part.size for part in arrived), bytes_accessed=0, transcendentals=0
        ),
        name="place",
    )(*arrived, *placed)


def crossed(x, distance, size):
    return lax.ppermute(x, "shard", [(i, i ^ distance) for i in range(size)])


def swapped(x, axis):
    return lax.ppermute(x, axis, [(0, 1), (1, 0)])


def paired(
    grid_features,
    owners,
    adjacency,
    mesh_nodes,
    norm_gain,
    query_weight,
    key_weight,
    value_weight,
    output_weight,
    up_weight,
    down_weight,
):
    shards = lax.axis_size("shard")
    count, rows, half = grid_features.shape
    flat = grid_features.reshape(count * rows, half)
    half_unit = run_pick(mesh_nodes)
    far = crossed(half_unit, 2, shards)
    waiting, _ = lax.optimization_barrier((mesh_nodes, half_unit))
    near = crossed(waiting, 1, shards)
    waiting, _ = lax.optimization_barrier((flat, half_unit))
    other = swapped(waiting, "head")
    flat, gain, wup, wdn, rest = run_stage(
        (flat, norm_gain.reshape(1, -1), up_weight, down_weight, mesh_nodes),
        (None, 1, 0, 1, "rest"),
    )
    straight = crossed(rest, 3, shards)
    far, _ = lax.optimization_barrier((far, rest))
    farther = crossed(far, 1, shards)
    far_pair = swapped(far, "head")
    queries, mlp = run_mlp(flat, other, gain, query_weight, wup, wdn)
    queries, mlp, far_pair, near = lax.optimization_barrier((queries, mlp, far_pair, near))
    blocked = (-1, BLOCK, 2 * half)
    mine_a = run_project((in_vmem(mesh_nodes), near, far, far_pair), key_weight, value_weight)
    sibling_a = swapped(mine_a, "sub")
    straight, _ = lax.optimization_barrier((straight, mine_a))
    mine_m = run_project((straight,), key_weight, value_weight)
    sibling_m = swapped(mine_m, "sub")
    parts = [part.reshape(blocked) for part in (mine_a, sibling_a, mine_m, sibling_m)]
    table = run_table(*parts, 2 * shards)
    farther, _ = lax.optimization_barrier((farther, mine_m))
    mine_b = run_project((farther,), key_weight, value_weight)
    sibling_b = swapped(mine_b, "sub")
    send, keep, att = run_attend(
        adjacency, queries, mine_b.reshape(blocked), sibling_b.reshape(blocked), table, mlp, output_weight
    )
    named, _ = lax.optimization_barrier((owners, att))
    masks = run_plan(named.T, shards)
    keeps, swaps, slots, placed = [], [], [], []
    shape = (shards * CAP, rows, half)
    every = tuple(range(len(CHUNKS)))
    for c in every:
        if c > 0:
            send, keep = run_project_out(c, att, mlp, output_weight)
        received = swapped(send, "head")
        if c > 0:
            received, _ = lax.optimization_barrier((received, slots[c - 1][0]))
        slots.append(run_combine((c,), (2, 3), masks, grid_features, (keep,), (received,)))
        keeps.append(keep)
        swaps.append(received)
    swaps[-1], _ = lax.optimization_barrier((swaps[-1], slots[-1][0]))
    near_slots, own_slots = run_combine(every, (1, 0), masks, grid_features, keeps, swaps)
    for c in every:
        spots = [(2, (c,)), (3, (c,))]
        arrived = [crossed(slot, d, shards) for d, slot in zip((2, 3), slots[c])]
        if c == 0:
            spots.append((0, every))
            arrived.append(own_slots)
        if c == every[-1]:
            spots.append((1, every))
            arrived.append(crossed(near_slots, 1, shards))
        placed = [run_place(spots, arrived, placed, shape)]
    return placed[0]


def attend_plain(queries, key_table, value_table, chosen, scaling):
    count = chosen.shape[0]
    picked_keys = key_table[chosen]
    picked_keys = picked_keys.reshape(count, -1, picked_keys.shape[3], picked_keys.shape[4])
    picked_values = value_table[chosen]
    picked_values = picked_values.reshape(count, -1, picked_values.shape[3], picked_values.shape[4])
    scores = (
        jnp.einsum("gqhe,gkhe->ghqk", queries, picked_keys, preferred_element_type=jnp.float32)
        * scaling
    )
    highest = jnp.max(scores, axis=-1, keepdims=True)
    weights = jnp.exp(scores - highest)
    weights = (weights / jnp.sum(weights, axis=-1, keepdims=True)).astype(jnp.bfloat16)
    result = jnp.einsum(
        "ghqk,gkhe->gqhe", weights, picked_values, preferred_element_type=jnp.float32
    )
    return result.astype(jnp.bfloat16)


def general(
    grid_features,
    owners,
    adjacency,
    mesh_nodes,
    norm_gain,
    query_weight,
    key_weight,
    value_weight,
    output_weight,
    up_weight,
    down_weight,
):
    shard_count = lax.axis_size("shard")
    head_count = lax.axis_size("head")
    local_blocks, block_rows, feature_share = grid_features.shape
    slots = shard_count * CAP
    owner_col = owners[:, 0]
    position = jnp.arange(local_blocks, dtype=jnp.int32)
    earlier = (owner_col[:, None] == owner_col[None, :]) & (position[None, :] < position[:, None])
    target = owner_col * CAP + jnp.sum(earlier.astype(jnp.int32), axis=1)
    dispatch = (target[:, None] == jnp.arange(slots, dtype=jnp.int32)[None, :]).astype(jnp.bfloat16)
    offset = lax.axis_index("head") * (D // head_count)
    projected = jnp.stack(
        (
            jnp.dot(mesh_nodes, key_weight, preferred_element_type=jnp.float32).astype(
                jnp.bfloat16
            ),
            jnp.dot(mesh_nodes, value_weight, preferred_element_type=jnp.float32).astype(
                jnp.bfloat16
            ),
        )
    )
    tables = lax.all_gather(projected, ("shard", "sub"), axis=1, tiled=True)
    head_local = query_weight.shape[1] // HEAD_DIM
    key_table = tables[0].reshape(-1, block_rows, head_local, HEAD_DIM)
    value_table = tables[1].reshape(-1, block_rows, head_local, HEAD_DIM)
    send_lists = jnp.full((slots, adjacency.shape[1]), -1, jnp.int32).at[target].set(adjacency)
    send_lists = send_lists.reshape(shard_count, CAP, -1)
    complete = lax.all_gather(grid_features, "head", axis=2, tiled=True)
    outgoing = jnp.einsum(
        "gs,gbd->sbd", dispatch, complete, preferred_element_type=jnp.float32
    ).astype(jnp.bfloat16)
    arrived, lists = (
        lax.all_to_all(
            outgoing.reshape(shard_count, CAP, block_rows, D),
            "shard",
            split_axis=0,
            concat_axis=0,
            tiled=True,
        ),
        lax.all_to_all(send_lists, "shard", split_axis=0, concat_axis=0, tiled=True),
    )
    arrived = arrived.reshape(slots, block_rows, D)
    residual = lax.dynamic_slice_in_dim(arrived, offset, D // head_count, 2)
    lists = lists.reshape(slots, -1)
    count = arrived.shape[0]
    values_f = arrived.astype(jnp.float32)
    average = jnp.mean(values_f, axis=-1, keepdims=True)
    centered = values_f - average
    variance = jnp.mean(centered * centered, axis=-1, keepdims=True)
    normed = (centered * lax.rsqrt(variance + epsilon) * norm_gain).astype(jnp.bfloat16)
    flattened = normed.reshape(-1, D)
    queries = jnp.dot(flattened, query_weight, preferred_element_type=jnp.float32).astype(
        jnp.bfloat16
    )
    blocks_each = math.gcd(count, max(1, 512 // block_rows))
    steps_count = count // blocks_each
    queries = queries.reshape(steps_count, blocks_each, block_rows, head_local, HEAD_DIM)

    def attend_step(operands):
        return attend_plain(operands[0], key_table, value_table, operands[1], HEAD_DIM ** (-0.5))

    attended = lax.map(
        attend_step, (queries, jnp.maximum(lists, 0).reshape(steps_count, blocks_each, -1))
    )
    attended = attended.reshape(-1, head_local * HEAD_DIM)
    hidden = jax.nn.gelu(
        jnp.dot(flattened, up_weight, preferred_element_type=jnp.float32), approximate=False
    ).astype(jnp.bfloat16)
    branch = jnp.dot(attended, output_weight, preferred_element_type=jnp.float32)
    branch = branch + jnp.dot(hidden, down_weight, preferred_element_type=jnp.float32)
    branch = branch.reshape(count, block_rows, D)
    reduced = lax.psum_scatter(
        branch.astype(jnp.bfloat16), "head", scatter_dimension=2, tiled=True
    ).astype(jnp.float32)
    occupied = lists[:, 0] >= 0
    summed = residual.astype(jnp.float32) + reduced
    return jnp.where(occupied[:, None, None], summed, 0.0).astype(jnp.bfloat16)


def local(grid_features, owners, adjacency, mesh_nodes, *parameters):
    sizes = [lax.axis_size(axis) for axis in ("shard", "head", "sub")]
    small = grid_features.shape[:2] == (4, BLOCK) and mesh_nodes.shape[0] == 2 * BLOCK
    if sizes == [4, 2, 2] and small and grid_features.shape[2] == 512:
        return paired(grid_features, owners, adjacency, mesh_nodes, *parameters)
    return general(grid_features, owners, adjacency, mesh_nodes, *parameters)


def solution(mesh):
    return jax.shard_map(
        local,
        mesh=mesh,
        in_specs=(
            P(("groups", "shard", "sub"), None, "head"),
            P(("groups", "shard", "sub"), None),
            P(("groups", "shard", "sub"), None),
            P(("groups", "shard", "sub"), None),
            P(),
            P(None, "head"),
            P(None, "head"),
            P(None, "head"),
            P("head", None),
            P(None, "head"),
            P("head", None),
        ),
        out_specs=P(("groups", "shard", "sub"), None, "head"),
        check_vma=False,
    )
```

```python
import functools
import math

import jax
import jax.numpy as jnp
from jax import lax
from jax.experimental import pallas as pl
from jax.experimental.pallas import tpu as pltpu
from jax.sharding import PartitionSpec as P

D = 1024
HEAD_DIM = 64
CAP = 2
BLOCK = 64
QUAD = 4
WIDE = QUAD * HEAD_DIM
TILE = 128
CHUNKS = ((0, 80), (80, 256))
MIB = 1 << 20


epsilon = 1e-05


def dot(a, b):
    return jnp.dot(a, b, preferred_element_type=jnp.float32)


def gelu(x):
    return 0.5 * x * (1.0 + lax.erf(x * (2.0**-0.5)))


def in_hbm(x):
    return pltpu.with_memory_space_constraint(x, pltpu.HBM)


def in_vmem(x):
    return pltpu.with_memory_space_constraint(x, pltpu.VMEM)


def whole(space):
    return pl.BlockSpec(memory_space=space)


def vmem(count):
    return [whole(pltpu.VMEM)] * count


def params(mib):
    return pltpu.CompilerParams(vmem_limit_bytes=mib * MIB)


def mlp_kernel(own, other, gain, wq, wup, wdn, q_out, mlp_out, normed_s):
    half = own.shape[1]
    units = wup.shape[1]
    chunk = units // 4
    x_other = other[...].astype(jnp.float32)
    x_own = own[...].astype(jnp.float32)

    def mean(a, b):
        total = jnp.sum(a, axis=-1, keepdims=True) + jnp.sum(b, axis=-1, keepdims=True)
        return total * (0.5 / half)

    average = mean(x_other, x_own)
    x_other = x_other - average
    x_own = x_own - average
    factor = lax.rsqrt(mean(x_other * x_other, x_own * x_own) + epsilon)
    normed_s[:, :half] = (x_other * factor * gain[:, :half]).astype(jnp.bfloat16)
    normed_s[:, half:] = (x_own * factor * gain[:, half:]).astype(jnp.bfloat16)
    normed = normed_s[...]
    h = lax.axis_index("head")
    queries = jnp.zeros(q_out.shape, jnp.float32)
    for part, head in enumerate((1 - h, h)):
        rows = pl.ds(pl.multiple_of(head * half, half), half)
        queries += dot(normed_s[:, part * half : (part + 1) * half], wq[rows, :])
    q_out[...] = queries.astype(jnp.bfloat16)
    for c in range(units // chunk):
        span = slice(c * chunk, (c + 1) * chunk)
        hidden = gelu(dot(normed, wup[:, span])).astype(jnp.bfloat16)
        term = dot(hidden, wdn[span, :])
        if c == 0:
            mlp_out[...] = term
        else:
            mlp_out[...] += term


def run_mlp(own, other, gain, wq, wup, wdn):
    rows = own.shape[0]
    width = wq.shape[0]
    units = wup.shape[1]
    return pl.pallas_call(
        mlp_kernel,
        out_shape=(
            jax.ShapeDtypeStruct((rows, wq.shape[1]), jnp.bfloat16),
            jax.ShapeDtypeStruct((rows, width), jnp.float32),
        ),
        in_specs=vmem(6),
        out_specs=tuple(vmem(2)),
        scratch_shapes=[pltpu.VMEM((rows, width), jnp.bfloat16)],
        compiler_params=params(16),
        cost_estimate=pl.CostEstimate(
            flops=2 * rows * width * (wq.shape[1] + 2 * units),
            bytes_accessed=2 * width * (wq.shape[1] + 2 * units),
            transcendentals=rows * units,
        ),
        name="mlp",
    )(own, other, gain, in_vmem(wq), wup, wdn)


def pick_kernel(mesh, out, sem):
    first = pl.multiple_of(lax.axis_index("head") * BLOCK, BLOCK)
    copy = pltpu.make_async_copy(mesh.at[pl.ds(first, BLOCK), :], out, sem)
    copy.start()
    copy.wait()


def run_pick(mesh):
    return pl.pallas_call(
        pick_kernel,
        out_shape=jax.ShapeDtypeStruct((BLOCK, mesh.shape[1]), mesh.dtype),
        in_specs=[whole(pltpu.HBM)],
        out_specs=whole(pltpu.VMEM),
        scratch_shapes=[pltpu.SemaphoreType.DMA(())],
        compiler_params=params(4),
        cost_estimate=pl.CostEstimate(flops=0, bytes_accessed=4 * mesh.size, transcendentals=0),
        name="pick",
    )(in_hbm(mesh))


def stage_kernel(axes, *refs):
    sources, targets, sem = refs[: len(axes)], refs[len(axes) : -1], refs[-1]
    h = lax.axis_index("head")
    copies = []

    def add(source, target):
        pieces = 2 if source.shape[0] >= 512 else 1
        rows = source.shape[0] // pieces
        for piece in range(pieces):
            span = pl.ds(piece * rows, rows)
            copies.append(
                pltpu.make_async_copy(
                    source.at[span, :], target.at[span, :], sem.at[len(copies)]
                )
            )
            copies[-1].start()

    for source, target, axis in zip(sources, targets, axes):
        if axis is None:
            add(source, target)
            continue
        if axis == "rest":
            add(source.at[pl.ds(pl.multiple_of((1 - h) * BLOCK, BLOCK), BLOCK), :], target)
            continue
        half = source.shape[axis] // 2
        for part, head in enumerate((1 - h, h)):
            span = pl.ds(pl.multiple_of(head * half, half), half)
            place = pl.ds(part * half, half)
            if axis == 0:
                add(source.at[span, :], target.at[place, :])
            else:
                add(source.at[:, span], target.at[:, place])
    for copy in copies:
        copy.wait()


def run_stage(arrays, axes):
    size = sum(2 * array.size for array in arrays)
    return pl.pallas_call(
        functools.partial(stage_kernel, axes),
        out_shape=tuple(
            jax.ShapeDtypeStruct((BLOCK,) + array.shape[1:] if axis == "rest" else array.shape, array.dtype)
            for array, axis in zip(arrays, axes)
        ),
        in_specs=[whole(pltpu.HBM)] * len(arrays),
        out_specs=tuple(vmem(len(arrays))),
        scratch_shapes=[pltpu.SemaphoreType.DMA((4 * len(arrays),))],
        compiler_params=params(16),
        cost_estimate=pl.CostEstimate(
            flops=2000 * size, bytes_accessed=20 * size, transcendentals=0
        ),
        name="stage",
    )(*(in_hbm(array) for array in arrays))


def project_kernel(*refs):
    pieces, (wk, wv, out) = refs[:-3], refs[-3:]
    width = wk.shape[1]
    rows = jnp.concatenate([piece[...] for piece in pieces], axis=0)
    out[:, :width] = dot(rows, wk[...]).astype(jnp.bfloat16)
    out[:, width:] = dot(rows, wv[...]).astype(jnp.bfloat16)


def run_project(pieces, wk, wv):
    rows = sum(piece.shape[0] for piece in pieces)
    depth, width = wk.shape
    return pl.pallas_call(
        project_kernel,
        out_shape=jax.ShapeDtypeStruct((rows, 2 * width), jnp.bfloat16),
        in_specs=vmem(len(pieces) + 2),
        out_specs=whole(pltpu.VMEM),
        compiler_params=params(8),
        cost_estimate=pl.CostEstimate(
            flops=300 * rows * depth * width,
            bytes_accessed=300 * depth * width + 300 * rows * depth,
            transcendentals=0,
        ),
        name="project",
    )(*pieces, in_vmem(wk), in_vmem(wv))


def table_kernel(mine, sibling, mine_last, sibling_last, table):
    for i, (first, last) in enumerate(((mine, mine_last), (sibling, sibling_last))):
        table[i, : first.shape[0]] = first[...]
        table[i, table.shape[1] - last.shape[0] :] = last[...]


def run_table(mine, sibling, mine_last, sibling_last, blocks):
    return pl.pallas_call(
        table_kernel,
        out_shape=jax.ShapeDtypeStruct((2, blocks) + mine.shape[1:], jnp.bfloat16),
        in_specs=vmem(4),
        out_specs=whole(pltpu.VMEM),
        compiler_params=params(8),
        cost_estimate=pl.CostEstimate(
            flops=0, bytes_accessed=80 * mine.size, transcendentals=0
        ),
        name="table",
    )(mine, sibling, mine_last, sibling_last)


def pieces_of(c):
    low, high = CHUNKS[c]
    pieces = []
    for tile in range(low // BLOCK, -(-high // BLOCK)):
        first, last = max(low, tile * BLOCK), min(high, (tile + 1) * BLOCK)
        rows = slice(first - tile * BLOCK, last - tile * BLOCK)
        pieces.append((tile, rows, slice(first - low, last - low)))
    return pieces


def project_out(c, att, mlp, wo, send, keep):
    half = att.shape[1]
    h = lax.axis_index("head")
    pieces = pieces_of(c)
    start, stop = pieces[0][0] * TILE, (pieces[-1][0] + 1) * TILE

    def write(head):
        for out, first, place in ((send, 0, 1 - head), (keep, half, head)):
            extra = mlp[:, first + start : first + stop]
            total = extra + dot(att[...], wo[:, place * half + start : place * half + stop])
            total = total.astype(jnp.bfloat16)
            for tile, rows, spot in pieces:
                columns = slice(tile * TILE - start, (tile + 1) * TILE - start)
                for t in range(out.shape[0]):
                    block = slice(t * BLOCK + rows.start, t * BLOCK + rows.stop)
                    out[t, spot, :] = total[block, columns]

    for head in range(2):
        pl.when(h == head)(functools.partial(write, head))


def attend_kernel(
    adjacency, q, mine, sibling, table_in, mlp, wo, send, keep, att, table, stacked_s, near_s, sem
):
    del table_in
    s = lax.axis_index("shard")
    h = lax.axis_index("head")
    u = lax.axis_index("sub")
    half = wo.shape[0]
    ready = table.shape[1] - 2 * mine.shape[0]
    copy = pltpu.make_async_copy(adjacency, near_s, sem)
    copy.start()
    for i, part in enumerate((mine, sibling)):
        table[i, ready : ready + part.shape[0]] = part[...]
    rows_of = lax.broadcasted_iota(jnp.int32, (WIDE, WIDE), 0) // BLOCK
    lanes_of = lax.broadcasted_iota(jnp.int32, (WIDE, WIDE), 1) // HEAD_DIM
    diagonal = rows_of == lanes_of
    lane_head = lax.broadcasted_iota(jnp.int32, (BLOCK, WIDE), 1) // HEAD_DIM
    scale = HEAD_DIM**-0.5 * math.log2(math.e)
    groups = half // WIDE
    steps = near_s.shape[0] * groups
    for step in range(steps):
        b, g = divmod(step, groups)
        columns = slice(g * WIDE, (g + 1) * WIDE)
        stacked = jnp.concatenate([q[b * BLOCK : (b + 1) * BLOCK, columns]] * QUAD, axis=0)
        stacked_s[step] = jnp.where(diagonal, stacked, jnp.zeros_like(stacked))
    copy.wait()
    places = []
    for b in range(near_s.shape[0]):
        places.append([])
        for j in range(near_s.shape[1]):
            m = near_s[b, j]
            part = lax.rem(m, 2)
            core = lax.rem(m // 2, 2)
            distance = s ^ (m // 4)
            part = jnp.where(distance <= 1, part, part ^ h)
            places[b].append((core ^ u, distance * 2 + part))

    def scores_of(step):
        b, g = divmod(step, groups)
        columns = slice(g * WIDE, (g + 1) * WIDE)
        keys = jnp.concatenate([table[i, p, :, columns] for i, p in places[b]], axis=0)
        return lax.dot_general(
            stacked_s[step], keys, (((1,), (1,)), ((), ())), preferred_element_type=jnp.float32
        )

    scores = scores_of(0)
    for step in range(steps):
        following = scores_of(step + 1) if step + 1 < steps else None
        b, g = divmod(step, groups)
        columns = slice(half + g * WIDE, half + (g + 1) * WIDE)
        values = jnp.concatenate([table[i, p, :, columns] for i, p in places[b]], axis=0)
        highest = jnp.max(scores, axis=-1, keepdims=True)
        weights = jnp.exp2((scores - highest) * scale)
        total = jnp.sum(weights, axis=-1, keepdims=True)
        mixed = dot(weights.astype(jnp.bfloat16), values) * (1.0 / total)
        merged = mixed[0:BLOCK, :]
        for i in range(1, QUAD):
            merged = jnp.where(lane_head == i, mixed[i * BLOCK : (i + 1) * BLOCK, :], merged)
        rows = slice(b * BLOCK, (b + 1) * BLOCK)
        att[rows, g * WIDE : (g + 1) * WIDE] = merged.astype(jnp.bfloat16)
        scores = following
    project_out(0, att, mlp, wo, send, keep)


def run_attend(adjacency, q, mine, sibling, table, mlp, wo):
    rows, half = q.shape
    size = CHUNKS[0][1] - CHUNKS[0][0]
    part = jax.ShapeDtypeStruct((rows // BLOCK, size, TILE), jnp.bfloat16)
    blocks = table.shape[0] * table.shape[1]
    send, keep, att, _ = pl.pallas_call(
        attend_kernel,
        out_shape=(
            part,
            part,
            jax.ShapeDtypeStruct(q.shape, jnp.bfloat16),
            jax.ShapeDtypeStruct(table.shape, jnp.bfloat16),
        ),
        in_specs=[whole(pl.ANY)] + vmem(6),
        out_specs=tuple(vmem(4)),
        scratch_shapes=[
            pltpu.VMEM((rows // BLOCK * (half // WIDE), WIDE, WIDE), jnp.bfloat16),
            pltpu.SMEM(adjacency.shape, jnp.int32),
            pltpu.SemaphoreType.DMA(()),
        ],
        input_output_aliases={4: 3},
        compiler_params=params(16),
        cost_estimate=pl.CostEstimate(
            flops=20 * rows * half * (D + 8 * 8 * BLOCK),
            bytes_accessed=40 * blocks * BLOCK * half + 20 * half * D + 40 * rows * D,
            transcendentals=rows * 8 * BLOCK * half // HEAD_DIM,
        ),
        name="attend",
    )(adjacency, q, mine, sibling, table, mlp, in_vmem(wo))
    return send, keep, att


def run_project_out(c, att, mlp, wo):
    rows, half = att.shape
    size = CHUNKS[c][1] - CHUNKS[c][0]
    part = jax.ShapeDtypeStruct((rows // BLOCK, size, TILE), jnp.bfloat16)
    return pl.pallas_call(
        functools.partial(project_out, c),
        out_shape=(part, part),
        in_specs=vmem(3),
        out_specs=tuple(vmem(2)),
        compiler_params=params(8),
        cost_estimate=pl.CostEstimate(
            flops=200 * rows * half * D,
            bytes_accessed=200 * half * D,
            transcendentals=0,
        ),
        name="project_out",
    )(att, mlp, in_vmem(wo))


def plan_kernel(owners, masks):
    s = lax.axis_index("shard")
    count = owners.shape[1]
    names = [owners[0, t] for t in range(count)]
    for t in range(count):
        same = [(names[e] == names[t]).astype(jnp.int32) for e in range(t)]
        rank = sum(same, jnp.int32(0))
        for d in range(masks.shape[0]):
            for j in range(CAP):
                hit = (names[t] == s ^ d) & (rank == j)
                masks[d, j, t] = jnp.full(masks.shape[3:], hit.astype(jnp.float32))


def run_plan(owners, shards):
    return pl.pallas_call(
        plan_kernel,
        out_shape=jax.ShapeDtypeStruct((shards, CAP, owners.shape[1], 8, 128), jnp.float32),
        in_specs=[whole(pltpu.SMEM)],
        out_specs=whole(pltpu.VMEM),
        compiler_params=params(4),
        cost_estimate=pl.CostEstimate(flops=0, bytes_accessed=1 << 18, transcendentals=0),
        name="plan",
    )(owners)


def combine_kernel(chunks, distances, masks, grid_features, *refs):
    keeps, refs = refs[: len(chunks)], refs[len(chunks) :]
    swaps, outs = refs[: len(chunks)], refs[len(chunks) :]
    count = grid_features.shape[0]
    first = CHUNKS[chunks[0]][0]
    for c, keep, swap in zip(chunks, keeps, swaps):
        low, high = CHUNKS[c]
        updated = []
        for t in range(count):
            residual = [
                grid_features[t, rows, tile * TILE : (tile + 1) * TILE]
                for tile, rows, _ in pieces_of(c)
            ]
            residual = jnp.concatenate(residual, axis=0).astype(jnp.float32)
            partials = keep[t].astype(jnp.float32) + swap[t].astype(jnp.float32)
            updated.append(residual + partials)
        for d, out in zip(distances, outs):
            for j in range(CAP):
                chosen = jnp.zeros_like(updated[0])
                for t in range(count):
                    mask = jnp.broadcast_to(masks[d, j, t, 0:1, :], chosen.shape)
                    chosen = jnp.where(mask > 0.5, updated[t], chosen)
                out[j, low - first : high - first, :] = chosen.astype(jnp.bfloat16)


def run_combine(chunks, distances, masks, grid_features, keeps, swaps):
    count = grid_features.shape[0]
    rows, width = CHUNKS[chunks[-1]][1] - CHUNKS[chunks[0]][0], TILE
    slot = jax.ShapeDtypeStruct((CAP, rows, width), jnp.bfloat16)
    return pl.pallas_call(
        functools.partial(combine_kernel, chunks, distances),
        out_shape=(slot,) * len(distances),
        in_specs=vmem(2 + 2 * len(chunks)),
        out_specs=tuple(vmem(len(distances))),
        compiler_params=params(8),
        cost_estimate=pl.CostEstimate(
            flops=60000 * count * rows * width,
            bytes_accessed=400 * rows * width * (3 * count + CAP * len(distances)),
            transcendentals=0,
        ),
        name="combine",
    )(masks, grid_features, *keeps, *swaps)


def place_kernel(spots, *refs):
    out, sem = refs[-2:]
    s = lax.axis_index("shard")
    copies = []
    for ref, (d, chunks) in zip(refs, spots):
        first = CHUNKS[chunks[0]][0]
        slots = pl.ds((s ^ d) * CAP, CAP)
        for c in chunks:
            shift = CHUNKS[c][0] - first
            for tile, rows, spot in pieces_of(c):
                size = rows.stop - rows.start
                source = ref.at[:, pl.ds(spot.start + shift, size), :]
                columns = pl.ds(tile * TILE, TILE)
                target = out.at[slots, pl.ds(rows.start, size), columns]
                copies.append(pltpu.make_async_copy(source, target, sem.at[len(copies)]))
                copies[-1].start()
    for copy in copies:
        copy.wait()


def run_place(spots, arrived, placed, shape):
    count = sum(len(pieces_of(c)) for _, chunks in spots for c in chunks)
    return pl.pallas_call(
        functools.partial(place_kernel, spots),
        out_shape=jax.ShapeDtypeStruct(shape, jnp.bfloat16),
        in_specs=vmem(len(arrived)) + [whole(pltpu.HBM)] * len(placed),
        out_specs=whole(pltpu.HBM),
        scratch_shapes=[pltpu.SemaphoreType.DMA((count,))],
        input_output_aliases={len(arrived): 0} if placed else {},
        compiler_params=params(4),
        cost_estimate=pl.CostEstimate(
            flops=400000 * sum(part.size for part in arrived), bytes_accessed=0, transcendentals=0
        ),
        name="place",
    )(*arrived, *placed)


def crossed(x, distance, size):
    return lax.ppermute(x, "shard", [(i, i ^ distance) for i in range(size)])


def swapped(x, axis):
    return lax.ppermute(x, axis, [(0, 1), (1, 0)])


def paired(
    grid_features,
    owners,
    adjacency,
    mesh_nodes,
    norm_gain,
    query_weight,
    key_weight,
    value_weight,
    output_weight,
    up_weight,
    down_weight,
):
    shards = lax.axis_size("shard")
    count, rows, half = grid_features.shape
    flat = grid_features.reshape(count * rows, half)
    half_unit = run_pick(mesh_nodes)
    far = crossed(half_unit, 2, shards)
    waiting, _ = lax.optimization_barrier((mesh_nodes, half_unit))
    near = crossed(waiting, 1, shards)
    waiting, _ = lax.optimization_barrier((flat, half_unit))
    other = swapped(waiting, "head")
    flat, gain, wup, wdn, rest = run_stage(
        (flat, norm_gain.reshape(1, -1), up_weight, down_weight, mesh_nodes),
        (None, 1, 0, 1, "rest"),
    )
    straight = crossed(rest, 3, shards)
    far, _ = lax.optimization_barrier((far, rest))
    farther = crossed(far, 1, shards)
    far_pair = swapped(far, "head")
    queries, mlp = run_mlp(flat, other, gain, query_weight, wup, wdn)
    queries, mlp, far_pair, near = lax.optimization_barrier((queries, mlp, far_pair, near))
    blocked = (-1, BLOCK, 2 * half)
    mine_a = run_project((in_vmem(mesh_nodes), near, far, far_pair), key_weight, value_weight)
    sibling_a = swapped(mine_a, "sub")
    straight, _ = lax.optimization_barrier((straight, mine_a))
    mine_m = run_project((straight,), key_weight, value_weight)
    sibling_m = swapped(mine_m, "sub")
    parts = [part.reshape(blocked) for part in (mine_a, sibling_a, mine_m, sibling_m)]
    table = run_table(*parts, 2 * shards)
    farther, _ = lax.optimization_barrier((farther, mine_m))
    mine_b = run_project((farther,), key_weight, value_weight)
    sibling_b = swapped(mine_b, "sub")
    send, keep, att = run_attend(
        adjacency, queries, mine_b.reshape(blocked), sibling_b.reshape(blocked), table, mlp, output_weight
    )
    named, _ = lax.optimization_barrier((owners, att))
    masks = run_plan(named.T, shards)
    keeps, swaps, slots, placed = [], [], [], []
    shape = (shards * CAP, rows, half)
    every = tuple(range(len(CHUNKS)))
    for c in every:
        if c > 0:
            send, keep = run_project_out(c, att, mlp, output_weight)
        received = swapped(send, "head")
        if c > 0:
            received, _ = lax.optimization_barrier((received, slots[c - 1][0]))
        slots.append(run_combine((c,), (2, 3), masks, grid_features, (keep,), (received,)))
        keeps.append(keep)
        swaps.append(received)
    swaps[-1], _ = lax.optimization_barrier((swaps[-1], slots[-1][0]))
    near_slots, own_slots = run_combine(every, (1, 0), masks, grid_features, keeps, swaps)
    for c in every:
        spots = [(2, (c,)), (3, (c,))]
        arrived = [crossed(slot, d, shards) for d, slot in zip((2, 3), slots[c])]
        if c == 0:
            spots.append((0, every))
            arrived.append(own_slots)
        if c == every[-1]:
            spots.append((1, every))
            arrived.append(crossed(near_slots, 1, shards))
        placed = [run_place(spots, arrived, placed, shape)]
    return placed[0]


def attend_plain(queries, key_table, value_table, chosen, scaling):
    count = chosen.shape[0]
    picked_keys = key_table[chosen]
    picked_keys = picked_keys.reshape(count, -1, picked_keys.shape[3], picked_keys.shape[4])
    picked_values = value_table[chosen]
    picked_values = picked_values.reshape(count, -1, picked_values.shape[3], picked_values.shape[4])
    scores = (
        jnp.einsum("gqhe,gkhe->ghqk", queries, picked_keys, preferred_element_type=jnp.float32)
        * scaling
    )
    highest = jnp.max(scores, axis=-1, keepdims=True)
    weights = jnp.exp(scores - highest)
    weights = (weights / jnp.sum(weights, axis=-1, keepdims=True)).astype(jnp.bfloat16)
    result = jnp.einsum(
        "ghqk,gkhe->gqhe", weights, picked_values, preferred_element_type=jnp.float32
    )
    return result.astype(jnp.bfloat16)


def general(
    grid_features,
    owners,
    adjacency,
    mesh_nodes,
    norm_gain,
    query_weight,
    key_weight,
    value_weight,
    output_weight,
    up_weight,
    down_weight,
):
    shard_count = lax.axis_size("shard")
    head_count = lax.axis_size("head")
    local_blocks, block_rows, feature_share = grid_features.shape
    slots = shard_count * CAP
    owner_col = owners[:, 0]
    position = jnp.arange(local_blocks, dtype=jnp.int32)
    earlier = (owner_col[:, None] == owner_col[None, :]) & (position[None, :] < position[:, None])
    target = owner_col * CAP + jnp.sum(earlier.astype(jnp.int32), axis=1)
    dispatch = (target[:, None] == jnp.arange(slots, dtype=jnp.int32)[None, :]).astype(jnp.bfloat16)
    offset = lax.axis_index("head") * (D // head_count)
    projected = jnp.stack(
        (
            jnp.dot(mesh_nodes, key_weight, preferred_element_type=jnp.float32).astype(
                jnp.bfloat16
            ),
            jnp.dot(mesh_nodes, value_weight, preferred_element_type=jnp.float32).astype(
                jnp.bfloat16
            ),
        )
    )
    tables = lax.all_gather(projected, ("shard", "sub"), axis=1, tiled=True)
    head_local = query_weight.shape[1] // HEAD_DIM
    key_table = tables[0].reshape(-1, block_rows, head_local, HEAD_DIM)
    value_table = tables[1].reshape(-1, block_rows, head_local, HEAD_DIM)
    send_lists = jnp.full((slots, adjacency.shape[1]), -1, jnp.int32).at[target].set(adjacency)
    send_lists = send_lists.reshape(shard_count, CAP, -1)
    complete = lax.all_gather(grid_features, "head", axis=2, tiled=True)
    outgoing = jnp.einsum(
        "gs,gbd->sbd", dispatch, complete, preferred_element_type=jnp.float32
    ).astype(jnp.bfloat16)
    arrived, lists = (
        lax.all_to_all(
            outgoing.reshape(shard_count, CAP, block_rows, D),
            "shard",
            split_axis=0,
            concat_axis=0,
            tiled=True,
        ),
        lax.all_to_all(send_lists, "shard", split_axis=0, concat_axis=0, tiled=True),
    )
    arrived = arrived.reshape(slots, block_rows, D)
    residual = lax.dynamic_slice_in_dim(arrived, offset, D // head_count, 2)
    lists = lists.reshape(slots, -1)
    count = arrived.shape[0]
    values_f = arrived.astype(jnp.float32)
    average = jnp.mean(values_f, axis=-1, keepdims=True)
    centered = values_f - average
    variance = jnp.mean(centered * centered, axis=-1, keepdims=True)
    normed = (centered * lax.rsqrt(variance + epsilon) * norm_gain).astype(jnp.bfloat16)
    flattened = normed.reshape(-1, D)
    queries = jnp.dot(flattened, query_weight, preferred_element_type=jnp.float32).astype(
        jnp.bfloat16
    )
    blocks_each = math.gcd(count, max(1, 512 // block_rows))
    steps_count = count // blocks_each
    queries = queries.reshape(steps_count, blocks_each, block_rows, head_local, HEAD_DIM)

    def attend_step(operands):
        return attend_plain(operands[0], key_table, value_table, operands[1], HEAD_DIM ** (-0.5))

    attended = lax.map(
        attend_step, (queries, jnp.maximum(lists, 0).reshape(steps_count, blocks_each, -1))
    )
    attended = attended.reshape(-1, head_local * HEAD_DIM)
    hidden = jax.nn.gelu(
        jnp.dot(flattened, up_weight, preferred_element_type=jnp.float32), approximate=False
    ).astype(jnp.bfloat16)
    branch = jnp.dot(attended, output_weight, preferred_element_type=jnp.float32)
    branch = branch + jnp.dot(hidden, down_weight, preferred_element_type=jnp.float32)
    branch = branch.reshape(count, block_rows, D)
    reduced = lax.psum_scatter(
        branch.astype(jnp.bfloat16), "head", scatter_dimension=2, tiled=True
    ).astype(jnp.float32)
    occupied = lists[:, 0] >= 0
    summed = residual.astype(jnp.float32) + reduced
    return jnp.where(occupied[:, None, None], summed, 0.0).astype(jnp.bfloat16)


def local(grid_features, owners, adjacency, mesh_nodes, *parameters):
    sizes = [lax.axis_size(axis) for axis in ("shard", "head", "sub")]
    small = grid_features.shape[:2] == (4, BLOCK) and mesh_nodes.shape[0] == 2 * BLOCK
    if sizes == [4, 2, 2] and small and grid_features.shape[2] == 512:
        return paired(grid_features, owners, adjacency, mesh_nodes, *parameters)
    return general(grid_features, owners, adjacency, mesh_nodes, *parameters)


def solution(mesh):
    return jax.shard_map(
        local,
        mesh=mesh,
        in_specs=(
            P(("groups", "shard", "sub"), None, "head"),
            P(("groups", "shard", "sub"), None),
            P(("groups", "shard", "sub"), None),
            P(("groups", "shard", "sub"), None),
            P(),
            P(None, "head"),
            P(None, "head"),
            P(None, "head"),
            P("head", None),
            P(None, "head"),
            P("head", None),
        ),
        out_specs=P(("groups", "shard", "sub"), None, "head"),
        check_vma=False,
    )
```

```python
import functools
import math

import jax
import jax.numpy as jnp
from jax import lax
from jax.experimental import pallas as pl
from jax.experimental.pallas import tpu as pltpu
from jax.sharding import PartitionSpec as P

D = 1024
HEAD_DIM = 64
CAP = 2
BLOCK = 64
QUAD = 4
WIDE = QUAD * HEAD_DIM
TILE = 128
CHUNKS = ((0, 96), (96, 256))
MIB = 1 << 20


epsilon = 1e-05


def dot(a, b):
    return jnp.dot(a, b, preferred_element_type=jnp.float32)


def gelu(x):
    return 0.5 * x * (1.0 + lax.erf(x * (2.0**-0.5)))


def in_hbm(x):
    return pltpu.with_memory_space_constraint(x, pltpu.HBM)


def in_vmem(x):
    return pltpu.with_memory_space_constraint(x, pltpu.VMEM)


def whole(space):
    return pl.BlockSpec(memory_space=space)


def vmem(count):
    return [whole(pltpu.VMEM)] * count


def params(mib):
    return pltpu.CompilerParams(vmem_limit_bytes=mib * MIB)


def mlp_kernel(own, other, gain, wq, wup, wdn, q_out, mlp_out, normed_s):
    half = own.shape[1]
    units = wup.shape[1]
    chunk = units // 4
    x_other = other[...].astype(jnp.float32)
    x_own = own[...].astype(jnp.float32)

    def mean(a, b):
        total = jnp.sum(a, axis=-1, keepdims=True) + jnp.sum(b, axis=-1, keepdims=True)
        return total * (0.5 / half)

    average = mean(x_other, x_own)
    x_other = x_other - average
    x_own = x_own - average
    factor = lax.rsqrt(mean(x_other * x_other, x_own * x_own) + epsilon)
    normed_s[:, :half] = (x_other * factor * gain[:, :half]).astype(jnp.bfloat16)
    normed_s[:, half:] = (x_own * factor * gain[:, half:]).astype(jnp.bfloat16)
    normed = normed_s[...]
    h = lax.axis_index("head")
    queries = jnp.zeros(q_out.shape, jnp.float32)
    for part, head in enumerate((1 - h, h)):
        rows = pl.ds(pl.multiple_of(head * half, half), half)
        queries += dot(normed_s[:, part * half : (part + 1) * half], wq[rows, :])
    q_out[...] = queries.astype(jnp.bfloat16)
    for c in range(units // chunk):
        span = slice(c * chunk, (c + 1) * chunk)
        hidden = gelu(dot(normed, wup[:, span])).astype(jnp.bfloat16)
        term = dot(hidden, wdn[span, :])
        if c == 0:
            mlp_out[...] = term
        else:
            mlp_out[...] += term


def run_mlp(own, other, gain, wq, wup, wdn):
    rows = own.shape[0]
    width = wq.shape[0]
    units = wup.shape[1]
    return pl.pallas_call(
        mlp_kernel,
        out_shape=(
            jax.ShapeDtypeStruct((rows, wq.shape[1]), jnp.bfloat16),
            jax.ShapeDtypeStruct((rows, width), jnp.float32),
        ),
        in_specs=vmem(6),
        out_specs=tuple(vmem(2)),
        scratch_shapes=[pltpu.VMEM((rows, width), jnp.bfloat16)],
        compiler_params=params(16),
        cost_estimate=pl.CostEstimate(
            flops=2 * rows * width * (wq.shape[1] + 2 * units),
            bytes_accessed=2 * width * (wq.shape[1] + 2 * units),
            transcendentals=rows * units,
        ),
        name="mlp",
    )(own, other, gain, in_vmem(wq), wup, wdn)


def pick_kernel(mesh, out, sem):
    first = pl.multiple_of(lax.axis_index("head") * BLOCK, BLOCK)
    copy = pltpu.make_async_copy(mesh.at[pl.ds(first, BLOCK), :], out, sem)
    copy.start()
    copy.wait()


def run_pick(mesh):
    return pl.pallas_call(
        pick_kernel,
        out_shape=jax.ShapeDtypeStruct((BLOCK, mesh.shape[1]), mesh.dtype),
        in_specs=[whole(pltpu.HBM)],
        out_specs=whole(pltpu.VMEM),
        scratch_shapes=[pltpu.SemaphoreType.DMA(())],
        compiler_params=params(4),
        cost_estimate=pl.CostEstimate(flops=0, bytes_accessed=4 * mesh.size, transcendentals=0),
        name="pick",
    )(in_hbm(mesh))


def stage_kernel(axes, *refs):
    sources, targets, sem = refs[: len(axes)], refs[len(axes) : -1], refs[-1]
    h = lax.axis_index("head")
    copies = []

    def add(source, target):
        pieces = 2 if source.shape[0] >= 512 else 1
        rows = source.shape[0] // pieces
        for piece in range(pieces):
            span = pl.ds(piece * rows, rows)
            copies.append(
                pltpu.make_async_copy(
                    source.at[span, :], target.at[span, :], sem.at[len(copies)]
                )
            )
            copies[-1].start()

    for source, target, axis in zip(sources, targets, axes):
        if axis is None:
            add(source, target)
            continue
        if axis == "rest":
            add(source.at[pl.ds(pl.multiple_of((1 - h) * BLOCK, BLOCK), BLOCK), :], target)
            continue
        half = source.shape[axis] // 2
        for part, head in enumerate((1 - h, h)):
            span = pl.ds(pl.multiple_of(head * half, half), half)
            place = pl.ds(part * half, half)
            if axis == 0:
                add(source.at[span, :], target.at[place, :])
            else:
                add(source.at[:, span], target.at[:, place])
    for copy in copies:
        copy.wait()


def run_stage(arrays, axes):
    size = sum(2 * array.size for array in arrays)
    return pl.pallas_call(
        functools.partial(stage_kernel, axes),
        out_shape=tuple(
            jax.ShapeDtypeStruct((BLOCK,) + array.shape[1:] if axis == "rest" else array.shape, array.dtype)
            for array, axis in zip(arrays, axes)
        ),
        in_specs=[whole(pltpu.HBM)] * len(arrays),
        out_specs=tuple(vmem(len(arrays))),
        scratch_shapes=[pltpu.SemaphoreType.DMA((4 * len(arrays),))],
        compiler_params=params(16),
        cost_estimate=pl.CostEstimate(
            flops=2000 * size, bytes_accessed=20 * size, transcendentals=0
        ),
        name="stage",
    )(*(in_hbm(array) for array in arrays))


def project_kernel(*refs):
    pieces, (wk, wv, out) = refs[:-3], refs[-3:]
    width = wk.shape[1]
    rows = jnp.concatenate([piece[...] for piece in pieces], axis=0)
    out[:, :width] = dot(rows, wk[...]).astype(jnp.bfloat16)
    out[:, width:] = dot(rows, wv[...]).astype(jnp.bfloat16)


def run_project(pieces, wk, wv):
    rows = sum(piece.shape[0] for piece in pieces)
    depth, width = wk.shape
    return pl.pallas_call(
        project_kernel,
        out_shape=jax.ShapeDtypeStruct((rows, 2 * width), jnp.bfloat16),
        in_specs=vmem(len(pieces) + 2),
        out_specs=whole(pltpu.VMEM),
        compiler_params=params(8),
        cost_estimate=pl.CostEstimate(
            flops=300 * rows * depth * width,
            bytes_accessed=300 * depth * width + 300 * rows * depth,
            transcendentals=0,
        ),
        name="project",
    )(*pieces, in_vmem(wk), in_vmem(wv))


def table_kernel(mine, sibling, mine_last, sibling_last, table):
    for i, (first, last) in enumerate(((mine, mine_last), (sibling, sibling_last))):
        table[i, : first.shape[0]] = first[...]
        table[i, table.shape[1] - last.shape[0] :] = last[...]


def run_table(mine, sibling, mine_last, sibling_last, blocks):
    return pl.pallas_call(
        table_kernel,
        out_shape=jax.ShapeDtypeStruct((2, blocks) + mine.shape[1:], jnp.bfloat16),
        in_specs=vmem(4),
        out_specs=whole(pltpu.VMEM),
        compiler_params=params(8),
        cost_estimate=pl.CostEstimate(
            flops=0, bytes_accessed=80 * mine.size, transcendentals=0
        ),
        name="table",
    )(mine, sibling, mine_last, sibling_last)


def pieces_of(c):
    low, high = CHUNKS[c]
    pieces = []
    for tile in range(low // BLOCK, -(-high // BLOCK)):
        first, last = max(low, tile * BLOCK), min(high, (tile + 1) * BLOCK)
        rows = slice(first - tile * BLOCK, last - tile * BLOCK)
        pieces.append((tile, rows, slice(first - low, last - low)))
    return pieces


def project_out(c, att, mlp, wo, send, keep):
    half = att.shape[1]
    h = lax.axis_index("head")
    pieces = pieces_of(c)
    start, stop = pieces[0][0] * TILE, (pieces[-1][0] + 1) * TILE

    def write(head):
        for out, first, place in ((send, 0, 1 - head), (keep, half, head)):
            extra = mlp[:, first + start : first + stop]
            total = extra + dot(att[...], wo[:, place * half + start : place * half + stop])
            total = total.astype(jnp.bfloat16)
            for tile, rows, spot in pieces:
                columns = slice(tile * TILE - start, (tile + 1) * TILE - start)
                for t in range(out.shape[0]):
                    block = slice(t * BLOCK + rows.start, t * BLOCK + rows.stop)
                    out[t, spot, :] = total[block, columns]

    for head in range(2):
        pl.when(h == head)(functools.partial(write, head))


def attend_kernel(
    adjacency, q, mine, sibling, table_in, mlp, wo, send, keep, att, table, stacked_s, near_s, sem
):
    del table_in
    s = lax.axis_index("shard")
    h = lax.axis_index("head")
    u = lax.axis_index("sub")
    half = wo.shape[0]
    ready = table.shape[1] - 2 * mine.shape[0]
    copy = pltpu.make_async_copy(adjacency, near_s, sem)
    copy.start()
    for i, part in enumerate((mine, sibling)):
        table[i, ready : ready + part.shape[0]] = part[...]
    rows_of = lax.broadcasted_iota(jnp.int32, (WIDE, WIDE), 0) // BLOCK
    lanes_of = lax.broadcasted_iota(jnp.int32, (WIDE, WIDE), 1) // HEAD_DIM
    diagonal = rows_of == lanes_of
    lane_head = lax.broadcasted_iota(jnp.int32, (BLOCK, WIDE), 1) // HEAD_DIM
    scale = HEAD_DIM**-0.5 * math.log2(math.e)
    groups = half // WIDE
    steps = near_s.shape[0] * groups
    for step in range(steps):
        b, g = divmod(step, groups)
        columns = slice(g * WIDE, (g + 1) * WIDE)
        stacked = jnp.concatenate([q[b * BLOCK : (b + 1) * BLOCK, columns]] * QUAD, axis=0)
        stacked_s[step] = jnp.where(diagonal, stacked, jnp.zeros_like(stacked))
    copy.wait()
    places = []
    for b in range(near_s.shape[0]):
        places.append([])
        for j in range(near_s.shape[1]):
            m = near_s[b, j]
            part = lax.rem(m, 2)
            core = lax.rem(m // 2, 2)
            distance = s ^ (m // 4)
            part = jnp.where(distance <= 1, part, part ^ h)
            places[b].append((core ^ u, distance * 2 + part))

    def scores_of(step):
        b, g = divmod(step, groups)
        columns = slice(g * WIDE, (g + 1) * WIDE)
        keys = jnp.concatenate([table[i, p, :, columns] for i, p in places[b]], axis=0)
        return lax.dot_general(
            stacked_s[step], keys, (((1,), (1,)), ((), ())), preferred_element_type=jnp.float32
        )

    scores = scores_of(0)
    for step in range(steps):
        following = scores_of(step + 1) if step + 1 < steps else None
        b, g = divmod(step, groups)
        columns = slice(half + g * WIDE, half + (g + 1) * WIDE)
        values = jnp.concatenate([table[i, p, :, columns] for i, p in places[b]], axis=0)
        highest = jnp.max(scores, axis=-1, keepdims=True)
        weights = jnp.exp2((scores - highest) * scale)
        total = jnp.sum(weights, axis=-1, keepdims=True)
        mixed = dot(weights.astype(jnp.bfloat16), values) * (1.0 / total)
        merged = mixed[0:BLOCK, :]
        for i in range(1, QUAD):
            merged = jnp.where(lane_head == i, mixed[i * BLOCK : (i + 1) * BLOCK, :], merged)
        rows = slice(b * BLOCK, (b + 1) * BLOCK)
        att[rows, g * WIDE : (g + 1) * WIDE] = merged.astype(jnp.bfloat16)
        scores = following
    project_out(0, att, mlp, wo, send, keep)


def run_attend(adjacency, q, mine, sibling, table, mlp, wo):
    rows, half = q.shape
    size = CHUNKS[0][1] - CHUNKS[0][0]
    part = jax.ShapeDtypeStruct((rows // BLOCK, size, TILE), jnp.bfloat16)
    blocks = table.shape[0] * table.shape[1]
    send, keep, att, _ = pl.pallas_call(
        attend_kernel,
        out_shape=(
            part,
            part,
            jax.ShapeDtypeStruct(q.shape, jnp.bfloat16),
            jax.ShapeDtypeStruct(table.shape, jnp.bfloat16),
        ),
        in_specs=[whole(pl.ANY)] + vmem(6),
        out_specs=tuple(vmem(4)),
        scratch_shapes=[
            pltpu.VMEM((rows // BLOCK * (half // WIDE), WIDE, WIDE), jnp.bfloat16),
            pltpu.SMEM(adjacency.shape, jnp.int32),
            pltpu.SemaphoreType.DMA(()),
        ],
        input_output_aliases={4: 3},
        compiler_params=params(16),
        cost_estimate=pl.CostEstimate(
            flops=20 * rows * half * (D + 8 * 8 * BLOCK),
            bytes_accessed=40 * blocks * BLOCK * half + 20 * half * D + 40 * rows * D,
            transcendentals=rows * 8 * BLOCK * half // HEAD_DIM,
        ),
        name="attend",
    )(adjacency, q, mine, sibling, table, mlp, in_vmem(wo))
    return send, keep, att


def run_project_out(c, att, mlp, wo):
    rows, half = att.shape
    size = CHUNKS[c][1] - CHUNKS[c][0]
    part = jax.ShapeDtypeStruct((rows // BLOCK, size, TILE), jnp.bfloat16)
    return pl.pallas_call(
        functools.partial(project_out, c),
        out_shape=(part, part),
        in_specs=vmem(3),
        out_specs=tuple(vmem(2)),
        compiler_params=params(8),
        cost_estimate=pl.CostEstimate(
            flops=200 * rows * half * D,
            bytes_accessed=200 * half * D,
            transcendentals=0,
        ),
        name="project_out",
    )(att, mlp, in_vmem(wo))


def plan_kernel(owners, masks):
    s = lax.axis_index("shard")
    count = owners.shape[1]
    names = [owners[0, t] for t in range(count)]
    for t in range(count):
        same = [(names[e] == names[t]).astype(jnp.int32) for e in range(t)]
        rank = sum(same, jnp.int32(0))
        for d in range(masks.shape[0]):
            for j in range(CAP):
                hit = (names[t] == s ^ d) & (rank == j)
                masks[d, j, t] = jnp.full(masks.shape[3:], hit.astype(jnp.float32))


def run_plan(owners, shards):
    return pl.pallas_call(
        plan_kernel,
        out_shape=jax.ShapeDtypeStruct((shards, CAP, owners.shape[1], 8, 128), jnp.float32),
        in_specs=[whole(pltpu.SMEM)],
        out_specs=whole(pltpu.VMEM),
        compiler_params=params(4),
        cost_estimate=pl.CostEstimate(flops=0, bytes_accessed=1 << 18, transcendentals=0),
        name="plan",
    )(owners)


def combine_kernel(chunks, distances, masks, grid_features, *refs):
    keeps, refs = refs[: len(chunks)], refs[len(chunks) :]
    swaps, outs = refs[: len(chunks)], refs[len(chunks) :]
    count = grid_features.shape[0]
    first = CHUNKS[chunks[0]][0]
    for c, keep, swap in zip(chunks, keeps, swaps):
        low, high = CHUNKS[c]
        updated = []
        for t in range(count):
            residual = [
                grid_features[t, rows, tile * TILE : (tile + 1) * TILE]
                for tile, rows, _ in pieces_of(c)
            ]
            residual = jnp.concatenate(residual, axis=0).astype(jnp.float32)
            partials = keep[t].astype(jnp.float32) + swap[t].astype(jnp.float32)
            updated.append(residual + partials)
        for d, out in zip(distances, outs):
            for j in range(CAP):
                chosen = jnp.zeros_like(updated[0])
                for t in range(count):
                    mask = jnp.broadcast_to(masks[d, j, t, 0:1, :], chosen.shape)
                    chosen = jnp.where(mask > 0.5, updated[t], chosen)
                out[j, low - first : high - first, :] = chosen.astype(jnp.bfloat16)


def run_combine(chunks, distances, masks, grid_features, keeps, swaps):
    count = grid_features.shape[0]
    rows, width = CHUNKS[chunks[-1]][1] - CHUNKS[chunks[0]][0], TILE
    slot = jax.ShapeDtypeStruct((CAP, rows, width), jnp.bfloat16)
    return pl.pallas_call(
        functools.partial(combine_kernel, chunks, distances),
        out_shape=(slot,) * len(distances),
        in_specs=vmem(2 + 2 * len(chunks)),
        out_specs=tuple(vmem(len(distances))),
        compiler_params=params(8),
        cost_estimate=pl.CostEstimate(
            flops=60000 * count * rows * width,
            bytes_accessed=400 * rows * width * (3 * count + CAP * len(distances)),
            transcendentals=0,
        ),
        name="combine",
    )(masks, grid_features, *keeps, *swaps)


def place_kernel(spots, *refs):
    out, sem = refs[-2:]
    s = lax.axis_index("shard")
    copies = []
    for ref, (d, chunks) in zip(refs, spots):
        first = CHUNKS[chunks[0]][0]
        slots = pl.ds((s ^ d) * CAP, CAP)
        for c in chunks:
            shift = CHUNKS[c][0] - first
            for tile, rows, spot in pieces_of(c):
                size = rows.stop - rows.start
                source = ref.at[:, pl.ds(spot.start + shift, size), :]
                columns = pl.ds(tile * TILE, TILE)
                target = out.at[slots, pl.ds(rows.start, size), columns]
                copies.append(pltpu.make_async_copy(source, target, sem.at[len(copies)]))
                copies[-1].start()
    for copy in copies:
        copy.wait()


def run_place(spots, arrived, placed, shape):
    count = sum(len(pieces_of(c)) for _, chunks in spots for c in chunks)
    return pl.pallas_call(
        functools.partial(place_kernel, spots),
        out_shape=jax.ShapeDtypeStruct(shape, jnp.bfloat16),
        in_specs=vmem(len(arrived)) + [whole(pltpu.HBM)] * len(placed),
        out_specs=whole(pltpu.HBM),
        scratch_shapes=[pltpu.SemaphoreType.DMA((count,))],
        input_output_aliases={len(arrived): 0} if placed else {},
        compiler_params=params(4),
        cost_estimate=pl.CostEstimate(
            flops=400000 * sum(part.size for part in arrived), bytes_accessed=0, transcendentals=0
        ),
        name="place",
    )(*arrived, *placed)


def crossed(x, distance, size):
    return lax.ppermute(x, "shard", [(i, i ^ distance) for i in range(size)])


def swapped(x, axis):
    return lax.ppermute(x, axis, [(0, 1), (1, 0)])


def paired(
    grid_features,
    owners,
    adjacency,
    mesh_nodes,
    norm_gain,
    query_weight,
    key_weight,
    value_weight,
    output_weight,
    up_weight,
    down_weight,
):
    shards = lax.axis_size("shard")
    count, rows, half = grid_features.shape
    flat = grid_features.reshape(count * rows, half)
    half_unit = run_pick(mesh_nodes)
    far = crossed(half_unit, 2, shards)
    waiting, _ = lax.optimization_barrier((mesh_nodes, half_unit))
    near = crossed(waiting, 1, shards)
    waiting, _ = lax.optimization_barrier((flat, half_unit))
    other = swapped(waiting, "head")
    flat, gain, wup, wdn, rest = run_stage(
        (flat, norm_gain.reshape(1, -1), up_weight, down_weight, mesh_nodes),
        (None, 1, 0, 1, "rest"),
    )
    straight = crossed(rest, 3, shards)
    far, _ = lax.optimization_barrier((far, rest))
    farther = crossed(far, 1, shards)
    far_pair = swapped(far, "head")
    queries, mlp = run_mlp(flat, other, gain, query_weight, wup, wdn)
    queries, mlp, far_pair, near = lax.optimization_barrier((queries, mlp, far_pair, near))
    blocked = (-1, BLOCK, 2 * half)
    mine_a = run_project((in_vmem(mesh_nodes), near, far, far_pair), key_weight, value_weight)
    sibling_a = swapped(mine_a, "sub")
    straight, _ = lax.optimization_barrier((straight, mine_a))
    mine_m = run_project((straight,), key_weight, value_weight)
    sibling_m = swapped(mine_m, "sub")
    parts = [part.reshape(blocked) for part in (mine_a, sibling_a, mine_m, sibling_m)]
    table = run_table(*parts, 2 * shards)
    farther, _ = lax.optimization_barrier((farther, mine_m))
    mine_b = run_project((farther,), key_weight, value_weight)
    sibling_b = swapped(mine_b, "sub")
    send, keep, att = run_attend(
        adjacency, queries, mine_b.reshape(blocked), sibling_b.reshape(blocked), table, mlp, output_weight
    )
    named, _ = lax.optimization_barrier((owners, att))
    masks = run_plan(named.T, shards)
    keeps, swaps, slots, placed = [], [], [], []
    shape = (shards * CAP, rows, half)
    every = tuple(range(len(CHUNKS)))
    for c in every:
        if c > 0:
            send, keep = run_project_out(c, att, mlp, output_weight)
        received = swapped(send, "head")
        if c > 0:
            received, _ = lax.optimization_barrier((received, slots[c - 1][0]))
        slots.append(run_combine((c,), (2, 3), masks, grid_features, (keep,), (received,)))
        keeps.append(keep)
        swaps.append(received)
    swaps[-1], _ = lax.optimization_barrier((swaps[-1], slots[-1][0]))
    near_slots, own_slots = run_combine(every, (1, 0), masks, grid_features, keeps, swaps)
    for c in every:
        spots = [(2, (c,)), (3, (c,))]
        arrived = [crossed(slot, d, shards) for d, slot in zip((2, 3), slots[c])]
        if c == 0:
            spots.append((0, every))
            arrived.append(own_slots)
        if c == every[-1]:
            spots.append((1, every))
            arrived.append(crossed(near_slots, 1, shards))
        placed = [run_place(spots, arrived, placed, shape)]
    return placed[0]


def attend_plain(queries, key_table, value_table, chosen, scaling):
    count = chosen.shape[0]
    picked_keys = key_table[chosen]
    picked_keys = picked_keys.reshape(count, -1, picked_keys.shape[3], picked_keys.shape[4])
    picked_values = value_table[chosen]
    picked_values = picked_values.reshape(count, -1, picked_values.shape[3], picked_values.shape[4])
    scores = (
        jnp.einsum("gqhe,gkhe->ghqk", queries, picked_keys, preferred_element_type=jnp.float32)
        * scaling
    )
    highest = jnp.max(scores, axis=-1, keepdims=True)
    weights = jnp.exp(scores - highest)
    weights = (weights / jnp.sum(weights, axis=-1, keepdims=True)).astype(jnp.bfloat16)
    result = jnp.einsum(
        "ghqk,gkhe->gqhe", weights, picked_values, preferred_element_type=jnp.float32
    )
    return result.astype(jnp.bfloat16)


def general(
    grid_features,
    owners,
    adjacency,
    mesh_nodes,
    norm_gain,
    query_weight,
    key_weight,
    value_weight,
    output_weight,
    up_weight,
    down_weight,
):
    shard_count = lax.axis_size("shard")
    head_count = lax.axis_size("head")
    local_blocks, block_rows, feature_share = grid_features.shape
    slots = shard_count * CAP
    owner_col = owners[:, 0]
    position = jnp.arange(local_blocks, dtype=jnp.int32)
    earlier = (owner_col[:, None] == owner_col[None, :]) & (position[None, :] < position[:, None])
    target = owner_col * CAP + jnp.sum(earlier.astype(jnp.int32), axis=1)
    dispatch = (target[:, None] == jnp.arange(slots, dtype=jnp.int32)[None, :]).astype(jnp.bfloat16)
    offset = lax.axis_index("head") * (D // head_count)
    projected = jnp.stack(
        (
            jnp.dot(mesh_nodes, key_weight, preferred_element_type=jnp.float32).astype(
                jnp.bfloat16
            ),
            jnp.dot(mesh_nodes, value_weight, preferred_element_type=jnp.float32).astype(
                jnp.bfloat16
            ),
        )
    )
    tables = lax.all_gather(projected, ("shard", "sub"), axis=1, tiled=True)
    head_local = query_weight.shape[1] // HEAD_DIM
    key_table = tables[0].reshape(-1, block_rows, head_local, HEAD_DIM)
    value_table = tables[1].reshape(-1, block_rows, head_local, HEAD_DIM)
    send_lists = jnp.full((slots, adjacency.shape[1]), -1, jnp.int32).at[target].set(adjacency)
    send_lists = send_lists.reshape(shard_count, CAP, -1)
    complete = lax.all_gather(grid_features, "head", axis=2, tiled=True)
    outgoing = jnp.einsum(
        "gs,gbd->sbd", dispatch, complete, preferred_element_type=jnp.float32
    ).astype(jnp.bfloat16)
    arrived, lists = (
        lax.all_to_all(
            outgoing.reshape(shard_count, CAP, block_rows, D),
            "shard",
            split_axis=0,
            concat_axis=0,
            tiled=True,
        ),
        lax.all_to_all(send_lists, "shard", split_axis=0, concat_axis=0, tiled=True),
    )
    arrived = arrived.reshape(slots, block_rows, D)
    residual = lax.dynamic_slice_in_dim(arrived, offset, D // head_count, 2)
    lists = lists.reshape(slots, -1)
    count = arrived.shape[0]
    values_f = arrived.astype(jnp.float32)
    average = jnp.mean(values_f, axis=-1, keepdims=True)
    centered = values_f - average
    variance = jnp.mean(centered * centered, axis=-1, keepdims=True)
    normed = (centered * lax.rsqrt(variance + epsilon) * norm_gain).astype(jnp.bfloat16)
    flattened = normed.reshape(-1, D)
    queries = jnp.dot(flattened, query_weight, preferred_element_type=jnp.float32).astype(
        jnp.bfloat16
    )
    blocks_each = math.gcd(count, max(1, 512 // block_rows))
    steps_count = count // blocks_each
    queries = queries.reshape(steps_count, blocks_each, block_rows, head_local, HEAD_DIM)

    def attend_step(operands):
        return attend_plain(operands[0], key_table, value_table, operands[1], HEAD_DIM ** (-0.5))

    attended = lax.map(
        attend_step, (queries, jnp.maximum(lists, 0).reshape(steps_count, blocks_each, -1))
    )
    attended = attended.reshape(-1, head_local * HEAD_DIM)
    hidden = jax.nn.gelu(
        jnp.dot(flattened, up_weight, preferred_element_type=jnp.float32), approximate=False
    ).astype(jnp.bfloat16)
    branch = jnp.dot(attended, output_weight, preferred_element_type=jnp.float32)
    branch = branch + jnp.dot(hidden, down_weight, preferred_element_type=jnp.float32)
    branch = branch.reshape(count, block_rows, D)
    reduced = lax.psum_scatter(
        branch.astype(jnp.bfloat16), "head", scatter_dimension=2, tiled=True
    ).astype(jnp.float32)
    occupied = lists[:, 0] >= 0
    summed = residual.astype(jnp.float32) + reduced
    return jnp.where(occupied[:, None, None], summed, 0.0).astype(jnp.bfloat16)


def local(grid_features, owners, adjacency, mesh_nodes, *parameters):
    sizes = [lax.axis_size(axis) for axis in ("shard", "head", "sub")]
    small = grid_features.shape[:2] == (4, BLOCK) and mesh_nodes.shape[0] == 2 * BLOCK
    if sizes == [4, 2, 2] and small and grid_features.shape[2] == 512:
        return paired(grid_features, owners, adjacency, mesh_nodes, *parameters)
    return general(grid_features, owners, adjacency, mesh_nodes, *parameters)


def solution(mesh):
    return jax.shard_map(
        local,
        mesh=mesh,
        in_specs=(
            P(("groups", "shard", "sub"), None, "head"),
            P(("groups", "shard", "sub"), None),
            P(("groups", "shard", "sub"), None),
            P(("groups", "shard", "sub"), None),
            P(),
            P(None, "head"),
            P(None, "head"),
            P(None, "head"),
            P("head", None),
            P(None, "head"),
            P("head", None),
        ),
        out_specs=P(("groups", "shard", "sub"), None, "head"),
        check_vma=False,
    )
```
